32 devices in a mesh: items: 4 (over y, x), heads: 8 (over z, core).
Axes of the slice: x: 2, y: 2, z: 4, core: 2. Of those that a mesh axis runs over, the one named last changes fastest.
Arguments:
- frames: bfloat16 [2, 8192, 1024], P(None, ('items', 'heads')), may hold values from -6 to 6
- cotangent: bfloat16 [2, 8192, 1024], P(None, ('items', 'heads')), may hold values from -6 to 6
- bucket_counts: int32 [2, 4, 2], P(None, 'items'), may hold values from 0 to 4, as said below
- gains: float32 [6, 1024], replicated, may hold values from 0.1 to 1.9
- w_ffn1_in: bfloat16 [1024, 4096], replicated, may hold values from -0.1875 to 0.1875
- w_ffn1_out: bfloat16 [4096, 1024], replicated, may hold values from -0.1875 to 0.1875
- w_qkv: bfloat16 [1024, 3072], replicated, may hold values from -0.1875 to 0.1875
- w_out: bfloat16 [1024, 1024], replicated, may hold values from -1 to 1
- w_point_in: bfloat16 [1024, 2048], replicated, may hold values from -0.1875 to 0.1875
- w_depth: bfloat16 [5, 1024], replicated, may hold values from -2.5 to 2.5
- w_point_out: bfloat16 [1024, 1024], replicated, may hold values from -0.1875 to 0.1875
- w_ffn2_in: bfloat16 [1024, 4096], replicated, may hold values from -0.1875 to 0.1875
- w_ffn2_out: bfloat16 [4096, 1024], replicated, may hold values from -0.1875 to 0.1875
Outputs:
- layer_out: bfloat16 [2, 8192, 1024], P(None, ('items', 'heads'))
- frames_grad: bfloat16 [2, 8192, 1024], P(None, ('items', 'heads'))
- gains_grad: float32 [6, 1024], replicated
- ffn1_in_grad: float32 [1024, 4096], P('heads', 'items')
- ffn1_out_grad: float32 [4096, 1024], P('heads', 'items')
- qkv_grad: float32 [1024, 3072], P('heads', 'items')
- out_grad: float32 [1024, 1024], P('heads', 'items')
- point_in_grad: float32 [1024, 2048], P('heads', 'items')
- depth_grad: float32 [5, 1024], replicated
- point_out_grad: float32 [1024, 1024], P('heads', 'items')
- ffn2_in_grad: float32 [1024, 4096], P('heads', 'items')
- ffn2_out_grad: float32 [4096, 1024], P('heads', 'items')
The draws below stay inside these ranges and needn't reach their ends.
Inputs may be any that keep to these rules, and one draw needn't show every extreme that they name: bucket_counts[m, g] = (n_long, n_short): group g of micro-batch m holds n_long utterances of 1500 frames first, then n_short = (2048 - n_long 1500) // 500 utterances of 500 frames, then any remaining frames as one more utterance.
All inputs are finite; a program needn't handle non-finite values.
Results may differ from the reference program's by a relative error of at most 0.02.
Values may be sent and summed in bfloat16 or wider, within the bound.
No kernel may reach another device: no remote copies, remote signals or barrier semaphores. Data moves between devices by JAX's collectives and lax.ppermute only.
A program may use at most 320 MiB of HBM per device.

```python
import jax
import jax.numpy as jnp
from jax import lax

D = 1024
FF = 4096
HEADS = 16
HEAD_DIM = 64
KERNEL = 5
LONG = 1500
SHORT = 500
MICRO = 2
GROUP = 2048
FRAMES = 8192
N_ITEMS = 4


def draw_bucket_counts(key, part):
    key = jax.random.fold_in(key, 7)
    long_count = jax.random.randint(key, (MICRO, N_ITEMS), 0, GROUP // LONG + 1)
    shorts = (GROUP - long_count * LONG) // SHORT
    return jnp.stack([long_count, shorts], -1).astype(jnp.int32)


def block_scale(rng, shape, pieces, smallest, high):
    factor_of, own = 1.0, jax.random.fold_in(rng, 6)
    for dim, blocks in pieces:
        steps = jnp.exp(jax.random.uniform(jax.random.fold_in(own, dim), (blocks,), jnp.float32, smallest / len(pieces), high / len(pieces)))
        factor_of = factor_of * jnp.repeat(steps, shape[dim] // blocks).reshape([-1 if axis == dim else 1 for axis in range(len(shape))])
    return factor_of


def normal_values(stream_key, extent, spread, reach, pieces=(), kind=jnp.bfloat16):
    values = spread * jax.random.normal(stream_key, extent, jnp.float32)
    if pieces:
        values = values * block_scale(stream_key, extent, pieces, -0.22, 0.18)
    return jnp.clip(values, -reach, reach).astype(kind)


def setup_inputs(seed: int = 0) -> dict:
    streams_of = jax.random.split(jax.random.key(seed), 14)
    return {
        "frames": normal_values(streams_of[0], (MICRO, FRAMES, D), 1.0, 6.0, ((1, 32),)),
        "cotangent": normal_values(streams_of[1], (MICRO, FRAMES, D), 1.0, 6.0, ((1, 32),)),
        "bucket_counts": draw_bucket_counts(jax.random.fold_in(streams_of[13], 71), 0),
        "gains": jnp.clip(1.0 + 0.18 * jax.random.normal(streams_of[3], (6, D), jnp.float32), 0.1, 1.9),
        "w_ffn1_in": normal_values(streams_of[4], (D, FF), D ** -0.5, 0.1875),
        "w_ffn1_out": normal_values(streams_of[5], (FF, D), (FF // 4) ** -0.5, 0.1875),
        "w_qkv": normal_values(streams_of[6], (D, 3 * D), D ** -0.5, 0.1875),
        "w_out": normal_values(streams_of[7], (D, D), (D // 32) ** -0.5, 1.0),
        "w_point_in": normal_values(streams_of[8], (D, 2 * D), D ** -0.5, 0.1875),
        "w_depth": normal_values(streams_of[9], (KERNEL, D), KERNEL ** -0.5, 2.5),
        "w_point_out": normal_values(streams_of[10], (D, D), D ** -0.5, 0.1875),
        "w_ffn2_in": normal_values(streams_of[11], (D, FF), D ** -0.5, 0.1875),
        "w_ffn2_out": normal_values(streams_of[12], (FF, D), (FF // 4) ** -0.5, 0.1875),
    }


@jax.custom_vjp
def low(v):
    return lax.optimization_barrier(v.astype(jnp.bfloat16)).astype(jnp.float32)

@jax.custom_vjp
def low_back(v):
    return v

def low_keep(v):
    return (low(v), None)

def low_pass(kept, grad):
    return (grad,)

def back_keep(v):
    return (v, None)

def back_low(kept, grad):
    return (low(grad),)
low.defvjp(low_keep, low_pass)
low_back.defvjp(back_keep, back_low)
EPS = 1e-05
MASKED = -1e+30
ROPE_BASE = 10000.0

def matmul(left, right):
    return jnp.dot(left, right, precision=lax.Precision.HIGHEST, preferred_element_type=jnp.float32)

def layer_norm(stream, gain_row):
    centred = stream - lax.optimization_barrier(jnp.mean(stream, -1, keepdims=True))
    return centred * lax.rsqrt(lax.optimization_barrier(jnp.mean(centred * centred, -1, keepdims=True)) + EPS) * gain_row

def rope_tables(position, half_dim):
    freqs = jnp.exp(-jnp.log(jnp.float32(ROPE_BASE)) * jnp.arange(half_dim, dtype=jnp.float32) / half_dim)
    angles = (position.astype(jnp.float32)[:, None] * freqs[None, :])[:, None, :]
    return (jnp.cos(angles), jnp.sin(angles))

def rotate(field, cosines, sines):
    half_dim = field.shape[-1] // 2
    first = field[..., :half_dim]
    second = field[..., half_dim:]
    return jnp.concatenate([first * cosines - second * sines, second * cosines + first * sines], -1)

def segment_ids(position, long_count, short_count, group_len):
    long_end = long_count * LONG
    short_end = long_end + short_count * SHORT
    segments = jnp.where(position < long_end, position // LONG, long_count + (position - long_end) // SHORT)
    segments = jnp.where(position < short_end, segments, long_count + short_count)
    return jnp.where((position < 0) | (position >= group_len), -1, segments).astype(jnp.int32)

def feed_forward(stream, gain_row, weight_in, weight_out):
    entered = low(layer_norm(stream, gain_row))
    pre_act = low_back(matmul(entered, weight_in))
    hidden = low(pre_act * jax.nn.sigmoid(pre_act))
    return low_back(matmul(hidden, weight_out))

def attention(queries, keys_all, values_all, segments):
    group_len = queries.shape[0]
    block_rows = min(512, group_len)
    starts = jnp.arange(group_len // block_rows, dtype=jnp.int32) * block_rows
    score_scale = HEAD_DIM ** (-0.5)

    @jax.checkpoint
    def one_block(begin_row):
        query_block = lax.dynamic_slice_in_dim(queries, begin_row, block_rows, 0)
        seg_block = lax.dynamic_slice_in_dim(segments, begin_row, block_rows, 0)
        scores = low_back(jnp.einsum('qhd,khd->hqk', query_block, keys_all, precision=lax.Precision.HIGHEST) * score_scale)
        same_utt = seg_block[:, None] == segments[None, :]
        scores = jnp.where(same_utt[None], scores, MASKED)
        row_max = lax.optimization_barrier(jnp.max(scores, -1, keepdims=True))
        powers = jnp.exp(scores - row_max)
        weights_low = low(powers / lax.optimization_barrier(jnp.sum(powers, -1, keepdims=True)))
        return jnp.einsum('hqk,khd->qhd', weights_low, values_all, precision=lax.Precision.HIGHEST)
    return lax.map(one_block, starts).reshape(group_len, HEADS, HEAD_DIM)

def depthwise(gated_low, w_depth, segments):
    reach_half = (KERNEL - 1) // 2
    group_len = gated_low.shape[0]
    padded = jnp.pad(gated_low, ((reach_half, reach_half), (0, 0)))
    seg_padded = jnp.pad(segments, (reach_half, reach_half), constant_values=-1)
    depth_out = jnp.zeros_like(gated_low)
    for offset in range(KERNEL):
        same_utt = (seg_padded[offset:offset + group_len] == segments)[:, None]
        depth_out = depth_out + w_depth[offset] * jnp.where(same_utt, padded[offset:offset + group_len], 0.0)
    return depth_out

def group_layer(stream, segments, params):
    gains, w_ffn1_in, w_ffn1_out, w_qkv, w_out, w_point_in, w_depth, w_point_out, w_ffn2_in, w_ffn2_out = params
    group_len = stream.shape[0]
    stream_one = stream + 0.5 * feed_forward(stream, gains[0], w_ffn1_in, w_ffn1_out)
    att_entered = low(layer_norm(stream_one, gains[1]))
    projected = low_back(matmul(att_entered, w_qkv))
    cosines, sines = rope_tables(jnp.arange(group_len, dtype=jnp.int32), HEAD_DIM // 2)
    head_shape = (group_len, HEADS, HEAD_DIM)
    queries = low_back(low(rotate(projected[:, :D].reshape(head_shape), cosines, sines)))
    keys_all = low_back(low(rotate(projected[:, D:2 * D].reshape(head_shape), cosines, sines)))
    values_all = low_back(low(projected[:, 2 * D:])).reshape(head_shape)
    context = attention(queries, keys_all, values_all, segments).reshape(group_len, D)
    context = low_back(low(context))
    stream_two = stream_one + low_back(matmul(context, w_out))
    conv_entered = low(layer_norm(stream_two, gains[2]))
    pointwise = low_back(matmul(conv_entered, w_point_in))
    gated_low = low(pointwise[:, :D] * jax.nn.sigmoid(pointwise[:, D:]))
    depth_out = low_back(depthwise(gated_low, w_depth, segments))
    normed = layer_norm(depth_out, gains[3])
    mixed = low(normed * jax.nn.sigmoid(normed))
    stream_three = stream_two + low_back(matmul(mixed, w_point_out))
    stream_four = stream_three + 0.5 * feed_forward(stream_three, gains[4], w_ffn2_in, w_ffn2_out)
    return layer_norm(stream_four, gains[5])

def reference(frames, cotangent, bucket_counts, gains, w_ffn1_in, w_ffn1_out, w_qkv, w_out, w_point_in, w_depth, w_point_out, w_ffn2_in, w_ffn2_out):
    params = tuple((weight.astype(jnp.float32) for weight in (gains, w_ffn1_in, w_ffn1_out, w_qkv, w_out, w_point_in, w_depth, w_point_out, w_ffn2_in, w_ffn2_out)))
    group_total = MICRO * N_ITEMS
    inputs = frames.astype(jnp.float32).reshape(group_total, GROUP, D)
    counts = bucket_counts.reshape(group_total, 2)
    position = jnp.arange(GROUP, dtype=jnp.int32)
    segments = jax.vmap(lambda count_pair: segment_ids(position, count_pair[0], count_pair[1], GROUP))(counts)

    def forward(weights, streams):

        def layer_step(carried, element):
            return (carried, group_layer(element[0], element[1], weights))
        unused, results = lax.scan(jax.checkpoint(layer_step), jnp.zeros((), jnp.float32), (streams, segments))
        return results
    results, pullback = jax.vjp(forward, params, inputs)
    grad_params, grad_inputs = pullback(cotangent.astype(jnp.float32).reshape(group_total, GROUP, D))
    full_shape = (MICRO, N_ITEMS * GROUP, D)
    return (results.reshape(full_shape).astype(jnp.bfloat16), grad_inputs.reshape(full_shape).astype(jnp.bfloat16), grad_params[0], grad_params[1], grad_params[2], grad_params[3], grad_params[4], grad_params[5], grad_params[6], grad_params[7], grad_params[8], grad_params[9])
```

```python
import functools

import jax
import jax.numpy as jnp
from jax import lax
from jax.experimental import pallas as pl
from jax.experimental.pallas import tpu as pltpu
from jax.sharding import PartitionSpec as P

HEADS = 16
KERNEL = 5
LONG = 1500
SHORT = 500
EPS = 1e-05
ROPE_BASE = 10000.0
BLOCK = 256
LANES = 128
BIG = 1e30
VMEM_LIMIT = 56 << 20
F32 = jnp.float32
BF16 = jnp.bfloat16
NN = (((1,), (0,)), ((), ()))
NT = (((1,), (1,)), ((), ()))
EVERY = ("items", "heads")


def dot(left, right, dims=NN):
    return lax.dot_general(left, right, dims, preferred_element_type=F32)


def matmul_left(left, right):
    return lax.dot_general(left, right, (((0,), (0,)), ((), ())), preferred_element_type=F32)


def silu_slope(field):
    gate_sig = jax.nn.sigmoid(field)
    return gate_sig * (1.0 + field * (1.0 - gate_sig))


def layer_norm(field, gain_row):
    centred = field - jnp.mean(field, -1, keepdims=True)
    inverse = lax.rsqrt(jnp.mean(centred * centred, -1, keepdims=True) + EPS)
    normed = centred * inverse
    return (normed * gain_row, normed, inverse)


def norm_back(upstream, normed, inverse, gain_row):
    scaled = upstream * gain_row
    through = inverse * (
        scaled
        - jnp.mean(scaled, -1, keepdims=True)
        - normed * jnp.mean(scaled * normed, -1, keepdims=True)
    )
    return (through, jnp.sum(upstream * normed, 0, keepdims=True))


def segment_ids(position, long_count, short_count, group_len):
    long_end = long_count * LONG
    short_end = long_end + short_count * SHORT
    segments = jnp.where(
        position < long_end, position // LONG, long_count + (position - long_end) // SHORT
    )
    segments = jnp.where(position < short_end, segments, long_count + short_count)
    return jnp.where((position < 0) | (position >= group_len), -1, segments)


def compiler_params():
    return pltpu.CompilerParams(vmem_limit_bytes=VMEM_LIMIT)


def whole(shape):
    return pl.BlockSpec(shape, lambda *_: (0,) * len(shape))


def cost(flops, bytes_accessed, transcendentals=0):
    return pl.CostEstimate(
        flops=flops, bytes_accessed=bytes_accessed, transcendentals=transcendentals
    )


def head_lanes(shape, head, size):
    lane = lax.broadcasted_iota(jnp.int32, shape, 1)
    return (lane >= head * size) & (lane < (head + 1) * size)


def split_three(v):
    hi = v.astype(BF16).astype(F32)
    rest = v - hi
    mid = rest.astype(BF16).astype(F32)
    return (hi, mid, rest - mid)


def spread_columns(columns, shape):
    lane = lax.broadcasted_iota(jnp.int32, shape, 1)
    out = jnp.zeros(shape, F32)
    for place, column in enumerate(columns):
        out = jnp.where(lane == place, column, out)
    return out


def attn_fwd_kernel(heads, size, group, low_ref, high_ref, qkv_ref, segc_ref, out_ref, full_ref, lse_ref, kcat, v_all, s_scr):
    step = pl.program_id(0)
    width = heads * size
    blocks = group // BLOCK

    @pl.when(step == 0)
    def _():
        k = qkv_ref[:, 1].reshape(group, width)
        seg = segc_ref[...]
        lane = lax.broadcasted_iota(jnp.int32, (group, LANES), 1)
        kcat[:, :width] = k
        if width < LANES:
            kcat[:, width:LANES] = jnp.zeros((group, LANES - width), BF16)
        kcat[:, LANES:] = jnp.where(lane == seg, 0.0, -BIG).astype(BF16)
        v_all[...] = qkv_ref[:, 2].reshape(group, width)

    chunk = qkv_ref.shape[2]
    per = BLOCK // chunk if BLOCK > chunk else 1
    rows = pl.ds(pl.multiple_of(step * BLOCK, BLOCK), BLOCK)
    if BLOCK == chunk:
        q = qkv_ref[step, 0]
    else:
        q = qkv_ref[pl.ds(step * per, per), 0].reshape(BLOCK, width)
    q = q.astype(F32) * (size ** -0.5)
    lane = lax.broadcasted_iota(jnp.int32, (BLOCK, LANES), 1)
    member = jnp.where(lane == segc_ref[rows, :], 1.0, 0.0).astype(BF16)
    queries = []
    for head in range(heads):
        mine = q if heads == 1 else jnp.where(head_lanes(q.shape, head, size), q, 0.0)
        mine = mine.astype(BF16)
        if width < LANES:
            mine = jnp.concatenate([mine, jnp.zeros((BLOCK, LANES - width), BF16)], 1)
        queries.append(jnp.concatenate([mine, member], 1))
    low, high = low_ref[step], high_ref[step]

    def scores(j, tops):
        keys = kcat[pl.ds(pl.multiple_of(j * BLOCK, BLOCK), BLOCK), :]
        new = []
        for head in range(heads):
            s = dot(queries[head], keys, NT)
            s_scr[head, j] = s
            top = tops[head]
            for part in range(BLOCK // LANES):
                top = jnp.maximum(top, s[:, part * LANES:(part + 1) * LANES])
            new.append(top)
        return tuple(new)

    start = tuple(jnp.full((BLOCK, LANES), -BIG, F32) for _ in range(heads))
    tops = lax.fori_loop(low, high, scores, start)
    tops = [jnp.max(t, 1, keepdims=True) for t in tops]
    tops = [jnp.broadcast_to(t, (BLOCK, LANES)) for t in tops]

    def weigh(j, carried):
        sums, accs = carried
        values = v_all[pl.ds(pl.multiple_of(j * BLOCK, BLOCK), BLOCK), :]
        new_sums, new_accs = [], []
        for head in range(heads):
            total = sums[head]
            parts = []
            for part in range(BLOCK // LANES):
                p = jnp.exp(s_scr[head, j, :, part * LANES:(part + 1) * LANES] - tops[head])
                total = total + p
                parts.append(p.astype(BF16))
            new_sums.append(total)
            new_accs.append(accs[head] + dot(jnp.concatenate(parts, 1), values))
        return (tuple(new_sums), tuple(new_accs))

    zeros = tuple(jnp.zeros((BLOCK, LANES), F32) for _ in range(heads))
    blank = tuple(jnp.zeros((BLOCK, width), F32) for _ in range(heads))
    sums, accs = lax.fori_loop(low, high, weigh, (zeros, blank))
    result = None
    for head in range(heads):
        total = jnp.sum(sums[head], 1, keepdims=True)
        mine = accs[head] / total
        result = mine if result is None else jnp.where(head_lanes(mine.shape, head, size), mine, result)
        lse_ref[head] = tops[head] + jnp.log(jnp.broadcast_to(total, (BLOCK, LANES)))
    full_ref[...] = result
    out_ref[...] = result.astype(BF16)


def attend_forward(qkv, seg_column, low, high, size):
    sources, _, chunk, width = qkv.shape
    group = sources * chunk
    heads = width // size
    steps = group // BLOCK
    smem = pl.BlockSpec(memory_space=pltpu.SMEM)
    return pl.pallas_call(
        functools.partial(attn_fwd_kernel, heads, size, group),
        grid=(steps,),
        in_specs=[
            smem,
            smem,
            pl.BlockSpec(qkv.shape, lambda i: (0, 0, 0, 0)),
            pl.BlockSpec((group, 1), lambda i: (0, 0)),
        ],
        out_specs=[
            pl.BlockSpec((BLOCK, width), lambda i: (i, 0)),
            pl.BlockSpec((BLOCK, width), lambda i: (i, 0)),
            pl.BlockSpec((heads, BLOCK, LANES), lambda i: (0, i, 0)),
        ],
        out_shape=[
            jax.ShapeDtypeStruct((group, width), BF16),
            jax.ShapeDtypeStruct((group, width), F32),
            jax.ShapeDtypeStruct((heads, group, LANES), F32),
        ],
        scratch_shapes=[
            pltpu.VMEM((group, 2 * LANES), BF16),
            pltpu.VMEM((group, width), BF16),
            pltpu.VMEM((heads, steps, BLOCK, BLOCK), F32),
        ],
        compiler_params=pltpu.CompilerParams(vmem_limit_bytes=VMEM_LIMIT),
        cost_estimate=pl.CostEstimate(flops=16 * group * group * LANES, bytes_accessed=6 << 20, transcendentals=heads * group * group),
        name="attend_forward",
    )(low, high, qkv, seg_column)


def attn_bwd_kernel(heads, size, group, low_ref, high_ref, qkv_ref, segc_ref, full_ref, lse_ref, grad_ref, out_ref, qcat, gcat, k_turned, dq_turned):
    step = pl.program_id(0)
    width = heads * size
    blocks = group // BLOCK
    chunk = qkv_ref.shape[2]
    per = BLOCK // chunk if BLOCK > chunk else 1

    def block_of(part, j):
        if BLOCK == chunk:
            return qkv_ref[j, part]
        return qkv_ref[pl.ds(j * per, per), part].reshape(BLOCK, width)

    def grad_of(j):
        if BLOCK == chunk:
            return grad_ref[j]
        return grad_ref[pl.ds(j * per, per)].reshape(BLOCK, width)

    def widened(v):
        if width < LANES:
            return jnp.concatenate([v, jnp.zeros((BLOCK, LANES - width), v.dtype)], 1)
        return v

    @pl.when(step == 0)
    def _():
        dq_turned[...] = jnp.zeros_like(dq_turned)

        def prepare(j, _):
            rows = pl.ds(pl.multiple_of(j * BLOCK, BLOCK), BLOCK)
            lane = lax.broadcasted_iota(jnp.int32, (BLOCK, LANES), 1)
            seg = segc_ref[rows, :]
            q = widened(block_of(0, j).astype(F32) * (size ** -0.5))
            g = widened(grad_of(j).astype(F32))
            o = widened(full_ref[rows, :])
            product = g * o
            member = jnp.where(lane == seg + 3, 1.0, 0.0)
            for head in range(heads):
                own = head_lanes((BLOCK, LANES), head, size)
                lse = lse_ref[head, rows, :]
                tail = jnp.where(lane < 3, -spread_columns(split_three(lse), (BLOCK, LANES)), member)
                delta = jnp.broadcast_to(jnp.sum(jnp.where(own, product, 0.0), 1, keepdims=True), (BLOCK, LANES))
                qcat[head, rows, :LANES] = jnp.where(own, q, 0.0).astype(BF16)
                qcat[head, rows, LANES:] = tail.astype(BF16)
                gcat[head, rows, :LANES] = jnp.where(own, g, 0.0).astype(BF16)
                gcat[head, rows, LANES:] = (-spread_columns(split_three(delta), (BLOCK, LANES))).astype(BF16)
            k = widened(block_of(1, j).astype(F32))
            k_turned[j] = jnp.transpose(k).astype(BF16)
            return 0

        lax.fori_loop(0, blocks, prepare, 0)

    lane = lax.broadcasted_iota(jnp.int32, (BLOCK, LANES), 1)
    rows = pl.ds(pl.multiple_of(step * BLOCK, BLOCK), BLOCK)
    seg = segc_ref[rows, :]
    tail = jnp.where(lane < 3, 1.0, jnp.where(lane == seg + 3, 0.0, -BIG)).astype(BF16)
    keys = jnp.concatenate([widened(block_of(1, step)), tail], 1)
    ones = jnp.where(lane < 3, 1.0, 0.0).astype(BF16)
    values = jnp.concatenate([widened(block_of(2, step)), ones], 1)

    def one(j, carried):
        dk, dv = carried
        cols = pl.ds(pl.multiple_of(j * BLOCK, BLOCK), BLOCK)
        for head in range(heads):
            qc = qcat[head, cols, :]
            gc = gcat[head, cols, :]
            p = jnp.exp(dot(keys, qc, NT))
            ds = (p * dot(values, gc, NT)).astype(BF16)
            dv = dv + dot(p.astype(BF16), gc[:, :LANES])
            dk = dk + dot(ds, qc[:, :LANES])
            turned = k_turned[step, head * size:(head + 1) * size, :]
            dq_turned[j, head * size:(head + 1) * size, :] += dot(turned, ds)
        return (dk, dv)

    zero = jnp.zeros((BLOCK, LANES), F32)
    dk, dv = lax.fori_loop(low_ref[step], high_ref[step], one, (zero, zero))
    dk = dk[:, :width].astype(BF16)
    dv = dv[:, :width].astype(BF16)
    if BLOCK == chunk:
        out_ref[step, 1] = dk
        out_ref[step, 2] = dv
    else:
        out_ref[pl.ds(step * per, per), 1] = dk.reshape(per, chunk, width)
        out_ref[pl.ds(step * per, per), 2] = dv.reshape(per, chunk, width)

    @pl.when(step == blocks - 1)
    def _():
        def finish(j, _):
            dq = (jnp.transpose(dq_turned[j]) * (size ** -0.5))[:, :width].astype(BF16)
            if BLOCK == chunk:
                out_ref[j, 0] = dq
            else:
                out_ref[pl.ds(j * per, per), 0] = dq.reshape(per, chunk, width)
            return 0

        lax.fori_loop(0, blocks, finish, 0)


def attend_backward(qkv, seg_column, low, high, size, full, lse, grad):
    sources, _, chunk, width = qkv.shape
    group = sources * chunk
    heads = width // size
    steps = group // BLOCK
    smem = pl.BlockSpec(memory_space=pltpu.SMEM)
    whole = lambda shape: pl.BlockSpec(shape, lambda i: (0,) * len(shape))
    return pl.pallas_call(
        functools.partial(attn_bwd_kernel, heads, size, group),
        grid=(steps,),
        in_specs=[
            smem,
            smem,
            whole(qkv.shape),
            whole((group, 1)),
            whole(full.shape),
            whole(lse.shape),
            whole(grad.shape),
        ],
        out_specs=whole(qkv.shape),
        out_shape=jax.ShapeDtypeStruct(qkv.shape, BF16),
        scratch_shapes=[
            pltpu.VMEM((heads, group, 2 * LANES), BF16),
            pltpu.VMEM((heads, group, 2 * LANES), BF16),
            pltpu.VMEM((steps, LANES, BLOCK), BF16),
            pltpu.VMEM((steps, LANES, BLOCK), F32),
        ],
        compiler_params=pltpu.CompilerParams(vmem_limit_bytes=VMEM_LIMIT),
        cost_estimate=pl.CostEstimate(flops=32 * group * group * LANES, bytes_accessed=9 << 20, transcendentals=heads * group * group),
        name="attend_backward",
    )(low, high, qkv, seg_column, full, lse, grad)


def block_ranges(seg):
    blocks = seg.reshape(-1, BLOCK)
    first, last = blocks[:, 0], blocks[:, -1]
    low = jnp.sum(seg[None, :] < first[:, None], 1) // BLOCK
    high = (jnp.sum(seg[None, :] <= last[:, None], 1) + BLOCK - 1) // BLOCK
    return (low.astype(jnp.int32), high.astype(jnp.int32))


def ffn_fwd_kernel(x_ref, gain_ref, win_ref, wout_ref, out_ref, pre_ref, entered, total):
    step = pl.program_id(0)

    @pl.when(step == 0)
    def _():
        entered[...] = layer_norm(x_ref[...].astype(F32), gain_ref[...])[0].astype(BF16)
        total[...] = jnp.zeros_like(total)

    pre = dot(entered[...], win_ref[...])
    pre_ref[...] = pre
    hidden = (pre * jax.nn.sigmoid(pre)).astype(BF16)
    total[...] += dot(hidden, wout_ref[...])

    @pl.when(step == pl.num_programs(0) - 1)
    def _():
        out_ref[...] = x_ref[...].astype(F32) + 0.5 * total[...]


def ffn_forward(stream, gain_row, weight_in, weight_out):
    rows, model = stream.shape
    hidden = weight_in.shape[1]
    wide = 512
    return pl.pallas_call(
        ffn_fwd_kernel,
        grid=(hidden // wide,),
        in_specs=[
            whole((rows, model)),
            whole((1, model)),
            pl.BlockSpec((model, wide), lambda s: (0, s)),
            pl.BlockSpec((wide, model), lambda s: (s, 0)),
        ],
        out_specs=[whole((rows, model)), pl.BlockSpec((rows, wide), lambda s: (0, s))],
        out_shape=[
            jax.ShapeDtypeStruct((rows, model), F32),
            jax.ShapeDtypeStruct((rows, hidden), F32),
        ],
        scratch_shapes=[pltpu.VMEM((rows, model), BF16), pltpu.VMEM((rows, model), F32)],
        compiler_params=compiler_params(),
        cost_estimate=cost(4 * rows * model * hidden, 4 * model * hidden + 4 * rows * hidden),
        name="ffn_forward",
    )(stream, gain_row, weight_in, weight_out)


def turned_rows(value, rows_each, core, target):
    model = value.shape[1]
    shares = model // rows_each
    for share in range(shares):
        part = jnp.transpose(value[:, share * rows_each : (share + 1) * rows_each]).astype(BF16)
        place = (share // 2) * rows_each + jnp.where(
            core == share % 2, 0, (shares // 2) * rows_each
        )
        target[pl.ds(pl.multiple_of(place, rows_each), rows_each), :] = part


def ffn_bwd_kernel(
    core_ref, x_ref, gain_ref, up_ref, pre_ref, win_ref, wout_ref,
    down_ref, gain_grad_ref, in_keep, in_send, out_keep, out_send,
    entered, turned, turned_up, total,
):
    step = pl.program_id(0)
    core = core_ref[0]
    model = x_ref.shape[1]
    rows_each = in_keep.shape[1]
    half = model // 2

    @pl.when(step == 0)
    def _():
        shaped = layer_norm(x_ref[...].astype(F32), gain_ref[...])[0]
        turned_rows(shaped, rows_each, core, turned)
        halved = 0.5 * up_ref[...]
        turned_up[...] = jnp.transpose(halved).astype(BF16)
        entered[...] = halved.astype(BF16)
        total[...] = jnp.zeros_like(total)

    pre = pre_ref[...]
    gate = jax.nn.sigmoid(pre)
    hidden = (pre * gate).astype(BF16)
    grad_hidden = dot(entered[...], wout_ref[...], NT)
    grad_pre = (grad_hidden * (gate * (1.0 + pre * (1.0 - gate)))).astype(BF16)
    total[...] += dot(grad_pre, win_ref[...], NT)
    grad_in = dot(turned[...], grad_pre).astype(BF16)
    in_keep[...] = grad_in[:half].reshape(in_keep.shape)
    in_send[...] = grad_in[half:].reshape(in_send.shape)
    grad_out = dot(turned_up[...], hidden).astype(BF16)
    wide = grad_out.shape[1]

    def place(target):
        for group in range(model // rows_each):
            target[0, :, group * wide : (group + 1) * wide] = grad_out[
                group * rows_each : (group + 1) * rows_each
            ]

    @pl.when(step % 2 == 0)
    def _():
        place(out_keep)

    @pl.when(step % 2 == 1)
    def _():
        place(out_send)

    @pl.when(step == pl.num_programs(0) - 1)
    def _():
        gain = gain_ref[...]
        normed, inverse = layer_norm(x_ref[...].astype(F32), gain)[1:]
        through, grad_gain = norm_back(total[...], normed, inverse, gain)
        down_ref[...] = (up_ref[...] + through).astype(down_ref.dtype)
        gain_grad_ref[...] = grad_gain


def ffn_backward(upstream, stream, pre_act, gain_row, weight_in, weight_out, heads, core, down_type):
    rows, model = stream.shape
    hidden = weight_in.shape[1]
    wide = hidden // heads
    rows_each = model // heads
    places = heads // 2

    def at(s, core):
        return 2 * (s // 2) + (s + core[0]) % 2

    share = jax.ShapeDtypeStruct((places, rows_each, hidden), BF16)
    grid_spec = pltpu.PrefetchScalarGridSpec(
        num_scalar_prefetch=1,
        grid=(heads,),
        in_specs=[
            whole((rows, model)),
            whole((1, model)),
            whole((rows, model)),
            pl.BlockSpec((rows, wide), lambda s, core: (0, at(s, core))),
            pl.BlockSpec((model, wide), lambda s, core: (0, at(s, core))),
            pl.BlockSpec((wide, model), lambda s, core: (at(s, core), 0)),
        ],
        out_specs=[
            whole((rows, model)),
            whole((1, model)),
            pl.BlockSpec((places, rows_each, wide), lambda s, core: (0, 0, at(s, core))),
            pl.BlockSpec((places, rows_each, wide), lambda s, core: (0, 0, at(s, core))),
            pl.BlockSpec((1, rows_each, hidden), lambda s, core: (s // 2, 0, 0)),
            pl.BlockSpec((1, rows_each, hidden), lambda s, core: (s // 2, 0, 0)),
        ],
        scratch_shapes=[
            pltpu.VMEM((rows, model), BF16),
            pltpu.VMEM((model, rows), BF16),
            pltpu.VMEM((model, rows), BF16),
            pltpu.VMEM((rows, model), F32),
        ],
    )
    return pl.pallas_call(
        ffn_bwd_kernel,
        grid_spec=grid_spec,
        out_shape=[
            jax.ShapeDtypeStruct((rows, model), down_type),
            jax.ShapeDtypeStruct((1, model), F32),
            share, share, share, share,
        ],
        compiler_params=compiler_params(),
        cost_estimate=cost(
            8 * rows * model * hidden, 8 * model * hidden + 4 * rows * hidden + 8 * rows * model
        ),
        name="ffn_backward",
    )(core, stream, gain_row, upstream, pre_act, weight_in, weight_out)


def turn(field, cosines, sines, size):
    lane = lax.broadcasted_iota(jnp.int32, field.shape, 1)
    half = size // 2
    width = field.shape[1]
    swapped = jnp.where(
        lane % size < half,
        pltpu.roll(field, width - half, 1),
        pltpu.roll(field, half, 1),
    )
    return field * cosines + swapped * sines


def rope_tables(position, size, width):
    half = size // 2
    lane = jnp.arange(width, dtype=jnp.int32)
    freqs = jnp.exp(
        -jnp.log(jnp.float32(ROPE_BASE)) * jnp.arange(half, dtype=jnp.float32) / half
    )
    angles = position.astype(jnp.float32)[:, None] * freqs[None, :]
    cosines, sines = jnp.cos(angles), jnp.sin(angles)
    repeats = width // size
    return (
        jnp.tile(jnp.concatenate([cosines, cosines], 1), (1, repeats)),
        jnp.tile(jnp.concatenate([-sines, sines], 1), (1, repeats)),
    )


def qkv_fwd_kernel(size, x_ref, gain_ref, wq_ref, wk_ref, wv_ref, cos_ref, sin_ref, *rest):
    outs, entered = rest[:-1], rest[-1]
    step = pl.program_id(0)

    @pl.when(step == 0)
    def _():
        entered[...] = layer_norm(x_ref[...], gain_ref[...])[0].astype(BF16)

    frames = outs[0].shape[2]
    width = outs[0].shape[3]
    for place, weight in enumerate((wq_ref, wk_ref, wv_ref)):
        made = dot(entered[...], weight[...])
        for number, out in enumerate(outs):
            part = made[number * frames : (number + 1) * frames]
            if place < 2:
                part = turn(part, cos_ref[...], sin_ref[...], size)
            part = part.astype(BF16)
            for target in range(out.shape[0]):
                out[target, place] = part[:, target * width : (target + 1) * width]


def qkv_forward(stream, gain_row, weight, cosines, sines, heads, batches, size):
    rows, model = stream.shape
    wide = cosines.shape[1]
    steps = model // wide
    width = model // heads
    frames = rows // batches
    out = jax.ShapeDtypeStruct((heads, 3, frames, width), BF16)
    return pl.pallas_call(
        functools.partial(qkv_fwd_kernel, size),
        grid=(steps,),
        in_specs=[
            whole((rows, model)),
            whole((1, model)),
            pl.BlockSpec((model, wide), lambda s: (0, s)),
            pl.BlockSpec((model, wide), lambda s: (0, steps + s)),
            pl.BlockSpec((model, wide), lambda s: (0, 2 * steps + s)),
            whole(cosines.shape),
            whole(sines.shape),
        ],
        out_specs=[
            pl.BlockSpec((wide // width, 3, frames, width), lambda s: (s, 0, 0, 0))
            for _ in range(batches)
        ],
        out_shape=[out] * batches,
        scratch_shapes=[pltpu.VMEM((rows, model), BF16)],
        compiler_params=compiler_params(),
        cost_estimate=cost(6 * rows * model * model, 6 * model * model + 10 * rows * model),
        name="qkv_forward",
    )(stream, gain_row, weight, weight, weight, cosines, sines)


def qkv_bwd_kernel(size, batches, steps, core_ref, *refs):
    backs, refs = refs[:batches], refs[batches:]
    (x_ref, gain_ref, up_ref, weight_ref, cos_ref, sin_ref,
     down_ref, gain_grad_ref, keep, send, turned, total) = refs
    step = pl.program_id(0)
    model = x_ref.shape[1]
    rows_each = keep.shape[1]
    half = model // 2

    @pl.when(step == 0)
    def _():
        shaped = layer_norm(x_ref[...], gain_ref[...])[0]
        turned_rows(shaped, rows_each, core_ref[0], turned)
        total[...] = jnp.zeros_like(total)

    parts = []
    rotated = step < 2 * steps
    cosines = jnp.where(rotated, cos_ref[...], 1.0)
    sines = jnp.where(rotated, -sin_ref[...], 0.0)
    for back in backs:
        field = jnp.concatenate([back[i, 0] for i in range(back.shape[0])], 1).astype(F32)
        parts.append(turn(field, cosines, sines, size).astype(BF16))
    grad = jnp.concatenate(parts, 0)
    total[...] += dot(grad, weight_ref[...], NT)
    made = dot(turned[...], grad).astype(BF16)
    keep[...] = made[:half].reshape(keep.shape)
    send[...] = made[half:].reshape(send.shape)

    @pl.when(step == pl.num_programs(0) - 1)
    def _():
        gain = gain_ref[...]
        normed, inverse = layer_norm(x_ref[...], gain)[1:]
        through, grad_gain = norm_back(total[...], normed, inverse, gain)
        down_ref[...] = up_ref[...] + through
        gain_grad_ref[...] = grad_gain


def qkv_backward(backs, stream, gain_row, upstream, weight, cosines, sines, heads, core, size):
    rows, model = stream.shape
    wide = cosines.shape[1]
    steps = model // wide
    width = model // heads
    frames = backs[0].shape[2]
    rows_each = model // heads
    places = heads // 2
    batches = len(backs)
    share = jax.ShapeDtypeStruct((places, rows_each, 3 * model), BF16)
    grid_spec = pltpu.PrefetchScalarGridSpec(
        num_scalar_prefetch=1,
        grid=(3 * steps,),
        in_specs=[
            pl.BlockSpec(
                (wide // width, 1, frames, width), lambda s, core: (s % steps, s // steps, 0, 0)
            )
            for _ in range(batches)
        ]
        + [
            whole((rows, model)),
            whole((1, model)),
            whole((rows, model)),
            pl.BlockSpec((model, wide), lambda s, core: (0, s)),
            whole(cosines.shape),
            whole(sines.shape),
        ],
        out_specs=[
            whole((rows, model)),
            whole((1, model)),
            pl.BlockSpec((places, rows_each, wide), lambda s, core: (0, 0, s)),
            pl.BlockSpec((places, rows_each, wide), lambda s, core: (0, 0, s)),
        ],
        scratch_shapes=[pltpu.VMEM((model, rows), BF16), pltpu.VMEM((rows, model), F32)],
    )
    return pl.pallas_call(
        functools.partial(qkv_bwd_kernel, size, batches, steps),
        grid_spec=grid_spec,
        out_shape=[
            jax.ShapeDtypeStruct((rows, model), F32),
            jax.ShapeDtypeStruct((1, model), F32),
            share,
            share,
        ],
        compiler_params=compiler_params(),
        cost_estimate=cost(12 * rows * model * model, 12 * model * model + 20 * rows * model),
        name="qkv_backward",
    )(core, *backs, stream, gain_row, upstream, weight, cosines, sines)


def flipped(axis_bit, count):
    axis, bit = axis_bit
    items, heads = count
    if axis == "items":
        return [(i * heads + h, (i ^ bit) * heads + h) for i in range(items) for h in range(heads)]
    return [(i * heads + h, i * heads + (h ^ bit)) for i in range(items) for h in range(heads)]


def swap(value, axis_bit):
    count = (lax.axis_size("items"), lax.axis_size("heads"))
    return lax.ppermute(value, EVERY, flipped(axis_bit, count))


def plus(left, right):
    return (left.astype(F32) + right.astype(F32)).astype(BF16)


def halves(value, rows_each):
    places = value.shape[0] // (2 * rows_each)
    cut = value.reshape(places, 2, rows_each, value.shape[1])
    core = lax.axis_index("heads") % 2
    return tuple(
        lax.dynamic_index_in_dim(cut, which, 1, keepdims=False) for which in (core, 1 - core)
    )


def columns(value, start, size):
    return lax.dynamic_slice_in_dim(value, start * size, size, 2)


def scatter(keep, send):
    items = lax.axis_size("items")
    value = plus(keep, swap(send, ("heads", 1)))
    places, rows, wide = value.shape
    size = wide // items
    if items == 4:
        own = lax.axis_index("items")
        top, low = value[:, : rows // 2], value[:, rows // 2 :]
        across, along = own ^ 1, own ^ 2
        beyond = own ^ 3
        got_top = swap(
            jnp.concatenate([columns(top, across, size), columns(top, beyond, size)], 1),
            ("items", 1),
        )
        got_low = swap(
            jnp.concatenate([columns(low, along, size), columns(low, beyond, size)], 1),
            ("items", 2),
        )
        half = rows // 2
        send_top = plus(columns(top, along, size), got_top[:, half:])
        keep_top = plus(columns(top, own, size), got_top[:, :half])
        send_low = plus(columns(low, across, size), got_low[:, half:])
        keep_low = plus(columns(low, own, size), got_low[:, :half])
        value = jnp.concatenate(
            [
                plus(keep_top, swap(send_top, ("items", 2))),
                plus(keep_low, swap(send_low, ("items", 1))),
            ],
            1,
        )
    else:
        value = lax.psum_scatter(value, "items", scatter_dimension=2, tiled=True)
    heads = lax.axis_size("heads")
    groups = [[core + 2 * z for z in range(heads // 2)] for core in range(2)]
    value = lax.psum_scatter(
        value, "heads", scatter_dimension=0, tiled=False, axis_index_groups=groups
    )
    return value


def sum_everywhere(value):
    for axis in EVERY:
        bit = 1
        while bit < lax.axis_size(axis):
            value = value + swap(value, (axis, bit))
            bit *= 2
    return value


def edges(block, width):
    count = lax.axis_size("heads")
    forward = [(i, i + 1) for i in range(count - 1)]
    backward = [(target, source) for source, target in forward]
    low = lax.ppermute(block[:, block.shape[1] - width :], "heads", forward)
    high = lax.ppermute(block[:, :width], "heads", backward)
    return jnp.concatenate([low, block, high], axis=1)


def body(
    frames, cotangent, bucket_counts, gains, w_ffn1_in, w_ffn1_out, w_qkv, w_out,
    w_point_in, w_depth, w_point_out, w_ffn2_in, w_ffn2_out,
):
    batches, here, model = frames.shape
    head_ways = lax.axis_size("heads")
    items = lax.axis_size("items")
    group_len = here * head_ways
    size = model // HEADS
    reach = (KERNEL - 1) // 2
    rows = batches * here
    rows_each = model // head_ways
    place = lax.axis_index("heads")
    core = (place % 2).astype(jnp.int32).reshape(1)
    first = place * here
    cosines, sines = rope_tables(
        first + jnp.arange(here, dtype=jnp.int32), size, max(2 * LANES, model // head_ways)
    )
    depth_rows = w_depth.astype(F32)
    gain = [gains[i : i + 1] for i in range(6)]
    wide_position = first - reach + jnp.arange(here + 2 * reach, dtype=jnp.int32)
    group_position = jnp.arange(group_len, dtype=jnp.int32)
    seg_wide = []
    seg_group = []
    for number in range(batches):
        counts = bucket_counts[number, 0]
        seg_wide.append(segment_ids(wide_position, counts[0], counts[1], group_len))
        seg_group.append(segment_ids(group_position, counts[0], counts[1], group_len))
    seg_wide = jnp.stack(seg_wide, 0)
    seg_own = seg_wide[:, reach : reach + here]
    ranges = [block_ranges(seg) for seg in seg_group]

    stream = frames.reshape(rows, model)
    stream_one, pre_one = ffn_forward(stream, gain[0], w_ffn1_in, w_ffn1_out)
    sent = qkv_forward(stream_one, gain[1], w_qkv, cosines, sines, head_ways, batches, size)
    qkv = [
        lax.all_to_all(part, "heads", split_axis=0, concat_axis=0, tiled=True) for part in sent
    ]
    contexts, fulls, lses = [], [], []
    for number in range(batches):
        out, full, lse = attend_forward(
            qkv[number], seg_group[number][:, None], *ranges[number], size
        )
        contexts.append(
            lax.all_to_all(
                out.reshape(head_ways, here, -1), "heads", split_axis=0, concat_axis=0, tiled=True
            )
        )
        fulls.append(full)
        lses.append(lse)
    context = jnp.concatenate(
        [part.transpose(1, 0, 2).reshape(here, model) for part in contexts], 0
    )
    stream_two = stream_one + dot(context, w_out)
    shaped, conv_normed, conv_inverse = layer_norm(stream_two, gain[2])
    conv_entered = shaped.astype(BF16)
    pointwise = dot(conv_entered, w_point_in)
    linear = pointwise[:, :model]
    sigmoid_gate = jax.nn.sigmoid(pointwise[:, model:])
    gated_low = (linear * sigmoid_gate).astype(BF16).reshape(batches, here, model)
    widened = edges(gated_low, reach)
    depth_out = jnp.zeros((batches, here, model), F32)
    for offset in range(KERNEL):
        same = (seg_wide[:, offset : offset + here] == seg_own)[:, :, None]
        depth_out = depth_out + depth_rows[offset] * jnp.where(
            same, widened[:, offset : offset + here], 0.0
        )
    depth_out = depth_out.reshape(rows, model)
    depth_shaped, depth_normed, depth_inverse = layer_norm(depth_out, gain[3])
    mixed_low = (depth_shaped * jax.nn.sigmoid(depth_shaped)).astype(BF16)
    stream_three = stream_two + dot(mixed_low, w_point_out)
    stream_four, pre_two = ffn_forward(stream_three, gain[4], w_ffn2_in, w_ffn2_out)
    shaped, final_normed, final_inverse = layer_norm(stream_four, gain[5])
    layer_out = shaped.astype(BF16).reshape(frames.shape)
    grad_four, gain_five = norm_back(
        cotangent.reshape(rows, model).astype(F32), final_normed, final_inverse, gain[5]
    )
    grad_three, gain_four, *shares_two = ffn_backward(
        grad_four, stream_three, pre_two, gain[4], w_ffn2_in, w_ffn2_out, head_ways, core, F32
    )
    f2_in = scatter(*shares_two[:2])
    f2_out = scatter(*shares_two[2:])
    grad_mix = grad_three.astype(BF16)
    point_out = scatter(*halves(matmul_left(mixed_low, grad_mix).astype(BF16), rows_each))
    grad_norm_in = dot(grad_mix, w_point_out, NT) * silu_slope(depth_shaped)
    grad_depth, gain_three = norm_back(grad_norm_in, depth_normed, depth_inverse, gain[3])
    grad_depth_low = grad_depth.astype(BF16).reshape(batches, here, model)
    grad_widened = edges(grad_depth_low, reach)
    grad_depth_full = grad_depth_low.astype(F32)
    taps = []
    grad_gated = jnp.zeros((batches, here, model), F32)
    for offset in range(KERNEL):
        same = (seg_wide[:, offset : offset + here] == seg_own)[:, :, None]
        taps.append(
            jnp.sum(
                jnp.where(same, grad_depth_full * widened[:, offset : offset + here], 0.0), (0, 1)
            )
        )
        mirror = 2 * reach - offset
        same_back = (seg_wide[:, mirror : mirror + here] == seg_own)[:, :, None]
        grad_gated = grad_gated + depth_rows[offset] * jnp.where(
            same_back, grad_widened[:, mirror : mirror + here], 0.0
        )
    grad_gated = grad_gated.reshape(rows, model)
    grad_point = jnp.concatenate(
        [grad_gated * sigmoid_gate, grad_gated * linear * sigmoid_gate * (1.0 - sigmoid_gate)], 1
    ).astype(BF16)
    through, gain_two = norm_back(
        dot(grad_point, w_point_in, NT), conv_normed, conv_inverse, gain[2]
    )
    grad_two = grad_three + through
    grad_attn_out = grad_two.astype(BF16)
    grad_context = dot(grad_attn_out, w_out, NT).astype(BF16)
    backs = []
    for number in range(batches):
        part = grad_context[number * here : (number + 1) * here]
        part = part.reshape(here, head_ways, -1).transpose(1, 0, 2)
        grad_heads = lax.all_to_all(part, "heads", split_axis=0, concat_axis=0, tiled=True)
        grads = attend_backward(
            qkv[number], seg_group[number][:, None], *ranges[number], size,
            fulls[number], lses[number], grad_heads,
        )
        backs.append(lax.all_to_all(grads, "heads", split_axis=0, concat_axis=0, tiled=True))
    point_in = scatter(*halves(matmul_left(conv_entered, grad_point).astype(BF16), rows_each))
    out_proj = scatter(*halves(matmul_left(context, grad_attn_out).astype(BF16), rows_each))
    grad_one, gain_one, *shares_qkv = qkv_backward(
        backs, stream_one, gain[1], grad_two, w_qkv, cosines, sines, head_ways, core, size
    )
    qkv_grad = scatter(*shares_qkv)
    grad_zero, gain_zero, *shares_one = ffn_backward(
        grad_one, stream, pre_one, gain[0], w_ffn1_in, w_ffn1_out, head_ways, core, BF16
    )
    f1_in = scatter(*shares_one[:2])
    f1_out = scatter(*shares_one[2:])
    small = sum_everywhere(
        jnp.concatenate(
            [gain_zero, gain_one, gain_two, gain_three, gain_four, gain_five]
            + [tap[None] for tap in taps],
            0,
        )
    )
    hidden = w_ffn1_in.shape[1]

    def unfolded(share):
        each, wide = share.shape
        span = hidden // head_ways
        parts = [share[:, i * span : (i + 1) * span] for i in range(wide // span)]
        return jnp.concatenate(parts, 0).T.astype(F32)

    return (
        layer_out,
        grad_zero.reshape(frames.shape),
        small[:6],
        f1_in.astype(F32),
        unfolded(f1_out),
        qkv_grad.astype(F32),
        out_proj.astype(F32),
        point_in.astype(F32),
        small[6:],
        point_out.astype(F32),
        f2_in.astype(F32),
        unfolded(f2_out),
    )


def solution(mesh):
    split = P(None, EVERY, None)
    shares = P("heads", "items")
    in_specs = (split, split, P(None, "items", None)) + (P(),) * 10
    out_specs = (split, split, P(), shares, shares, shares, shares, shares, P()) + (shares,) * 3
    return jax.shard_map(body, mesh=mesh, in_specs=in_specs, out_specs=out_specs, check_vma=False)
```

```python
import functools

import jax
import jax.numpy as jnp
from jax import lax
from jax.experimental import pallas as pl
from jax.experimental.pallas import tpu as pltpu
from jax.sharding import PartitionSpec as P

HEADS = 16
KERNEL = 5
LONG = 1500
SHORT = 500
EPS = 1e-05
ROPE_BASE = 10000.0
BLOCK = 256
LANES = 128
BIG = 1e30
VMEM_LIMIT = 56 << 20
F32 = jnp.float32
BF16 = jnp.bfloat16
NN = (((1,), (0,)), ((), ()))
NT = (((1,), (1,)), ((), ()))
EVERY = ("items", "heads")


def dot(left, right, dims=NN):
    return lax.dot_general(left, right, dims, preferred_element_type=F32)


def matmul_left(left, right):
    return lax.dot_general(left, right, (((0,), (0,)), ((), ())), preferred_element_type=F32)


def silu_slope(field):
    gate_sig = jax.nn.sigmoid(field)
    return gate_sig * (1.0 + field * (1.0 - gate_sig))


def layer_norm(field, gain_row):
    centred = field - jnp.mean(field, -1, keepdims=True)
    inverse = lax.rsqrt(jnp.mean(centred * centred, -1, keepdims=True) + EPS)
    normed = centred * inverse
    return (normed * gain_row, normed, inverse)


def norm_back(upstream, normed, inverse, gain_row):
    scaled = upstream * gain_row
    through = inverse * (
        scaled
        - jnp.mean(scaled, -1, keepdims=True)
        - normed * jnp.mean(scaled * normed, -1, keepdims=True)
    )
    return (through, jnp.sum(upstream * normed, 0, keepdims=True))


def segment_ids(position, long_count, short_count, group_len):
    long_end = long_count * LONG
    short_end = long_end + short_count * SHORT
    segments = jnp.where(
        position < long_end, position // LONG, long_count + (position - long_end) // SHORT
    )
    segments = jnp.where(position < short_end, segments, long_count + short_count)
    return jnp.where((position < 0) | (position >= group_len), -1, segments)


def compiler_params():
    return pltpu.CompilerParams(vmem_limit_bytes=VMEM_LIMIT)


def whole(shape):
    return pl.BlockSpec(shape, lambda *_: (0,) * len(shape))


def cost(flops, bytes_accessed, transcendentals=0):
    return pl.CostEstimate(
        flops=flops, bytes_accessed=bytes_accessed, transcendentals=transcendentals
    )


def segment_bounds(counts, place, group):
    longs, shorts = counts
    long_end = longs * LONG
    short_end = long_end + shorts * SHORT
    start = jnp.where(place < longs, place * LONG, long_end + (place - longs) * SHORT)
    size = jnp.where(place < longs, LONG, SHORT)
    last = place == longs + shorts
    return (jnp.where(last, short_end, start), jnp.where(last, group, start + size), place <= longs + shorts)


def member_lanes(counts, first, rows, group, shift=0):
    shape = (rows, LANES)
    place = lax.broadcasted_iota(jnp.int32, (8, LANES), 1) - shift
    start, end, there = segment_bounds(counts, place, group)
    start = jnp.where(there & (place >= 0), start, group)
    start, end = start[:1], end[:1]
    frame = first + lax.broadcasted_iota(jnp.int32, shape, 0)
    return (frame >= start) & (frame < end)


def block_range(counts, step, group):
    longs, shorts = counts
    long_end = longs * LONG
    short_end = long_end + shorts * SHORT

    def number(frame):
        place = jnp.where(frame < long_end, frame // LONG, longs + (frame - long_end) // SHORT)
        return jnp.where(frame < short_end, place, longs + shorts)

    first = segment_bounds(counts, number(step * BLOCK), group)[0]
    last = segment_bounds(counts, number(step * BLOCK + BLOCK - 1), group)[1]
    return (first // BLOCK, jnp.minimum(last + BLOCK - 1, group) // BLOCK)


def head_lanes(shape, head, size):
    lane = lax.broadcasted_iota(jnp.int32, shape, 1)
    return (lane >= head * size) & (lane < (head + 1) * size)


def split_three(v):
    hi = v.astype(BF16).astype(F32)
    rest = v - hi
    mid = rest.astype(BF16).astype(F32)
    return (hi, mid, rest - mid)


def spread_columns(columns, shape):
    lane = lax.broadcasted_iota(jnp.int32, shape, 1)
    out = jnp.zeros(shape, F32)
    for place, column in enumerate(columns):
        out = jnp.where(lane == place, column, out)
    return out


def attn_fwd_kernel(heads, size, group, counts_ref, qkv_ref, out_ref, full_ref, lse_ref, kcat, v_all, s_scr):
    step = pl.program_id(0)
    counts = (counts_ref[0], counts_ref[1])
    width = heads * size
    blocks = group // BLOCK

    @pl.when(step == 0)
    def _():
        k = qkv_ref[:, 1].reshape(group, width)
        kcat[:, :width] = k
        if width < LANES:
            kcat[:, width:LANES] = jnp.zeros((group, LANES - width), BF16)
        kcat[:, LANES:] = jnp.where(member_lanes(counts, 0, group, group), 0.0, -BIG).astype(BF16)
        v_all[...] = qkv_ref[:, 2].reshape(group, width)

    chunk = qkv_ref.shape[2]
    per = BLOCK // chunk if BLOCK > chunk else 1
    rows = pl.ds(pl.multiple_of(step * BLOCK, BLOCK), BLOCK)
    if BLOCK == chunk:
        q = qkv_ref[step, 0]
    else:
        q = qkv_ref[pl.ds(step * per, per), 0].reshape(BLOCK, width)
    q = q.astype(F32) * (size ** -0.5)
    member = jnp.where(member_lanes(counts, step * BLOCK, BLOCK, group), 1.0, 0.0).astype(BF16)
    queries = []
    for head in range(heads):
        mine = q if heads == 1 else jnp.where(head_lanes(q.shape, head, size), q, 0.0)
        mine = mine.astype(BF16)
        if width < LANES:
            mine = jnp.concatenate([mine, jnp.zeros((BLOCK, LANES - width), BF16)], 1)
        queries.append(jnp.concatenate([mine, member], 1))
    low, high = block_range(counts, step, group)

    def scores(j, tops):
        keys = kcat[pl.ds(pl.multiple_of(j * BLOCK, BLOCK), BLOCK), :]
        new = []
        for head in range(heads):
            s = dot(queries[head], keys, NT)
            s_scr[head, j] = s
            top = tops[head]
            for part in range(BLOCK // LANES):
                top = jnp.maximum(top, s[:, part * LANES:(part + 1) * LANES])
            new.append(top)
        return tuple(new)

    start = tuple(jnp.full((BLOCK, LANES), -BIG, F32) for _ in range(heads))
    tops = lax.fori_loop(low, high, scores, start)
    tops = [jnp.max(t, 1, keepdims=True) for t in tops]
    tops = [jnp.broadcast_to(t, (BLOCK, LANES)) for t in tops]

    def weigh(j, carried):
        sums, accs = carried
        values = v_all[pl.ds(pl.multiple_of(j * BLOCK, BLOCK), BLOCK), :]
        new_sums, new_accs = [], []
        for head in range(heads):
            total = sums[head]
            parts = []
            for part in range(BLOCK // LANES):
                p = jnp.exp(s_scr[head, j, :, part * LANES:(part + 1) * LANES] - tops[head])
                total = total + p
                parts.append(p.astype(BF16))
            new_sums.append(total)
            new_accs.append(accs[head] + dot(jnp.concatenate(parts, 1), values))
        return (tuple(new_sums), tuple(new_accs))

    zeros = tuple(jnp.zeros((BLOCK, LANES), F32) for _ in range(heads))
    blank = tuple(jnp.zeros((BLOCK, width), F32) for _ in range(heads))
    sums, accs = lax.fori_loop(low, high, weigh, (zeros, blank))
    result = None
    for head in range(heads):
        total = jnp.sum(sums[head], 1, keepdims=True)
        mine = accs[head] / total
        result = mine if result is None else jnp.where(head_lanes(mine.shape, head, size), mine, result)
        lse_ref[head] = tops[head] + jnp.log(jnp.broadcast_to(total, (BLOCK, LANES)))
    full_ref[...] = result
    out_ref[...] = result.astype(BF16)


def attend_forward(qkv, counts, size):
    sources, _, chunk, width = qkv.shape
    group = sources * chunk
    heads = width // size
    steps = group // BLOCK
    smem = pl.BlockSpec(memory_space=pltpu.SMEM)
    return pl.pallas_call(
        functools.partial(attn_fwd_kernel, heads, size, group),
        grid=(steps,),
        in_specs=[
            smem,
            pl.BlockSpec(qkv.shape, lambda i: (0, 0, 0, 0)),
        ],
        out_specs=[
            pl.BlockSpec((BLOCK, width), lambda i: (i, 0)),
            pl.BlockSpec((BLOCK, width), lambda i: (i, 0)),
            pl.BlockSpec((heads, BLOCK, LANES), lambda i: (0, i, 0)),
        ],
        out_shape=[
            jax.ShapeDtypeStruct((group, width), BF16),
            jax.ShapeDtypeStruct((group, width), F32),
            jax.ShapeDtypeStruct((heads, group, LANES), F32),
        ],
        scratch_shapes=[
            pltpu.VMEM((group, 2 * LANES), BF16),
            pltpu.VMEM((group, width), BF16),
            pltpu.VMEM((heads, steps, BLOCK, BLOCK), F32),
        ],
        compiler_params=pltpu.CompilerParams(vmem_limit_bytes=VMEM_LIMIT),
        cost_estimate=pl.CostEstimate(flops=16 * group * group * LANES, bytes_accessed=6 << 20, transcendentals=heads * group * group),
        name="attend_forward",
    )(counts, qkv)


def attn_bwd_kernel(heads, size, group, counts_ref, qkv_ref, full_ref, lse_ref, grad_ref, out_ref, qcat, gcat, k_turned, dq_turned):
    step = pl.program_id(0)
    counts = (counts_ref[0], counts_ref[1])
    width = heads * size
    blocks = group // BLOCK
    chunk = qkv_ref.shape[2]
    per = BLOCK // chunk if BLOCK > chunk else 1

    def block_of(part, j):
        if BLOCK == chunk:
            return qkv_ref[j, part]
        return qkv_ref[pl.ds(j * per, per), part].reshape(BLOCK, width)

    def grad_of(j):
        if BLOCK == chunk:
            return grad_ref[j]
        return grad_ref[pl.ds(j * per, per)].reshape(BLOCK, width)

    def widened(v):
        if width < LANES:
            return jnp.concatenate([v, jnp.zeros((BLOCK, LANES - width), v.dtype)], 1)
        return v

    @pl.when(step == 0)
    def _():
        dq_turned[...] = jnp.zeros_like(dq_turned)

        def prepare(j, _):
            rows = pl.ds(pl.multiple_of(j * BLOCK, BLOCK), BLOCK)
            lane = lax.broadcasted_iota(jnp.int32, (BLOCK, LANES), 1)
            q = widened(block_of(0, j).astype(F32) * (size ** -0.5))
            g = widened(grad_of(j).astype(F32))
            o = widened(full_ref[rows, :])
            product = g * o
            member = jnp.where(member_lanes(counts, j * BLOCK, BLOCK, group, 3), 1.0, 0.0)
            for head in range(heads):
                own = head_lanes((BLOCK, LANES), head, size)
                lse = lse_ref[head, rows, :]
                tail = jnp.where(lane < 3, -spread_columns(split_three(lse), (BLOCK, LANES)), member)
                delta = jnp.broadcast_to(jnp.sum(jnp.where(own, product, 0.0), 1, keepdims=True), (BLOCK, LANES))
                qcat[head, rows, :LANES] = jnp.where(own, q, 0.0).astype(BF16)
                qcat[head, rows, LANES:] = tail.astype(BF16)
                gcat[head, rows, :LANES] = jnp.where(own, g, 0.0).astype(BF16)
                gcat[head, rows, LANES:] = (-spread_columns(split_three(delta), (BLOCK, LANES))).astype(BF16)
            k = widened(block_of(1, j).astype(F32))
            k_turned[j] = jnp.transpose(k).astype(BF16)
            return 0

        lax.fori_loop(0, blocks, prepare, 0)

    lane = lax.broadcasted_iota(jnp.int32, (BLOCK, LANES), 1)
    rows = pl.ds(pl.multiple_of(step * BLOCK, BLOCK), BLOCK)
    member = member_lanes(counts, step * BLOCK, BLOCK, group, 3)
    tail = jnp.where(lane < 3, 1.0, jnp.where(member, 0.0, -BIG)).astype(BF16)
    keys = jnp.concatenate([widened(block_of(1, step)), tail], 1)
    ones = jnp.where(lane < 3, 1.0, 0.0).astype(BF16)
    values = jnp.concatenate([widened(block_of(2, step)), ones], 1)

    def one(j, carried):
        dk, dv = carried
        cols = pl.ds(pl.multiple_of(j * BLOCK, BLOCK), BLOCK)
        for head in range(heads):
            qc = qcat[head, cols, :]
            gc = gcat[head, cols, :]
            p = jnp.exp(dot(keys, qc, NT))
            ds = (p * dot(values, gc, NT)).astype(BF16)
            dv = dv + dot(p.astype(BF16), gc[:, :LANES])
            dk = dk + dot(ds, qc[:, :LANES])
            turned = k_turned[step, head * size:(head + 1) * size, :]
            dq_turned[j, head * size:(head + 1) * size, :] += dot(turned, ds)
        return (dk, dv)

    zero = jnp.zeros((BLOCK, LANES), F32)
    low, high = block_range(counts, step, group)
    dk, dv = lax.fori_loop(low, high, one, (zero, zero))
    dk = dk[:, :width].astype(BF16)
    dv = dv[:, :width].astype(BF16)
    if BLOCK == chunk:
        out_ref[step, 1] = dk
        out_ref[step, 2] = dv
    else:
        out_ref[pl.ds(step * per, per), 1] = dk.reshape(per, chunk, width)
        out_ref[pl.ds(step * per, per), 2] = dv.reshape(per, chunk, width)

    @pl.when(step == blocks - 1)
    def _():
        def finish(j, _):
            dq = (jnp.transpose(dq_turned[j]) * (size ** -0.5))[:, :width].astype(BF16)
            if BLOCK == chunk:
                out_ref[j, 0] = dq
            else:
                out_ref[pl.ds(j * per, per), 0] = dq.reshape(per, chunk, width)
            return 0

        lax.fori_loop(0, blocks, finish, 0)


def attend_backward(qkv, counts, size, full, lse, grad):
    sources, _, chunk, width = qkv.shape
    group = sources * chunk
    heads = width // size
    steps = group // BLOCK
    smem = pl.BlockSpec(memory_space=pltpu.SMEM)
    return pl.pallas_call(
        functools.partial(attn_bwd_kernel, heads, size, group),
        grid=(steps,),
        in_specs=[
            smem,
            whole(qkv.shape),
            whole(full.shape),
            whole(lse.shape),
            whole(grad.shape),
        ],
        out_specs=whole(qkv.shape),
        out_shape=jax.ShapeDtypeStruct(qkv.shape, BF16),
        scratch_shapes=[
            pltpu.VMEM((heads, group, 2 * LANES), BF16),
            pltpu.VMEM((heads, group, 2 * LANES), BF16),
            pltpu.VMEM((steps, LANES, BLOCK), BF16),
            pltpu.VMEM((steps, LANES, BLOCK), F32),
        ],
        compiler_params=pltpu.CompilerParams(vmem_limit_bytes=VMEM_LIMIT),
        cost_estimate=pl.CostEstimate(flops=32 * group * group * LANES, bytes_accessed=9 << 20, transcendentals=heads * group * group),
        name="attend_backward",
    )(counts, qkv, full, lse, grad)


def half_gate(field):
    return 0.5 * jnp.tanh(0.5 * field) + 0.5


def ffn_fwd_kernel(x_ref, gain_ref, win_ref, wout_ref, out_ref, pre_ref, entered, total):
    step = pl.program_id(0)

    @pl.when(step == 0)
    def _():
        entered[...] = layer_norm(x_ref[...].astype(F32), gain_ref[...])[0].astype(BF16)
        total[...] = jnp.zeros_like(total)

    pre = dot(entered[...], win_ref[...])
    pre_ref[...] = pre
    hidden = (pre * half_gate(pre)).astype(BF16)
    total[...] += dot(hidden, wout_ref[...])

    @pl.when(step == pl.num_programs(0) - 1)
    def _():
        out_ref[...] = x_ref[...].astype(F32) + 0.5 * total[...]


def ffn_forward(stream, gain_row, weight_in, weight_out):
    rows, model = stream.shape
    hidden = weight_in.shape[1]
    wide = 512
    return pl.pallas_call(
        ffn_fwd_kernel,
        grid=(hidden // wide,),
        in_specs=[
            whole((rows, model)),
            whole((1, model)),
            pl.BlockSpec((model, wide), lambda s: (0, s)),
            pl.BlockSpec((wide, model), lambda s: (s, 0)),
        ],
        out_specs=[whole((rows, model)), pl.BlockSpec((rows, wide), lambda s: (0, s))],
        out_shape=[
            jax.ShapeDtypeStruct((rows, model), F32),
            jax.ShapeDtypeStruct((rows, hidden), F32),
        ],
        scratch_shapes=[pltpu.VMEM((rows, model), BF16), pltpu.VMEM((rows, model), F32)],
        compiler_params=compiler_params(),
        cost_estimate=cost(4 * rows * model * hidden, 4 * model * hidden + 4 * rows * hidden),
        name="ffn_forward",
    )(stream, gain_row, weight_in, weight_out)


def turned_rows(value, rows_each, core, target):
    model = value.shape[1]
    shares = model // rows_each
    for share in range(shares):
        part = jnp.transpose(value[:, share * rows_each : (share + 1) * rows_each]).astype(BF16)
        place = (share // 2) * rows_each + jnp.where(
            core == share % 2, 0, (shares // 2) * rows_each
        )
        target[pl.ds(pl.multiple_of(place, rows_each), rows_each), :] = part


def ffn_out_kernel(core_ref, up_ref, pre_ref, keep, send, turned_up):
    step = pl.program_id(0)
    model = up_ref.shape[1]
    items, _, rows_each, wide_each = keep.shape

    @pl.when(step == 0)
    def _():
        turned_up[...] = jnp.transpose(0.5 * up_ref[...]).astype(BF16)

    pre = pre_ref[...]
    hidden = (pre * half_gate(pre)).astype(BF16)
    grad = dot(turned_up[...], hidden).astype(BF16)
    wide = grad.shape[1]
    parts = model // rows_each // items

    def place(target):
        for group in range(model // rows_each):
            part = group % parts
            target[group // parts, 0, :, part * wide : (part + 1) * wide] = grad[
                group * rows_each : (group + 1) * rows_each
            ]

    @pl.when(step % 2 == 0)
    def _():
        place(keep)

    @pl.when(step % 2 == 1)
    def _():
        place(send)


def paired(s, core):
    return 2 * (s // 2) + (s + core[0]) % 2


def ffn_out_grad(upstream, pre_act, heads, core, items):
    rows, model = upstream.shape
    hidden = pre_act.shape[1]
    wide = hidden // heads
    rows_each = model // heads
    share = jax.ShapeDtypeStruct((items, heads // 2, rows_each, hidden // items), BF16)
    block = pl.BlockSpec(
        (items, 1, rows_each, hidden // items), lambda s, core: (0, s // 2, 0, 0)
    )
    grid_spec = pltpu.PrefetchScalarGridSpec(
        num_scalar_prefetch=1,
        grid=(heads,),
        in_specs=[
            whole((rows, model)),
            pl.BlockSpec((rows, wide), lambda s, core: (0, paired(s, core))),
        ],
        out_specs=[block, block],
        scratch_shapes=[pltpu.VMEM((model, rows), BF16)],
    )
    return pl.pallas_call(
        ffn_out_kernel,
        grid_spec=grid_spec,
        out_shape=[share, share],
        compiler_params=compiler_params(),
        cost_estimate=cost(2 * rows * model * hidden, 2 * model * hidden + 4 * rows * hidden),
        name="ffn_out_grad",
    )(core, upstream, pre_act)


def ffn_bwd_kernel(
    core_ref, x_ref, gain_ref, up_ref, pre_ref, win_ref, wout_ref,
    down_ref, gain_grad_ref, keep, send, entered, turned, total,
):
    step = pl.program_id(0)
    model = x_ref.shape[1]
    rows_each = keep.shape[2]
    half = model // 2

    @pl.when(step == 0)
    def _():
        shaped = layer_norm(x_ref[...].astype(F32), gain_ref[...])[0]
        turned_rows(shaped, rows_each, core_ref[0], turned)
        entered[...] = (0.5 * up_ref[...]).astype(BF16)
        total[...] = jnp.zeros_like(total)

    pre = pre_ref[...]
    gate = half_gate(pre)
    grad_hidden = dot(entered[...], wout_ref[...], NT)
    grad_pre = (grad_hidden * (gate * (1.0 + pre * (1.0 - gate)))).astype(BF16)
    total[...] += dot(grad_pre, win_ref[...], NT)
    grad_in = dot(turned[...], grad_pre).astype(BF16)
    keep[...] = grad_in[:half].reshape(keep.shape)
    send[...] = grad_in[half:].reshape(send.shape)

    @pl.when(step == pl.num_programs(0) - 1)
    def _():
        gain = gain_ref[...]
        normed, inverse = layer_norm(x_ref[...].astype(F32), gain)[1:]
        through, grad_gain = norm_back(total[...], normed, inverse, gain)
        down_ref[...] = (up_ref[...] + through).astype(down_ref.dtype)
        gain_grad_ref[...] = grad_gain


def ffn_backward(
    upstream, stream, pre_act, gain_row, weight_in, weight_out, heads, core, items, down_type
):
    rows, model = stream.shape
    hidden = weight_in.shape[1]
    wide = hidden // heads
    rows_each = model // heads
    places = heads // 2
    each = hidden // items // wide
    share = jax.ShapeDtypeStruct((items, places, rows_each, hidden // items), BF16)
    block = pl.BlockSpec((1, places, rows_each, wide), lambda s, core: (s // each, 0, 0, s % each))
    grid_spec = pltpu.PrefetchScalarGridSpec(
        num_scalar_prefetch=1,
        grid=(heads,),
        in_specs=[
            whole((rows, model)),
            whole((1, model)),
            whole((rows, model)),
            pl.BlockSpec((rows, wide), lambda s, core: (0, s)),
            pl.BlockSpec((model, wide), lambda s, core: (0, s)),
            pl.BlockSpec((wide, model), lambda s, core: (s, 0)),
        ],
        out_specs=[whole((rows, model)), whole((1, model)), block, block],
        scratch_shapes=[
            pltpu.VMEM((rows, model), BF16),
            pltpu.VMEM((model, rows), BF16),
            pltpu.VMEM((rows, model), F32),
        ],
    )
    return pl.pallas_call(
        ffn_bwd_kernel,
        grid_spec=grid_spec,
        out_shape=[
            jax.ShapeDtypeStruct((rows, model), down_type),
            jax.ShapeDtypeStruct((1, model), F32),
            share,
            share,
        ],
        compiler_params=compiler_params(),
        cost_estimate=cost(
            6 * rows * model * hidden, 6 * model * hidden + 4 * rows * hidden + 8 * rows * model
        ),
        name="ffn_backward",
    )(core, stream, gain_row, upstream, pre_act, weight_in, weight_out)


def turn(field, cosines, sines, size):
    lane = lax.broadcasted_iota(jnp.int32, field.shape, 1)
    half = size // 2
    width = field.shape[1]
    swapped = jnp.where(
        lane % size < half,
        pltpu.roll(field, width - half, 1),
        pltpu.roll(field, half, 1),
    )
    return field * cosines + swapped * sines


def rope_tables(position, size, width):
    half = size // 2
    lane = jnp.arange(width, dtype=jnp.int32)
    freqs = jnp.exp(
        -jnp.log(jnp.float32(ROPE_BASE)) * jnp.arange(half, dtype=jnp.float32) / half
    )
    angles = position.astype(jnp.float32)[:, None] * freqs[None, :]
    cosines, sines = jnp.cos(angles), jnp.sin(angles)
    repeats = width // size
    return (
        jnp.tile(jnp.concatenate([cosines, cosines], 1), (1, repeats)),
        jnp.tile(jnp.concatenate([-sines, sines], 1), (1, repeats)),
    )


def qkv_fwd_kernel(size, x_ref, gain_ref, wq_ref, wk_ref, wv_ref, cos_ref, sin_ref, *rest):
    outs, entered = rest[:-1], rest[-1]
    step = pl.program_id(0)

    @pl.when(step == 0)
    def _():
        entered[...] = layer_norm(x_ref[...], gain_ref[...])[0].astype(BF16)

    frames = outs[0].shape[2]
    width = outs[0].shape[3]
    for place, weight in enumerate((wq_ref, wk_ref, wv_ref)):
        made = dot(entered[...], weight[...])
        for number, out in enumerate(outs):
            part = made[number * frames : (number + 1) * frames]
            if place < 2:
                part = turn(part, cos_ref[...], sin_ref[...], size)
            part = part.astype(BF16)
            for target in range(out.shape[0]):
                out[target, place] = part[:, target * width : (target + 1) * width]


def qkv_forward(stream, gain_row, weight, cosines, sines, heads, batches, size):
    rows, model = stream.shape
    wide = cosines.shape[1]
    steps = model // wide
    width = model // heads
    frames = rows // batches
    out = jax.ShapeDtypeStruct((heads, 3, frames, width), BF16)
    return pl.pallas_call(
        functools.partial(qkv_fwd_kernel, size),
        grid=(steps,),
        in_specs=[
            whole((rows, model)),
            whole((1, model)),
            pl.BlockSpec((model, wide), lambda s: (0, s)),
            pl.BlockSpec((model, wide), lambda s: (0, steps + s)),
            pl.BlockSpec((model, wide), lambda s: (0, 2 * steps + s)),
            whole(cosines.shape),
            whole(sines.shape),
        ],
        out_specs=[
            pl.BlockSpec((wide // width, 3, frames, width), lambda s: (s, 0, 0, 0))
            for _ in range(batches)
        ],
        out_shape=[out] * batches,
        scratch_shapes=[pltpu.VMEM((rows, model), BF16)],
        compiler_params=compiler_params(),
        cost_estimate=cost(6 * rows * model * model, 6 * model * model + 10 * rows * model),
        name="qkv_forward",
    )(stream, gain_row, weight, weight, weight, cosines, sines)


def qkv_bwd_kernel(size, batches, steps, core_ref, *refs):
    backs, refs = refs[:batches], refs[batches:]
    (x_ref, gain_ref, up_ref, weight_ref, cos_ref, sin_ref,
     down_ref, gain_grad_ref, keep, send, turned, total) = refs
    step = pl.program_id(0)
    model = x_ref.shape[1]
    rows_each = keep.shape[2]
    half = model // 2

    @pl.when(step == 0)
    def _():
        shaped = layer_norm(x_ref[...], gain_ref[...])[0]
        turned_rows(shaped, rows_each, core_ref[0], turned)
        total[...] = jnp.zeros_like(total)

    parts = []
    rotated = step < 2 * steps
    cosines = jnp.where(rotated, cos_ref[...], 1.0)
    sines = jnp.where(rotated, -sin_ref[...], 0.0)
    for back in backs:
        field = jnp.concatenate([back[i, 0] for i in range(back.shape[0])], 1).astype(F32)
        parts.append(turn(field, cosines, sines, size).astype(BF16))
    grad = jnp.concatenate(parts, 0)
    total[...] += dot(grad, weight_ref[...], NT)
    made = dot(turned[...], grad).astype(BF16)
    keep[...] = made[:half].reshape(keep.shape)
    send[...] = made[half:].reshape(send.shape)

    @pl.when(step == pl.num_programs(0) - 1)
    def _():
        gain = gain_ref[...]
        normed, inverse = layer_norm(x_ref[...], gain)[1:]
        through, grad_gain = norm_back(total[...], normed, inverse, gain)
        down_ref[...] = up_ref[...] + through
        gain_grad_ref[...] = grad_gain


def qkv_backward(backs, stream, gain_row, upstream, weight, cosines, sines, heads, core, items, size):
    rows, model = stream.shape
    wide = cosines.shape[1]
    steps = model // wide
    width = model // heads
    frames = backs[0].shape[2]
    rows_each = model // heads
    places = heads // 2
    batches = len(backs)
    share = jax.ShapeDtypeStruct((items, places, rows_each, 3 * model // items), BF16)
    each = 3 * model // items // wide
    block = pl.BlockSpec((1, places, rows_each, wide), lambda s, core: (s // each, 0, 0, s % each))
    grid_spec = pltpu.PrefetchScalarGridSpec(
        num_scalar_prefetch=1,
        grid=(3 * steps,),
        in_specs=[
            pl.BlockSpec(
                (wide // width, 1, frames, width), lambda s, core: (s % steps, s // steps, 0, 0)
            )
            for _ in range(batches)
        ]
        + [
            whole((rows, model)),
            whole((1, model)),
            whole((rows, model)),
            pl.BlockSpec((model, wide), lambda s, core: (0, s)),
            whole(cosines.shape),
            whole(sines.shape),
        ],
        out_specs=[
            whole((rows, model)),
            whole((1, model)),
            block,
            block,
        ],
        scratch_shapes=[pltpu.VMEM((model, rows), BF16), pltpu.VMEM((rows, model), F32)],
    )
    return pl.pallas_call(
        functools.partial(qkv_bwd_kernel, size, batches, steps),
        grid_spec=grid_spec,
        out_shape=[
            jax.ShapeDtypeStruct((rows, model), F32),
            jax.ShapeDtypeStruct((1, model), F32),
            share,
            share,
        ],
        compiler_params=compiler_params(),
        cost_estimate=cost(12 * rows * model * model, 12 * model * model + 20 * rows * model),
        name="qkv_backward",
    )(core, *backs, stream, gain_row, upstream, weight, cosines, sines)


def flipped(axis_bit, count):
    axis, bit = axis_bit
    items, heads = count
    if axis == "items":
        return [(i * heads + h, (i ^ bit) * heads + h) for i in range(items) for h in range(heads)]
    return [(i * heads + h, i * heads + (h ^ bit)) for i in range(items) for h in range(heads)]


def swap(value, axis_bit):
    count = (lax.axis_size("items"), lax.axis_size("heads"))
    return lax.ppermute(value, EVERY, flipped(axis_bit, count))


def plus(*terms):
    total = terms[0].astype(F32)
    for term in terms[1:]:
        total = total + term.astype(F32)
    return total.astype(BF16)


def halves(value, rows_each):
    places = value.shape[0] // (2 * rows_each)
    items = lax.axis_size("items")
    cut = value.reshape(places, 2, rows_each, items, -1).transpose(1, 3, 0, 2, 4)
    core = lax.axis_index("heads") % 2
    return tuple(
        lax.dynamic_index_in_dim(cut, which, 0, keepdims=False) for which in (core, 1 - core)
    )


def pick(value, place, dim):
    return lax.dynamic_index_in_dim(value, place, dim, keepdims=False)


class Scatter:
    def __init__(self, keep, send):
        self.keep, self.other = keep, swap(send, ("heads", 1))
        self.sends = (send,)
        self.spread = lax.axis_size("items") == 4

    def first(self):
        if not self.spread:
            return
        own = lax.axis_index("items")
        self.x, self.y = own % 2, own // 2
        shape = (2, 2) + self.keep.shape[1:]
        keep, other = self.keep.reshape(shape), self.other.reshape(shape)
        half = shape[3] // 2
        self.top = [part[:, :, :, :half] for part in (keep, other)]
        self.low = [part[:, :, :, half:] for part in (keep, other)]
        top = plus(*[pick(part, 1 - self.x, 1) for part in self.top])
        low = plus(*[pick(part, 1 - self.y, 0) for part in self.low])
        self.sends = (top, low)
        self.got_top, self.got_low = swap(top, ("items", 1)), swap(low, ("items", 2))

    def second(self):
        if not self.spread:
            return
        top = [pick(part, self.x, 1) for part in self.top] + [self.got_top]
        low = [pick(part, self.y, 0) for part in self.low] + [self.got_low]
        send_top = plus(*[pick(part, 1 - self.y, 0) for part in top])
        send_low = plus(*[pick(part, 1 - self.x, 0) for part in low])
        self.top = [pick(part, self.y, 0) for part in top]
        self.low = [pick(part, self.x, 0) for part in low]
        self.sends = (send_top, send_low)
        self.last_top, self.last_low = swap(send_top, ("items", 2)), swap(send_low, ("items", 1))

    def third(self):
        if self.spread:
            value = jnp.concatenate(
                [plus(*self.top, self.last_top), plus(*self.low, self.last_low)], 1
            )
        else:
            value = plus(self.keep, self.other)[0]
            value = lax.psum_scatter(value, "items", scatter_dimension=2, tiled=True)
        heads = lax.axis_size("heads")
        groups = [[core + 2 * z for z in range(heads // 2)] for core in range(2)]
        self.sends = (value,)
        self.result = lax.psum_scatter(
            value, "heads", scatter_dimension=0, tiled=False, axis_index_groups=groups
        )


def after(value, *scatters):
    sends = [send for scatter in scatters for send in scatter.sends]
    return lax.optimization_barrier((value, *sends))[0]


def sum_everywhere(value):
    for axis in EVERY:
        bit = 1
        while bit < lax.axis_size(axis):
            value = value + swap(value, (axis, bit))
            bit *= 2
    return value


def edges(block, width):
    count = lax.axis_size("heads")
    forward = [(i, i + 1) for i in range(count - 1)]
    backward = [(target, source) for source, target in forward]
    low = lax.ppermute(block[:, block.shape[1] - width :], "heads", forward)
    high = lax.ppermute(block[:, :width], "heads", backward)
    return jnp.concatenate([low, block, high], axis=1)


def body(
    frames, cotangent, bucket_counts, gains, w_ffn1_in, w_ffn1_out, w_qkv, w_out,
    w_point_in, w_depth, w_point_out, w_ffn2_in, w_ffn2_out,
):
    batches, here, model = frames.shape
    head_ways = lax.axis_size("heads")
    items = 4 if lax.axis_size("items") == 4 else 1
    group_len = here * head_ways
    size = model // HEADS
    reach = (KERNEL - 1) // 2
    rows = batches * here
    rows_each = model // head_ways
    place = lax.axis_index("heads")
    core = (place % 2).astype(jnp.int32).reshape(1)
    first = place * here
    cosines, sines = rope_tables(
        first + jnp.arange(here, dtype=jnp.int32), size, max(2 * LANES, model // head_ways)
    )
    depth_rows = w_depth.astype(F32)
    gain = [gains[i : i + 1] for i in range(6)]
    wide_position = first - reach + jnp.arange(here + 2 * reach, dtype=jnp.int32)
    seg_wide = []
    seg_counts = []
    for number in range(batches):
        counts = bucket_counts[number, 0]
        seg_wide.append(segment_ids(wide_position, counts[0], counts[1], group_len))
        seg_counts.append(counts)
    seg_wide = jnp.stack(seg_wide, 0)
    seg_own = seg_wide[:, reach : reach + here]

    stream = frames.reshape(rows, model)
    stream_one, pre_one = ffn_forward(stream, gain[0], w_ffn1_in, w_ffn1_out)
    sent = qkv_forward(stream_one, gain[1], w_qkv, cosines, sines, head_ways, batches, size)
    qkv = [
        lax.all_to_all(part, "heads", split_axis=0, concat_axis=0, tiled=True) for part in sent
    ]
    contexts, fulls, lses = [], [], []
    for number in range(batches):
        out, full, lse = attend_forward(
            qkv[number], seg_counts[number], size
        )
        contexts.append(
            lax.all_to_all(
                out.reshape(head_ways, here, -1), "heads", split_axis=0, concat_axis=0, tiled=True
            )
        )
        fulls.append(full)
        lses.append(lse)
    context = jnp.concatenate(
        [part.transpose(1, 0, 2).reshape(here, model) for part in contexts], 0
    )
    stream_two = stream_one + dot(context, w_out)
    shaped, conv_normed, conv_inverse = layer_norm(stream_two, gain[2])
    conv_entered = shaped.astype(BF16)
    pointwise = dot(conv_entered, w_point_in)
    linear = pointwise[:, :model]
    sigmoid_gate = jax.nn.sigmoid(pointwise[:, model:])
    gated_low = (linear * sigmoid_gate).astype(BF16).reshape(batches, here, model)
    widened = edges(gated_low, reach)
    depth_out = jnp.zeros((batches, here, model), F32)
    for offset in range(KERNEL):
        same = (seg_wide[:, offset : offset + here] == seg_own)[:, :, None]
        depth_out = depth_out + depth_rows[offset] * jnp.where(
            same, widened[:, offset : offset + here], 0.0
        )
    depth_out = depth_out.reshape(rows, model)
    depth_shaped, depth_normed, depth_inverse = layer_norm(depth_out, gain[3])
    mixed_low = (depth_shaped * jax.nn.sigmoid(depth_shaped)).astype(BF16)
    stream_three = stream_two + dot(mixed_low, w_point_out)
    stream_four, pre_two = ffn_forward(stream_three, gain[4], w_ffn2_in, w_ffn2_out)
    shaped, final_normed, final_inverse = layer_norm(stream_four, gain[5])
    layer_out = shaped.astype(BF16).reshape(frames.shape)
    grad_four, gain_five = norm_back(
        cotangent.reshape(rows, model).astype(F32), final_normed, final_inverse, gain[5]
    )
    two_out = Scatter(*ffn_out_grad(grad_four, pre_two, head_ways, core, items))
    grad_four = after(grad_four, two_out)
    grad_three, gain_four, *shares = ffn_backward(
        grad_four, stream_three, pre_two, gain[4], w_ffn2_in, w_ffn2_out, head_ways, core, items, F32
    )
    two_in = Scatter(*shares)
    two_out.first()
    grad_three = after(grad_three, two_in, two_out)
    grad_mix = grad_three.astype(BF16)
    point_out = matmul_left(mixed_low, grad_mix).astype(BF16)
    grad_norm_in = dot(grad_mix, w_point_out, NT) * silu_slope(depth_shaped)
    grad_depth, gain_three = norm_back(grad_norm_in, depth_normed, depth_inverse, gain[3])
    grad_depth_low = grad_depth.astype(BF16).reshape(batches, here, model)
    grad_widened = edges(grad_depth_low, reach)
    grad_depth_full = grad_depth_low.astype(F32)
    taps = []
    grad_gated = jnp.zeros((batches, here, model), F32)
    for offset in range(KERNEL):
        same = (seg_wide[:, offset : offset + here] == seg_own)[:, :, None]
        taps.append(
            jnp.sum(
                jnp.where(same, grad_depth_full * widened[:, offset : offset + here], 0.0), (0, 1)
            )
        )
        mirror = 2 * reach - offset
        same_back = (seg_wide[:, mirror : mirror + here] == seg_own)[:, :, None]
        grad_gated = grad_gated + depth_rows[offset] * jnp.where(
            same_back, grad_widened[:, mirror : mirror + here], 0.0
        )
    two_in.first()
    grad_gated = after(grad_gated.reshape(rows, model), two_in)
    grad_point = jnp.concatenate(
        [grad_gated * sigmoid_gate, grad_gated * linear * sigmoid_gate * (1.0 - sigmoid_gate)], 1
    ).astype(BF16)
    through, gain_two = norm_back(
        dot(grad_point, w_point_in, NT), conv_normed, conv_inverse, gain[2]
    )
    grad_two = grad_three + through
    grad_attn_out = grad_two.astype(BF16)
    grad_context = dot(grad_attn_out, w_out, NT).astype(BF16)
    point_in = matmul_left(conv_entered, grad_point).astype(BF16)
    out_proj = matmul_left(context, grad_attn_out).astype(BF16)
    middle = [halves(part, rows_each) for part in (point_out, point_in, out_proj)]
    middle = [jnp.concatenate([part[i] for part in middle], 3) for i in range(2)]
    if items == 1:
        middle = [
            part.transpose(1, 2, 0, 3).reshape(1, part.shape[1], part.shape[2], -1)
            for part in middle
        ]
    middle = Scatter(*middle)
    grad_heads = []
    for number in range(batches):
        part = grad_context[number * here : (number + 1) * here]
        part = part.reshape(here, head_ways, -1).transpose(1, 0, 2)
        grad_heads.append(
            lax.all_to_all(part, "heads", split_axis=0, concat_axis=0, tiled=True)
        )
    backs = []
    for number in range(batches):
        if number == 0:
            two_out.second()
            grad_heads[number] = after(grad_heads[number], two_out, middle)
        if number == 1:
            two_out.third()
            two_in.second()
            middle.first()
            grad_heads[number] = after(grad_heads[number], two_out, two_in, middle)
        grads = attend_backward(
            qkv[number], seg_counts[number], size, fulls[number], lses[number], grad_heads[number]
        )
        backs.append(lax.all_to_all(grads, "heads", split_axis=0, concat_axis=0, tiled=True))
    two_in.third()
    middle.second()
    backs[-1] = after(backs[-1], two_in, middle)
    grad_one, gain_one, *shares = qkv_backward(
        backs, stream_one, gain[1], grad_two, w_qkv, cosines, sines, head_ways, core, items, size
    )
    attn = Scatter(*shares)
    middle.third()
    grad_one = after(grad_one, attn, middle)
    one_out = Scatter(*ffn_out_grad(grad_one, pre_one, head_ways, core, items))
    attn.first()
    grad_one = after(grad_one, one_out, attn)
    grad_zero, gain_zero, *shares = ffn_backward(
        grad_one, stream, pre_one, gain[0], w_ffn1_in, w_ffn1_out, head_ways, core, items, BF16
    )
    one_in = Scatter(*shares)
    one_out.first()
    attn.second()
    one_in.first()
    one_out.second()
    attn.third()
    one_in.second()
    one_out.third()
    one_in.third()
    small = sum_everywhere(
        jnp.concatenate(
            [gain_zero, gain_one, gain_two, gain_three, gain_four, gain_five]
            + [tap[None] for tap in taps],
            0,
        )
    )
    hidden = w_ffn1_in.shape[1]

    def unfolded(share):
        each, wide = share.shape
        span = hidden // head_ways
        parts = [share[:, i * span : (i + 1) * span] for i in range(wide // span)]
        return jnp.concatenate(parts, 0).T.astype(F32)

    middle_parts = []
    start = 0
    for weight in (w_point_out, w_point_in, w_out):
        each = weight.shape[1] // lax.axis_size("items")
        middle_parts.append(middle.result[:, start : start + each].astype(F32))
        start += each
    return (
        layer_out,
        grad_zero.reshape(frames.shape),
        small[:6],
        one_in.result.astype(F32),
        unfolded(one_out.result),
        attn.result.astype(F32),
        middle_parts[2],
        middle_parts[1],
        small[6:],
        middle_parts[0],
        two_in.result.astype(F32),
        unfolded(two_out.result),
    )


def solution(mesh):
    split = P(None, EVERY, None)
    shares = P("heads", "items")
    in_specs = (split, split, P(None, "items", None)) + (P(),) * 10
    out_specs = (split, split, P(), shares, shares, shares, shares, shares, P()) + (shares,) * 3
    return jax.shard_map(body, mesh=mesh, in_specs=in_specs, out_specs=out_specs, check_vma=False)
```

```python
import copy
import functools

import jax
import jax.numpy as jnp
from jax import lax
from jax.experimental import pallas as pl
from jax.experimental.pallas import tpu as pltpu
from jax.sharding import PartitionSpec as P

HEADS = 16
KERNEL = 5
LONG = 1500
SHORT = 500
EPS = 1e-05
ROPE_BASE = 10000.0
BLOCK = 256
LANES = 128
BIG = 1e30
VMEM_LIMIT = 56 << 20
F32 = jnp.float32
BF16 = jnp.bfloat16
NN = (((1,), (0,)), ((), ()))
NT = (((1,), (1,)), ((), ()))
EVERY = ("items", "heads")
FIRST = [("items", 1), ("items", 2)]


def dot(left, right, dims=NN):
    return lax.dot_general(left, right, dims, preferred_element_type=F32)


def silu_slope(field):
    gate_sig = jax.nn.sigmoid(field)
    return gate_sig * (1.0 + field * (1.0 - gate_sig))


def layer_norm(field, gain_row):
    centred = field - jnp.mean(field, -1, keepdims=True)
    inverse = lax.rsqrt(jnp.mean(centred * centred, -1, keepdims=True) + EPS)
    normed = centred * inverse
    return (normed * gain_row, normed, inverse)


def norm_back(upstream, normed, inverse, gain_row):
    scaled = upstream * gain_row
    through = inverse * (
        scaled
        - jnp.mean(scaled, -1, keepdims=True)
        - normed * jnp.mean(scaled * normed, -1, keepdims=True)
    )
    return (through, jnp.sum(upstream * normed, 0, keepdims=True))


def segment_ids(position, long_count, short_count, group_len):
    long_end = long_count * LONG
    short_end = long_end + short_count * SHORT
    segments = jnp.where(
        position < long_end, position // LONG, long_count + (position - long_end) // SHORT
    )
    segments = jnp.where(position < short_end, segments, long_count + short_count)
    return jnp.where((position < 0) | (position >= group_len), -1, segments)


def compiler_params():
    return pltpu.CompilerParams(vmem_limit_bytes=VMEM_LIMIT)


def whole(shape):
    return pl.BlockSpec(shape, lambda *_: (0,) * len(shape))


def cost(flops, bytes_accessed, transcendentals=0):
    return pl.CostEstimate(
        flops=flops, bytes_accessed=bytes_accessed, transcendentals=transcendentals
    )


def segment_bounds(counts, place, group):
    longs, shorts = counts
    long_end = longs * LONG
    short_end = long_end + shorts * SHORT
    start = jnp.where(place < longs, place * LONG, long_end + (place - longs) * SHORT)
    size = jnp.where(place < longs, LONG, SHORT)
    last = place == longs + shorts
    return (jnp.where(last, short_end, start), jnp.where(last, group, start + size), place <= longs + shorts)


def member_lanes(counts, first, rows, group, shift=0):
    shape = (rows, LANES)
    place = lax.broadcasted_iota(jnp.int32, (8, LANES), 1) - shift
    start, end, there = segment_bounds(counts, place, group)
    start = jnp.where(there & (place >= 0), start, group)
    start, end = start[:1], end[:1]
    frame = first + lax.broadcasted_iota(jnp.int32, shape, 0)
    return (frame >= start) & (frame < end)


def block_range(counts, step, group):
    longs, shorts = counts
    long_end = longs * LONG
    short_end = long_end + shorts * SHORT

    def number(frame):
        place = jnp.where(frame < long_end, frame // LONG, longs + (frame - long_end) // SHORT)
        return jnp.where(frame < short_end, place, longs + shorts)

    first = segment_bounds(counts, number(step * BLOCK), group)[0]
    last = segment_bounds(counts, number(step * BLOCK + BLOCK - 1), group)[1]
    return (first // BLOCK, jnp.minimum(last + BLOCK - 1, group) // BLOCK)


def head_lanes(shape, head, size):
    lane = lax.broadcasted_iota(jnp.int32, shape, 1)
    return (lane >= head * size) & (lane < (head + 1) * size)


def split_three(v):
    hi = v.astype(BF16).astype(F32)
    rest = v - hi
    mid = rest.astype(BF16).astype(F32)
    return (hi, mid, rest - mid)


def spread_columns(columns, shape):
    lane = lax.broadcasted_iota(jnp.int32, shape, 1)
    out = jnp.zeros(shape, F32)
    for place, column in enumerate(columns):
        out = jnp.where(lane == place, column, out)
    return out


def attn_fwd_kernel(heads, size, group, counts_ref, qkv_ref, out_ref, full_ref, lse_ref, kcat, v_all, s_scr):
    step = pl.program_id(0)
    counts = (counts_ref[0], counts_ref[1])
    width = heads * size
    blocks = group // BLOCK

    @pl.when(step == 0)
    def _():
        k = qkv_ref[:, 1].reshape(group, width)
        kcat[:, :width] = k
        if width < LANES:
            kcat[:, width:LANES] = jnp.zeros((group, LANES - width), BF16)
        kcat[:, LANES:] = jnp.where(member_lanes(counts, 0, group, group), 0.0, -BIG).astype(BF16)
        v_all[...] = qkv_ref[:, 2].reshape(group, width)

    chunk = qkv_ref.shape[2]
    per = BLOCK // chunk if BLOCK > chunk else 1
    rows = pl.ds(pl.multiple_of(step * BLOCK, BLOCK), BLOCK)
    if BLOCK == chunk:
        q = qkv_ref[step, 0]
    else:
        q = qkv_ref[pl.ds(step * per, per), 0].reshape(BLOCK, width)
    q = q.astype(F32) * (size ** -0.5)
    member = jnp.where(member_lanes(counts, step * BLOCK, BLOCK, group), 1.0, 0.0).astype(BF16)
    queries = []
    for head in range(heads):
        mine = q if heads == 1 else jnp.where(head_lanes(q.shape, head, size), q, 0.0)
        mine = mine.astype(BF16)
        if width < LANES:
            mine = jnp.concatenate([mine, jnp.zeros((BLOCK, LANES - width), BF16)], 1)
        queries.append(jnp.concatenate([mine, member], 1))
    low, high = block_range(counts, step, group)

    def scores(j, tops):
        keys = kcat[pl.ds(pl.multiple_of(j * BLOCK, BLOCK), BLOCK), :]
        new = []
        for head in range(heads):
            s = dot(queries[head], keys, NT)
            s_scr[head, j] = s
            top = tops[head]
            for part in range(BLOCK // LANES):
                top = jnp.maximum(top, s[:, part * LANES:(part + 1) * LANES])
            new.append(top)
        return tuple(new)

    start = tuple(jnp.full((BLOCK, LANES), -BIG, F32) for _ in range(heads))
    tops = lax.fori_loop(low, high, scores, start)
    tops = [jnp.max(t, 1, keepdims=True) for t in tops]
    tops = [jnp.broadcast_to(t, (BLOCK, LANES)) for t in tops]

    def weigh(j, carried):
        sums, accs = carried
        values = v_all[pl.ds(pl.multiple_of(j * BLOCK, BLOCK), BLOCK), :]
        new_sums, new_accs = [], []
        for head in range(heads):
            total = sums[head]
            parts = []
            for part in range(BLOCK // LANES):
                p = jnp.exp(s_scr[head, j, :, part * LANES:(part + 1) * LANES] - tops[head])
                total = total + p
                parts.append(p.astype(BF16))
            new_sums.append(total)
            new_accs.append(accs[head] + dot(jnp.concatenate(parts, 1), values))
        return (tuple(new_sums), tuple(new_accs))

    zeros = tuple(jnp.zeros((BLOCK, LANES), F32) for _ in range(heads))
    blank = tuple(jnp.zeros((BLOCK, width), F32) for _ in range(heads))
    sums, accs = lax.fori_loop(low, high, weigh, (zeros, blank))
    result = None
    for head in range(heads):
        total = jnp.sum(sums[head], 1, keepdims=True)
        mine = accs[head] / total
        result = mine if result is None else jnp.where(head_lanes(mine.shape, head, size), mine, result)
        lse_ref[head] = tops[head] + jnp.log(jnp.broadcast_to(total, (BLOCK, LANES)))
    full_ref[...] = result
    out_ref[...] = result.astype(BF16)


def attend_forward(qkv, counts, size):
    sources, _, chunk, width = qkv.shape
    group = sources * chunk
    heads = width // size
    steps = group // BLOCK
    smem = pl.BlockSpec(memory_space=pltpu.SMEM)
    return pl.pallas_call(
        functools.partial(attn_fwd_kernel, heads, size, group),
        grid=(steps,),
        in_specs=[
            smem,
            pl.BlockSpec(qkv.shape, lambda i: (0, 0, 0, 0)),
        ],
        out_specs=[
            pl.BlockSpec((BLOCK, width), lambda i: (i, 0)),
            pl.BlockSpec((BLOCK, width), lambda i: (i, 0)),
            pl.BlockSpec((heads, BLOCK, LANES), lambda i: (0, i, 0)),
        ],
        out_shape=[
            jax.ShapeDtypeStruct((group, width), BF16),
            jax.ShapeDtypeStruct((group, width), F32),
            jax.ShapeDtypeStruct((heads, group, LANES), F32),
        ],
        scratch_shapes=[
            pltpu.VMEM((group, 2 * LANES), BF16),
            pltpu.VMEM((group, width), BF16),
            pltpu.VMEM((heads, steps, BLOCK, BLOCK), F32),
        ],
        compiler_params=pltpu.CompilerParams(vmem_limit_bytes=VMEM_LIMIT),
        cost_estimate=pl.CostEstimate(flops=16 * group * group * LANES, bytes_accessed=6 << 20, transcendentals=heads * group * group),
        name="attend_forward",
    )(counts, qkv)


def attn_bwd_kernel(heads, size, group, counts_ref, qkv_ref, full_ref, lse_ref, grad_ref, out_ref, qcat, gcat, k_turned, dq_turned):
    step = pl.program_id(0)
    counts = (counts_ref[0], counts_ref[1])
    width = heads * size
    blocks = group // BLOCK
    chunk = qkv_ref.shape[2]
    per = BLOCK // chunk if BLOCK > chunk else 1

    def block_of(part, j):
        if BLOCK == chunk:
            return qkv_ref[j, part]
        return qkv_ref[pl.ds(j * per, per), part].reshape(BLOCK, width)

    def grad_of(j):
        if BLOCK == chunk:
            return grad_ref[j]
        return grad_ref[pl.ds(j * per, per)].reshape(BLOCK, width)

    def widened(v):
        if width < LANES:
            return jnp.concatenate([v, jnp.zeros((BLOCK, LANES - width), v.dtype)], 1)
        return v

    @pl.when(step == 0)
    def _():
        dq_turned[...] = jnp.zeros_like(dq_turned)

        def prepare(j, _):
            rows = pl.ds(pl.multiple_of(j * BLOCK, BLOCK), BLOCK)
            lane = lax.broadcasted_iota(jnp.int32, (BLOCK, LANES), 1)
            q = widened(block_of(0, j).astype(F32) * (size ** -0.5))
            g = widened(grad_of(j).astype(F32))
            o = widened(full_ref[rows, :])
            product = g * o
            member = jnp.where(member_lanes(counts, j * BLOCK, BLOCK, group, 3), 1.0, 0.0)
            for head in range(heads):
                own = head_lanes((BLOCK, LANES), head, size)
                lse = lse_ref[head, rows, :]
                tail = jnp.where(lane < 3, -spread_columns(split_three(lse), (BLOCK, LANES)), member)
                delta = jnp.broadcast_to(jnp.sum(jnp.where(own, product, 0.0), 1, keepdims=True), (BLOCK, LANES))
                qcat[head, rows, :LANES] = jnp.where(own, q, 0.0).astype(BF16)
                qcat[head, rows, LANES:] = tail.astype(BF16)
                gcat[head, rows, :LANES] = jnp.where(own, g, 0.0).astype(BF16)
                gcat[head, rows, LANES:] = (-spread_columns(split_three(delta), (BLOCK, LANES))).astype(BF16)
            k = widened(block_of(1, j).astype(F32))
            k_turned[j] = jnp.transpose(k).astype(BF16)
            return 0

        lax.fori_loop(0, blocks, prepare, 0)

    lane = lax.broadcasted_iota(jnp.int32, (BLOCK, LANES), 1)
    rows = pl.ds(pl.multiple_of(step * BLOCK, BLOCK), BLOCK)
    member = member_lanes(counts, step * BLOCK, BLOCK, group, 3)
    tail = jnp.where(lane < 3, 1.0, jnp.where(member, 0.0, -BIG)).astype(BF16)
    keys = jnp.concatenate([widened(block_of(1, step)), tail], 1)
    ones = jnp.where(lane < 3, 1.0, 0.0).astype(BF16)
    values = jnp.concatenate([widened(block_of(2, step)), ones], 1)

    def one(j, carried):
        dk, dv = carried
        cols = pl.ds(pl.multiple_of(j * BLOCK, BLOCK), BLOCK)
        for head in range(heads):
            qc = qcat[head, cols, :]
            gc = gcat[head, cols, :]
            p = jnp.exp(dot(keys, qc, NT))
            ds = (p * dot(values, gc, NT)).astype(BF16)
            dv = dv + dot(p.astype(BF16), gc[:, :LANES])
            dk = dk + dot(ds, qc[:, :LANES])
            turned = k_turned[step, head * size:(head + 1) * size, :]
            dq_turned[j, head * size:(head + 1) * size, :] += dot(turned, ds)
        return (dk, dv)

    zero = jnp.zeros((BLOCK, LANES), F32)
    low, high = block_range(counts, step, group)
    dk, dv = lax.fori_loop(low, high, one, (zero, zero))
    dk = dk[:, :width].astype(BF16)
    dv = dv[:, :width].astype(BF16)
    if BLOCK == chunk:
        out_ref[step, 1] = dk
        out_ref[step, 2] = dv
    else:
        out_ref[pl.ds(step * per, per), 1] = dk.reshape(per, chunk, width)
        out_ref[pl.ds(step * per, per), 2] = dv.reshape(per, chunk, width)

    @pl.when(step == blocks - 1)
    def _():
        def finish(j, _):
            dq = (jnp.transpose(dq_turned[j]) * (size ** -0.5))[:, :width].astype(BF16)
            if BLOCK == chunk:
                out_ref[j, 0] = dq
            else:
                out_ref[pl.ds(j * per, per), 0] = dq.reshape(per, chunk, width)
            return 0

        lax.fori_loop(0, blocks, finish, 0)


def attend_backward(qkv, counts, size, full, lse, grad):
    sources, _, chunk, width = qkv.shape
    group = sources * chunk
    heads = width // size
    steps = group // BLOCK
    smem = pl.BlockSpec(memory_space=pltpu.SMEM)
    return pl.pallas_call(
        functools.partial(attn_bwd_kernel, heads, size, group),
        grid=(steps,),
        in_specs=[
            smem,
            whole(qkv.shape),
            whole(full.shape),
            whole(lse.shape),
            whole(grad.shape),
        ],
        out_specs=whole(qkv.shape),
        out_shape=jax.ShapeDtypeStruct(qkv.shape, BF16),
        scratch_shapes=[
            pltpu.VMEM((heads, group, 2 * LANES), BF16),
            pltpu.VMEM((heads, group, 2 * LANES), BF16),
            pltpu.VMEM((steps, LANES, BLOCK), BF16),
            pltpu.VMEM((steps, LANES, BLOCK), F32),
        ],
        compiler_params=pltpu.CompilerParams(vmem_limit_bytes=VMEM_LIMIT),
        cost_estimate=pl.CostEstimate(flops=32 * group * group * LANES, bytes_accessed=9 << 20, transcendentals=heads * group * group),
        name="attend_backward",
    )(counts, qkv, full, lse, grad)


def half_gate(field):
    return 0.5 * jnp.tanh(0.5 * field) + 0.5


def ffn_fwd_kernel(
    x_ref, gain_ref, win_ref, wout_ref, out_ref, pre_ref, hid_ref, entered_ref, total
):
    step = pl.program_id(0)

    @pl.when(step == 0)
    def _():
        entered_ref[...] = layer_norm(x_ref[...].astype(F32), gain_ref[...])[0].astype(BF16)
        total[...] = jnp.zeros_like(total)

    pre = dot(entered_ref[...], win_ref[...])
    pre_ref[...] = pre
    hidden = (pre * half_gate(pre)).astype(BF16)
    hid_ref[...] = hidden
    total[...] += dot(hidden, wout_ref[...])

    @pl.when(step == pl.num_programs(0) - 1)
    def _():
        out_ref[...] = x_ref[...].astype(F32) + 0.5 * total[...]


def ffn_forward(stream, gain_row, weight_in, weight_out):
    rows, model = stream.shape
    units = weight_in.shape[1]
    wide = 512
    return pl.pallas_call(
        ffn_fwd_kernel,
        grid=(units // wide,),
        in_specs=[
            whole((rows, model)),
            whole((1, model)),
            pl.BlockSpec((model, wide), lambda s: (0, s)),
            pl.BlockSpec((wide, model), lambda s: (s, 0)),
        ],
        out_specs=[whole((rows, model))]
        + [pl.BlockSpec((rows, wide), lambda s: (0, s))] * 2
        + [whole((rows, model))],
        out_shape=[
            jax.ShapeDtypeStruct((rows, model), F32),
            jax.ShapeDtypeStruct((rows, units), F32),
            jax.ShapeDtypeStruct((rows, units), BF16),
            jax.ShapeDtypeStruct((rows, model), BF16),
        ],
        scratch_shapes=[pltpu.VMEM((rows, model), F32)],
        compiler_params=compiler_params(),
        cost_estimate=cost(4 * rows * model * units, 4 * model * units + 6 * rows * units),
        name="ffn_forward",
    )(stream, gain_row, weight_in, weight_out)


def slope(pre):
    gate = half_gate(pre)
    return gate * (1.0 + pre * (1.0 - gate))


def ffn_bwd_kernel(
    x_ref, gain_ref, up_ref, pre_ref, win_ref, wout_ref,
    down_ref, gain_grad_ref, half_ref, grad_ref, total,
):
    step = pl.program_id(0)

    @pl.when(step == 0)
    def _():
        half_ref[...] = (0.5 * up_ref[...]).astype(BF16)
        total[...] = jnp.zeros_like(total)

    grad = (dot(half_ref[...], wout_ref[...], NT) * slope(pre_ref[...])).astype(BF16)
    grad_ref[...] = grad
    total[...] += dot(grad, win_ref[...], NT)

    @pl.when(step == pl.num_programs(0) - 1)
    def _():
        gain = gain_ref[...]
        normed, inverse = layer_norm(x_ref[...].astype(F32), gain)[1:]
        through, grad_gain = norm_back(total[...], normed, inverse, gain)
        down_ref[...] = up_ref[...] + through
        gain_grad_ref[...] = grad_gain


def ffn_backward(upstream, stream, pre_act, gain_row, weight_in, weight_out):
    rows, model = stream.shape
    units = weight_in.shape[1]
    wide = 512
    return pl.pallas_call(
        ffn_bwd_kernel,
        grid=(units // wide,),
        in_specs=[
            whole((rows, model)),
            whole((1, model)),
            whole((rows, model)),
            pl.BlockSpec((rows, wide), lambda s: (0, s)),
            pl.BlockSpec((model, wide), lambda s: (0, s)),
            pl.BlockSpec((wide, model), lambda s: (s, 0)),
        ],
        out_specs=[
            whole((rows, model)),
            whole((1, model)),
            whole((rows, model)),
            pl.BlockSpec((rows, wide), lambda s: (0, s)),
        ],
        out_shape=[
            jax.ShapeDtypeStruct((rows, model), F32),
            jax.ShapeDtypeStruct((1, model), F32),
            jax.ShapeDtypeStruct((rows, model), BF16),
            jax.ShapeDtypeStruct((rows, units), BF16),
        ],
        scratch_shapes=[pltpu.VMEM((rows, model), F32)],
        compiler_params=compiler_params(),
        cost_estimate=cost(4 * rows * model * units, 4 * model * units + 6 * rows * units),
        name="ffn_backward",
    )(stream, gain_row, upstream, pre_act, weight_in, weight_out)


def hidden_kernel(up_ref, pre_ref, wout_ref, half_ref, grad_ref):
    @pl.when(pl.program_id(0) == 0)
    def _():
        half_ref[...] = (0.5 * up_ref[...]).astype(BF16)

    grad_ref[...] = (dot(half_ref[...], wout_ref[...], NT) * slope(pre_ref[...])).astype(BF16)


def hidden_gradient(upstream, pre_act, weight_out):
    rows, model = upstream.shape
    units = weight_out.shape[0]
    wide = 512
    return pl.pallas_call(
        hidden_kernel,
        grid=(units // wide,),
        in_specs=[
            whole((rows, model)),
            pl.BlockSpec((rows, wide), lambda s: (0, s)),
            pl.BlockSpec((wide, model), lambda s: (s, 0)),
        ],
        out_specs=[whole((rows, model)), pl.BlockSpec((rows, wide), lambda s: (0, s))],
        out_shape=[
            jax.ShapeDtypeStruct((rows, model), BF16),
            jax.ShapeDtypeStruct((rows, units), BF16),
        ],
        compiler_params=compiler_params(),
        cost_estimate=cost(2 * rows * model * units, 2 * model * units + 6 * rows * units),
        name="hidden_gradient",
    )(upstream, pre_act, weight_out)


def down_kernel(
    x_ref, gain_ref, up_ref, grad_ref, weight_ref, down_ref, half_ref, gain_grad_ref, total
):
    step = pl.program_id(0)

    @pl.when(step == 0)
    def _():
        total[...] = jnp.zeros_like(total)

    total[...] += dot(grad_ref[...], weight_ref[...], NT)

    @pl.when(step == pl.num_programs(0) - 1)
    def _():
        gain = gain_ref[...]
        normed, inverse = layer_norm(x_ref[...].astype(F32), gain)[1:]
        through, grad_gain = norm_back(total[...], normed, inverse, gain)
        down = up_ref[...] + through
        down_ref[...] = down.astype(down_ref.dtype)
        half_ref[...] = (0.5 * down).astype(BF16)
        gain_grad_ref[...] = grad_gain


def stream_gradient(upstream, stream, grad, gain_row, weight, down_type):
    rows, model = stream.shape
    units = weight.shape[1]
    wide = 512
    return pl.pallas_call(
        down_kernel,
        grid=(units // wide,),
        in_specs=[
            whole((rows, model)),
            whole((1, model)),
            whole((rows, model)),
            pl.BlockSpec((rows, wide), lambda s: (0, s)),
            pl.BlockSpec((model, wide), lambda s: (0, s)),
        ],
        out_specs=[whole((rows, model)), whole((rows, model)), whole((1, model))],
        out_shape=[
            jax.ShapeDtypeStruct((rows, model), down_type),
            jax.ShapeDtypeStruct((rows, model), BF16),
            jax.ShapeDtypeStruct((1, model), F32),
        ],
        scratch_shapes=[pltpu.VMEM((rows, model), F32)],
        compiler_params=compiler_params(),
        cost_estimate=cost(2 * rows * model * units, 2 * model * units + 2 * rows * units),
        name="stream_gradient",
    )(stream, gain_row, upstream, grad, weight)


def turn(field, cosines, sines, size):
    lane = lax.broadcasted_iota(jnp.int32, field.shape, 1)
    half = size // 2
    width = field.shape[1]
    swapped = jnp.where(
        lane % size < half,
        pltpu.roll(field, width - half, 1),
        pltpu.roll(field, half, 1),
    )
    return field * cosines + swapped * sines


def rope_tables(position, size, width):
    half = size // 2
    lane = jnp.arange(width, dtype=jnp.int32)
    freqs = jnp.exp(
        -jnp.log(jnp.float32(ROPE_BASE)) * jnp.arange(half, dtype=jnp.float32) / half
    )
    angles = position.astype(jnp.float32)[:, None] * freqs[None, :]
    cosines, sines = jnp.cos(angles), jnp.sin(angles)
    repeats = width // size
    return (
        jnp.tile(jnp.concatenate([cosines, cosines], 1), (1, repeats)),
        jnp.tile(jnp.concatenate([-sines, sines], 1), (1, repeats)),
    )


def qkv_fwd_kernel(size, x_ref, gain_ref, wq_ref, wk_ref, wv_ref, cos_ref, sin_ref, *rest):
    outs, entered = rest[:-1], rest[-1]
    step = pl.program_id(0)

    @pl.when(step == 0)
    def _():
        entered[...] = layer_norm(x_ref[...], gain_ref[...])[0].astype(BF16)

    frames = outs[0].shape[2]
    width = outs[0].shape[3]
    for place, weight in enumerate((wq_ref, wk_ref, wv_ref)):
        made = dot(entered[...], weight[...])
        for number, out in enumerate(outs):
            part = made[number * frames : (number + 1) * frames]
            if place < 2:
                part = turn(part, cos_ref[...], sin_ref[...], size)
            part = part.astype(BF16)
            for target in range(out.shape[0]):
                out[target, place] = part[:, target * width : (target + 1) * width]


def qkv_forward(stream, gain_row, weight, cosines, sines, heads, batches, size):
    rows, model = stream.shape
    wide = cosines.shape[1]
    steps = model // wide
    width = model // heads
    frames = rows // batches
    out = jax.ShapeDtypeStruct((heads, 3, frames, width), BF16)
    return pl.pallas_call(
        functools.partial(qkv_fwd_kernel, size),
        grid=(steps,),
        in_specs=[
            whole((rows, model)),
            whole((1, model)),
            pl.BlockSpec((model, wide), lambda s: (0, s)),
            pl.BlockSpec((model, wide), lambda s: (0, steps + s)),
            pl.BlockSpec((model, wide), lambda s: (0, 2 * steps + s)),
            whole(cosines.shape),
            whole(sines.shape),
        ],
        out_specs=[
            pl.BlockSpec((wide // width, 3, frames, width), lambda s: (s, 0, 0, 0))
            for _ in range(batches)
        ]
        + [whole((rows, model))],
        out_shape=[out] * batches + [jax.ShapeDtypeStruct((rows, model), BF16)],
        compiler_params=compiler_params(),
        cost_estimate=cost(6 * rows * model * model, 6 * model * model + 10 * rows * model),
        name="qkv_forward",
    )(stream, gain_row, weight, weight, weight, cosines, sines)


def unturn_kernel(size, batches, cos_ref, sin_ref, *refs):
    backs, out = refs[:batches], refs[batches]
    rotated = pl.program_id(0) < 2
    cosines = jnp.where(rotated, cos_ref[...], 1.0)
    sines = jnp.where(rotated, -sin_ref[...], 0.0)
    heads, _, frames, width = backs[0].shape
    wide = cosines.shape[1]
    for number, back in enumerate(backs):
        for first in range(0, heads, wide // width):
            field = jnp.concatenate([back[first + i, 0] for i in range(wide // width)], 1)
            made = turn(field.astype(F32), cosines, sines, size).astype(BF16)
            out[number * frames : (number + 1) * frames, first * width : first * width + wide] = made


def unturned(backs, cosines, sines, size):
    heads, kinds, frames, width = backs[0].shape
    batches = len(backs)
    block = pl.BlockSpec((heads, 1, frames, width), lambda s: (0, s, 0, 0))
    model = heads * width
    return pl.pallas_call(
        functools.partial(unturn_kernel, size, batches),
        grid=(kinds,),
        in_specs=[whole(cosines.shape), whole(sines.shape)] + [block] * batches,
        out_specs=pl.BlockSpec((batches * frames, model), lambda s: (0, s)),
        out_shape=jax.ShapeDtypeStruct((batches * frames, kinds * model), BF16),
        compiler_params=compiler_params(),
        cost_estimate=cost(0, 4 * batches * frames * kinds * model),
        name="unturned",
    )(cosines, sines, *backs)


def flipped(axis_bit, count):
    axis, bit = axis_bit
    items, heads = count
    if axis == "items":
        return [(i * heads + h, (i ^ bit) * heads + h) for i in range(items) for h in range(heads)]
    return [(i * heads + h, i * heads + (h ^ bit)) for i in range(items) for h in range(heads)]


def swap(value, axis_bit):
    count = (lax.axis_size("items"), lax.axis_size("heads"))
    return lax.ppermute(value, EVERY, flipped(axis_bit, count))


def fenced(always, scatters, work):
    def run():
        return (work(), [scatter.move() for scatter in scatters])

    def empty():
        return jax.tree.map(lambda leaf: jnp.zeros(leaf.shape, leaf.dtype), jax.eval_shape(run))

    result, moved = lax.optimization_barrier(lax.cond(always, run, empty))
    for scatter, parts in zip(scatters, moved):
        scatter.take(parts)
    return result


def moved(scatter):
    scatter.take(scatter.move())


def other_core(value):
    return swap(value, ("heads", 1))


def exchange(value):
    return lax.all_to_all(value, "heads", split_axis=0, concat_axis=0, tiled=True)


def own_rows(left_ref, heads, core, target, first):
    rows, model = left_ref.shape
    each = model // heads
    for place in range(heads // 2):
        if each % LANES == 0:
            start = pl.multiple_of((2 * place + core) * each, each)
            mine = jnp.transpose(left_ref[:, pl.ds(start, each)].astype(F32)).astype(BF16)
        else:
            pair = left_ref[:, 2 * place * each : 2 * (place + 1) * each]
            pair = jnp.transpose(pair.astype(F32))
            mine = jnp.where(core == 0, pair[:each], pair[each:]).astype(BF16)
        for half in range(2):
            start = (half * (heads // 2) + place) * (each // 2)
            target[start : start + each // 2, first : first + rows] = mine[
                half * (each // 2) : (half + 1) * (each // 2)
            ]


def turned_items(left, items, own, target, first):
    rows, model = left.shape
    each = model // items
    for item in range(items):
        part = jnp.transpose(left[:, item * each : (item + 1) * each].astype(F32)).astype(BF16)
        place = pl.multiple_of((own ^ item) * each, each)
        target[pl.ds(place, each), first : first + rows] = part


def share_shapes(items, heads, model, columns):
    lead = 2 if items > 1 else 1
    shape = (lead, heads // 2, model // heads // 2, columns // items)
    return [jax.ShapeDtypeStruct(shape, BF16)] * (4 if items > 1 else 2)


def out_grad_kernel(place_ref, up_own, up_other, hid_own, hid_other, *refs):
    targets, turned = refs[:-1], refs[-1]
    rows, model = up_own.shape
    items = 4 if len(targets) == 4 else 1

    @pl.when(pl.program_id(0) == 0)
    def _():
        turned_items(up_own[...], items, place_ref[1], turned, 0)
        turned_items(up_other[...], items, place_ref[1], turned, rows)

    hidden = jnp.concatenate([hid_own[...], hid_other[...]], 0)
    grad = dot(turned[...], hidden).astype(BF16)
    wide = grad.shape[1]
    each = targets[0].shape[2]
    parts = model // items // (2 * each)
    for r in range(items):
        for part in range(parts):
            for half in range(2):
                first = ((r * parts + part) * 2 + half) * each
                piece = grad[first : first + each]
                if half == 0:
                    target, at = targets[2 * (r % 2)], r // 2
                else:
                    target, at = targets[1 + 2 * (r // 2)], r % 2
                target[at, 0, :, part * wide : (part + 1) * wide] = piece


def out_grad(upstream, hidden, heads, place, items):
    rows, model = upstream[0].shape
    units = hidden[0].shape[1]
    wide = units // heads
    shapes = share_shapes(items, heads, model, units)
    block = (shapes[0].shape[0], 1) + shapes[0].shape[2:]
    hid_block = pl.BlockSpec((rows, wide), lambda s, place: (0, 2 * s + place[0]))
    grid_spec = pltpu.PrefetchScalarGridSpec(
        num_scalar_prefetch=1,
        grid=(heads // 2,),
        in_specs=[whole((rows, model))] * 2 + [hid_block] * 2,
        out_specs=[pl.BlockSpec(block, lambda s, place: (0, s, 0, 0))] * len(shapes),
        scratch_shapes=[pltpu.VMEM((model, 2 * rows), BF16)],
    )
    return pl.pallas_call(
        out_grad_kernel,
        grid_spec=grid_spec,
        out_shape=shapes,
        compiler_params=compiler_params(),
        cost_estimate=cost(2 * rows * model * units, 2 * model * units + 4 * rows * units),
        name="out_grad",
    )(place, *upstream, *hidden)


def column_grad_kernel(heads, count, place_ref, *refs):
    lefts, refs = refs[: 2 * count], refs[2 * count :]
    rights, refs = refs[: 2 * count], refs[2 * count :]
    targets, turned = refs[:-count], refs[-count:]
    r = pl.program_id(0)
    rows = lefts[0].shape[0]

    @pl.when(r == 0)
    def _():
        for number in range(count):
            for other in range(2):
                own_rows(
                    lefts[2 * number + other], heads, place_ref[0], turned[number], other * rows
                )

    made = []
    for number in range(count):
        right = jnp.concatenate([rights[2 * number][...], rights[2 * number + 1][...]], 0)
        made.append(dot(turned[number][...], right).astype(BF16))
    made = made[0] if count == 1 else jnp.concatenate(made, 1)
    half = made.shape[0] // 2
    top, low = made[:half].reshape(targets[0].shape), made[half:].reshape(targets[0].shape)
    if len(targets) == 2:
        targets[0][...] = top
        targets[1][...] = low
        return

    @pl.when(r % 2 == 0)
    def _():
        targets[0][...] = top

    @pl.when(r % 2 == 1)
    def _():
        targets[2][...] = top

    @pl.when(r < 2)
    def _():
        targets[1][...] = low

    @pl.when(r >= 2)
    def _():
        targets[3][...] = low


def column_grads(lefts, rights, heads, place, items):
    rows, model = lefts[0][0].shape
    columns = sum(right[0].shape[1] for right in rights)
    shapes = share_shapes(items, heads, model, columns)
    block = (1,) + shapes[0].shape[1:]
    maps = [
        lambda r, place: (r // 2, 0, 0, 0),
        lambda r, place: (jnp.minimum(r, 1), 0, 0, 0),
        lambda r, place: (r // 3, 0, 0, 0),
        lambda r, place: (r // 3, 0, 0, 0),
    ]
    grid_spec = pltpu.PrefetchScalarGridSpec(
        num_scalar_prefetch=1,
        grid=(items,),
        in_specs=[whole((rows, model))] * (2 * len(lefts))
        + [
            pl.BlockSpec((rows, right[0].shape[1] // items), lambda r, place: (0, r ^ place[1]))
            for right in rights
            for _ in range(2)
        ],
        out_specs=[pl.BlockSpec(block, index) for index in maps[: len(shapes)]],
        scratch_shapes=[pltpu.VMEM((model // 2, 2 * rows), BF16)] * len(lefts),
    )
    return pl.pallas_call(
        functools.partial(column_grad_kernel, heads, len(lefts)),
        grid_spec=grid_spec,
        out_shape=shapes,
        compiler_params=compiler_params(),
        cost_estimate=cost(2 * rows * model * columns, 4 * model * columns),
        name="column_grads",
    )(place, *[part for left in lefts for part in left], *[part for right in rights for part in right])


class Scatter:
    def __init__(self, keep_top, keep_low, *sends):
        self.keep = [keep_top, keep_low]
        self.got, self.early = [], []
        self.route(list(sends), FIRST[: len(sends)])

    def route(self, sends, routes):
        self.sends, self.routes = sends, routes

    def move(self):
        return [swap(send, route) for send, route in zip(self.sends, self.routes)]

    def take(self, moved):
        self.early, self.got = self.got, moved
        self.route([], [])

    def second(self, sends):
        self.route(sends, FIRST[::-1][: len(sends)])


def second_kernel(*refs):
    count = len(refs) // 3
    for number in range(count):
        keep, got, out = refs[2 * number], refs[2 * number + 1], refs[2 * count + number]
        out[...] = (keep[0].astype(F32) + got[0].astype(F32)).astype(BF16)


def second_sums(*scatters):
    terms = [
        part
        for scatter in scatters
        if scatter.got
        for keep, got in zip(scatter.keep, scatter.got)
        for part in (keep, got)
    ]
    if not terms:
        return [[] for _ in scatters]
    shape = terms[0].shape
    outs = []
    in_specs, out_specs = [], []
    for term in terms:
        in_specs.append(
            pl.BlockSpec((1, 2) + term.shape[2:], lambda g: (1, g, 0, 0))
        )
    for term in terms[::2]:
        out_specs.append(pl.BlockSpec((2,) + term.shape[2:], lambda g: (g, 0, 0)))
        outs.append(jax.ShapeDtypeStruct(term.shape[1:], BF16))
    made = pl.pallas_call(
        second_kernel,
        grid=(shape[1] // 2,),
        in_specs=in_specs,
        out_specs=out_specs,
        out_shape=outs,
        compiler_params=compiler_params(),
        cost_estimate=cost(0, 6 * sum(out.size for out in outs)),
        name="second_sums",
    )(*terms)
    return [list(made[2 * i : 2 * i + 2]) for i in range(len(scatters))]


def last_kernel(*refs):
    out = refs[-1]
    for number in range(out.shape[1]):
        for half in range(2):
            terms = refs[6 * number + 3 * half : 6 * number + 3 * half + 3]
            out[:, number, half] = (
                terms[0][0].astype(F32) + terms[1][0].astype(F32) + terms[2][...].astype(F32)
            ).astype(BF16)


def last_sum(*scatters, columns=None):
    if not scatters[0].got:
        items = lax.axis_size("items")
        values = []
        for scatter in scatters:
            value = jnp.stack([keep[0] for keep in scatter.keep], 1)
            if columns is not None:
                starts = [sum(columns[:i]) for i in range(len(columns))]
                parts = [
                    value[..., start : start + size].reshape(value.shape[:3] + (items, -1))
                    for start, size in zip(starts, columns)
                ]
                value = jnp.concatenate(parts, 4).reshape(value.shape)
            values.append(lax.psum_scatter(value, "items", scatter_dimension=3, tiled=True))
        return jnp.stack(values, 1)
    terms = [
        part
        for scatter in scatters
        for parts in zip(scatter.keep, scatter.early, scatter.got)
        for part in parts
    ]
    _, places, rows, wide = terms[0].shape
    held = pl.BlockSpec((1, 2, rows, wide), lambda g: (0, g, 0, 0))
    late = pl.BlockSpec((2, rows, wide), lambda g: (g, 0, 0))
    shape = (places, len(scatters), 2, rows, wide)
    return pl.pallas_call(
        last_kernel,
        grid=(places // 2,),
        in_specs=[held, held, late] * (2 * len(scatters)),
        out_specs=pl.BlockSpec((2,) + shape[1:], lambda g: (g, 0, 0, 0, 0)),
        out_shape=jax.ShapeDtypeStruct(shape, BF16),
        compiler_params=compiler_params(),
        cost_estimate=cost(0, 8 * places * len(scatters) * 2 * rows * wide),
        name="last_sum",
    )(*terms)


def along_z(value):
    heads = lax.axis_size("heads")
    groups = [[core + 2 * z for z in range(heads // 2)] for core in range(2)]
    made = lax.psum_scatter(
        value, "heads", scatter_dimension=0, tiled=False, axis_index_groups=groups
    )
    return [made[i].reshape(-1, made.shape[-1]) for i in range(made.shape[0])]


def sum_everywhere(value):
    for axis in EVERY:
        bit = 1
        while bit < lax.axis_size(axis):
            value = value + swap(value, (axis, bit))
            bit *= 2
    return value


def edges(block, width):
    count = lax.axis_size("heads")
    forward = [(i, i + 1) for i in range(count - 1)]
    backward = [(target, source) for source, target in forward]
    low = lax.ppermute(block[:, block.shape[1] - width :], "heads", forward)
    high = lax.ppermute(block[:, :width], "heads", backward)
    return jnp.concatenate([low, block, high], axis=1)


def body(
    frames, cotangent, bucket_counts, gains, w_ffn1_in, w_ffn1_out, w_qkv, w_out,
    w_point_in, w_depth, w_point_out, w_ffn2_in, w_ffn2_out,
):
    batches, here, model = frames.shape
    head_ways = lax.axis_size("heads")
    items = 4 if lax.axis_size("items") == 4 else 1
    group_len = here * head_ways
    size = model // HEADS
    reach = (KERNEL - 1) // 2
    rows = batches * here
    place = lax.axis_index("heads")
    where = jnp.stack([place % 2, lax.axis_index("items") if items > 1 else 0 * place]).astype(jnp.int32)
    first = place * here
    cosines, sines = rope_tables(
        first + jnp.arange(here, dtype=jnp.int32), size, max(2 * LANES, model // head_ways)
    )
    depth_rows = w_depth.astype(F32)
    always = jnp.min(bucket_counts) >= 0
    gain = [gains[i : i + 1] for i in range(6)]
    wide_position = first - reach + jnp.arange(here + 2 * reach, dtype=jnp.int32)
    seg_wide = []
    seg_counts = []
    for number in range(batches):
        counts = bucket_counts[number, 0]
        seg_wide.append(segment_ids(wide_position, counts[0], counts[1], group_len))
        seg_counts.append(counts)
    seg_wide = jnp.stack(seg_wide, 0)
    seg_own = seg_wide[:, reach : reach + here]

    stream = frames.reshape(rows, model)
    stream_one, pre_one, hid_one, ent_one = ffn_forward(stream, gain[0], w_ffn1_in, w_ffn1_out)
    *sent, ent_att = qkv_forward(
        stream_one, gain[1], w_qkv, cosines, sines, head_ways, batches, size
    )
    qkv = [exchange(sent[0])]
    kept, contexts = [], []
    for number in range(batches):

        def attend_now():
            return attend_forward(qkv[number], seg_counts[number], size)

        def beside():
            extra = [other_core(part) for part in ([hid_one, ent_one] if number == 0 else [ent_att])]
            if number + 1 < batches:
                extra.append(exchange(sent[number + 1]))
            if number > 0:
                extra.append(exchange(kept[number - 1][0].reshape(head_ways, here, -1)))
            return extra

        made, extra = fenced(always, (), lambda: (attend_now(), beside()))
        kept.append(made)
        if number == 0:
            hid_one, ent_one = (hid_one, extra[0]), (ent_one, extra[1])
            extra = extra[2:]
        else:
            ent_att = (ent_att, extra[0]) if number == 1 else ent_att
            extra = extra[1:]
        if number + 1 < batches:
            qkv.append(extra.pop(0))
        if number > 0:
            contexts.append(extra.pop(0))
    contexts.append(exchange(kept[-1][0].reshape(head_ways, here, -1)))
    fulls = [made[1] for made in kept]
    lses = [made[2] for made in kept]
    context = jnp.concatenate(
        [part.transpose(1, 0, 2).reshape(here, model) for part in contexts], 0
    )
    stream_two = stream_one + dot(context, w_out)
    shaped, conv_normed, conv_inverse = layer_norm(stream_two, gain[2])
    conv_entered = shaped.astype(BF16)
    pointwise = dot(conv_entered, w_point_in)
    linear = pointwise[:, :model]
    sigmoid_gate = jax.nn.sigmoid(pointwise[:, model:])
    gated_low = (linear * sigmoid_gate).astype(BF16).reshape(batches, here, model)
    widened = edges(gated_low, reach)
    depth_out = jnp.zeros((batches, here, model), F32)
    for offset in range(KERNEL):
        same = (seg_wide[:, offset : offset + here] == seg_own)[:, :, None]
        depth_out = depth_out + depth_rows[offset] * jnp.where(
            same, widened[:, offset : offset + here], 0.0
        )
    depth_out = depth_out.reshape(rows, model)
    depth_shaped, depth_normed, depth_inverse = layer_norm(depth_out, gain[3])
    mixed_low = (depth_shaped * jax.nn.sigmoid(depth_shaped)).astype(BF16)
    stream_three = stream_two + dot(mixed_low, w_point_out)
    stream_four, pre_two, hid_two, ent_two = ffn_forward(
        stream_three, gain[4], w_ffn2_in, w_ffn2_out
    )
    shaped, final_normed, final_inverse = layer_norm(stream_four, gain[5])
    layer_out = shaped.astype(BF16).reshape(frames.shape)
    grad_four, gain_five = norm_back(
        cotangent.reshape(rows, model).astype(F32), final_normed, final_inverse, gain[5]
    )
    (grad_three, gain_four, half_two, grad_pre_two), hid_other, ent_other = fenced(
        always,
        (),
        lambda: (
            ffn_backward(grad_four, stream_three, pre_two, gain[4], w_ffn2_in, w_ffn2_out),
            other_core(hid_two),
            other_core(ent_two),
        ),
    )
    half_other, grad_pre_other = other_core(half_two), other_core(grad_pre_two)
    grad_mix = grad_three.astype(BF16)
    grad_norm_in = dot(grad_mix, w_point_out, NT) * silu_slope(depth_shaped)
    grad_depth, gain_three = norm_back(grad_norm_in, depth_normed, depth_inverse, gain[3])
    grad_depth_low = grad_depth.astype(BF16).reshape(batches, here, model)
    grad_widened = edges(grad_depth_low, reach)
    grad_depth_full = grad_depth_low.astype(F32)
    taps = []
    grad_gated = jnp.zeros((batches, here, model), F32)
    for offset in range(KERNEL):
        same = (seg_wide[:, offset : offset + here] == seg_own)[:, :, None]
        taps.append(
            jnp.sum(
                jnp.where(same, grad_depth_full * widened[:, offset : offset + here], 0.0), (0, 1)
            )
        )
        mirror = 2 * reach - offset
        same_back = (seg_wide[:, mirror : mirror + here] == seg_own)[:, :, None]
        grad_gated = grad_gated + depth_rows[offset] * jnp.where(
            same_back, grad_widened[:, mirror : mirror + here], 0.0
        )
    grad_gated = grad_gated.reshape(rows, model)
    grad_point = jnp.concatenate(
        [grad_gated * sigmoid_gate, grad_gated * linear * sigmoid_gate * (1.0 - sigmoid_gate)], 1
    ).astype(BF16)
    through, gain_two = norm_back(
        dot(grad_point, w_point_in, NT), conv_normed, conv_inverse, gain[2]
    )
    grad_two = grad_three + through
    grad_attn_out = grad_two.astype(BF16)
    grad_context = dot(grad_attn_out, w_out, NT).astype(BF16)
    grad_heads = []
    for number in range(batches):
        part = grad_context[number * here : (number + 1) * here]
        grad_heads.append(part.reshape(here, head_ways, -1).transpose(1, 0, 2))

    def ffn_grads():
        return (
            exchange(grad_heads[0]),
            out_grad((half_two, half_other), (hid_two, hid_other), head_ways, where, items),
            column_grads(
                [(ent_two, ent_other)], [(grad_pre_two, grad_pre_other)],
                head_ways, where, items,
            ),
        )

    grad_heads[0], shares_out, shares_in = fenced(always, (), ffn_grads)
    two_out, two_in = Scatter(*shares_out), Scatter(*shares_in)
    grads, backs = [], []
    for number in range(batches):

        def beside():
            extra = []
            if number + 1 < batches:
                extra.append(exchange(grad_heads[number + 1]))
            if number > 0:
                extra.append(exchange(grads[number - 1]))
            return extra

        def attend_now():
            return attend_backward(
                qkv[number], seg_counts[number], size, fulls[number], lses[number],
                grad_heads[number],
            )

        made, extra = fenced(
            always, (two_out, two_in) if number < 2 else (), lambda: (attend_now(), beside())
        )
        grads.append(made)
        if number + 1 < batches:
            grad_heads[number + 1] = extra.pop(0)
        if number > 0:
            backs.append(extra.pop(0))
        if number == 0:
            for scatter, sends in zip((two_out, two_in), second_sums(two_out, two_in)):
                scatter.second(sends)

    def middle_part():
        back = exchange(grads[-1])
        lefts = [(part, other_core(part)) for part in (mixed_low, conv_entered, context)]
        rights = [(part, other_core(part)) for part in (grad_mix, grad_point, grad_attn_out)]
        shares = column_grads(lefts, rights, head_ways, where, items)
        return (back, shares, last_sum(two_out, two_in))

    back, shares, two_sum = fenced(always, (), middle_part)
    backs.append(back)
    middle = Scatter(*shares)

    def attention_part():
        two_grads = along_z(two_sum)
        scatter = copy.copy(middle)

        def qkv_part():
            grad_proj = unturned(backs, cosines, sines, size)
            proj_other = other_core(grad_proj)
            down = stream_gradient(grad_two, stream_one, grad_proj, gain[1], w_qkv, F32)
            shares = column_grads(
                [ent_att], [(grad_proj, proj_other)], head_ways, where, items
            )
            return (down, shares)

        (grad_one, half_one, gain_one), shares = fenced(always, (scatter,), qkv_part)
        first = scatter.got
        scatter.second(second_sums(scatter)[0])
        attn = Scatter(*shares)
        (half_own, grad_pre), half_other = fenced(
            always,
            (attn,),
            lambda: (hidden_gradient(grad_one, pre_one, w_ffn1_out), other_core(half_one)),
        )
        pre_other, shares_out = fenced(
            always,
            (scatter,),
            lambda: (
                other_core(grad_pre),
                out_grad((half_own, half_other), hid_one, head_ways, where, items),
            ),
        )
        return (
            two_grads, first, scatter.got, (grad_one, gain_one), shares[:2], attn.got,
            (grad_pre, pre_other), shares_out,
        )

    two_grads, first, got, (grad_one, gain_one), shares, attn_got, grad_pre, shares_out = fenced(
        always, (), attention_part
    )
    middle.take(first)
    middle.take(got)
    attn = Scatter(*shares)
    attn.take(attn_got)
    attn.second(second_sums(attn)[0])
    one_out = Scatter(*shares_out)
    middle_columns = [w.shape[1] for w in (w_point_out, w_point_in, w_out)]
    middle_sum = last_sum(middle, columns=middle_columns)

    def first_part():
        return (
            along_z(middle_sum),
            column_grads([ent_one], [grad_pre], head_ways, where, items),
            stream_gradient(grad_one, stream, grad_pre[0], gain[0], w_ffn1_in, BF16),
        )

    middle_grad, shares_in, (grad_zero, _, gain_zero) = fenced(
        always, (one_out, attn), first_part
    )
    one_in = Scatter(*shares_in)
    one_out.second(second_sums(one_out)[0])

    attn_grad = fenced(always, (one_in, one_out), lambda: along_z(last_sum(attn)))
    one_in.second(second_sums(one_in)[0])

    def last_part():
        out = along_z(last_sum(one_out))
        scatter = copy.copy(one_in)
        moved(scatter)
        small = sum_everywhere(
            jnp.concatenate(
                [gain_zero, gain_one, gain_two, gain_three, gain_four, gain_five]
                + [tap[None] for tap in taps],
                0,
            )
        )
        return (out, along_z(last_sum(scatter)), small)

    one_out_grad, one_in_grad, small = fenced(always, (), last_part)
    hidden = w_ffn1_in.shape[1]

    def unfolded(share):
        each, wide = share.shape
        span = hidden // head_ways
        halves = share.reshape(2, each // 2, wide)
        parts = [
            halves[half, :, i * span : (i + 1) * span]
            for i in range(wide // span)
            for half in range(2)
        ]
        return jnp.concatenate(parts, 0).T.astype(F32)

    middle_parts = []
    start = 0
    for weight in (w_point_out, w_point_in, w_out):
        each = weight.shape[1] // lax.axis_size("items")
        middle_parts.append(middle_grad[0][:, start : start + each].astype(F32))
        start += each
    return (
        layer_out,
        grad_zero.reshape(frames.shape),
        small[:6],
        one_in_grad[0].astype(F32),
        unfolded(one_out_grad[0]),
        attn_grad[0].astype(F32),
        middle_parts[2],
        middle_parts[1],
        small[6:],
        middle_parts[0],
        two_grads[1].astype(F32),
        unfolded(two_grads[0]),
    )


def solution(mesh):
    split = P(None, EVERY, None)
    shares = P("heads", "items")
    in_specs = (split, split, P(None, "items", None)) + (P(),) * 10
    out_specs = (split, split, P(), shares, shares, shares, shares, shares, P()) + (shares,) * 3
    return jax.shard_map(body, mesh=mesh, in_specs=in_specs, out_specs=out_specs, check_vma=False)
```

```python
import copy
import functools

import jax
import jax.numpy as jnp
from jax import lax
from jax.experimental import pallas as pl
from jax.experimental.pallas import tpu as pltpu
from jax.sharding import PartitionSpec as P

HEADS = 16
KERNEL = 5
LONG = 1500
SHORT = 500
EPS = 1e-05
ROPE_BASE = 10000.0
BLOCK = 512
INNER_FWD = 1024
INNER_BWD = 512
LANES = 128
BIG = 1e30
VMEM_LIMIT = 56 << 20
F32 = jnp.float32
BF16 = jnp.bfloat16
NN = (((1,), (0,)), ((), ()))
NT = (((1,), (1,)), ((), ()))
EVERY = ("items", "heads")
FIRST = [("items", 1), ("items", 2)]


def dot(left, right, dims=NN):
    return lax.dot_general(left, right, dims, preferred_element_type=F32)


def silu_slope(field):
    gate_sig = jax.nn.sigmoid(field)
    return gate_sig * (1.0 + field * (1.0 - gate_sig))


def layer_norm(field, gain_row):
    centred = field - jnp.mean(field, -1, keepdims=True)
    inverse = lax.rsqrt(jnp.mean(centred * centred, -1, keepdims=True) + EPS)
    normed = centred * inverse
    return (normed * gain_row, normed, inverse)


def norm_back(upstream, normed, inverse, gain_row):
    scaled = upstream * gain_row
    through = inverse * (
        scaled
        - jnp.mean(scaled, -1, keepdims=True)
        - normed * jnp.mean(scaled * normed, -1, keepdims=True)
    )
    return (through, jnp.sum(upstream * normed, 0, keepdims=True))


def segment_ids(position, long_count, short_count, group_len):
    long_end = long_count * LONG
    short_end = long_end + short_count * SHORT
    segments = jnp.where(
        position < long_end, position // LONG, long_count + (position - long_end) // SHORT
    )
    segments = jnp.where(position < short_end, segments, long_count + short_count)
    return jnp.where((position < 0) | (position >= group_len), -1, segments)


def compiler_params():
    return pltpu.CompilerParams(vmem_limit_bytes=VMEM_LIMIT)


def whole(shape):
    return pl.BlockSpec(shape, lambda *_: (0,) * len(shape))


def cost(flops, bytes_accessed, transcendentals=0):
    return pl.CostEstimate(
        flops=flops, bytes_accessed=bytes_accessed, transcendentals=transcendentals
    )


def segment_bounds(counts, place, group):
    longs, shorts = counts
    long_end = longs * LONG
    short_end = long_end + shorts * SHORT
    start = jnp.where(place < longs, place * LONG, long_end + (place - longs) * SHORT)
    size = jnp.where(place < longs, LONG, SHORT)
    last = place == longs + shorts
    return (jnp.where(last, short_end, start), jnp.where(last, group, start + size), place <= longs + shorts)


def member_lanes(counts, first, rows, group, shift=0):
    shape = (rows, LANES)
    place = lax.broadcasted_iota(jnp.int32, (8, LANES), 1) - shift
    start, end, there = segment_bounds(counts, place, group)
    start = jnp.where(there & (place >= 0), start, group)
    start, end = start[:1], end[:1]
    frame = first + lax.broadcasted_iota(jnp.int32, shape, 0)
    return (frame >= start) & (frame < end)


def block_range(counts, step, group, inner):
    longs, shorts = counts
    long_end = longs * LONG
    short_end = long_end + shorts * SHORT

    def number(frame):
        place = jnp.where(frame < long_end, frame // LONG, longs + (frame - long_end) // SHORT)
        return jnp.where(frame < short_end, place, longs + shorts)

    first = segment_bounds(counts, number(step * BLOCK), group)[0]
    last = segment_bounds(counts, number(step * BLOCK + BLOCK - 1), group)[1]
    return (first // inner, (last + inner - 1) // inner)


def head_lanes(shape, head, size):
    lane = lax.broadcasted_iota(jnp.int32, shape, 1)
    return (lane >= head * size) & (lane < (head + 1) * size)


def split_three(v):
    hi = v.astype(BF16).astype(F32)
    rest = v - hi
    mid = rest.astype(BF16).astype(F32)
    return (hi, mid, rest - mid)


def spread_columns(columns, shape):
    lane = lax.broadcasted_iota(jnp.int32, shape, 1)
    out = jnp.zeros(shape, F32)
    for place, column in enumerate(columns):
        out = jnp.where(lane == place, column, out)
    return out


def chunk_rows(ref, lead, step):
    places, chunks, frames = ref.shape[0], ref.shape[-3], ref.shape[-2]
    per = BLOCK // frames
    steps = places // per
    at = (pl.ds(step % steps * per, per),) + lead + (step // steps,)
    return ref[at].reshape(BLOCK, LANES)


def attn_fwd_kernel(
    heads, size, group, counts_ref, qkv_ref, out_ref, full_ref, lse_ref, kcat, v_all, s_scr
):
    step = pl.program_id(0)
    counts = (counts_ref[0], counts_ref[1])

    @pl.when(step == 0)
    def _():
        chunks = qkv_ref.shape[2]
        span = group // chunks
        for chunk in range(chunks):
            rows = slice(chunk * span, (chunk + 1) * span)
            kcat[rows, :LANES] = qkv_ref[:, 1, chunk].reshape(span, LANES)
            v_all[rows, :] = qkv_ref[:, 2, chunk].reshape(span, LANES)
        kcat[:, LANES:] = jnp.where(member_lanes(counts, 0, group, group), 0.0, -BIG).astype(BF16)

    q = chunk_rows(qkv_ref, (0,), step).astype(F32) * (size ** -0.5)
    member = jnp.where(member_lanes(counts, step * BLOCK, BLOCK, group), 1.0, 0.0).astype(BF16)
    queries = []
    for head in range(heads):
        mine = jnp.where(head_lanes(q.shape, head, size), q, 0.0).astype(BF16)
        queries.append(jnp.concatenate([mine, member], 1))
    low, high = block_range(counts, step, group, INNER_FWD)

    def scores(j, tops):
        keys = kcat[pl.ds(pl.multiple_of(j * INNER_FWD, INNER_FWD), INNER_FWD), :]
        new = []
        for head in range(heads):
            s = dot(queries[head], keys, NT)
            s_scr[head, j] = s
            top = tops[head]
            for part in range(INNER_FWD // LANES):
                top = jnp.maximum(top, s[:, part * LANES : (part + 1) * LANES])
            new.append(top)
        return tuple(new)

    start = tuple(jnp.full((BLOCK, LANES), -BIG, F32) for _ in range(heads))
    tops = lax.fori_loop(low, high, scores, start)
    tops = [jnp.max(t, 1, keepdims=True) for t in tops]
    tops = [jnp.broadcast_to(t, (BLOCK, LANES)) for t in tops]

    def weigh(j, carried):
        sums, accs = carried
        values = v_all[pl.ds(pl.multiple_of(j * INNER_FWD, INNER_FWD), INNER_FWD), :]
        new_sums, new_accs = [], []
        for head in range(heads):
            total = sums[head]
            parts = []
            for part in range(INNER_FWD // LANES):
                p = jnp.exp(s_scr[head, j, :, part * LANES : (part + 1) * LANES] - tops[head])
                total = total + p
                parts.append(p.astype(BF16))
            new_sums.append(total)
            new_accs.append(accs[head] + dot(jnp.concatenate(parts, 1), values))
        return (tuple(new_sums), tuple(new_accs))

    zeros = tuple(jnp.zeros((BLOCK, LANES), F32) for _ in range(heads))
    sums, accs = lax.fori_loop(low, high, weigh, (zeros, zeros))
    result = None
    for head in range(heads):
        total = jnp.sum(sums[head], 1, keepdims=True)
        mine = accs[head] / total
        if result is None:
            result = mine
        else:
            result = jnp.where(head_lanes(mine.shape, head, size), mine, result)
        lse_ref[head] = tops[head] + jnp.log(jnp.broadcast_to(total, (BLOCK, LANES)))
    full_ref[...] = result
    out_ref[...] = result.astype(BF16).reshape(out_ref.shape)


def attend_forward(qkv, counts, size):
    places, _, chunks, frames, _ = qkv.shape
    group = places * chunks * frames
    heads = LANES // size
    per = BLOCK // frames
    each = places // per
    return pl.pallas_call(
        functools.partial(attn_fwd_kernel, heads, size, group),
        grid=(group // BLOCK,),
        in_specs=[pl.BlockSpec(memory_space=pltpu.SMEM), whole(qkv.shape)],
        out_specs=[
            pl.BlockSpec((per, 1, frames, LANES), lambda i: (i % each, i // each, 0, 0)),
            pl.BlockSpec((BLOCK, LANES), lambda i: (i, 0)),
            pl.BlockSpec((heads, BLOCK, LANES), lambda i: (0, i, 0)),
        ],
        out_shape=[
            jax.ShapeDtypeStruct((places, chunks, frames, LANES), BF16),
            jax.ShapeDtypeStruct((group, LANES), F32),
            jax.ShapeDtypeStruct((heads, group, LANES), F32),
        ],
        scratch_shapes=[
            pltpu.VMEM((group, 2 * LANES), BF16),
            pltpu.VMEM((group, LANES), BF16),
            pltpu.VMEM((heads, group // INNER_FWD, BLOCK, INNER_FWD), F32),
        ],
        compiler_params=compiler_params(),
        cost_estimate=cost(16 * group * group * LANES, 6 << 20, heads * group * group),
        name="attend_forward",
    )(counts, qkv)


def attn_bwd_kernel(
    heads, size, group, counts_ref, qkv_ref, full_ref, lse_ref, grad_ref, out_ref,
    qcat, gcat, k_turned, dq_turned,
):
    step = pl.program_id(0)
    counts = (counts_ref[0], counts_ref[1])
    blocks = group // BLOCK
    places, _, _, frames, _ = qkv_ref.shape
    per = BLOCK // frames
    each = places // per

    def put(part, j, value):
        out_ref[pl.ds(j % each * per, per), part, j // each] = value.astype(BF16).reshape(
            per, frames, LANES
        )

    @pl.when(step == 0)
    def _():
        dq_turned[...] = jnp.zeros_like(dq_turned)

        def prepare(j, _):
            rows = pl.ds(pl.multiple_of(j * BLOCK, BLOCK), BLOCK)
            lane = lax.broadcasted_iota(jnp.int32, (BLOCK, LANES), 1)
            q = chunk_rows(qkv_ref, (0,), j).astype(F32) * (size ** -0.5)
            g = chunk_rows(grad_ref, (), j).astype(F32)
            product = g * full_ref[rows, :]
            member = jnp.where(member_lanes(counts, j * BLOCK, BLOCK, group, 3), 1.0, 0.0)
            for head in range(heads):
                own = head_lanes((BLOCK, LANES), head, size)
                lse = lse_ref[head, rows, :]
                spread = spread_columns(split_three(lse), (BLOCK, LANES))
                delta = jnp.sum(jnp.where(own, product, 0.0), 1, keepdims=True)
                delta = jnp.broadcast_to(delta, (BLOCK, LANES))
                qcat[head, rows, :LANES] = jnp.where(own, q, 0.0).astype(BF16)
                qcat[head, rows, LANES:] = jnp.where(lane < 3, -spread, member).astype(BF16)
                gcat[head, rows, :LANES] = jnp.where(own, g, 0.0).astype(BF16)
                spread = spread_columns(split_three(delta), (BLOCK, LANES))
                gcat[head, rows, LANES:] = (-spread).astype(BF16)
            k = chunk_rows(qkv_ref, (1,), j).astype(F32)
            k_turned[j] = jnp.transpose(k).astype(BF16)
            return 0

        lax.fori_loop(0, blocks, prepare, 0)

    lane = lax.broadcasted_iota(jnp.int32, (BLOCK, LANES), 1)
    member = member_lanes(counts, step * BLOCK, BLOCK, group, 3)
    tail = jnp.where(lane < 3, 1.0, jnp.where(member, 0.0, -BIG)).astype(BF16)
    keys = jnp.concatenate([chunk_rows(qkv_ref, (1,), step), tail], 1)
    ones = jnp.where(lane < 3, 1.0, 0.0).astype(BF16)
    values = jnp.concatenate([chunk_rows(qkv_ref, (2,), step), ones], 1)

    def one(j, carried):
        dk, dv = carried
        cols = pl.ds(pl.multiple_of(j * INNER_BWD, INNER_BWD), INNER_BWD)
        for head in range(heads):
            qc = qcat[head, cols, :]
            gc = gcat[head, cols, :]
            p = jnp.exp(dot(keys, qc, NT))
            ds = (p * dot(values, gc, NT)).astype(BF16)
            dv = dv + dot(p.astype(BF16), gc[:, :LANES])
            dk = dk + dot(ds, qc[:, :LANES])
            mine = slice(head * size, (head + 1) * size)
            dq_turned[j, mine, :] += dot(k_turned[step, mine, :], ds)
        return (dk, dv)

    zero = jnp.zeros((BLOCK, LANES), F32)
    low, high = block_range(counts, step, group, INNER_BWD)
    dk, dv = lax.fori_loop(low, high, one, (zero, zero))
    put(1, step, dk)
    put(2, step, dv)

    @pl.when(step == blocks - 1)
    def _():
        def finish(j, _):
            put(0, j, jnp.transpose(dq_turned[j]) * (size ** -0.5))
            return 0

        lax.fori_loop(0, blocks, finish, 0)


def attend_backward(qkv, counts, size, full, lse, grad):
    places, _, chunks, frames, _ = qkv.shape
    group = places * chunks * frames
    heads = LANES // size
    steps = group // BLOCK
    return pl.pallas_call(
        functools.partial(attn_bwd_kernel, heads, size, group),
        grid=(steps,),
        in_specs=[
            pl.BlockSpec(memory_space=pltpu.SMEM),
            whole(qkv.shape),
            whole(full.shape),
            whole(lse.shape),
            whole(grad.shape),
        ],
        out_specs=whole(qkv.shape),
        out_shape=jax.ShapeDtypeStruct(qkv.shape, BF16),
        scratch_shapes=[
            pltpu.VMEM((heads, group, 2 * LANES), BF16),
            pltpu.VMEM((heads, group, 2 * LANES), BF16),
            pltpu.VMEM((steps, LANES, BLOCK), BF16),
            pltpu.VMEM((group // INNER_BWD, LANES, INNER_BWD), F32),
        ],
        compiler_params=compiler_params(),
        cost_estimate=cost(32 * group * group * LANES, 9 << 20, heads * group * group),
        name="attend_backward",
    )(counts, qkv, full, lse, grad)


def half_gate(field):
    return 0.5 * jnp.tanh(0.5 * field) + 0.5


def hidden_units(pre):
    gate = half_gate(pre)
    hidden = pre * gate
    return (hidden.astype(BF16), (gate + hidden * (1.0 - gate)).astype(BF16))


def ffn_fwd_kernel(
    x_ref, gain_ref, last_gain_ref, up_ref, win_ref, wout_ref,
    out_ref, down_ref, gain_grad_ref, slope_ref, hid_ref, entered_ref, total,
):
    step = pl.program_id(0)

    @pl.when(step == 0)
    def _():
        entered_ref[...] = layer_norm(x_ref[...], gain_ref[...])[0].astype(BF16)
        total[...] = jnp.zeros_like(total)

    hidden, slope = hidden_units(dot(entered_ref[...], win_ref[...]))
    slope_ref[...] = slope
    hid_ref[...] = hidden
    total[...] += dot(hidden, wout_ref[...])

    @pl.when(step == pl.num_programs(0) - 1)
    def _():
        gain = last_gain_ref[...]
        shaped, normed, inverse = layer_norm(x_ref[...] + 0.5 * total[...], gain)
        out_ref[...] = shaped.astype(BF16)
        through, grad_gain = norm_back(up_ref[...].astype(F32), normed, inverse, gain)
        down_ref[...] = through
        gain_grad_ref[...] = grad_gain


def ffn_forward(stream, gain_row, weight_in, weight_out, last_gain, upstream):
    rows, model = stream.shape
    units = weight_in.shape[1]
    wide = 512
    return pl.pallas_call(
        ffn_fwd_kernel,
        grid=(units // wide,),
        in_specs=[
            whole((rows, model)),
            whole((1, model)),
            whole((1, model)),
            whole((rows, model)),
            pl.BlockSpec((model, wide), lambda s: (0, s)),
            pl.BlockSpec((wide, model), lambda s: (s, 0)),
        ],
        out_specs=[whole((rows, model)), whole((rows, model)), whole((1, model))]
        + [pl.BlockSpec((rows, wide), lambda s: (0, s))] * 2
        + [whole((rows, model))],
        out_shape=[
            jax.ShapeDtypeStruct((rows, model), BF16),
            jax.ShapeDtypeStruct((rows, model), F32),
            jax.ShapeDtypeStruct((1, model), F32),
            jax.ShapeDtypeStruct((rows, units), BF16),
            jax.ShapeDtypeStruct((rows, units), BF16),
            jax.ShapeDtypeStruct((rows, model), BF16),
        ],
        scratch_shapes=[pltpu.VMEM((rows, model), F32)],
        compiler_params=compiler_params(),
        cost_estimate=cost(4 * rows * model * units, 4 * model * units + 4 * rows * units),
        name="ffn_forward",
    )(stream, gain_row, last_gain, upstream, weight_in, weight_out)


def ffn_bwd_kernel(
    x_ref, gain_ref, up_ref, slope_ref, win_ref, wout_ref,
    down_ref, gain_grad_ref, half_ref, grad_ref, total,
):
    step = pl.program_id(0)

    @pl.when(step == 0)
    def _():
        half_ref[...] = (0.5 * up_ref[...]).astype(BF16)
        total[...] = jnp.zeros_like(total)

    grad = (dot(half_ref[...], wout_ref[...], NT) * slope_ref[...].astype(F32)).astype(BF16)
    grad_ref[...] = grad
    total[...] += dot(grad, win_ref[...], NT)

    @pl.when(step == pl.num_programs(0) - 1)
    def _():
        gain = gain_ref[...]
        normed, inverse = layer_norm(x_ref[...].astype(F32), gain)[1:]
        through, grad_gain = norm_back(total[...], normed, inverse, gain)
        down_ref[...] = up_ref[...] + through
        gain_grad_ref[...] = grad_gain


def ffn_backward(upstream, stream, slope, gain_row, weight_in, weight_out):
    rows, model = stream.shape
    units = weight_in.shape[1]
    wide = 512
    return pl.pallas_call(
        ffn_bwd_kernel,
        grid=(units // wide,),
        in_specs=[
            whole((rows, model)),
            whole((1, model)),
            whole((rows, model)),
            pl.BlockSpec((rows, wide), lambda s: (0, s)),
            pl.BlockSpec((model, wide), lambda s: (0, s)),
            pl.BlockSpec((wide, model), lambda s: (s, 0)),
        ],
        out_specs=[
            whole((rows, model)),
            whole((1, model)),
            whole((rows, model)),
            pl.BlockSpec((rows, wide), lambda s: (0, s)),
        ],
        out_shape=[
            jax.ShapeDtypeStruct((rows, model), F32),
            jax.ShapeDtypeStruct((1, model), F32),
            jax.ShapeDtypeStruct((rows, model), BF16),
            jax.ShapeDtypeStruct((rows, units), BF16),
        ],
        scratch_shapes=[pltpu.VMEM((rows, model), F32)],
        compiler_params=compiler_params(),
        cost_estimate=cost(4 * rows * model * units, 4 * model * units + 6 * rows * units),
        name="ffn_backward",
    )(stream, gain_row, upstream, slope, weight_in, weight_out)


def hidden_kernel(up_ref, slope_ref, wout_ref, half_ref, grad_ref):
    @pl.when(pl.program_id(0) == 0)
    def _():
        half_ref[...] = (0.5 * up_ref[...]).astype(BF16)

    grad = dot(half_ref[...], wout_ref[...], NT) * slope_ref[...].astype(F32)
    grad_ref[...] = grad.astype(BF16)


def hidden_gradient(upstream, slope, weight_out):
    rows, model = upstream.shape
    units = weight_out.shape[0]
    wide = 512
    return pl.pallas_call(
        hidden_kernel,
        grid=(units // wide,),
        in_specs=[
            whole((rows, model)),
            pl.BlockSpec((rows, wide), lambda s: (0, s)),
            pl.BlockSpec((wide, model), lambda s: (s, 0)),
        ],
        out_specs=[whole((rows, model)), pl.BlockSpec((rows, wide), lambda s: (0, s))],
        out_shape=[
            jax.ShapeDtypeStruct((rows, model), BF16),
            jax.ShapeDtypeStruct((rows, units), BF16),
        ],
        compiler_params=compiler_params(),
        cost_estimate=cost(2 * rows * model * units, 2 * model * units + 6 * rows * units),
        name="hidden_gradient",
    )(upstream, slope, weight_out)


def down_kernel(
    x_ref, gain_ref, up_ref, grad_ref, weight_ref, down_ref, half_ref, gain_grad_ref, total
):
    step = pl.program_id(0)

    @pl.when(step == 0)
    def _():
        total[...] = jnp.zeros_like(total)

    total[...] += dot(grad_ref[...], weight_ref[...], NT)

    @pl.when(step == pl.num_programs(0) - 1)
    def _():
        gain = gain_ref[...]
        normed, inverse = layer_norm(x_ref[...].astype(F32), gain)[1:]
        through, grad_gain = norm_back(total[...], normed, inverse, gain)
        down = up_ref[...] + through
        down_ref[...] = down.astype(down_ref.dtype)
        half_ref[...] = (0.5 * down).astype(BF16)
        gain_grad_ref[...] = grad_gain


def stream_gradient(upstream, stream, grad, gain_row, weight, down_type):
    rows, model = stream.shape
    units = weight.shape[1]
    wide = 512
    return pl.pallas_call(
        down_kernel,
        grid=(units // wide,),
        in_specs=[
            whole((rows, model)),
            whole((1, model)),
            whole((rows, model)),
            pl.BlockSpec((rows, wide), lambda s: (0, s)),
            pl.BlockSpec((model, wide), lambda s: (0, s)),
        ],
        out_specs=[whole((rows, model)), whole((rows, model)), whole((1, model))],
        out_shape=[
            jax.ShapeDtypeStruct((rows, model), down_type),
            jax.ShapeDtypeStruct((rows, model), BF16),
            jax.ShapeDtypeStruct((1, model), F32),
        ],
        scratch_shapes=[pltpu.VMEM((rows, model), F32)],
        compiler_params=compiler_params(),
        cost_estimate=cost(2 * rows * model * units, 2 * model * units + 2 * rows * units),
        name="stream_gradient",
    )(stream, gain_row, upstream, grad, weight)


def turn(field, cosines, sines, size):
    lane = lax.broadcasted_iota(jnp.int32, field.shape, 1)
    half = size // 2
    width = field.shape[1]
    swapped = jnp.where(
        lane % size < half,
        pltpu.roll(field, width - half, 1),
        pltpu.roll(field, half, 1),
    )
    return field * cosines + swapped * sines


def rope_tables(position, size, width):
    half = size // 2
    freqs = jnp.exp(
        -jnp.log(jnp.float32(ROPE_BASE)) * jnp.arange(half, dtype=jnp.float32) / half
    )
    angles = position.astype(jnp.float32)[:, None] * freqs[None, :]
    cosines, sines = jnp.cos(angles), jnp.sin(angles)
    repeats = width // size
    return (
        jnp.tile(jnp.concatenate([cosines, cosines], 1), (1, repeats)),
        jnp.tile(jnp.concatenate([-sines, sines], 1), (1, repeats)),
    )


def front_kernel(
    size, ffn_steps, pieces, row_ref, x_ref, gain_ref, next_gain_ref, win_ref, wout_ref,
    wq_ref, wk_ref, wv_ref, cos_ref, sin_ref, *refs,
):
    refs = refs[-(6 + pieces) :]
    out_ref, slope_ref, hid_ref, entered_ref, next_ref = refs[:5]
    outs, total = refs[5:-1], refs[-1]
    step = pl.program_id(0)

    @pl.when(step == 0)
    def _():
        entered_ref[...] = layer_norm(x_ref[...].astype(F32), gain_ref[...])[0].astype(BF16)
        total[...] = jnp.zeros_like(total)

    @pl.when(step < ffn_steps)
    def _():
        hidden, slope = hidden_units(dot(entered_ref[...], win_ref[...]))
        slope_ref[...] = slope
        hid_ref[...] = hidden
        total[...] += dot(hidden, wout_ref[...])

    @pl.when(step == ffn_steps)
    def _():
        out = x_ref[...].astype(F32) + 0.5 * total[...]
        out_ref[...] = out
        next_ref[...] = layer_norm(out, next_gain_ref[...])[0].astype(BF16)

    each = (pl.num_programs(0) - ffn_steps) // pieces
    for piece, out in enumerate(outs):

        @pl.when((step >= ffn_steps) & ((step - ffn_steps) // each == piece))
        def _():
            for place, weight in enumerate((wq_ref, wk_ref, wv_ref)):
                made = dot(next_ref[...], weight[...])
                if place < 2:
                    made = turn(made, cos_ref[...], sin_ref[...], size)
                made = made.astype(BF16)
                for target in range(out.shape[0]):
                    out[target, place, 0] = made[:, target * LANES : (target + 1) * LANES]


def front(
    frames, row, gain_row, weight_in, weight_out, next_gain, weight, cosines, sines,
    places, chunks, size, before=(),
):
    rows, model = frames.shape
    units = weight_in.shape[1]
    wide = 512
    ffn_steps = units // wide
    turned_wide = cosines.shape[1]
    turns = model // turned_wide
    pieces = model // (places * LANES)
    each = turns // pieces
    piece = jax.ShapeDtypeStruct((places, 3, chunks, rows, LANES), BF16)

    def ffn_at(s, row):
        return jnp.minimum(s, ffn_steps - 1)

    def turn_at(s):
        return jnp.maximum(s - ffn_steps, 0)

    def piece_at(number):
        return lambda s, row: (
            jnp.clip(s - ffn_steps - number * each, 0, each - 1), 0, row[0], 0, 0
        )

    row_block = pl.BlockSpec((rows, model), lambda s, row: (row[0], 0))
    unit_block = pl.BlockSpec((rows, wide), lambda s, row: (row[0], ffn_at(s, row)))
    angle_block = pl.BlockSpec((rows, turned_wide), lambda s, row: (row[0], 0))
    out_shape = [
        jax.ShapeDtypeStruct((chunks * rows, model), F32),
        jax.ShapeDtypeStruct((chunks * rows, units), BF16),
        jax.ShapeDtypeStruct((chunks * rows, units), BF16),
        jax.ShapeDtypeStruct((chunks * rows, model), BF16),
        jax.ShapeDtypeStruct((chunks * rows, model), BF16),
    ] + [piece] * pieces
    in_specs = [
        whole((rows, model)),
        whole((1, model)),
        whole((1, model)),
        pl.BlockSpec((model, wide), lambda s, row: (0, ffn_at(s, row))),
        pl.BlockSpec((wide, model), lambda s, row: (ffn_at(s, row), 0)),
        pl.BlockSpec((model, turned_wide), lambda s, row: (0, turn_at(s))),
        pl.BlockSpec((model, turned_wide), lambda s, row: (0, turns + turn_at(s))),
        pl.BlockSpec((model, turned_wide), lambda s, row: (0, 2 * turns + turn_at(s))),
        angle_block,
        angle_block,
    ]
    grid_spec = pltpu.PrefetchScalarGridSpec(
        num_scalar_prefetch=1,
        grid=(ffn_steps + turns,),
        in_specs=in_specs + [pl.BlockSpec(memory_space=pl.ANY)] * len(before),
        out_specs=[row_block, unit_block, unit_block, row_block, row_block]
        + [
            pl.BlockSpec((turned_wide // LANES, 3, 1, rows, LANES), piece_at(number))
            for number in range(pieces)
        ],
        scratch_shapes=[pltpu.VMEM((rows, model), F32)],
    )
    return pl.pallas_call(
        functools.partial(front_kernel, size, ffn_steps, pieces),
        grid_spec=grid_spec,
        out_shape=out_shape,
        input_output_aliases={1 + len(in_specs) + i: i for i in range(len(before))},
        compiler_params=compiler_params(),
        cost_estimate=cost(
            4 * rows * model * units + 6 * rows * model * model,
            4 * model * units + 6 * model * model + 4 * rows * units + 16 * rows * model,
        ),
        name="front",
    )(
        row, frames, gain_row, next_gain, weight_in, weight_out, weight, weight, weight,
        cosines, sines, *before,
    )


def unturn_kernel(size, pieces, cos_ref, sin_ref, *refs):
    backs, out = refs[:pieces], refs[pieces]
    rotated = pl.program_id(0) < 2
    cosines = jnp.where(rotated, cos_ref[...], 1.0)
    sines = jnp.where(rotated, -sin_ref[...], 0.0)
    places, _, chunks, frames, _ = backs[0].shape
    wide = cosines.shape[1]
    per = wide // LANES
    for piece, back in enumerate(backs):
        for first in range(0, places, per):
            for chunk in range(chunks):
                rows = slice(chunk * frames, (chunk + 1) * frames)
                field = jnp.concatenate([back[first + i, 0, chunk] for i in range(per)], 1)
                made = turn(field.astype(F32), cosines[rows], sines[rows], size).astype(BF16)
                start = (piece * places + first) * LANES
                out[rows, start : start + wide] = made


def unturned(backs, cosines, sines, size):
    places, kinds, chunks, frames, _ = backs[0].shape
    pieces = len(backs)
    block = pl.BlockSpec((places, 1, chunks, frames, LANES), lambda s: (0, s, 0, 0, 0))
    model = pieces * places * LANES
    return pl.pallas_call(
        functools.partial(unturn_kernel, size, pieces),
        grid=(kinds,),
        in_specs=[whole(cosines.shape), whole(sines.shape)] + [block] * pieces,
        out_specs=pl.BlockSpec((chunks * frames, model), lambda s: (0, s)),
        out_shape=jax.ShapeDtypeStruct((chunks * frames, kinds * model), BF16),
        compiler_params=compiler_params(),
        cost_estimate=cost(0, 4 * chunks * frames * kinds * model),
        name="unturned",
    )(cosines, sines, *backs)


def flipped(axis_bit, count):
    axis, bit = axis_bit
    items, heads = count
    if axis == "items":
        return [(i * heads + h, (i ^ bit) * heads + h) for i in range(items) for h in range(heads)]
    return [(i * heads + h, i * heads + (h ^ bit)) for i in range(items) for h in range(heads)]


def swap(value, axis_bit):
    count = (lax.axis_size("items"), lax.axis_size("heads"))
    return lax.ppermute(value, EVERY, flipped(axis_bit, count))


def fenced(always, scatters, work):
    def run():
        return (work(), [scatter.move() for scatter in scatters])

    def empty():
        return jax.tree.map(lambda leaf: jnp.zeros(leaf.shape, leaf.dtype), jax.eval_shape(run))

    result, moved = lax.optimization_barrier(lax.cond(always, run, empty))
    for scatter, parts in zip(scatters, moved):
        scatter.take(parts)
    return result


def moved(scatter):
    scatter.take(scatter.move())


def other_core(value):
    return swap(value, ("heads", 1))


def exchange(value):
    half = lax.axis_size("heads") // 2
    groups = [[side * half + i for i in range(half)] for side in range(2)]
    return lax.all_to_all(
        value, "heads", split_axis=0, concat_axis=0, tiled=True, axis_index_groups=groups
    )


def across(value):
    return swap(value, ("heads", lax.axis_size("heads") // 2))


def gathered(own, other, side):
    return jnp.concatenate([jnp.where(side == 0, own, other), jnp.where(side == 0, other, own)], 0)


def parted(value, side):
    low, high = jnp.split(value, 2, 0)
    return (jnp.where(side == 0, low, high), jnp.where(side == 0, high, low))


def own_rows(left_ref, heads, core, target, first):
    rows, model = left_ref.shape
    each = model // heads
    for place in range(heads // 2):
        if each % LANES == 0:
            start = pl.multiple_of((2 * place + core) * each, each)
            mine = jnp.transpose(left_ref[:, pl.ds(start, each)].astype(F32)).astype(BF16)
        else:
            pair = left_ref[:, 2 * place * each : 2 * (place + 1) * each]
            pair = jnp.transpose(pair.astype(F32))
            mine = jnp.where(core == 0, pair[:each], pair[each:]).astype(BF16)
        for half in range(2):
            start = (half * (heads // 2) + place) * (each // 2)
            target[start : start + each // 2, first : first + rows] = mine[
                half * (each // 2) : (half + 1) * (each // 2)
            ]


def turned_items(left, items, own, target, first):
    rows, model = left.shape
    each = model // items
    for item in range(items):
        part = jnp.transpose(left[:, item * each : (item + 1) * each].astype(F32)).astype(BF16)
        place = pl.multiple_of((own ^ item) * each, each)
        target[pl.ds(place, each), first : first + rows] = part


def share_shapes(items, heads, model, columns):
    lead = 2 if items > 1 else 1
    shape = (lead, heads // 2, model // heads // 2, columns // items)
    return [jax.ShapeDtypeStruct(shape, BF16)] * (4 if items > 1 else 2)


def out_grad_kernel(place_ref, up_own, up_other, hid_own, hid_other, *refs):
    targets, turned = refs[:-1], refs[-1]
    rows, model = up_own.shape
    items = 4 if len(targets) == 4 else 1

    @pl.when(pl.program_id(0) == 0)
    def _():
        turned_items(up_own[...], items, place_ref[1], turned, 0)
        turned_items(up_other[...], items, place_ref[1], turned, rows)

    hidden = jnp.concatenate([hid_own[...], hid_other[...]], 0)
    grad = dot(turned[...], hidden).astype(BF16)
    wide = grad.shape[1]
    each = targets[0].shape[2]
    parts = model // items // (2 * each)
    for r in range(items):
        for part in range(parts):
            for half in range(2):
                first = ((r * parts + part) * 2 + half) * each
                piece = grad[first : first + each]
                if half == 0:
                    target, at = targets[2 * (r % 2)], r // 2
                else:
                    target, at = targets[1 + 2 * (r // 2)], r % 2
                target[at, 0, :, part * wide : (part + 1) * wide] = piece


def out_grad(upstream, hidden, heads, place, items):
    rows, model = upstream[0].shape
    units = hidden[0].shape[1]
    wide = units // heads
    shapes = share_shapes(items, heads, model, units)
    block = (shapes[0].shape[0], 1) + shapes[0].shape[2:]
    hid_block = pl.BlockSpec((rows, wide), lambda s, place: (0, 2 * s + place[0]))
    grid_spec = pltpu.PrefetchScalarGridSpec(
        num_scalar_prefetch=1,
        grid=(heads // 2,),
        in_specs=[whole((rows, model))] * 2 + [hid_block] * 2,
        out_specs=[pl.BlockSpec(block, lambda s, place: (0, s, 0, 0))] * len(shapes),
        scratch_shapes=[pltpu.VMEM((model, 2 * rows), BF16)],
    )
    return pl.pallas_call(
        out_grad_kernel,
        grid_spec=grid_spec,
        out_shape=shapes,
        compiler_params=compiler_params(),
        cost_estimate=cost(2 * rows * model * units, 2 * model * units + 4 * rows * units),
        name="out_grad",
    )(place, *upstream, *hidden)


def column_grad_kernel(heads, count, place_ref, *refs):
    lefts, refs = refs[: 2 * count], refs[2 * count :]
    rights, refs = refs[: 2 * count], refs[2 * count :]
    targets, turned = refs[:-count], refs[-count:]
    r = pl.program_id(0)
    rows = lefts[0].shape[0]

    @pl.when(r == 0)
    def _():
        for number in range(count):
            for other in range(2):
                own_rows(
                    lefts[2 * number + other], heads, place_ref[0], turned[number], other * rows
                )

    made = []
    for number in range(count):
        right = jnp.concatenate([rights[2 * number][...], rights[2 * number + 1][...]], 0)
        made.append(dot(turned[number][...], right).astype(BF16))
    made = made[0] if count == 1 else jnp.concatenate(made, 1)
    half = made.shape[0] // 2
    top, low = made[:half].reshape(targets[0].shape), made[half:].reshape(targets[0].shape)
    if len(targets) == 2:
        targets[0][...] = top
        targets[1][...] = low
        return

    @pl.when(r % 2 == 0)
    def _():
        targets[0][...] = top

    @pl.when(r % 2 == 1)
    def _():
        targets[2][...] = top

    @pl.when(r < 2)
    def _():
        targets[1][...] = low

    @pl.when(r >= 2)
    def _():
        targets[3][...] = low


def column_grads(lefts, rights, heads, place, items):
    rows, model = lefts[0][0].shape
    columns = sum(right[0].shape[1] for right in rights)
    shapes = share_shapes(items, heads, model, columns)
    block = (1,) + shapes[0].shape[1:]
    maps = [
        lambda r, place: (r // 2, 0, 0, 0),
        lambda r, place: (jnp.minimum(r, 1), 0, 0, 0),
        lambda r, place: (r // 3, 0, 0, 0),
        lambda r, place: (r // 3, 0, 0, 0),
    ]
    grid_spec = pltpu.PrefetchScalarGridSpec(
        num_scalar_prefetch=1,
        grid=(items,),
        in_specs=[whole((rows, model))] * (2 * len(lefts))
        + [
            pl.BlockSpec((rows, right[0].shape[1] // items), lambda r, place: (0, r ^ place[1]))
            for right in rights
            for _ in range(2)
        ],
        out_specs=[pl.BlockSpec(block, index) for index in maps[: len(shapes)]],
        scratch_shapes=[pltpu.VMEM((model // 2, 2 * rows), BF16)] * len(lefts),
    )
    return pl.pallas_call(
        functools.partial(column_grad_kernel, heads, len(lefts)),
        grid_spec=grid_spec,
        out_shape=shapes,
        compiler_params=compiler_params(),
        cost_estimate=cost(2 * rows * model * columns, 4 * model * columns),
        name="column_grads",
    )(place, *[part for left in lefts for part in left], *[part for right in rights for part in right])


class Scatter:
    def __init__(self, keep_top, keep_low, *sends):
        self.keep = [keep_top, keep_low]
        self.got, self.early = [], []
        self.route(list(sends), FIRST[: len(sends)])

    def route(self, sends, routes):
        self.sends, self.routes = sends, routes

    def move(self):
        return [swap(send, route) for send, route in zip(self.sends, self.routes)]

    def take(self, moved):
        self.early, self.got = self.got, moved
        self.route([], [])

    def second(self, sends):
        self.route(sends, FIRST[::-1][: len(sends)])


def second_kernel(*refs):
    count = len(refs) // 3
    for number in range(count):
        keep, got, out = refs[2 * number], refs[2 * number + 1], refs[2 * count + number]
        out[...] = (keep[0].astype(F32) + got[0].astype(F32)).astype(BF16)


def second_sums(*scatters):
    terms = [
        part
        for scatter in scatters
        if scatter.got
        for keep, got in zip(scatter.keep, scatter.got)
        for part in (keep, got)
    ]
    if not terms:
        return [[] for _ in scatters]
    shape = terms[0].shape
    outs = []
    in_specs, out_specs = [], []
    for term in terms:
        in_specs.append(
            pl.BlockSpec((1, 2) + term.shape[2:], lambda g: (1, g, 0, 0))
        )
    for term in terms[::2]:
        out_specs.append(pl.BlockSpec((2,) + term.shape[2:], lambda g: (g, 0, 0)))
        outs.append(jax.ShapeDtypeStruct(term.shape[1:], BF16))
    made = pl.pallas_call(
        second_kernel,
        grid=(shape[1] // 2,),
        in_specs=in_specs,
        out_specs=out_specs,
        out_shape=outs,
        compiler_params=compiler_params(),
        cost_estimate=cost(0, 6 * sum(out.size for out in outs)),
        name="second_sums",
    )(*terms)
    return [list(made[2 * i : 2 * i + 2]) for i in range(len(scatters))]


def last_kernel(*refs):
    out = refs[-1]
    for number in range(out.shape[1]):
        for half in range(2):
            terms = refs[6 * number + 3 * half : 6 * number + 3 * half + 3]
            out[:, number, half] = (
                terms[0][0].astype(F32) + terms[1][0].astype(F32) + terms[2][...].astype(F32)
            ).astype(BF16)


def last_sum(*scatters, columns=None):
    if not scatters[0].got:
        items = lax.axis_size("items")
        values = []
        for scatter in scatters:
            value = jnp.stack([keep[0] for keep in scatter.keep], 1)
            if columns is not None:
                starts = [sum(columns[:i]) for i in range(len(columns))]
                parts = [
                    value[..., start : start + size].reshape(value.shape[:3] + (items, -1))
                    for start, size in zip(starts, columns)
                ]
                value = jnp.concatenate(parts, 4).reshape(value.shape)
            values.append(lax.psum_scatter(value, "items", scatter_dimension=3, tiled=True))
        return jnp.stack(values, 1)
    terms = [
        part
        for scatter in scatters
        for parts in zip(scatter.keep, scatter.early, scatter.got)
        for part in parts
    ]
    _, places, rows, wide = terms[0].shape
    held = pl.BlockSpec((1, 2, rows, wide), lambda g: (0, g, 0, 0))
    late = pl.BlockSpec((2, rows, wide), lambda g: (g, 0, 0))
    shape = (places, len(scatters), 2, rows, wide)
    return pl.pallas_call(
        last_kernel,
        grid=(places // 2,),
        in_specs=[held, held, late] * (2 * len(scatters)),
        out_specs=pl.BlockSpec((2,) + shape[1:], lambda g: (g, 0, 0, 0, 0)),
        out_shape=jax.ShapeDtypeStruct(shape, BF16),
        compiler_params=compiler_params(),
        cost_estimate=cost(0, 8 * places * len(scatters) * 2 * rows * wide),
        name="last_sum",
    )(*terms)


def along_z(value):
    heads = lax.axis_size("heads")
    groups = [[core + 2 * z for z in range(heads // 2)] for core in range(2)]
    made = lax.psum_scatter(
        value, "heads", scatter_dimension=0, tiled=False, axis_index_groups=groups
    )
    return [made[i].reshape(-1, made.shape[-1]) for i in range(made.shape[0])]


def sum_everywhere(value):
    for axis in EVERY:
        bit = 1
        while bit < lax.axis_size(axis):
            value = value + swap(value, (axis, bit))
            bit *= 2
    return value


def edges(block, width):
    ways = lax.axis_size("heads")
    half = ways // 2
    place = lax.axis_index("heads") % half
    ring = [(side * half + i, side * half + (i + 1) % half) for side in range(2) for i in range(half)]
    low = lax.ppermute(block[:, block.shape[1] - width :], "heads", ring)
    high = lax.ppermute(block[:, :width], "heads", [(to, at) for at, to in ring])
    low = jnp.where(place == 0, jnp.roll(low, 1, 0), low)
    high = jnp.where(place == half - 1, jnp.roll(high, -1, 0), high)
    return jnp.concatenate([low, block, high], axis=1)


def body(
    frames, cotangent, bucket_counts, gains, w_ffn1_in, w_ffn1_out, w_qkv, w_out,
    w_point_in, w_depth, w_point_out, w_ffn2_in, w_ffn2_out,
):
    chunks, here, model = frames.shape
    ways = lax.axis_size("heads")
    half = ways // 2
    items = 4 if lax.axis_size("items") == 4 else 1
    span = here * half
    group_len = here * ways
    size = model // HEADS
    reach = (KERNEL - 1) // 2
    rows = chunks * here
    pieces = model // (half * LANES)
    place = lax.axis_index("heads")
    side = place // half
    where = jnp.stack(
        [place % 2, lax.axis_index("items") if items > 1 else 0 * place]
    ).astype(jnp.int32)
    always = jnp.min(bucket_counts) >= 0
    first = jnp.arange(chunks, dtype=jnp.int32)[:, None] * span + place % half * here
    position = first + jnp.arange(here, dtype=jnp.int32)[None]
    cosines, sines = rope_tables(position.reshape(-1), size, 2 * LANES)
    depth_rows = w_depth.astype(F32)
    gain = [gains[i : i + 1] for i in range(6)]
    counts = lax.dynamic_index_in_dim(bucket_counts[:, 0], side, 0, keepdims=False)
    wide_position = first - reach + jnp.arange(here + 2 * reach, dtype=jnp.int32)[None]
    seg_wide = segment_ids(wide_position, counts[0], counts[1], group_len)
    seg_own = seg_wide[:, reach : reach + here]

    def mine(value):
        return lax.dynamic_index_in_dim(value, side, 0, keepdims=False)

    def theirs(value):
        return lax.dynamic_index_in_dim(value, 1 - side, 0, keepdims=False)

    def begin(chunk, row, before=()):
        return front(
            chunk, row.reshape(1).astype(jnp.int32), gain[0], w_ffn1_in, w_ffn1_out, gain[1],
            w_qkv, cosines, sines, half, chunks, size, before,
        )

    own_frames = mine(frames)
    before, other_frames = fenced(
        always, (), lambda: (begin(own_frames, side), across(theirs(frames)))
    )
    stream = gathered(own_frames, other_frames, side)
    stream_one, slope_one, hid_one, ent_one, ent_att, *sent = begin(
        other_frames, 1 - side, before
    )
    qkv = [exchange(sent[0])]
    kept, contexts = [], []
    for number in range(pieces):

        def attend_now():
            return attend_forward(qkv[number], counts, size)

        def beside():
            extra = []
            if number + 1 < pieces:
                extra.append(exchange(sent[number + 1]))
            if number > 0:
                extra.append(exchange(kept[number - 1][0]))
            return extra

        def early():
            if number == 0:
                return [other_core(part) for part in (hid_one, ent_one, ent_att)]
            return [across(theirs(cotangent))] if number == 1 else []

        made, extra, others = fenced(always, (), lambda: (attend_now(), beside(), early()))
        kept.append(made)
        if number == 0:
            hid_one, ent_one, ent_att = zip((hid_one, ent_one, ent_att), others)
        elif number == 1:
            cot_other = others[0]
        if number + 1 < pieces:
            qkv.append(extra.pop(0))
        if number > 0:
            contexts.append(extra.pop(0))
    contexts.append(exchange(kept[-1][0]))
    if pieces == 1:
        cot_other = across(theirs(cotangent))
    fulls = [made[1] for made in kept]
    lses = [made[2] for made in kept]
    context = jnp.concatenate(
        [part.transpose(1, 2, 0, 3).reshape(rows, -1) for part in contexts], 1
    )
    stream_two = stream_one + dot(context, w_out)
    shaped, conv_normed, conv_inverse = layer_norm(stream_two, gain[2])
    conv_entered = shaped.astype(BF16)
    pointwise = dot(conv_entered, w_point_in)
    linear = pointwise[:, :model]
    sigmoid_gate = jax.nn.sigmoid(pointwise[:, model:])
    gated_low = (linear * sigmoid_gate).astype(BF16).reshape(chunks, here, model)
    widened = edges(gated_low, reach)
    depth_out = jnp.zeros((chunks, here, model), F32)
    for offset in range(KERNEL):
        same = (seg_wide[:, offset : offset + here] == seg_own)[:, :, None]
        depth_out = depth_out + depth_rows[offset] * jnp.where(
            same, widened[:, offset : offset + here], 0.0
        )
    depth_out = depth_out.reshape(rows, model)
    depth_shaped, depth_normed, depth_inverse = layer_norm(depth_out, gain[3])
    mixed_low = (depth_shaped * jax.nn.sigmoid(depth_shaped)).astype(BF16)
    stream_three = stream_two + dot(mixed_low, w_point_out)
    layer_out, grad_four, gain_five, slope_two, hid_two, ent_two = ffn_forward(
        stream_three, gain[4], w_ffn2_in, w_ffn2_out, gain[5],
        gathered(mine(cotangent), cot_other, side),
    )
    (grad_three, gain_four, half_two, grad_pre_two), hid_other, ent_other = fenced(
        always,
        (),
        lambda: (
            ffn_backward(grad_four, stream_three, slope_two, gain[4], w_ffn2_in, w_ffn2_out),
            other_core(hid_two),
            other_core(ent_two),
        ),
    )
    half_other, grad_pre_other = other_core(half_two), other_core(grad_pre_two)
    grad_mix = grad_three.astype(BF16)
    grad_norm_in = dot(grad_mix, w_point_out, NT) * silu_slope(depth_shaped)
    grad_depth, gain_three = norm_back(grad_norm_in, depth_normed, depth_inverse, gain[3])
    grad_depth_low = grad_depth.astype(BF16).reshape(chunks, here, model)
    grad_widened = edges(grad_depth_low, reach)
    grad_depth_full = grad_depth_low.astype(F32)
    taps = []
    grad_gated = jnp.zeros((chunks, here, model), F32)
    for offset in range(KERNEL):
        same = (seg_wide[:, offset : offset + here] == seg_own)[:, :, None]
        taps.append(
            jnp.sum(
                jnp.where(same, grad_depth_full * widened[:, offset : offset + here], 0.0), (0, 1)
            )
        )
        mirror = 2 * reach - offset
        same_back = (seg_wide[:, mirror : mirror + here] == seg_own)[:, :, None]
        grad_gated = grad_gated + depth_rows[offset] * jnp.where(
            same_back, grad_widened[:, mirror : mirror + here], 0.0
        )
    grad_gated = grad_gated.reshape(rows, model)
    grad_point = jnp.concatenate(
        [grad_gated * sigmoid_gate, grad_gated * linear * sigmoid_gate * (1.0 - sigmoid_gate)], 1
    ).astype(BF16)
    through, gain_two = norm_back(
        dot(grad_point, w_point_in, NT), conv_normed, conv_inverse, gain[2]
    )
    grad_two = grad_three + through
    grad_attn_out = grad_two.astype(BF16)
    grad_context = dot(grad_attn_out, w_out, NT).astype(BF16)
    grad_heads = []
    for number in range(pieces):
        columns = half * LANES
        part = grad_context[:, number * columns : (number + 1) * columns]
        grad_heads.append(part.reshape(chunks, here, half, LANES).transpose(2, 0, 1, 3))

    lefts = (mixed_low, conv_entered, context)
    rights = (grad_mix, grad_point, grad_attn_out)

    def ffn_grads():
        return (
            [other_core(part) for part in lefts + rights[:2]],
            exchange(grad_heads[0]),
            out_grad((half_two, half_other), (hid_two, hid_other), ways, where, items),
            column_grads(
                [(ent_two, ent_other)], [(grad_pre_two, grad_pre_other)], ways, where, items
            ),
        )

    others, grad_heads[0], shares_out, shares_in = fenced(always, (), ffn_grads)
    two_out, two_in = Scatter(*shares_out), Scatter(*shares_in)
    out_own, out_theirs = parted(layer_out, side)
    grads, backs = [], []
    for number in range(pieces):
        last = number == pieces - 1

        def beside():
            extra = []
            if not last:
                extra.append(exchange(grad_heads[number + 1]))
            if number > 0:
                extra.append(exchange(grads[number - 1]))
            if number == 0:
                extra.append(across(out_theirs))
                extra.append(other_core(rights[2]))
            return extra

        def attend_now():
            return attend_backward(
                qkv[number], counts, size, fulls[number], lses[number], grad_heads[number]
            )

        moving = (two_out,) if number == 0 else (two_out, two_in) if number == 1 else ()
        made, extra = fenced(always, moving, lambda: (attend_now(), beside()))
        grads.append(made)
        if not last:
            grad_heads[number + 1] = extra.pop(0)
        if number > 0:
            backs.append(extra.pop(0))
        if number == 0:
            out_other = extra.pop(0)
            others.append(extra.pop(0))
            two_out.second(second_sums(two_out)[0])
    two_in.second(second_sums(two_in)[0])

    def middle_part():
        back = exchange(grads[-1])
        scatter = copy.copy(two_in)
        moved(scatter)
        shares = column_grads(
            list(zip(lefts, others[:3])), list(zip(rights, others[3:])), ways, where, items
        )
        return (back, shares, last_sum(two_out, scatter))

    back, shares, two_sum = fenced(always, (), middle_part)
    backs.append(back)
    middle = Scatter(*shares)

    def attention_part():
        two_grads = along_z(two_sum)
        scatter = copy.copy(middle)

        def qkv_part():
            grad_proj = unturned(backs, cosines, sines, size)
            proj_other = other_core(grad_proj)
            down = stream_gradient(grad_two, stream_one, grad_proj, gain[1], w_qkv, F32)
            shares = column_grads(
                [ent_att], [(grad_proj, proj_other)], ways, where, items
            )
            return (down, shares)

        (grad_one, half_one, gain_one), shares = fenced(always, (scatter,), qkv_part)
        first = scatter.got
        scatter.second(second_sums(scatter)[0])
        attn = Scatter(*shares)
        (half_own, grad_pre), half_other = fenced(
            always,
            (attn,),
            lambda: (hidden_gradient(grad_one, slope_one, w_ffn1_out), other_core(half_one)),
        )
        pre_other, shares_out = fenced(
            always,
            (scatter,),
            lambda: (
                other_core(grad_pre),
                out_grad((half_own, half_other), hid_one, ways, where, items),
            ),
        )
        return (
            two_grads, first, scatter.got, (grad_one, gain_one), shares[:2], attn.got,
            (grad_pre, pre_other), shares_out,
        )

    two_grads, first, got, (grad_one, gain_one), shares, attn_got, grad_pre, shares_out = fenced(
        always, (), attention_part
    )
    middle.take(first)
    middle.take(got)
    attn = Scatter(*shares)
    attn.take(attn_got)
    attn.second(second_sums(attn)[0])
    one_out = Scatter(*shares_out)
    middle_columns = [w.shape[1] for w in (w_point_out, w_point_in, w_out)]
    middle_sum = last_sum(middle, columns=middle_columns)

    middle_grad, shares, (grad_zero, _, gain_zero) = fenced(
        always,
        (one_out, attn),
        lambda: (
            along_z(middle_sum),
            column_grads([ent_one], [grad_pre], ways, where, items),
            stream_gradient(grad_one, stream, grad_pre[0], gain[0], w_ffn1_in, BF16),
        ),
    )
    one_in = Scatter(*shares)
    one_out.second(second_sums(one_out)[0])
    attn_sum = last_sum(attn)
    grad_own, grad_theirs = parted(grad_zero, side)
    attn_grad, grad_other = fenced(
        always, (one_in, one_out), lambda: (along_z(attn_sum), across(grad_theirs))
    )
    one_in.second(second_sums(one_in)[0])

    def last_part():
        out_grads = along_z(last_sum(one_out))
        scatter = copy.copy(one_in)
        moved(scatter)
        small = sum_everywhere(
            jnp.concatenate(
                [gain_zero, gain_one, gain_two, gain_three, gain_four, gain_five]
                + [tap[None] for tap in taps],
                0,
            )
        )
        return (out_grads, along_z(last_sum(scatter)), small)

    one_out_grad, one_in_grad, small = fenced(always, (), last_part)
    hidden = w_ffn1_in.shape[1]

    def unfolded(share):
        each, wide = share.shape
        span = hidden // ways
        halves = share.reshape(2, each // 2, wide)
        parts = [
            halves[half, :, i * span : (i + 1) * span]
            for i in range(wide // span)
            for half in range(2)
        ]
        return jnp.concatenate(parts, 0).T.astype(F32)

    middle_parts = []
    start = 0
    for weight in (w_point_out, w_point_in, w_out):
        each = weight.shape[1] // lax.axis_size("items")
        middle_parts.append(middle_grad[0][:, start : start + each].astype(F32))
        start += each
    return (
        gathered(out_own[None], out_other[None], side),
        gathered(grad_own[None], grad_other[None], side),
        small[:6],
        one_in_grad[0].astype(F32),
        unfolded(one_out_grad[0]),
        attn_grad[0].astype(F32),
        middle_parts[2],
        middle_parts[1],
        small[6:],
        middle_parts[0],
        two_grads[1].astype(F32),
        unfolded(two_grads[0]),
    )


def solution(mesh):
    split = P(None, EVERY, None)
    shares = P("heads", "items")
    in_specs = (split, split, P(None, "items", None)) + (P(),) * 10
    out_specs = (split, split, P(), shares, shares, shares, shares, shares, P()) + (shares,) * 3
    return jax.shard_map(body, mesh=mesh, in_specs=in_specs, out_specs=out_specs, check_vma=False)
```

```python
import copy
import functools

import jax
import jax.numpy as jnp
from jax import lax
from jax.experimental import pallas as pl
from jax.experimental.pallas import tpu as pltpu
from jax.sharding import PartitionSpec as P

HEADS = 16
KERNEL = 5
LONG = 1500
SHORT = 500
EPS = 1e-05
ROPE_BASE = 10000.0
BLOCK = 512
INNER_FWD = 1024
INNER_BWD = 512
TURNED = 512
LANES = 128
BIG = 1e30
VMEM_LIMIT = 56 << 20
F32 = jnp.float32
BF16 = jnp.bfloat16
NN = (((1,), (0,)), ((), ()))
NT = (((1,), (1,)), ((), ()))
EVERY = ("items", "heads")
FIRST = [("items", 1), ("items", 2)]


def dot(left, right, dims=NN):
    return lax.dot_general(left, right, dims, preferred_element_type=F32)


def silu_slope(field):
    gate_sig = jax.nn.sigmoid(field)
    return gate_sig * (1.0 + field * (1.0 - gate_sig))


def layer_norm(field, gain_row):
    centred = field - jnp.mean(field, -1, keepdims=True)
    inverse = lax.rsqrt(jnp.mean(centred * centred, -1, keepdims=True) + EPS)
    normed = centred * inverse
    return (normed * gain_row, normed, inverse)


def norm_back(upstream, normed, inverse, gain_row):
    scaled = upstream * gain_row
    through = inverse * (
        scaled
        - jnp.mean(scaled, -1, keepdims=True)
        - normed * jnp.mean(scaled * normed, -1, keepdims=True)
    )
    return (through, jnp.sum(upstream * normed, 0, keepdims=True))


def segment_ids(position, long_count, short_count, group_len):
    long_end = long_count * LONG
    short_end = long_end + short_count * SHORT
    segments = jnp.where(
        position < long_end, position // LONG, long_count + (position - long_end) // SHORT
    )
    segments = jnp.where(position < short_end, segments, long_count + short_count)
    return jnp.where((position < 0) | (position >= group_len), -1, segments)


def compiler_params():
    return pltpu.CompilerParams(vmem_limit_bytes=VMEM_LIMIT)


def whole(shape):
    return pl.BlockSpec(shape, lambda *_: (0,) * len(shape))


def cost(flops, bytes_accessed, transcendentals=0):
    return pl.CostEstimate(
        flops=flops, bytes_accessed=bytes_accessed, transcendentals=transcendentals
    )


def segment_bounds(counts, place, group):
    longs, shorts = counts
    long_end = longs * LONG
    short_end = long_end + shorts * SHORT
    start = jnp.where(place < longs, place * LONG, long_end + (place - longs) * SHORT)
    size = jnp.where(place < longs, LONG, SHORT)
    last = place == longs + shorts
    return (jnp.where(last, short_end, start), jnp.where(last, group, start + size), place <= longs + shorts)


def member_lanes(counts, first, rows, group, shift=0):
    shape = (rows, LANES)
    place = lax.broadcasted_iota(jnp.int32, (8, LANES), 1) - shift
    start, end, there = segment_bounds(counts, place, group)
    start = jnp.where(there & (place >= 0), start, group)
    start, end = start[:1], end[:1]
    frame = first + lax.broadcasted_iota(jnp.int32, shape, 0)
    return (frame >= start) & (frame < end)


def block_range(counts, step, group, inner):
    longs, shorts = counts
    long_end = longs * LONG
    short_end = long_end + shorts * SHORT

    def number(frame):
        place = jnp.where(frame < long_end, frame // LONG, longs + (frame - long_end) // SHORT)
        return jnp.where(frame < short_end, place, longs + shorts)

    first = segment_bounds(counts, number(step * BLOCK), group)[0]
    last = segment_bounds(counts, number(step * BLOCK + BLOCK - 1), group)[1]
    return (first // inner, (last + inner - 1) // inner)


def head_lanes(shape, head, size):
    lane = lax.broadcasted_iota(jnp.int32, shape, 1)
    return (lane >= head * size) & (lane < (head + 1) * size)


def split_three(v):
    hi = v.astype(BF16).astype(F32)
    rest = v - hi
    mid = rest.astype(BF16).astype(F32)
    return (hi, mid, rest - mid)


def spread_columns(columns, shape):
    lane = lax.broadcasted_iota(jnp.int32, shape, 1)
    out = jnp.zeros(shape, F32)
    for place, column in enumerate(columns):
        out = jnp.where(lane == place, column, out)
    return out


def chunk_rows(ref, lead, step):
    places, chunks, frames = ref.shape[0], ref.shape[-3], ref.shape[-2]
    per = BLOCK // frames
    steps = places // per
    at = (pl.ds(step % steps * per, per),) + lead + (step // steps,)
    return ref[at].reshape(BLOCK, LANES)


def attn_fwd_kernel(
    heads, size, group, counts_ref, qkv_ref, out_ref, full_ref, lse_ref, kcat, v_all, s_scr
):
    step = pl.program_id(0)
    counts = (counts_ref[0], counts_ref[1])

    @pl.when(step == 0)
    def _():
        chunks = qkv_ref.shape[2]
        span = group // chunks
        for chunk in range(chunks):
            rows = slice(chunk * span, (chunk + 1) * span)
            kcat[rows, :LANES] = qkv_ref[:, 1, chunk].reshape(span, LANES)
            v_all[rows, :] = qkv_ref[:, 2, chunk].reshape(span, LANES)
        kcat[:, LANES:] = jnp.where(member_lanes(counts, 0, group, group), 0.0, -BIG).astype(BF16)

    q = chunk_rows(qkv_ref, (0,), step).astype(F32) * (size ** -0.5)
    member = jnp.where(member_lanes(counts, step * BLOCK, BLOCK, group), 1.0, 0.0).astype(BF16)
    queries = []
    for head in range(heads):
        mine = jnp.where(head_lanes(q.shape, head, size), q, 0.0).astype(BF16)
        queries.append(jnp.concatenate([mine, member], 1))
    low, high = block_range(counts, step, group, INNER_FWD)

    def scores(j, tops):
        keys = kcat[pl.ds(pl.multiple_of(j * INNER_FWD, INNER_FWD), INNER_FWD), :]
        new = []
        for head in range(heads):
            s = dot(queries[head], keys, NT)
            s_scr[head, j] = s
            top = tops[head]
            for part in range(INNER_FWD // LANES):
                top = jnp.maximum(top, s[:, part * LANES : (part + 1) * LANES])
            new.append(top)
        return tuple(new)

    start = tuple(jnp.full((BLOCK, LANES), -BIG, F32) for _ in range(heads))
    tops = lax.fori_loop(low, high, scores, start)
    tops = [jnp.max(t, 1, keepdims=True) for t in tops]
    tops = [jnp.broadcast_to(t, (BLOCK, LANES)) for t in tops]

    def weigh(j, carried):
        sums, accs = carried
        values = v_all[pl.ds(pl.multiple_of(j * INNER_FWD, INNER_FWD), INNER_FWD), :]
        new_sums, new_accs = [], []
        for head in range(heads):
            total = sums[head]
            parts = []
            for part in range(INNER_FWD // LANES):
                p = jnp.exp(s_scr[head, j, :, part * LANES : (part + 1) * LANES] - tops[head])
                total = total + p
                parts.append(p.astype(BF16))
            new_sums.append(total)
            new_accs.append(accs[head] + dot(jnp.concatenate(parts, 1), values))
        return (tuple(new_sums), tuple(new_accs))

    zeros = tuple(jnp.zeros((BLOCK, LANES), F32) for _ in range(heads))
    sums, accs = lax.fori_loop(low, high, weigh, (zeros, zeros))
    result = None
    for head in range(heads):
        total = jnp.sum(sums[head], 1, keepdims=True)
        mine = accs[head] / total
        if result is None:
            result = mine
        else:
            result = jnp.where(head_lanes(mine.shape, head, size), mine, result)
        lse_ref[head] = tops[head] + jnp.log(jnp.broadcast_to(total, (BLOCK, LANES)))
    full_ref[...] = result
    out_ref[...] = result.astype(BF16).reshape(out_ref.shape)


def attend_forward(qkv, counts, size):
    places, _, chunks, frames, _ = qkv.shape
    group = places * chunks * frames
    heads = LANES // size
    per = BLOCK // frames
    each = places // per
    return pl.pallas_call(
        functools.partial(attn_fwd_kernel, heads, size, group),
        grid=(group // BLOCK,),
        in_specs=[pl.BlockSpec(memory_space=pltpu.SMEM), whole(qkv.shape)],
        out_specs=[
            pl.BlockSpec((per, 1, frames, LANES), lambda i: (i % each, i // each, 0, 0)),
            pl.BlockSpec((BLOCK, LANES), lambda i: (i, 0)),
            pl.BlockSpec((heads, BLOCK, LANES), lambda i: (0, i, 0)),
        ],
        out_shape=[
            jax.ShapeDtypeStruct((places, chunks, frames, LANES), BF16),
            jax.ShapeDtypeStruct((group, LANES), F32),
            jax.ShapeDtypeStruct((heads, group, LANES), F32),
        ],
        scratch_shapes=[
            pltpu.VMEM((group, 2 * LANES), BF16),
            pltpu.VMEM((group, LANES), BF16),
            pltpu.VMEM((heads, group // INNER_FWD, BLOCK, INNER_FWD), F32),
        ],
        compiler_params=compiler_params(),
        cost_estimate=cost(16 * group * group * LANES, 6 << 20, heads * group * group),
        name="attend_forward",
    )(counts, qkv)


def attn_bwd_kernel(
    heads, size, group, counts_ref, qkv_ref, full_ref, lse_ref, grad_ref, out_ref,
    qcat, gcat, k_turned, dq_turned,
):
    step = pl.program_id(0)
    counts = (counts_ref[0], counts_ref[1])
    blocks = group // BLOCK
    places, _, _, frames, _ = qkv_ref.shape
    per = BLOCK // frames
    each = places // per

    def put(part, j, value):
        out_ref[pl.ds(j % each * per, per), part, j // each] = value.astype(BF16).reshape(
            per, frames, LANES
        )

    @pl.when(step == 0)
    def _():
        dq_turned[...] = jnp.zeros_like(dq_turned)

        def prepare(j, _):
            rows = pl.ds(pl.multiple_of(j * BLOCK, BLOCK), BLOCK)
            lane = lax.broadcasted_iota(jnp.int32, (BLOCK, LANES), 1)
            q = chunk_rows(qkv_ref, (0,), j).astype(F32) * (size ** -0.5)
            g = chunk_rows(grad_ref, (), j).astype(F32)
            product = g * full_ref[rows, :]
            member = jnp.where(member_lanes(counts, j * BLOCK, BLOCK, group, 3), 1.0, 0.0)
            for head in range(heads):
                own = head_lanes((BLOCK, LANES), head, size)
                lse = lse_ref[head, rows, :]
                spread = spread_columns(split_three(lse), (BLOCK, LANES))
                delta = jnp.sum(jnp.where(own, product, 0.0), 1, keepdims=True)
                delta = jnp.broadcast_to(delta, (BLOCK, LANES))
                qcat[head, rows, :LANES] = jnp.where(own, q, 0.0).astype(BF16)
                qcat[head, rows, LANES:] = jnp.where(lane < 3, -spread, member).astype(BF16)
                gcat[head, rows, :LANES] = jnp.where(own, g, 0.0).astype(BF16)
                spread = spread_columns(split_three(delta), (BLOCK, LANES))
                gcat[head, rows, LANES:] = (-spread).astype(BF16)
            k = chunk_rows(qkv_ref, (1,), j).astype(F32)
            k_turned[j] = jnp.transpose(k).astype(BF16)
            return 0

        lax.fori_loop(0, blocks, prepare, 0)

    lane = lax.broadcasted_iota(jnp.int32, (BLOCK, LANES), 1)
    member = member_lanes(counts, step * BLOCK, BLOCK, group, 3)
    tail = jnp.where(lane < 3, 1.0, jnp.where(member, 0.0, -BIG)).astype(BF16)
    keys = jnp.concatenate([chunk_rows(qkv_ref, (1,), step), tail], 1)
    ones = jnp.where(lane < 3, 1.0, 0.0).astype(BF16)
    values = jnp.concatenate([chunk_rows(qkv_ref, (2,), step), ones], 1)

    def one(j, carried):
        dk, dv = carried
        cols = pl.ds(pl.multiple_of(j * INNER_BWD, INNER_BWD), INNER_BWD)
        for head in range(heads):
            qc = qcat[head, cols, :]
            gc = gcat[head, cols, :]
            p = jnp.exp(dot(keys, qc, NT))
            ds = (p * dot(values, gc, NT)).astype(BF16)
            dv = dv + dot(p.astype(BF16), gc[:, :LANES])
            dk = dk + dot(ds, qc[:, :LANES])
            mine = slice(head * size, (head + 1) * size)
            dq_turned[j, mine, :] += dot(k_turned[step, mine, :], ds)
        return (dk, dv)

    zero = jnp.zeros((BLOCK, LANES), F32)
    low, high = block_range(counts, step, group, INNER_BWD)
    dk, dv = lax.fori_loop(low, high, one, (zero, zero))
    put(1, step, dk)
    put(2, step, dv)

    @pl.when(step == blocks - 1)
    def _():
        def finish(j, _):
            put(0, j, jnp.transpose(dq_turned[j]) * (size ** -0.5))
            return 0

        lax.fori_loop(0, blocks, finish, 0)


def attend_backward(qkv, counts, size, full, lse, grad):
    places, _, chunks, frames, _ = qkv.shape
    group = places * chunks * frames
    heads = LANES // size
    steps = group // BLOCK
    return pl.pallas_call(
        functools.partial(attn_bwd_kernel, heads, size, group),
        grid=(steps,),
        in_specs=[
            pl.BlockSpec(memory_space=pltpu.SMEM),
            whole(qkv.shape),
            whole(full.shape),
            whole(lse.shape),
            whole(grad.shape),
        ],
        out_specs=whole(qkv.shape),
        out_shape=jax.ShapeDtypeStruct(qkv.shape, BF16),
        scratch_shapes=[
            pltpu.VMEM((heads, group, 2 * LANES), BF16),
            pltpu.VMEM((heads, group, 2 * LANES), BF16),
            pltpu.VMEM((steps, LANES, BLOCK), BF16),
            pltpu.VMEM((group // INNER_BWD, LANES, INNER_BWD), F32),
        ],
        compiler_params=compiler_params(),
        cost_estimate=cost(32 * group * group * LANES, 9 << 20, heads * group * group),
        name="attend_backward",
    )(counts, qkv, full, lse, grad)


def half_gate(field):
    return 0.5 * jnp.tanh(0.5 * field) + 0.5


def hidden_units(pre):
    gate = half_gate(pre)
    hidden = pre * gate
    return (hidden.astype(BF16), (gate + hidden * (1.0 - gate)).astype(BF16))


def ffn_fwd_kernel(
    x_ref, gain_ref, last_gain_ref, up_ref, win_ref, wout_ref,
    out_ref, down_ref, gain_grad_ref, slope_ref, hid_ref, entered_ref, total,
):
    step = pl.program_id(0)

    @pl.when(step == 0)
    def _():
        entered_ref[...] = layer_norm(x_ref[...], gain_ref[...])[0].astype(BF16)
        total[...] = jnp.zeros_like(total)

    hidden, slope = hidden_units(dot(entered_ref[...], win_ref[...]))
    slope_ref[...] = slope
    hid_ref[...] = hidden
    total[...] += dot(hidden, wout_ref[...])

    @pl.when(step == pl.num_programs(0) - 1)
    def _():
        gain = last_gain_ref[...]
        shaped, normed, inverse = layer_norm(x_ref[...] + 0.5 * total[...], gain)
        out_ref[...] = shaped.astype(BF16)
        through, grad_gain = norm_back(up_ref[...].astype(F32), normed, inverse, gain)
        down_ref[...] = through
        gain_grad_ref[...] = grad_gain


def ffn_forward(stream, gain_row, weight_in, weight_out, last_gain, upstream):
    rows, model = stream.shape
    units = weight_in.shape[1]
    wide = min(units, 1024)
    return pl.pallas_call(
        ffn_fwd_kernel,
        grid=(units // wide,),
        in_specs=[
            whole((rows, model)),
            whole((1, model)),
            whole((1, model)),
            whole((rows, model)),
            pl.BlockSpec((model, wide), lambda s: (0, s)),
            pl.BlockSpec((wide, model), lambda s: (s, 0)),
        ],
        out_specs=[whole((rows, model)), whole((rows, model)), whole((1, model))]
        + [pl.BlockSpec((rows, wide), lambda s: (0, s))] * 2
        + [whole((rows, model))],
        out_shape=[
            jax.ShapeDtypeStruct((rows, model), BF16),
            jax.ShapeDtypeStruct((rows, model), F32),
            jax.ShapeDtypeStruct((1, model), F32),
            jax.ShapeDtypeStruct((rows, units), BF16),
            jax.ShapeDtypeStruct((rows, units), BF16),
            jax.ShapeDtypeStruct((rows, model), BF16),
        ],
        scratch_shapes=[pltpu.VMEM((rows, model), F32)],
        compiler_params=compiler_params(),
        cost_estimate=cost(4 * rows * model * units, 4 * model * units + 4 * rows * units),
        name="ffn_forward",
    )(stream, gain_row, last_gain, upstream, weight_in, weight_out)


def ffn_bwd_kernel(
    x_ref, gain_ref, up_ref, slope_ref, win_ref, wout_ref,
    down_ref, gain_grad_ref, half_ref, grad_ref, total,
):
    step = pl.program_id(0)

    @pl.when(step == 0)
    def _():
        half_ref[...] = (0.5 * up_ref[...]).astype(BF16)
        total[...] = jnp.zeros_like(total)

    grad = (dot(half_ref[...], wout_ref[...], NT) * slope_ref[...].astype(F32)).astype(BF16)
    grad_ref[...] = grad
    total[...] += dot(grad, win_ref[...], NT)

    @pl.when(step == pl.num_programs(0) - 1)
    def _():
        gain = gain_ref[...]
        normed, inverse = layer_norm(x_ref[...].astype(F32), gain)[1:]
        through, grad_gain = norm_back(total[...], normed, inverse, gain)
        down_ref[...] = up_ref[...] + through
        gain_grad_ref[...] = grad_gain


def ffn_backward(upstream, stream, slope, gain_row, weight_in, weight_out):
    rows, model = stream.shape
    units = weight_in.shape[1]
    wide = min(units, 1024)
    return pl.pallas_call(
        ffn_bwd_kernel,
        grid=(units // wide,),
        in_specs=[
            whole((rows, model)),
            whole((1, model)),
            whole((rows, model)),
            pl.BlockSpec((rows, wide), lambda s: (0, s)),
            pl.BlockSpec((model, wide), lambda s: (0, s)),
            pl.BlockSpec((wide, model), lambda s: (s, 0)),
        ],
        out_specs=[
            whole((rows, model)),
            whole((1, model)),
            whole((rows, model)),
            pl.BlockSpec((rows, wide), lambda s: (0, s)),
        ],
        out_shape=[
            jax.ShapeDtypeStruct((rows, model), F32),
            jax.ShapeDtypeStruct((1, model), F32),
            jax.ShapeDtypeStruct((rows, model), BF16),
            jax.ShapeDtypeStruct((rows, units), BF16),
        ],
        scratch_shapes=[pltpu.VMEM((rows, model), F32)],
        compiler_params=compiler_params(),
        cost_estimate=cost(4 * rows * model * units, 4 * model * units + 6 * rows * units),
        name="ffn_backward",
    )(stream, gain_row, upstream, slope, weight_in, weight_out)


def hidden_kernel(up_ref, slope_ref, wout_ref, half_ref, grad_ref):
    @pl.when(pl.program_id(0) == 0)
    def _():
        half_ref[...] = (0.5 * up_ref[...]).astype(BF16)

    grad = dot(half_ref[...], wout_ref[...], NT) * slope_ref[...].astype(F32)
    grad_ref[...] = grad.astype(BF16)


def hidden_gradient(upstream, slope, weight_out):
    rows, model = upstream.shape
    units = weight_out.shape[0]
    wide = min(units, 1024)
    return pl.pallas_call(
        hidden_kernel,
        grid=(units // wide,),
        in_specs=[
            whole((rows, model)),
            pl.BlockSpec((rows, wide), lambda s: (0, s)),
            pl.BlockSpec((wide, model), lambda s: (s, 0)),
        ],
        out_specs=[whole((rows, model)), pl.BlockSpec((rows, wide), lambda s: (0, s))],
        out_shape=[
            jax.ShapeDtypeStruct((rows, model), BF16),
            jax.ShapeDtypeStruct((rows, units), BF16),
        ],
        compiler_params=compiler_params(),
        cost_estimate=cost(2 * rows * model * units, 2 * model * units + 6 * rows * units),
        name="hidden_gradient",
    )(upstream, slope, weight_out)


def down_kernel(
    x_ref, gain_ref, up_ref, grad_ref, weight_ref, down_ref, half_ref, gain_grad_ref, total
):
    step = pl.program_id(0)

    @pl.when(step == 0)
    def _():
        total[...] = jnp.zeros_like(total)

    total[...] += dot(grad_ref[...], weight_ref[...], NT)

    @pl.when(step == pl.num_programs(0) - 1)
    def _():
        gain = gain_ref[...]
        normed, inverse = layer_norm(x_ref[...].astype(F32), gain)[1:]
        through, grad_gain = norm_back(total[...], normed, inverse, gain)
        down = up_ref[...] + through
        down_ref[...] = down.astype(down_ref.dtype)
        half_ref[...] = (0.5 * down).astype(BF16)
        gain_grad_ref[...] = grad_gain


def stream_gradient(upstream, stream, grad, gain_row, weight, down_type):
    rows, model = stream.shape
    units = weight.shape[1]
    wide = min(units, 1024)
    return pl.pallas_call(
        down_kernel,
        grid=(units // wide,),
        in_specs=[
            whole((rows, model)),
            whole((1, model)),
            whole((rows, model)),
            pl.BlockSpec((rows, wide), lambda s: (0, s)),
            pl.BlockSpec((model, wide), lambda s: (0, s)),
        ],
        out_specs=[whole((rows, model)), whole((rows, model)), whole((1, model))],
        out_shape=[
            jax.ShapeDtypeStruct((rows, model), down_type),
            jax.ShapeDtypeStruct((rows, model), BF16),
            jax.ShapeDtypeStruct((1, model), F32),
        ],
        scratch_shapes=[pltpu.VMEM((rows, model), F32)],
        compiler_params=compiler_params(),
        cost_estimate=cost(2 * rows * model * units, 2 * model * units + 2 * rows * units),
        name="stream_gradient",
    )(stream, gain_row, upstream, grad, weight)


def turn(field, cosines, sines, size):
    repeats = field.shape[1] // cosines.shape[1]
    cosines = jnp.concatenate([cosines] * repeats, 1)
    sines = jnp.concatenate([sines] * repeats, 1)
    lane = lax.broadcasted_iota(jnp.int32, field.shape, 1)
    half = size // 2
    width = field.shape[1]
    swapped = jnp.where(
        lane % size < half,
        pltpu.roll(field, width - half, 1),
        pltpu.roll(field, half, 1),
    )
    return field * cosines + swapped * sines


def rope_tables(position, size):
    half = size // 2
    lane = jnp.arange(LANES, dtype=jnp.int32)
    freqs = jnp.exp(
        -jnp.log(jnp.float32(ROPE_BASE)) * (lane % half).astype(jnp.float32) / half
    )
    angles = position.astype(jnp.float32)[:, None] * freqs[None, :]
    signs = jnp.where(lane % size < half, -1.0, 1.0)
    return (jnp.cos(angles), jnp.sin(angles) * signs[None, :])


def front_kernel(
    size, ffn_steps, pieces, row_ref, x_ref, gain_ref, next_gain_ref, win_ref, wout_ref,
    wq_ref, wk_ref, wv_ref, cos_ref, sin_ref, *refs,
):
    refs = refs[-(6 + pieces) :]
    out_ref, slope_ref, hid_ref, entered_ref, next_ref = refs[:5]
    outs, total = refs[5:-1], refs[-1]
    step = pl.program_id(0)

    @pl.when(step == 0)
    def _():
        entered_ref[...] = layer_norm(x_ref[...].astype(F32), gain_ref[...])[0].astype(BF16)
        total[...] = jnp.zeros_like(total)

    @pl.when(step < ffn_steps)
    def _():
        hidden, slope = hidden_units(dot(entered_ref[...], win_ref[...]))
        slope_ref[...] = slope
        hid_ref[...] = hidden
        total[...] += dot(hidden, wout_ref[...])

    @pl.when(step == ffn_steps)
    def _():
        out = x_ref[...].astype(F32) + 0.5 * total[...]
        out_ref[...] = out
        next_ref[...] = layer_norm(out, next_gain_ref[...])[0].astype(BF16)

    each = (pl.num_programs(0) - ffn_steps) // pieces
    for piece, out in enumerate(outs):

        @pl.when((step >= ffn_steps) & ((step - ffn_steps) // each == piece))
        def _():
            for place, weight in enumerate((wq_ref, wk_ref, wv_ref)):
                made = dot(next_ref[...], weight[...])
                if place < 2:
                    made = turn(made, cos_ref[...], sin_ref[...], size)
                made = made.astype(BF16)
                for target in range(out.shape[0]):
                    out[target, place, 0] = made[:, target * LANES : (target + 1) * LANES]


def front(
    frames, row, gain_row, weight_in, weight_out, next_gain, weight, cosines, sines,
    places, chunks, size, before=(),
):
    rows, model = frames.shape
    units = weight_in.shape[1]
    wide = min(units, 1024)
    ffn_steps = units // wide
    turned_wide = TURNED
    turns = model // turned_wide
    pieces = model // (places * LANES)
    each = turns // pieces
    piece = jax.ShapeDtypeStruct((places, 3, chunks, rows, LANES), BF16)

    def ffn_at(s, row):
        return jnp.minimum(s, ffn_steps - 1)

    def turn_at(s):
        return jnp.maximum(s - ffn_steps, 0)

    def piece_at(number):
        return lambda s, row: (
            jnp.clip(s - ffn_steps - number * each, 0, each - 1), 0, row[0], 0, 0
        )

    row_block = pl.BlockSpec((rows, model), lambda s, row: (row[0], 0))
    unit_block = pl.BlockSpec((rows, wide), lambda s, row: (row[0], ffn_at(s, row)))
    angle_block = pl.BlockSpec((rows, LANES), lambda s, row: (row[0], 0))
    out_shape = [
        jax.ShapeDtypeStruct((chunks * rows, model), F32),
        jax.ShapeDtypeStruct((chunks * rows, units), BF16),
        jax.ShapeDtypeStruct((chunks * rows, units), BF16),
        jax.ShapeDtypeStruct((chunks * rows, model), BF16),
        jax.ShapeDtypeStruct((chunks * rows, model), BF16),
    ] + [piece] * pieces
    in_specs = [
        whole((rows, model)),
        whole((1, model)),
        whole((1, model)),
        pl.BlockSpec((model, wide), lambda s, row: (0, ffn_at(s, row))),
        pl.BlockSpec((wide, model), lambda s, row: (ffn_at(s, row), 0)),
        pl.BlockSpec((model, turned_wide), lambda s, row: (0, turn_at(s))),
        pl.BlockSpec((model, turned_wide), lambda s, row: (0, turns + turn_at(s))),
        pl.BlockSpec((model, turned_wide), lambda s, row: (0, 2 * turns + turn_at(s))),
        angle_block,
        angle_block,
    ]
    grid_spec = pltpu.PrefetchScalarGridSpec(
        num_scalar_prefetch=1,
        grid=(ffn_steps + turns,),
        in_specs=in_specs + [pl.BlockSpec(memory_space=pl.ANY)] * len(before),
        out_specs=[row_block, unit_block, unit_block, row_block, row_block]
        + [
            pl.BlockSpec((turned_wide // LANES, 3, 1, rows, LANES), piece_at(number))
            for number in range(pieces)
        ],
        scratch_shapes=[pltpu.VMEM((rows, model), F32)],
    )
    return pl.pallas_call(
        functools.partial(front_kernel, size, ffn_steps, pieces),
        grid_spec=grid_spec,
        out_shape=out_shape,
        input_output_aliases={1 + len(in_specs) + i: i for i in range(len(before))},
        compiler_params=compiler_params(),
        cost_estimate=cost(
            4 * rows * model * units + 6 * rows * model * model,
            4 * model * units + 6 * model * model + 4 * rows * units + 16 * rows * model,
        ),
        name="front",
    )(
        row, frames, gain_row, next_gain, weight_in, weight_out, weight, weight, weight,
        cosines, sines, *before,
    )


def unturn_kernel(size, pieces, cos_ref, sin_ref, *refs):
    backs, out = refs[:pieces], refs[pieces]
    rotated = pl.program_id(0) < 2
    cosines = jnp.where(rotated, cos_ref[...], 1.0)
    sines = jnp.where(rotated, -sin_ref[...], 0.0)
    places, _, chunks, frames, _ = backs[0].shape
    wide = TURNED
    per = wide // LANES
    for piece, back in enumerate(backs):
        for first in range(0, places, per):
            for chunk in range(chunks):
                rows = slice(chunk * frames, (chunk + 1) * frames)
                field = jnp.concatenate([back[first + i, 0, chunk] for i in range(per)], 1)
                made = turn(field.astype(F32), cosines[rows], sines[rows], size).astype(BF16)
                start = (piece * places + first) * LANES
                out[rows, start : start + wide] = made


def unturned(backs, cosines, sines, size):
    places, kinds, chunks, frames, _ = backs[0].shape
    pieces = len(backs)
    block = pl.BlockSpec((places, 1, chunks, frames, LANES), lambda s: (0, s, 0, 0, 0))
    model = pieces * places * LANES
    return pl.pallas_call(
        functools.partial(unturn_kernel, size, pieces),
        grid=(kinds,),
        in_specs=[whole(cosines.shape), whole(sines.shape)] + [block] * pieces,
        out_specs=pl.BlockSpec((chunks * frames, model), lambda s: (0, s)),
        out_shape=jax.ShapeDtypeStruct((chunks * frames, kinds * model), BF16),
        compiler_params=compiler_params(),
        cost_estimate=cost(0, 4 * chunks * frames * kinds * model),
        name="unturned",
    )(cosines, sines, *backs)


def flipped(axis_bit, count):
    axis, bit = axis_bit
    items, heads = count
    if axis == "items":
        return [(i * heads + h, (i ^ bit) * heads + h) for i in range(items) for h in range(heads)]
    return [(i * heads + h, i * heads + (h ^ bit)) for i in range(items) for h in range(heads)]


def swap(value, axis_bit):
    count = (lax.axis_size("items"), lax.axis_size("heads"))
    return lax.ppermute(value, EVERY, flipped(axis_bit, count))


def fenced(always, scatters, work):
    def run():
        return (work(), [scatter.move() for scatter in scatters])

    def empty():
        return jax.tree.map(lambda leaf: jnp.zeros(leaf.shape, leaf.dtype), jax.eval_shape(run))

    result, moved = lax.optimization_barrier(lax.cond(always, run, empty))
    for scatter, parts in zip(scatters, moved):
        scatter.take(parts)
    return result


def moved(scatter):
    scatter.take(scatter.move())


def other_core(value):
    return swap(value, ("heads", 1))


def exchange(value):
    half = lax.axis_size("heads") // 2
    groups = [[side * half + i for i in range(half)] for side in range(2)]
    return lax.all_to_all(
        value, "heads", split_axis=0, concat_axis=0, tiled=True, axis_index_groups=groups
    )


def across(value):
    return swap(value, ("heads", lax.axis_size("heads") // 2))


def gathered(own, other, side):
    return jnp.concatenate([jnp.where(side == 0, own, other), jnp.where(side == 0, other, own)], 0)


def parted(value, side):
    low, high = jnp.split(value, 2, 0)
    return (jnp.where(side == 0, low, high), jnp.where(side == 0, high, low))


def own_rows(left_ref, heads, core, target, first):
    rows, model = left_ref.shape
    each = model // heads
    for place in range(heads // 2):
        if each % LANES == 0:
            start = pl.multiple_of((2 * place + core) * each, each)
            mine = jnp.transpose(left_ref[:, pl.ds(start, each)].astype(F32)).astype(BF16)
        else:
            pair = left_ref[:, 2 * place * each : 2 * (place + 1) * each]
            pair = jnp.transpose(pair.astype(F32))
            mine = jnp.where(core == 0, pair[:each], pair[each:]).astype(BF16)
        for half in range(2):
            start = (half * (heads // 2) + place) * (each // 2)
            target[start : start + each // 2, first : first + rows] = mine[
                half * (each // 2) : (half + 1) * (each // 2)
            ]


def turned_items(left, items, own, target, first):
    rows, model = left.shape
    each = model // items
    for item in range(items):
        part = jnp.transpose(left[:, item * each : (item + 1) * each].astype(F32)).astype(BF16)
        place = pl.multiple_of((own ^ item) * each, each)
        target[pl.ds(place, each), first : first + rows] = part


def share_shapes(items, heads, model, columns):
    lead = 2 if items > 1 else 1
    shape = (lead, heads // 2, model // heads // 2, columns // items)
    return [jax.ShapeDtypeStruct(shape, BF16)] * (4 if items > 1 else 2)


def out_grad_kernel(place_ref, up_own, up_other, hid_own, hid_other, *refs):
    targets, turned = refs[:-1], refs[-1]
    rows, model = up_own.shape
    items = 4 if len(targets) == 4 else 1

    @pl.when(pl.program_id(0) == 0)
    def _():
        turned_items(up_own[...], items, place_ref[1], turned, 0)
        turned_items(up_other[...], items, place_ref[1], turned, rows)

    hidden = jnp.concatenate([hid_own[...], hid_other[...]], 0)
    grad = dot(turned[...], hidden).astype(BF16)
    wide = grad.shape[1]
    each = targets[0].shape[2]
    parts = model // items // (2 * each)
    for r in range(items):
        for part in range(parts):
            for half in range(2):
                first = ((r * parts + part) * 2 + half) * each
                piece = grad[first : first + each]
                if half == 0:
                    target, at = targets[2 * (r % 2)], r // 2
                else:
                    target, at = targets[1 + 2 * (r // 2)], r % 2
                target[at, 0, :, part * wide : (part + 1) * wide] = piece


def out_grad(upstream, hidden, heads, place, items):
    rows, model = upstream[0].shape
    units = hidden[0].shape[1]
    wide = units // heads
    shapes = share_shapes(items, heads, model, units)
    block = (shapes[0].shape[0], 1) + shapes[0].shape[2:]
    hid_block = pl.BlockSpec((rows, wide), lambda s, place: (0, 2 * s + place[0]))
    grid_spec = pltpu.PrefetchScalarGridSpec(
        num_scalar_prefetch=1,
        grid=(heads // 2,),
        in_specs=[whole((rows, model))] * 2 + [hid_block] * 2,
        out_specs=[pl.BlockSpec(block, lambda s, place: (0, s, 0, 0))] * len(shapes),
        scratch_shapes=[pltpu.VMEM((model, 2 * rows), BF16)],
    )
    return pl.pallas_call(
        out_grad_kernel,
        grid_spec=grid_spec,
        out_shape=shapes,
        compiler_params=compiler_params(),
        cost_estimate=cost(2 * rows * model * units, 2 * model * units + 4 * rows * units),
        name="out_grad",
    )(place, *upstream, *hidden)


def column_grad_kernel(heads, count, place_ref, *refs):
    lefts, refs = refs[: 2 * count], refs[2 * count :]
    rights, refs = refs[: 2 * count], refs[2 * count :]
    targets, turned = refs[:-count], refs[-count:]
    r = pl.program_id(0)
    rows = lefts[0].shape[0]

    @pl.when(r == 0)
    def _():
        for number in range(count):
            for other in range(2):
                own_rows(
                    lefts[2 * number + other], heads, place_ref[0], turned[number], other * rows
                )

    made = []
    for number in range(count):
        right = jnp.concatenate([rights[2 * number][...], rights[2 * number + 1][...]], 0)
        made.append(dot(turned[number][...], right).astype(BF16))
    made = made[0] if count == 1 else jnp.concatenate(made, 1)
    half = made.shape[0] // 2
    top, low = made[:half].reshape(targets[0].shape), made[half:].reshape(targets[0].shape)
    if len(targets) == 2:
        targets[0][...] = top
        targets[1][...] = low
        return

    @pl.when(r % 2 == 0)
    def _():
        targets[0][...] = top

    @pl.when(r % 2 == 1)
    def _():
        targets[2][...] = top

    @pl.when(r < 2)
    def _():
        targets[1][...] = low

    @pl.when(r >= 2)
    def _():
        targets[3][...] = low


def column_grads(lefts, rights, heads, place, items):
    rows, model = lefts[0][0].shape
    columns = sum(right[0].shape[1] for right in rights)
    shapes = share_shapes(items, heads, model, columns)
    block = (1,) + shapes[0].shape[1:]
    maps = [
        lambda r, place: (r // 2, 0, 0, 0),
        lambda r, place: (jnp.minimum(r, 1), 0, 0, 0),
        lambda r, place: (r // 3, 0, 0, 0),
        lambda r, place: (r // 3, 0, 0, 0),
    ]
    grid_spec = pltpu.PrefetchScalarGridSpec(
        num_scalar_prefetch=1,
        grid=(items,),
        in_specs=[whole((rows, model))] * (2 * len(lefts))
        + [
            pl.BlockSpec((rows, right[0].shape[1] // items), lambda r, place: (0, r ^ place[1]))
            for right in rights
            for _ in range(2)
        ],
        out_specs=[pl.BlockSpec(block, index) for index in maps[: len(shapes)]],
        scratch_shapes=[pltpu.VMEM((model // 2, 2 * rows), BF16)] * len(lefts),
    )
    return pl.pallas_call(
        functools.partial(column_grad_kernel, heads, len(lefts)),
        grid_spec=grid_spec,
        out_shape=shapes,
        compiler_params=compiler_params(),
        cost_estimate=cost(2 * rows * model * columns, 4 * model * columns),
        name="column_grads",
    )(place, *[part for left in lefts for part in left], *[part for right in rights for part in right])


class Scatter:
    def __init__(self, keep_top, keep_low, *sends):
        self.keep = [keep_top, keep_low]
        self.got, self.early = [], []
        self.route(list(sends), FIRST[: len(sends)])

    def route(self, sends, routes):
        self.sends, self.routes = sends, routes

    def move(self):
        return [swap(send, route) for send, route in zip(self.sends, self.routes)]

    def take(self, moved):
        self.early, self.got = self.got, moved
        self.route([], [])

    def second(self, sends):
        self.route(sends, FIRST[::-1][: len(sends)])


def second_kernel(*refs):
    count = len(refs) // 3
    for number in range(count):
        keep, got, out = refs[2 * number], refs[2 * number + 1], refs[2 * count + number]
        out[...] = (keep[0].astype(F32) + got[0].astype(F32)).astype(BF16)


def second_sums(*scatters):
    terms = [
        part
        for scatter in scatters
        if scatter.got
        for keep, got in zip(scatter.keep, scatter.got)
        for part in (keep, got)
    ]
    if not terms:
        return [[] for _ in scatters]
    shape = terms[0].shape
    outs = []
    in_specs, out_specs = [], []
    for term in terms:
        in_specs.append(
            pl.BlockSpec((1, 2) + term.shape[2:], lambda g: (1, g, 0, 0))
        )
    for term in terms[::2]:
        out_specs.append(pl.BlockSpec((2,) + term.shape[2:], lambda g: (g, 0, 0)))
        outs.append(jax.ShapeDtypeStruct(term.shape[1:], BF16))
    made = pl.pallas_call(
        second_kernel,
        grid=(shape[1] // 2,),
        in_specs=in_specs,
        out_specs=out_specs,
        out_shape=outs,
        compiler_params=compiler_params(),
        cost_estimate=cost(0, 6 * sum(out.size for out in outs)),
        name="second_sums",
    )(*terms)
    return [list(made[2 * i : 2 * i + 2]) for i in range(len(scatters))]


def last_kernel(*refs):
    out = refs[-1]
    for number in range(out.shape[1]):
        for half in range(2):
            terms = refs[6 * number + 3 * half : 6 * number + 3 * half + 3]
            out[:, number, half] = (
                terms[0][0].astype(F32) + terms[1][0].astype(F32) + terms[2][...].astype(F32)
            ).astype(BF16)


def last_sum(*scatters, columns=None):
    if not scatters[0].got:
        items = lax.axis_size("items")
        values = []
        for scatter in scatters:
            value = jnp.stack([keep[0] for keep in scatter.keep], 1)
            if columns is not None:
                starts = [sum(columns[:i]) for i in range(len(columns))]
                parts = [
                    value[..., start : start + size].reshape(value.shape[:3] + (items, -1))
                    for start, size in zip(starts, columns)
                ]
                value = jnp.concatenate(parts, 4).reshape(value.shape)
            values.append(lax.psum_scatter(value, "items", scatter_dimension=3, tiled=True))
        return jnp.stack(values, 1)
    terms = [
        part
        for scatter in scatters
        for parts in zip(scatter.keep, scatter.early, scatter.got)
        for part in parts
    ]
    _, places, rows, wide = terms[0].shape
    held = pl.BlockSpec((1, 2, rows, wide), lambda g: (0, g, 0, 0))
    late = pl.BlockSpec((2, rows, wide), lambda g: (g, 0, 0))
    shape = (places, len(scatters), 2, rows, wide)
    return pl.pallas_call(
        last_kernel,
        grid=(places // 2,),
        in_specs=[held, held, late] * (2 * len(scatters)),
        out_specs=pl.BlockSpec((2,) + shape[1:], lambda g: (g, 0, 0, 0, 0)),
        out_shape=jax.ShapeDtypeStruct(shape, BF16),
        compiler_params=compiler_params(),
        cost_estimate=cost(0, 8 * places * len(scatters) * 2 * rows * wide),
        name="last_sum",
    )(*terms)


def along_z(value):
    heads = lax.axis_size("heads")
    groups = [[core + 2 * z for z in range(heads // 2)] for core in range(2)]
    made = lax.psum_scatter(
        value, "heads", scatter_dimension=0, tiled=False, axis_index_groups=groups
    )
    return [made[i].reshape(-1, made.shape[-1]) for i in range(made.shape[0])]


def sum_everywhere(value):
    for axis in EVERY:
        bit = 1
        while bit < lax.axis_size(axis):
            value = value + swap(value, (axis, bit))
            bit *= 2
    return value


def edges(block, width):
    ways = lax.axis_size("heads")
    half = ways // 2
    place = lax.axis_index("heads") % half
    ring = [(side * half + i, side * half + (i + 1) % half) for side in range(2) for i in range(half)]
    low = lax.ppermute(block[:, block.shape[1] - width :], "heads", ring)
    high = lax.ppermute(block[:, :width], "heads", [(to, at) for at, to in ring])
    low = jnp.where(place == 0, jnp.roll(low, 1, 0), low)
    high = jnp.where(place == half - 1, jnp.roll(high, -1, 0), high)
    return jnp.concatenate([low, block, high], axis=1)


def body(
    frames, cotangent, bucket_counts, gains, w_ffn1_in, w_ffn1_out, w_qkv, w_out,
    w_point_in, w_depth, w_point_out, w_ffn2_in, w_ffn2_out,
):
    chunks, here, model = frames.shape
    ways = lax.axis_size("heads")
    half = ways // 2
    items = 4 if lax.axis_size("items") == 4 else 1
    span = here * half
    group_len = here * ways
    size = model // HEADS
    reach = (KERNEL - 1) // 2
    rows = chunks * here
    pieces = model // (half * LANES)
    place = lax.axis_index("heads")
    side = place // half
    where = jnp.stack(
        [place % 2, lax.axis_index("items") if items > 1 else 0 * place]
    ).astype(jnp.int32)
    always = bucket_counts[0, 0, 0] >= 0
    first = jnp.arange(chunks, dtype=jnp.int32)[:, None] * span + place % half * here
    position = first + jnp.arange(here, dtype=jnp.int32)[None]
    cosines, sines = rope_tables(position.reshape(-1), size)
    depth_rows = w_depth.astype(F32)
    gain = [gains[i : i + 1] for i in range(6)]
    counts = lax.dynamic_index_in_dim(bucket_counts[:, 0], side, 0, keepdims=False)
    wide_position = first - reach + jnp.arange(here + 2 * reach, dtype=jnp.int32)[None]
    seg_wide = segment_ids(wide_position, counts[0], counts[1], group_len)
    seg_own = seg_wide[:, reach : reach + here]

    def mine(value):
        return lax.dynamic_index_in_dim(value, side, 0, keepdims=False)

    def theirs(value):
        return lax.dynamic_index_in_dim(value, 1 - side, 0, keepdims=False)

    def begin(chunk, row, before=()):
        return front(
            chunk, row.reshape(1).astype(jnp.int32), gain[0], w_ffn1_in, w_ffn1_out, gain[1],
            w_qkv, cosines, sines, half, chunks, size, before,
        )

    own_frames = mine(frames)
    before, other_frames = fenced(
        always, (), lambda: (begin(own_frames, side), across(theirs(frames)))
    )
    stream = gathered(own_frames, other_frames, side)
    stream_one, slope_one, hid_one, ent_one, ent_att, *sent = begin(
        other_frames, 1 - side, before
    )
    qkv = [exchange(sent[0])]
    kept, contexts = [], []
    for number in range(pieces):

        def attend_now():
            return attend_forward(qkv[number], counts, size)

        def beside():
            extra = []
            if number + 1 < pieces:
                extra.append(exchange(sent[number + 1]))
            if number > 0:
                extra.append(exchange(kept[number - 1][0]))
            return extra

        def early():
            if number == 0:
                return [other_core(part) for part in (hid_one, ent_one, ent_att)]
            return [across(theirs(cotangent))] if number == 1 else []

        made, extra, others = fenced(always, (), lambda: (attend_now(), beside(), early()))
        kept.append(made)
        if number == 0:
            hid_one, ent_one, ent_att = zip((hid_one, ent_one, ent_att), others)
        elif number == 1:
            cot_other = others[0]
        if number + 1 < pieces:
            qkv.append(extra.pop(0))
        if number > 0:
            contexts.append(extra.pop(0))
    contexts.append(exchange(kept[-1][0]))
    if pieces == 1:
        cot_other = across(theirs(cotangent))
    fulls = [made[1] for made in kept]
    lses = [made[2] for made in kept]
    context = jnp.concatenate(
        [part.transpose(1, 2, 0, 3).reshape(rows, -1) for part in contexts], 1
    )
    stream_two = stream_one + dot(context, w_out)
    shaped, conv_normed, conv_inverse = layer_norm(stream_two, gain[2])
    conv_entered = shaped.astype(BF16)
    pointwise = dot(conv_entered, w_point_in)
    linear = pointwise[:, :model]
    sigmoid_gate = jax.nn.sigmoid(pointwise[:, model:])
    gated_low = (linear * sigmoid_gate).astype(BF16).reshape(chunks, here, model)
    widened = edges(gated_low, reach)
    depth_out = jnp.zeros((chunks, here, model), F32)
    for offset in range(KERNEL):
        same = (seg_wide[:, offset : offset + here] == seg_own)[:, :, None]
        depth_out = depth_out + depth_rows[offset] * jnp.where(
            same, widened[:, offset : offset + here], 0.0
        )
    depth_out = depth_out.reshape(rows, model)
    depth_shaped, depth_normed, depth_inverse = layer_norm(depth_out, gain[3])
    mixed_low = (depth_shaped * jax.nn.sigmoid(depth_shaped)).astype(BF16)
    stream_three = stream_two + dot(mixed_low, w_point_out)
    layer_out, grad_four, gain_five, slope_two, hid_two, ent_two = ffn_forward(
        stream_three, gain[4], w_ffn2_in, w_ffn2_out, gain[5],
        gathered(mine(cotangent), cot_other, side),
    )
    (grad_three, gain_four, half_two, grad_pre_two), hid_other, ent_other = fenced(
        always,
        (),
        lambda: (
            ffn_backward(grad_four, stream_three, slope_two, gain[4], w_ffn2_in, w_ffn2_out),
            other_core(hid_two),
            other_core(ent_two),
        ),
    )
    half_other, grad_pre_other = other_core(half_two), other_core(grad_pre_two)
    grad_mix = grad_three.astype(BF16)
    grad_norm_in = dot(grad_mix, w_point_out, NT) * silu_slope(depth_shaped)
    grad_depth, gain_three = norm_back(grad_norm_in, depth_normed, depth_inverse, gain[3])
    grad_depth_low = grad_depth.astype(BF16).reshape(chunks, here, model)
    grad_widened = edges(grad_depth_low, reach)
    grad_depth_full = grad_depth_low.astype(F32)
    taps = []
    grad_gated = jnp.zeros((chunks, here, model), F32)
    for offset in range(KERNEL):
        same = (seg_wide[:, offset : offset + here] == seg_own)[:, :, None]
        taps.append(
            jnp.sum(
                jnp.where(same, grad_depth_full * widened[:, offset : offset + here], 0.0), (0, 1)
            )
        )
        mirror = 2 * reach - offset
        same_back = (seg_wide[:, mirror : mirror + here] == seg_own)[:, :, None]
        grad_gated = grad_gated + depth_rows[offset] * jnp.where(
            same_back, grad_widened[:, mirror : mirror + here], 0.0
        )
    grad_gated = grad_gated.reshape(rows, model)
    grad_point = jnp.concatenate(
        [grad_gated * sigmoid_gate, grad_gated * linear * sigmoid_gate * (1.0 - sigmoid_gate)], 1
    ).astype(BF16)
    through, gain_two = norm_back(
        dot(grad_point, w_point_in, NT), conv_normed, conv_inverse, gain[2]
    )
    grad_two = grad_three + through
    grad_attn_out = grad_two.astype(BF16)
    grad_context = dot(grad_attn_out, w_out, NT).astype(BF16)
    grad_heads = []
    for number in range(pieces):
        columns = half * LANES
        part = grad_context[:, number * columns : (number + 1) * columns]
        grad_heads.append(part.reshape(chunks, here, half, LANES).transpose(2, 0, 1, 3))

    lefts = (mixed_low, conv_entered, context)
    rights = (grad_mix, grad_point, grad_attn_out)

    def ffn_grads():
        return (
            [other_core(part) for part in lefts + rights[:2]],
            exchange(grad_heads[0]),
            out_grad((half_two, half_other), (hid_two, hid_other), ways, where, items),
            column_grads(
                [(ent_two, ent_other)], [(grad_pre_two, grad_pre_other)], ways, where, items
            ),
        )

    others, grad_heads[0], shares_out, shares_in = fenced(always, (), ffn_grads)
    two_out, two_in = Scatter(*shares_out), Scatter(*shares_in)
    out_own, out_theirs = parted(layer_out, side)
    grads, backs = [], []
    for number in range(pieces):
        last = number == pieces - 1

        def beside():
            extra = []
            if not last:
                extra.append(exchange(grad_heads[number + 1]))
            if number > 0:
                extra.append(exchange(grads[number - 1]))
            if number == 0:
                extra.append(across(out_theirs))
                extra.append(other_core(rights[2]))
            return extra

        def attend_now():
            return attend_backward(
                qkv[number], counts, size, fulls[number], lses[number], grad_heads[number]
            )

        moving = (two_out,) if number == 0 else (two_out, two_in) if number == 1 else ()
        made, extra = fenced(always, moving, lambda: (attend_now(), beside()))
        grads.append(made)
        if not last:
            grad_heads[number + 1] = extra.pop(0)
        if number > 0:
            backs.append(extra.pop(0))
        if number == 0:
            out_other = extra.pop(0)
            others.append(extra.pop(0))
            two_out.second(second_sums(two_out)[0])
    two_in.second(second_sums(two_in)[0])

    def middle_part():
        back = exchange(grads[-1])
        scatter = copy.copy(two_in)
        moved(scatter)
        shares = column_grads(
            list(zip(lefts, others[:3])), list(zip(rights, others[3:])), ways, where, items
        )
        return (back, shares, last_sum(two_out, scatter))

    back, shares, two_sum = fenced(always, (), middle_part)
    backs.append(back)
    middle = Scatter(*shares)

    def attention_part():
        two_grads = along_z(two_sum)
        scatter = copy.copy(middle)

        def qkv_part():
            grad_proj = unturned(backs, cosines, sines, size)
            proj_other = other_core(grad_proj)
            down = stream_gradient(grad_two, stream_one, grad_proj, gain[1], w_qkv, F32)
            shares = column_grads(
                [ent_att], [(grad_proj, proj_other)], ways, where, items
            )
            return (down, shares)

        (grad_one, half_one, gain_one), shares = fenced(always, (scatter,), qkv_part)
        first = scatter.got
        scatter.second(second_sums(scatter)[0])
        attn = Scatter(*shares)
        (half_own, grad_pre), half_other = fenced(
            always,
            (attn,),
            lambda: (hidden_gradient(grad_one, slope_one, w_ffn1_out), other_core(half_one)),
        )
        pre_other, shares_out = fenced(
            always,
            (scatter,),
            lambda: (
                other_core(grad_pre),
                out_grad((half_own, half_other), hid_one, ways, where, items),
            ),
        )
        return (
            two_grads, first, scatter.got, (grad_one, gain_one), shares[:2], attn.got,
            (grad_pre, pre_other), shares_out,
        )

    two_grads, first, got, (grad_one, gain_one), shares, attn_got, grad_pre, shares_out = fenced(
        always, (), attention_part
    )
    middle.take(first)
    middle.take(got)
    attn = Scatter(*shares)
    attn.take(attn_got)
    attn.second(second_sums(attn)[0])
    one_out = Scatter(*shares_out)
    middle_columns = [w.shape[1] for w in (w_point_out, w_point_in, w_out)]
    middle_grad, shares, (grad_zero, _, gain_zero) = fenced(
        always,
        (one_out, attn),
        lambda: (
            along_z(last_sum(middle, columns=middle_columns)),
            column_grads([ent_one], [grad_pre], ways, where, items),
            stream_gradient(grad_one, stream, grad_pre[0], gain[0], w_ffn1_in, BF16),
        ),
    )
    one_in = Scatter(*shares)
    one_out.second(second_sums(one_out)[0])
    grad_own, grad_theirs = parted(grad_zero, side)
    attn_grad, grad_other = fenced(
        always, (one_in, one_out), lambda: (along_z(last_sum(attn)), across(grad_theirs))
    )
    one_in.second(second_sums(one_in)[0])

    hidden = w_ffn1_in.shape[1]

    def unfolded(share):
        each, wide = share.shape
        span = hidden // ways
        halves = share.reshape(2, each // 2, wide)
        parts = [
            halves[half, :, i * span : (i + 1) * span]
            for i in range(wide // span)
            for half in range(2)
        ]
        return jnp.concatenate(parts, 0).T.astype(F32)

    def last_part():
        out_grads = along_z(last_sum(one_out))
        scatter = copy.copy(one_in)
        moved(scatter)
        small = sum_everywhere(
            jnp.concatenate(
                [gain_zero, gain_one, gain_two, gain_three, gain_four, gain_five]
                + [tap[None] for tap in taps],
                0,
            )
        )
        middle_parts = []
        start = 0
        for columns in middle_columns:
            each = columns // lax.axis_size("items")
            middle_parts.append(middle_grad[0][:, start : start + each].astype(F32))
            start += each
        ready = (
            gathered(out_own[None], out_other[None], side),
            gathered(grad_own[None], grad_other[None], side),
            attn_grad[0].astype(F32),
            middle_parts,
            two_grads[1].astype(F32),
            unfolded(two_grads[0]),
        )
        return (out_grads, along_z(last_sum(scatter)), small, ready)

    one_out_grad, one_in_grad, small, ready = fenced(always, (), last_part)
    out, grad_in, attn_full, middle_parts, two_in_full, two_out_full = ready
    return (
        out,
        grad_in,
        small[:6],
        one_in_grad[0].astype(F32),
        unfolded(one_out_grad[0]),
        attn_full,
        middle_parts[2],
        middle_parts[1],
        small[6:],
        middle_parts[0],
        two_in_full,
        two_out_full,
    )


def solution(mesh):
    split = P(None, EVERY, None)
    shares = P("heads", "items")
    in_specs = (split, split, P(None, "items", None)) + (P(),) * 10
    out_specs = (split, split, P(), shares, shares, shares, shares, shares, P()) + (shares,) * 3
    return jax.shard_map(body, mesh=mesh, in_specs=in_specs, out_specs=out_specs, check_vma=False)
```

```python
import copy
import functools

import jax
import jax.numpy as jnp
from jax import lax
from jax.experimental import pallas as pl
from jax.experimental.pallas import tpu as pltpu
from jax.sharding import PartitionSpec as P

HEADS = 16
KERNEL = 5
LONG = 1500
SHORT = 500
EPS = 1e-05
ROPE_BASE = 10000.0
BLOCK = 512
INNER_FWD = 1024
INNER_BWD = 512
TURNED = 512
LANES = 128
BIG = 1e30
VMEM_LIMIT = 56 << 20
F32 = jnp.float32
BF16 = jnp.bfloat16
NN = (((1,), (0,)), ((), ()))
NT = (((1,), (1,)), ((), ()))
EVERY = ("items", "heads")
FIRST = [("items", 1), ("items", 2)]


def dot(left, right, dims=NN):
    return lax.dot_general(left, right, dims, preferred_element_type=F32)


def silu_slope(field):
    gate_sig = jax.nn.sigmoid(field)
    return gate_sig * (1.0 + field * (1.0 - gate_sig))


def layer_norm(field, gain_row):
    centred = field - jnp.mean(field, -1, keepdims=True)
    inverse = lax.rsqrt(jnp.mean(centred * centred, -1, keepdims=True) + EPS)
    normed = centred * inverse
    return (normed * gain_row, normed, inverse)


def norm_back(upstream, normed, inverse, gain_row):
    scaled = upstream * gain_row
    through = inverse * (
        scaled
        - jnp.mean(scaled, -1, keepdims=True)
        - normed * jnp.mean(scaled * normed, -1, keepdims=True)
    )
    return (through, jnp.sum(upstream * normed, 0, keepdims=True))


def segment_ids(position, long_count, short_count, group_len):
    long_end = long_count * LONG
    short_end = long_end + short_count * SHORT
    segments = jnp.where(
        position < long_end, position // LONG, long_count + (position - long_end) // SHORT
    )
    segments = jnp.where(position < short_end, segments, long_count + short_count)
    return jnp.where((position < 0) | (position >= group_len), -1, segments)


def compiler_params():
    return pltpu.CompilerParams(vmem_limit_bytes=VMEM_LIMIT)


def whole(shape):
    return pl.BlockSpec(shape, lambda *_: (0,) * len(shape))


def cost(flops, bytes_accessed, transcendentals=0):
    return pl.CostEstimate(
        flops=flops, bytes_accessed=bytes_accessed, transcendentals=transcendentals
    )


def segment_bounds(counts, place, group):
    longs, shorts = counts
    long_end = longs * LONG
    short_end = long_end + shorts * SHORT
    start = jnp.where(place < longs, place * LONG, long_end + (place - longs) * SHORT)
    size = jnp.where(place < longs, LONG, SHORT)
    last = place == longs + shorts
    return (jnp.where(last, short_end, start), jnp.where(last, group, start + size), place <= longs + shorts)


def member_lanes(counts, first, rows, group, shift=0):
    shape = (rows, LANES)
    place = lax.broadcasted_iota(jnp.int32, (8, LANES), 1) - shift
    start, end, there = segment_bounds(counts, place, group)
    start = jnp.where(there & (place >= 0), start, group)
    start, end = start[:1], end[:1]
    frame = first + lax.broadcasted_iota(jnp.int32, shape, 0)
    return (frame >= start) & (frame < end)


def block_range(counts, step, group, inner):
    longs, shorts = counts
    long_end = longs * LONG
    short_end = long_end + shorts * SHORT

    def number(frame):
        place = jnp.where(frame < long_end, frame // LONG, longs + (frame - long_end) // SHORT)
        return jnp.where(frame < short_end, place, longs + shorts)

    first = segment_bounds(counts, number(step * BLOCK), group)[0]
    last = segment_bounds(counts, number(step * BLOCK + BLOCK - 1), group)[1]
    return (first // inner, (last + inner - 1) // inner)


def head_lanes(shape, head, size):
    lane = lax.broadcasted_iota(jnp.int32, shape, 1)
    return (lane >= head * size) & (lane < (head + 1) * size)


def split_three(v):
    hi = v.astype(BF16).astype(F32)
    rest = v - hi
    mid = rest.astype(BF16).astype(F32)
    return (hi, mid, rest - mid)


def spread_columns(columns, shape):
    lane = lax.broadcasted_iota(jnp.int32, shape, 1)
    out = jnp.zeros(shape, F32)
    for place, column in enumerate(columns):
        out = jnp.where(lane == place, column, out)
    return out


def chunk_rows(ref, lead, step):
    places, chunks, frames = ref.shape[0], ref.shape[-3], ref.shape[-2]
    per = BLOCK // frames
    steps = places // per
    at = (pl.ds(step % steps * per, per),) + lead + (step // steps,)
    return ref[at].reshape(BLOCK, LANES)


def attn_fwd_kernel(
    heads, size, group, counts_ref, qkv_ref, out_ref, full_ref, lse_ref, kcat, v_all, s_scr
):
    step = pl.program_id(0)
    counts = (counts_ref[0], counts_ref[1])

    @pl.when(step == 0)
    def _():
        chunks = qkv_ref.shape[2]
        span = group // chunks
        for chunk in range(chunks):
            rows = slice(chunk * span, (chunk + 1) * span)
            kcat[rows, :LANES] = qkv_ref[:, 1, chunk].reshape(span, LANES)
            v_all[rows, :] = qkv_ref[:, 2, chunk].reshape(span, LANES)
        kcat[:, LANES:] = jnp.where(member_lanes(counts, 0, group, group), 0.0, -BIG).astype(BF16)

    q = chunk_rows(qkv_ref, (0,), step).astype(F32) * (size ** -0.5)
    member = jnp.where(member_lanes(counts, step * BLOCK, BLOCK, group), 1.0, 0.0).astype(BF16)
    queries = []
    for head in range(heads):
        mine = jnp.where(head_lanes(q.shape, head, size), q, 0.0).astype(BF16)
        queries.append(jnp.concatenate([mine, member], 1))
    low, high = block_range(counts, step, group, INNER_FWD)

    def scores(j, tops):
        keys = kcat[pl.ds(pl.multiple_of(j * INNER_FWD, INNER_FWD), INNER_FWD), :]
        new = []
        for head in range(heads):
            s = dot(queries[head], keys, NT)
            s_scr[head, j] = s
            top = tops[head]
            for part in range(INNER_FWD // LANES):
                top = jnp.maximum(top, s[:, part * LANES : (part + 1) * LANES])
            new.append(top)
        return tuple(new)

    start = tuple(jnp.full((BLOCK, LANES), -BIG, F32) for _ in range(heads))
    tops = lax.fori_loop(low, high, scores, start)
    tops = [jnp.max(t, 1, keepdims=True) for t in tops]
    tops = [jnp.broadcast_to(t, (BLOCK, LANES)) for t in tops]

    def weigh(j, carried):
        sums, accs = carried
        values = v_all[pl.ds(pl.multiple_of(j * INNER_FWD, INNER_FWD), INNER_FWD), :]
        new_sums, new_accs = [], []
        for head in range(heads):
            total = sums[head]
            parts = []
            for part in range(INNER_FWD // LANES):
                p = jnp.exp(s_scr[head, j, :, part * LANES : (part + 1) * LANES] - tops[head])
                total = total + p
                parts.append(p.astype(BF16))
            new_sums.append(total)
            new_accs.append(accs[head] + dot(jnp.concatenate(parts, 1), values))
        return (tuple(new_sums), tuple(new_accs))

    zeros = tuple(jnp.zeros((BLOCK, LANES), F32) for _ in range(heads))
    sums, accs = lax.fori_loop(low, high, weigh, (zeros, zeros))
    result = None
    for head in range(heads):
        total = jnp.sum(sums[head], 1, keepdims=True)
        mine = accs[head] / total
        if result is None:
            result = mine
        else:
            result = jnp.where(head_lanes(mine.shape, head, size), mine, result)
        lse_ref[head] = tops[head] + jnp.log(jnp.broadcast_to(total, (BLOCK, LANES)))
    full_ref[...] = result
    out_ref[...] = result.astype(BF16).reshape(out_ref.shape)


def attend_forward(qkv, counts, size):
    places, _, chunks, frames, _ = qkv.shape
    group = places * chunks * frames
    heads = LANES // size
    per = BLOCK // frames
    each = places // per
    return pl.pallas_call(
        functools.partial(attn_fwd_kernel, heads, size, group),
        grid=(group // BLOCK,),
        in_specs=[pl.BlockSpec(memory_space=pltpu.SMEM), whole(qkv.shape)],
        out_specs=[
            pl.BlockSpec((per, 1, frames, LANES), lambda i: (i % each, i // each, 0, 0)),
            pl.BlockSpec((BLOCK, LANES), lambda i: (i, 0)),
            pl.BlockSpec((heads, BLOCK, LANES), lambda i: (0, i, 0)),
        ],
        out_shape=[
            jax.ShapeDtypeStruct((places, chunks, frames, LANES), BF16),
            jax.ShapeDtypeStruct((group, LANES), F32),
            jax.ShapeDtypeStruct((heads, group, LANES), F32),
        ],
        scratch_shapes=[
            pltpu.VMEM((group, 2 * LANES), BF16),
            pltpu.VMEM((group, LANES), BF16),
            pltpu.VMEM((heads, group // INNER_FWD, BLOCK, INNER_FWD), F32),
        ],
        compiler_params=compiler_params(),
        cost_estimate=cost(16 * group * group * LANES, 6 << 20, heads * group * group),
        name="attend_forward",
    )(counts, qkv)


def attn_bwd_kernel(
    heads, size, group, counts_ref, qkv_ref, full_ref, lse_ref, grad_ref, out_ref,
    qcat, gcat, k_turned, dq_turned,
):
    step = pl.program_id(0)
    counts = (counts_ref[0], counts_ref[1])
    blocks = group // BLOCK
    places, _, _, frames, _ = qkv_ref.shape
    per = BLOCK // frames
    each = places // per

    def put(part, j, value):
        out_ref[pl.ds(j % each * per, per), part, j // each] = value.astype(BF16).reshape(
            per, frames, LANES
        )

    @pl.when(step == 0)
    def _():
        dq_turned[...] = jnp.zeros_like(dq_turned)

        def prepare(j, _):
            rows = pl.ds(pl.multiple_of(j * BLOCK, BLOCK), BLOCK)
            lane = lax.broadcasted_iota(jnp.int32, (BLOCK, LANES), 1)
            q = chunk_rows(qkv_ref, (0,), j).astype(F32) * (size ** -0.5)
            g = chunk_rows(grad_ref, (), j).astype(F32)
            product = g * full_ref[rows, :]
            member = jnp.where(member_lanes(counts, j * BLOCK, BLOCK, group, 3), 1.0, 0.0)
            for head in range(heads):
                own = head_lanes((BLOCK, LANES), head, size)
                lse = lse_ref[head, rows, :]
                spread = spread_columns(split_three(lse), (BLOCK, LANES))
                delta = jnp.sum(jnp.where(own, product, 0.0), 1, keepdims=True)
                delta = jnp.broadcast_to(delta, (BLOCK, LANES))
                qcat[head, rows, :LANES] = jnp.where(own, q, 0.0).astype(BF16)
                qcat[head, rows, LANES:] = jnp.where(lane < 3, -spread, member).astype(BF16)
                gcat[head, rows, :LANES] = jnp.where(own, g, 0.0).astype(BF16)
                spread = spread_columns(split_three(delta), (BLOCK, LANES))
                gcat[head, rows, LANES:] = (-spread).astype(BF16)
            k = chunk_rows(qkv_ref, (1,), j).astype(F32)
            k_turned[j] = jnp.transpose(k).astype(BF16)
            return 0

        lax.fori_loop(0, blocks, prepare, 0)

    lane = lax.broadcasted_iota(jnp.int32, (BLOCK, LANES), 1)
    member = member_lanes(counts, step * BLOCK, BLOCK, group, 3)
    tail = jnp.where(lane < 3, 1.0, jnp.where(member, 0.0, -BIG)).astype(BF16)
    keys = jnp.concatenate([chunk_rows(qkv_ref, (1,), step), tail], 1)
    ones = jnp.where(lane < 3, 1.0, 0.0).astype(BF16)
    values = jnp.concatenate([chunk_rows(qkv_ref, (2,), step), ones], 1)

    def one(j, carried):
        dk, dv = carried
        cols = pl.ds(pl.multiple_of(j * INNER_BWD, INNER_BWD), INNER_BWD)
        for head in range(heads):
            qc = qcat[head, cols, :]
            gc = gcat[head, cols, :]
            p = jnp.exp(dot(keys, qc, NT))
            ds = (p * dot(values, gc, NT)).astype(BF16)
            dv = dv + dot(p.astype(BF16), gc[:, :LANES])
            dk = dk + dot(ds, qc[:, :LANES])
            mine = slice(head * size, (head + 1) * size)
            dq_turned[j, mine, :] += dot(k_turned[step, mine, :], ds)
        return (dk, dv)

    zero = jnp.zeros((BLOCK, LANES), F32)
    low, high = block_range(counts, step, group, INNER_BWD)
    dk, dv = lax.fori_loop(low, high, one, (zero, zero))
    put(1, step, dk)
    put(2, step, dv)

    @pl.when(step == blocks - 1)
    def _():
        def finish(j, _):
            put(0, j, jnp.transpose(dq_turned[j]) * (size ** -0.5))
            return 0

        lax.fori_loop(0, blocks, finish, 0)


def attend_backward(qkv, counts, size, full, lse, grad):
    places, _, chunks, frames, _ = qkv.shape
    group = places * chunks * frames
    heads = LANES // size
    steps = group // BLOCK
    return pl.pallas_call(
        functools.partial(attn_bwd_kernel, heads, size, group),
        grid=(steps,),
        in_specs=[
            pl.BlockSpec(memory_space=pltpu.SMEM),
            whole(qkv.shape),
            whole(full.shape),
            whole(lse.shape),
            whole(grad.shape),
        ],
        out_specs=whole(qkv.shape),
        out_shape=jax.ShapeDtypeStruct(qkv.shape, BF16),
        scratch_shapes=[
            pltpu.VMEM((heads, group, 2 * LANES), BF16),
            pltpu.VMEM((heads, group, 2 * LANES), BF16),
            pltpu.VMEM((steps, LANES, BLOCK), BF16),
            pltpu.VMEM((group // INNER_BWD, LANES, INNER_BWD), F32),
        ],
        compiler_params=compiler_params(),
        cost_estimate=cost(32 * group * group * LANES, 9 << 20, heads * group * group),
        name="attend_backward",
    )(counts, qkv, full, lse, grad)


def half_gate(field):
    return 0.5 * jnp.tanh(0.5 * field) + 0.5


def hidden_units(pre):
    gate = half_gate(pre)
    hidden = pre * gate
    return (hidden.astype(BF16), (gate + hidden * (1.0 - gate)).astype(BF16))


def ffn_fwd_kernel(
    x_ref, gain_ref, last_gain_ref, up_ref, win_ref, wout_ref,
    out_ref, down_ref, gain_grad_ref, slope_ref, hid_ref, entered_ref, total,
):
    step = pl.program_id(0)

    @pl.when(step == 0)
    def _():
        entered_ref[...] = layer_norm(x_ref[...], gain_ref[...])[0].astype(BF16)
        total[...] = jnp.zeros_like(total)

    hidden, slope = hidden_units(dot(entered_ref[...], win_ref[...]))
    slope_ref[...] = slope
    hid_ref[...] = hidden
    total[...] += dot(hidden, wout_ref[...])

    @pl.when(step == pl.num_programs(0) - 1)
    def _():
        gain = last_gain_ref[...]
        shaped, normed, inverse = layer_norm(x_ref[...] + 0.5 * total[...], gain)
        out_ref[...] = shaped.astype(BF16)
        through, grad_gain = norm_back(up_ref[...].astype(F32), normed, inverse, gain)
        down_ref[...] = through
        gain_grad_ref[...] = grad_gain


def ffn_forward(stream, gain_row, weight_in, weight_out, last_gain, upstream):
    rows, model = stream.shape
    units = weight_in.shape[1]
    wide = min(units, 1024)
    return pl.pallas_call(
        ffn_fwd_kernel,
        grid=(units // wide,),
        in_specs=[
            whole((rows, model)),
            whole((1, model)),
            whole((1, model)),
            whole((rows, model)),
            pl.BlockSpec((model, wide), lambda s: (0, s)),
            pl.BlockSpec((wide, model), lambda s: (s, 0)),
        ],
        out_specs=[whole((rows, model)), whole((rows, model)), whole((1, model))]
        + [pl.BlockSpec((rows, wide), lambda s: (0, s))] * 2
        + [whole((rows, model))],
        out_shape=[
            jax.ShapeDtypeStruct((rows, model), BF16),
            jax.ShapeDtypeStruct((rows, model), F32),
            jax.ShapeDtypeStruct((1, model), F32),
            jax.ShapeDtypeStruct((rows, units), BF16),
            jax.ShapeDtypeStruct((rows, units), BF16),
            jax.ShapeDtypeStruct((rows, model), BF16),
        ],
        scratch_shapes=[pltpu.VMEM((rows, model), F32)],
        compiler_params=compiler_params(),
        cost_estimate=cost(4 * rows * model * units, 4 * model * units + 4 * rows * units),
        name="ffn_forward",
    )(stream, gain_row, last_gain, upstream, weight_in, weight_out)


def ffn_bwd_kernel(
    x_ref, gain_ref, up_ref, slope_ref, win_ref, wout_ref,
    down_ref, gain_grad_ref, half_ref, grad_ref, total,
):
    step = pl.program_id(0)

    @pl.when(step == 0)
    def _():
        half_ref[...] = (0.5 * up_ref[...]).astype(BF16)
        total[...] = jnp.zeros_like(total)

    grad = (dot(half_ref[...], wout_ref[...], NT) * slope_ref[...].astype(F32)).astype(BF16)
    grad_ref[...] = grad
    total[...] += dot(grad, win_ref[...], NT)

    @pl.when(step == pl.num_programs(0) - 1)
    def _():
        gain = gain_ref[...]
        normed, inverse = layer_norm(x_ref[...].astype(F32), gain)[1:]
        through, grad_gain = norm_back(total[...], normed, inverse, gain)
        down_ref[...] = up_ref[...] + through
        gain_grad_ref[...] = grad_gain


def ffn_backward(upstream, stream, slope, gain_row, weight_in, weight_out):
    rows, model = stream.shape
    units = weight_in.shape[1]
    wide = min(units, 1024)
    return pl.pallas_call(
        ffn_bwd_kernel,
        grid=(units // wide,),
        in_specs=[
            whole((rows, model)),
            whole((1, model)),
            whole((rows, model)),
            pl.BlockSpec((rows, wide), lambda s: (0, s)),
            pl.BlockSpec((model, wide), lambda s: (0, s)),
            pl.BlockSpec((wide, model), lambda s: (s, 0)),
        ],
        out_specs=[
            whole((rows, model)),
            whole((1, model)),
            whole((rows, model)),
            pl.BlockSpec((rows, wide), lambda s: (0, s)),
        ],
        out_shape=[
            jax.ShapeDtypeStruct((rows, model), F32),
            jax.ShapeDtypeStruct((1, model), F32),
            jax.ShapeDtypeStruct((rows, model), BF16),
            jax.ShapeDtypeStruct((rows, units), BF16),
        ],
        scratch_shapes=[pltpu.VMEM((rows, model), F32)],
        compiler_params=compiler_params(),
        cost_estimate=cost(4 * rows * model * units, 4 * model * units + 6 * rows * units),
        name="ffn_backward",
    )(stream, gain_row, upstream, slope, weight_in, weight_out)


def hidden_kernel(up_ref, slope_ref, wout_ref, half_ref, grad_ref):
    @pl.when(pl.program_id(0) == 0)
    def _():
        half_ref[...] = (0.5 * up_ref[...]).astype(BF16)

    grad = dot(half_ref[...], wout_ref[...], NT) * slope_ref[...].astype(F32)
    grad_ref[...] = grad.astype(BF16)


def hidden_gradient(upstream, slope, weight_out):
    rows, model = upstream.shape
    units = weight_out.shape[0]
    wide = min(units, 1024)
    return pl.pallas_call(
        hidden_kernel,
        grid=(units // wide,),
        in_specs=[
            whole((rows, model)),
            pl.BlockSpec((rows, wide), lambda s: (0, s)),
            pl.BlockSpec((wide, model), lambda s: (s, 0)),
        ],
        out_specs=[whole((rows, model)), pl.BlockSpec((rows, wide), lambda s: (0, s))],
        out_shape=[
            jax.ShapeDtypeStruct((rows, model), BF16),
            jax.ShapeDtypeStruct((rows, units), BF16),
        ],
        compiler_params=compiler_params(),
        cost_estimate=cost(2 * rows * model * units, 2 * model * units + 6 * rows * units),
        name="hidden_gradient",
    )(upstream, slope, weight_out)


def down_kernel(
    x_ref, gain_ref, up_ref, grad_ref, weight_ref, down_ref, half_ref, gain_grad_ref, total
):
    step = pl.program_id(0)

    @pl.when(step == 0)
    def _():
        total[...] = jnp.zeros_like(total)

    total[...] += dot(grad_ref[...], weight_ref[...], NT)

    @pl.when(step == pl.num_programs(0) - 1)
    def _():
        gain = gain_ref[...]
        normed, inverse = layer_norm(x_ref[...].astype(F32), gain)[1:]
        through, grad_gain = norm_back(total[...], normed, inverse, gain)
        down = up_ref[...] + through
        down_ref[...] = down.astype(down_ref.dtype)
        half_ref[...] = (0.5 * down).astype(BF16)
        gain_grad_ref[...] = grad_gain


def stream_gradient(upstream, stream, grad, gain_row, weight, down_type):
    rows, model = stream.shape
    units = weight.shape[1]
    wide = min(units, 1024)
    return pl.pallas_call(
        down_kernel,
        grid=(units // wide,),
        in_specs=[
            whole((rows, model)),
            whole((1, model)),
            whole((rows, model)),
            pl.BlockSpec((rows, wide), lambda s: (0, s)),
            pl.BlockSpec((model, wide), lambda s: (0, s)),
        ],
        out_specs=[whole((rows, model)), whole((rows, model)), whole((1, model))],
        out_shape=[
            jax.ShapeDtypeStruct((rows, model), down_type),
            jax.ShapeDtypeStruct((rows, model), BF16),
            jax.ShapeDtypeStruct((1, model), F32),
        ],
        scratch_shapes=[pltpu.VMEM((rows, model), F32)],
        compiler_params=compiler_params(),
        cost_estimate=cost(2 * rows * model * units, 2 * model * units + 2 * rows * units),
        name="stream_gradient",
    )(stream, gain_row, upstream, grad, weight)


def turn(field, cosines, sines, size):
    repeats = field.shape[1] // cosines.shape[1]
    cosines = jnp.concatenate([cosines] * repeats, 1)
    sines = jnp.concatenate([sines] * repeats, 1)
    lane = lax.broadcasted_iota(jnp.int32, field.shape, 1)
    half = size // 2
    width = field.shape[1]
    swapped = jnp.where(
        lane % size < half,
        pltpu.roll(field, width - half, 1),
        pltpu.roll(field, half, 1),
    )
    return field * cosines + swapped * sines


def rope_tables(position, size):
    half = size // 2
    lane = jnp.arange(LANES, dtype=jnp.int32)
    freqs = jnp.exp(
        -jnp.log(jnp.float32(ROPE_BASE)) * (lane % half).astype(jnp.float32) / half
    )
    angles = position.astype(jnp.float32)[:, None] * freqs[None, :]
    signs = jnp.where(lane % size < half, -1.0, 1.0)
    return (jnp.cos(angles), jnp.sin(angles) * signs[None, :])


def front_kernel(
    size, ffn_steps, pieces, row_ref, x_ref, gain_ref, win_ref, wout_ref,
    wq_ref, wk_ref, wv_ref, cos_ref, sin_ref, *refs,
):
    refs = refs[-(6 + pieces) :]
    out_ref, slope_ref, hid_ref, entered_ref, next_ref = refs[:5]
    outs, total = refs[5:-1], refs[-1]
    step = pl.program_id(0)

    @pl.when(step == 0)
    def _():
        gain = gain_ref[0:1, :]
        entered_ref[...] = layer_norm(x_ref[0].astype(F32), gain)[0].astype(BF16)
        total[...] = jnp.zeros_like(total)

    @pl.when(step < ffn_steps)
    def _():
        hidden, slope = hidden_units(dot(entered_ref[...], win_ref[...]))
        slope_ref[...] = slope
        hid_ref[...] = hidden
        total[...] += dot(hidden, wout_ref[...])

    @pl.when(step == ffn_steps)
    def _():
        out = x_ref[0].astype(F32) + 0.5 * total[...]
        out_ref[...] = out
        next_ref[...] = layer_norm(out, gain_ref[1:2, :])[0].astype(BF16)

    each = (pl.num_programs(0) - ffn_steps) // pieces
    for piece, out in enumerate(outs):

        @pl.when((step >= ffn_steps) & ((step - ffn_steps) // each == piece))
        def _():
            for place, weight in enumerate((wq_ref, wk_ref, wv_ref)):
                made = dot(next_ref[...], weight[...])
                if place < 2:
                    made = turn(made, cos_ref[...], sin_ref[...], size)
                made = made.astype(BF16)
                for target in range(out.shape[0]):
                    out[target, place, 0] = made[:, target * LANES : (target + 1) * LANES]


def front(
    frames, row, gains, weight_in, weight_out, weight, cosines, sines,
    places, chunks, size, before=(),
):
    given, rows, model = frames.shape
    units = weight_in.shape[1]
    wide = min(units, 1024)
    ffn_steps = units // wide
    turned_wide = TURNED
    turns = model // turned_wide
    pieces = model // (places * LANES)
    each = turns // pieces
    piece = jax.ShapeDtypeStruct((places, 3, chunks, rows, LANES), BF16)

    def ffn_at(s, row):
        return jnp.minimum(s, ffn_steps - 1)

    def turn_at(s):
        return jnp.maximum(s - ffn_steps, 0)

    def piece_at(number):
        return lambda s, row: (
            jnp.clip(s - ffn_steps - number * each, 0, each - 1), 0, row[0], 0, 0
        )

    row_block = pl.BlockSpec((rows, model), lambda s, row: (row[0], 0))
    unit_block = pl.BlockSpec((rows, wide), lambda s, row: (row[0], ffn_at(s, row)))
    angle_block = pl.BlockSpec((rows, LANES), lambda s, row: (row[0], 0))
    out_shape = [
        jax.ShapeDtypeStruct((chunks * rows, model), F32),
        jax.ShapeDtypeStruct((chunks * rows, units), BF16),
        jax.ShapeDtypeStruct((chunks * rows, units), BF16),
        jax.ShapeDtypeStruct((chunks * rows, model), BF16),
        jax.ShapeDtypeStruct((chunks * rows, model), BF16),
    ] + [piece] * pieces
    in_specs = [
        pl.BlockSpec((1, rows, model), lambda s, row: (row[0] if given > 1 else 0, 0, 0)),
        whole(gains.shape),
        pl.BlockSpec((model, wide), lambda s, row: (0, ffn_at(s, row))),
        pl.BlockSpec((wide, model), lambda s, row: (ffn_at(s, row), 0)),
        pl.BlockSpec((model, turned_wide), lambda s, row: (0, turn_at(s))),
        pl.BlockSpec((model, turned_wide), lambda s, row: (0, turns + turn_at(s))),
        pl.BlockSpec((model, turned_wide), lambda s, row: (0, 2 * turns + turn_at(s))),
        angle_block,
        angle_block,
    ]
    grid_spec = pltpu.PrefetchScalarGridSpec(
        num_scalar_prefetch=1,
        grid=(ffn_steps + turns,),
        in_specs=in_specs + [pl.BlockSpec(memory_space=pl.ANY)] * len(before),
        out_specs=[row_block, unit_block, unit_block, row_block, row_block]
        + [
            pl.BlockSpec((turned_wide // LANES, 3, 1, rows, LANES), piece_at(number))
            for number in range(pieces)
        ],
        scratch_shapes=[pltpu.VMEM((rows, model), F32)],
    )
    return pl.pallas_call(
        functools.partial(front_kernel, size, ffn_steps, pieces),
        grid_spec=grid_spec,
        out_shape=out_shape,
        input_output_aliases={1 + len(in_specs) + i: i for i in range(len(before))},
        compiler_params=compiler_params(),
        cost_estimate=cost(
            4 * rows * model * units + 6 * rows * model * model,
            4 * model * units + 6 * model * model + 4 * rows * units + 16 * rows * model,
        ),
        name="front",
    )(
        row, frames, gains, weight_in, weight_out, weight, weight, weight,
        cosines, sines, *before,
    )


def projection_kernel(
    size, pieces, cos_ref, sin_ref, x_ref, gain_ref, up_ref, weight_ref, *refs
):
    backs, refs = refs[:pieces], refs[pieces:]
    grad_ref, down_ref, half_ref, gain_grad_ref, total = refs
    step = pl.program_id(0)

    @pl.when(step == 0)
    def _():
        total[...] = jnp.zeros_like(total)

    rotated = step < 2
    cosines = jnp.where(rotated, cos_ref[...], 1.0)
    sines = jnp.where(rotated, -sin_ref[...], 0.0)
    places, _, chunks, frames, _ = backs[0].shape
    per = TURNED // LANES
    for piece, back in enumerate(backs):
        for first in range(0, places, per):
            for chunk in range(chunks):
                rows = slice(chunk * frames, (chunk + 1) * frames)
                field = jnp.concatenate([back[first + i, 0, chunk] for i in range(per)], 1)
                made = turn(field.astype(F32), cosines[rows], sines[rows], size).astype(BF16)
                start = (piece * places + first) * LANES
                grad_ref[rows, start : start + TURNED] = made
    total[...] += dot(grad_ref[...], weight_ref[...], NT)

    @pl.when(step == pl.num_programs(0) - 1)
    def _():
        gain = gain_ref[...]
        normed, inverse = layer_norm(x_ref[...], gain)[1:]
        through, grad_gain = norm_back(total[...], normed, inverse, gain)
        down = up_ref[...] + through
        down_ref[...] = down
        half_ref[...] = (0.5 * down).astype(BF16)
        gain_grad_ref[...] = grad_gain


def projection_backward(backs, cosines, sines, size, upstream, stream, gain_row, weight):
    places, kinds, chunks, frames, _ = backs[0].shape
    pieces = len(backs)
    rows, model = stream.shape
    block = pl.BlockSpec((places, 1, chunks, frames, LANES), lambda s: (0, s, 0, 0, 0))
    return pl.pallas_call(
        functools.partial(projection_kernel, size, pieces),
        grid=(kinds,),
        in_specs=[
            whole(cosines.shape),
            whole(sines.shape),
            whole((rows, model)),
            whole((1, model)),
            whole((rows, model)),
            pl.BlockSpec((model, model), lambda s: (0, s)),
        ]
        + [block] * pieces,
        out_specs=[
            pl.BlockSpec((rows, model), lambda s: (0, s)),
            whole((rows, model)),
            whole((rows, model)),
            whole((1, model)),
        ],
        out_shape=[
            jax.ShapeDtypeStruct((rows, kinds * model), BF16),
            jax.ShapeDtypeStruct((rows, model), F32),
            jax.ShapeDtypeStruct((rows, model), BF16),
            jax.ShapeDtypeStruct((1, model), F32),
        ],
        scratch_shapes=[pltpu.VMEM((rows, model), F32)],
        compiler_params=compiler_params(),
        cost_estimate=cost(6 * rows * model * model, 6 * model * model + 22 * rows * model),
        name="projection_backward",
    )(cosines, sines, stream, gain_row, upstream, weight, *backs)


def flipped(axis_bit, count):
    axis, bit = axis_bit
    items, heads = count
    if axis == "items":
        return [(i * heads + h, (i ^ bit) * heads + h) for i in range(items) for h in range(heads)]
    return [(i * heads + h, i * heads + (h ^ bit)) for i in range(items) for h in range(heads)]


def swap(value, axis_bit):
    count = (lax.axis_size("items"), lax.axis_size("heads"))
    return lax.ppermute(value, EVERY, flipped(axis_bit, count))


def fenced(always, scatters, work):
    def run():
        return (work(), [scatter.move() for scatter in scatters])

    def empty():
        return jax.tree.map(lambda leaf: jnp.zeros(leaf.shape, leaf.dtype), jax.eval_shape(run))

    result, moved = lax.optimization_barrier(lax.cond(always, run, empty))
    for scatter, parts in zip(scatters, moved):
        scatter.take(parts)
    return result


def moved(scatter):
    scatter.take(scatter.move())


def other_core(value):
    return swap(value, ("heads", 1))


def exchange(value):
    half = lax.axis_size("heads") // 2
    groups = [[side * half + i for i in range(half)] for side in range(2)]
    return lax.all_to_all(
        value, "heads", split_axis=0, concat_axis=0, tiled=True, axis_index_groups=groups
    )


def across(value):
    return swap(value, ("heads", lax.axis_size("heads") // 2))


def gathered(own, other, side):
    return jnp.concatenate([jnp.where(side == 0, own, other), jnp.where(side == 0, other, own)], 0)


def parted(value, side):
    low, high = jnp.split(value, 2, 0)
    return (jnp.where(side == 0, low, high), jnp.where(side == 0, high, low))


def own_rows(left_ref, heads, core, target, first):
    rows, model = left_ref.shape
    each = model // heads
    for place in range(heads // 2):
        if each % LANES == 0:
            start = pl.multiple_of((2 * place + core) * each, each)
            mine = jnp.transpose(left_ref[:, pl.ds(start, each)].astype(F32)).astype(BF16)
        else:
            pair = left_ref[:, 2 * place * each : 2 * (place + 1) * each]
            pair = jnp.transpose(pair.astype(F32))
            mine = jnp.where(core == 0, pair[:each], pair[each:]).astype(BF16)
        for half in range(2):
            start = (half * (heads // 2) + place) * (each // 2)
            target[start : start + each // 2, first : first + rows] = mine[
                half * (each // 2) : (half + 1) * (each // 2)
            ]


def turned_items(left, items, own, target, first):
    rows, model = left.shape
    each = model // items
    for item in range(items):
        part = jnp.transpose(left[:, item * each : (item + 1) * each].astype(F32)).astype(BF16)
        place = pl.multiple_of((own ^ item) * each, each)
        target[pl.ds(place, each), first : first + rows] = part


def share_shapes(items, heads, model, columns):
    lead = 2 if items > 1 else 1
    shape = (lead, heads // 2, model // heads // 2, columns // items)
    return [jax.ShapeDtypeStruct(shape, BF16)] * (4 if items > 1 else 2)


def out_grad_kernel(place_ref, up_own, up_other, hid_own, hid_other, *refs):
    targets, turned = refs[:-1], refs[-1]
    rows, model = up_own.shape
    items = 4 if len(targets) == 4 else 1

    @pl.when(pl.program_id(0) == 0)
    def _():
        turned_items(up_own[...], items, place_ref[1], turned, 0)
        turned_items(up_other[...], items, place_ref[1], turned, rows)

    hidden = jnp.concatenate([hid_own[...], hid_other[...]], 0)
    grad = dot(turned[...], hidden).astype(BF16)
    wide = grad.shape[1]
    each = targets[0].shape[2]
    parts = model // items // (2 * each)
    for r in range(items):
        for part in range(parts):
            for half in range(2):
                first = ((r * parts + part) * 2 + half) * each
                piece = grad[first : first + each]
                if half == 0:
                    target, at = targets[2 * (r % 2)], r // 2
                else:
                    target, at = targets[1 + 2 * (r // 2)], r % 2
                target[at, 0, :, part * wide : (part + 1) * wide] = piece


def out_grad(upstream, hidden, heads, place, items):
    rows, model = upstream[0].shape
    units = hidden[0].shape[1]
    wide = units // heads
    shapes = share_shapes(items, heads, model, units)
    block = (shapes[0].shape[0], 1) + shapes[0].shape[2:]
    hid_block = pl.BlockSpec((rows, wide), lambda s, place: (0, 2 * s + place[0]))
    grid_spec = pltpu.PrefetchScalarGridSpec(
        num_scalar_prefetch=1,
        grid=(heads // 2,),
        in_specs=[whole((rows, model))] * 2 + [hid_block] * 2,
        out_specs=[pl.BlockSpec(block, lambda s, place: (0, s, 0, 0))] * len(shapes),
        scratch_shapes=[pltpu.VMEM((model, 2 * rows), BF16)],
    )
    return pl.pallas_call(
        out_grad_kernel,
        grid_spec=grid_spec,
        out_shape=shapes,
        compiler_params=compiler_params(),
        cost_estimate=cost(2 * rows * model * units, 2 * model * units + 4 * rows * units),
        name="out_grad",
    )(place, *upstream, *hidden)


def column_grad_kernel(heads, items, split, place_ref, *refs):
    count = len(split)
    lefts, refs = refs[: 2 * count], refs[2 * count :]
    rights, refs = refs[: 2 * (count + sum(split))], refs[2 * (count + sum(split)) :]
    targets, turned = refs[:-count], refs[-count:]
    r = pl.program_id(0)
    rows = lefts[0].shape[0]

    @pl.when(r == 0)
    def _():
        for number in range(count):
            for other in range(2):
                own_rows(
                    lefts[2 * number + other], heads, place_ref[0], turned[number], other * rows
                )

    made = []
    at = 0
    for number in range(count):
        right = jnp.concatenate([rights[at][...], rights[at + 1][...]], 0)
        at += 2
        if split[number]:
            second = jnp.concatenate([rights[at][...], rights[at + 1][...]], 0)
            at += 2
            right = jnp.where((r ^ place_ref[1]) < items // 2, right, second)
        made.append(dot(turned[number][...], right).astype(BF16))
    made = made[0] if count == 1 else jnp.concatenate(made, 1)
    half = made.shape[0] // 2
    top, low = made[:half].reshape(targets[0].shape), made[half:].reshape(targets[0].shape)
    if len(targets) == 2:
        targets[0][...] = top
        targets[1][...] = low
        return

    @pl.when(r % 2 == 0)
    def _():
        targets[0][...] = top

    @pl.when(r % 2 == 1)
    def _():
        targets[2][...] = top

    @pl.when(r < 2)
    def _():
        targets[1][...] = low

    @pl.when(r >= 2)
    def _():
        targets[3][...] = low


def column_grads(lefts, rights, heads, place, items):
    if items == 1:
        flat = [
            (left, part)
            for left, right in zip(lefts, rights)
            for part in (right if isinstance(right[0], tuple) else (right,))
        ]
        lefts, rights = [left for left, _ in flat], [right for _, right in flat]
    split = [isinstance(right[0], tuple) for right in rights]
    rows, model = lefts[0][0].shape
    parts = []
    for right, two in zip(rights, split):
        parts += [part for pair in right for part in pair] if two else list(right)
    columns = sum(part.shape[1] for part in parts) // 2
    shapes = share_shapes(items, heads, model, columns)
    block = (1,) + shapes[0].shape[1:]
    right_specs = []
    for right, two in zip(rights, split):
        if two:
            share = pl.BlockSpec(
                (rows, right[0][0].shape[1] * 2 // items),
                lambda r, place: (0, (r ^ place[1]) % (items // 2)),
            )
            right_specs += [share] * 4
        else:
            share = pl.BlockSpec(
                (rows, right[0].shape[1] // items), lambda r, place: (0, r ^ place[1])
            )
            right_specs += [share] * 2
    maps = [
        lambda r, place: (r // 2, 0, 0, 0),
        lambda r, place: (jnp.minimum(r, 1), 0, 0, 0),
        lambda r, place: (r // 3, 0, 0, 0),
        lambda r, place: (r // 3, 0, 0, 0),
    ]
    grid_spec = pltpu.PrefetchScalarGridSpec(
        num_scalar_prefetch=1,
        grid=(items,),
        in_specs=[whole((rows, model))] * (2 * len(lefts)) + right_specs,
        out_specs=[pl.BlockSpec(block, index) for index in maps[: len(shapes)]],
        scratch_shapes=[pltpu.VMEM((model // 2, 2 * rows), BF16)] * len(lefts),
    )
    return pl.pallas_call(
        functools.partial(column_grad_kernel, heads, items, split),
        grid_spec=grid_spec,
        out_shape=shapes,
        compiler_params=compiler_params(),
        cost_estimate=cost(2 * rows * model * columns, 4 * model * columns),
        name="column_grads",
    )(place, *[part for left in lefts for part in left], *parts)


class Scatter:
    def __init__(self, keep_top, keep_low, *sends):
        self.keep = [keep_top, keep_low]
        self.got, self.early = [], []
        self.route(list(sends), FIRST[: len(sends)])

    def route(self, sends, routes):
        self.sends, self.routes = sends, routes

    def move(self):
        return [swap(send, route) for send, route in zip(self.sends, self.routes)]

    def take(self, moved):
        self.early, self.got = self.got, moved
        self.route([], [])

    def second(self, sends):
        self.route(sends, FIRST[::-1][: len(sends)])


def second_kernel(*refs):
    count = len(refs) // 3
    for number in range(count):
        keep, got, out = refs[2 * number], refs[2 * number + 1], refs[2 * count + number]
        out[...] = (keep[0].astype(F32) + got[0].astype(F32)).astype(BF16)


def second_sums(*scatters):
    terms = [
        part
        for scatter in scatters
        if scatter.got
        for keep, got in zip(scatter.keep, scatter.got)
        for part in (keep, got)
    ]
    if not terms:
        return [[] for _ in scatters]
    shape = terms[0].shape
    outs = []
    in_specs, out_specs = [], []
    for term in terms:
        in_specs.append(
            pl.BlockSpec((1, 2) + term.shape[2:], lambda g: (1, g, 0, 0))
        )
    for term in terms[::2]:
        out_specs.append(pl.BlockSpec((2,) + term.shape[2:], lambda g: (g, 0, 0)))
        outs.append(jax.ShapeDtypeStruct(term.shape[1:], BF16))
    made = pl.pallas_call(
        second_kernel,
        grid=(shape[1] // 2,),
        in_specs=in_specs,
        out_specs=out_specs,
        out_shape=outs,
        compiler_params=compiler_params(),
        cost_estimate=cost(0, 6 * sum(out.size for out in outs)),
        name="second_sums",
    )(*terms)
    return [list(made[2 * i : 2 * i + 2]) for i in range(len(scatters))]


def last_kernel(*refs):
    out = refs[-1]
    for number in range(out.shape[1]):
        for half in range(2):
            terms = refs[6 * number + 3 * half : 6 * number + 3 * half + 3]
            out[:, number, half] = (
                terms[0][0].astype(F32) + terms[1][0].astype(F32) + terms[2][...].astype(F32)
            ).astype(BF16)


def last_sum(*scatters, columns=None):
    if not scatters[0].got:
        items = lax.axis_size("items")
        values = []
        for scatter in scatters:
            value = jnp.stack([keep[0] for keep in scatter.keep], 1)
            if columns is not None:
                starts = [sum(columns[:i]) for i in range(len(columns))]
                parts = [
                    value[..., start : start + size].reshape(value.shape[:3] + (items, -1))
                    for start, size in zip(starts, columns)
                ]
                value = jnp.concatenate(parts, 4).reshape(value.shape)
            values.append(lax.psum_scatter(value, "items", scatter_dimension=3, tiled=True))
        return jnp.stack(values, 1)
    terms = [
        part
        for scatter in scatters
        for parts in zip(scatter.keep, scatter.early, scatter.got)
        for part in parts
    ]
    _, places, rows, wide = terms[0].shape
    held = pl.BlockSpec((1, 2, rows, wide), lambda g: (0, g, 0, 0))
    late = pl.BlockSpec((2, rows, wide), lambda g: (g, 0, 0))
    shape = (places, len(scatters), 2, rows, wide)
    return pl.pallas_call(
        last_kernel,
        grid=(places // 2,),
        in_specs=[held, held, late] * (2 * len(scatters)),
        out_specs=pl.BlockSpec((2,) + shape[1:], lambda g: (g, 0, 0, 0, 0)),
        out_shape=jax.ShapeDtypeStruct(shape, BF16),
        compiler_params=compiler_params(),
        cost_estimate=cost(0, 8 * places * len(scatters) * 2 * rows * wide),
        name="last_sum",
    )(*terms)


def along_z(value):
    heads = lax.axis_size("heads")
    groups = [[core + 2 * z for z in range(heads // 2)] for core in range(2)]
    made = lax.psum_scatter(
        value, "heads", scatter_dimension=0, tiled=False, axis_index_groups=groups
    )
    return [made[i].reshape(-1, made.shape[-1]) for i in range(made.shape[0])]


def unfold_kernel(share_ref, out_ref):
    each = share_ref.shape[0]
    span = out_ref.shape[0]
    for part in range(share_ref.shape[1] // span):
        turned = jnp.transpose(share_ref[:, part * span : (part + 1) * span].astype(F32))
        out_ref[:, part * each : (part + 1) * each] = turned


def unfolded(share, span):
    each, wide = share.shape
    shape = (span, each * wide // span)
    return pl.pallas_call(
        unfold_kernel,
        out_shape=jax.ShapeDtypeStruct(shape, F32),
        cost_estimate=cost(0, 6 * each * wide),
        name="unfolded",
    )(share)


def heads_kernel(grad_ref, weight_ref, *outs):
    step = pl.program_id(0)
    made = dot(grad_ref[...], weight_ref[...], NT).astype(BF16)
    for piece, out in enumerate(outs):

        @pl.when(step == piece)
        def _():
            places, chunks, frames, _ = out.shape
            for place in range(places):
                for chunk in range(chunks):
                    out[place, chunk] = made[
                        chunk * frames : (chunk + 1) * frames, place * LANES : (place + 1) * LANES
                    ]


def heads_gradient(grad, weight, places, chunks):
    rows, model = grad.shape
    wide = places * LANES
    pieces = model // wide
    shape = (places, chunks, rows // chunks, LANES)
    return pl.pallas_call(
        heads_kernel,
        grid=(pieces,),
        in_specs=[whole((rows, model)), pl.BlockSpec((wide, model), lambda s: (s, 0))],
        out_specs=[whole(shape)] * pieces,
        out_shape=[jax.ShapeDtypeStruct(shape, BF16)] * pieces,
        compiler_params=compiler_params(),
        cost_estimate=cost(2 * rows * model * model, 2 * model * model + 4 * rows * model),
        name="heads_gradient",
    )(grad, weight)


def sum_everywhere(value):
    for axis in EVERY:
        bit = 1
        while bit < lax.axis_size(axis):
            value = value + swap(value, (axis, bit))
            bit *= 2
    return value


def edges(block, width):
    ways = lax.axis_size("heads")
    half = ways // 2
    place = lax.axis_index("heads") % half
    ring = [(side * half + i, side * half + (i + 1) % half) for side in range(2) for i in range(half)]
    low = lax.ppermute(block[:, block.shape[1] - width :], "heads", ring)
    high = lax.ppermute(block[:, :width], "heads", [(to, at) for at, to in ring])
    low = jnp.where(place == 0, jnp.roll(low, 1, 0), low)
    high = jnp.where(place == half - 1, jnp.roll(high, -1, 0), high)
    return jnp.concatenate([low, block, high], axis=1)


def body(
    frames, cotangent, bucket_counts, gains, w_ffn1_in, w_ffn1_out, w_qkv, w_out,
    w_point_in, w_depth, w_point_out, w_ffn2_in, w_ffn2_out,
):
    chunks, here, model = frames.shape
    ways = lax.axis_size("heads")
    half = ways // 2
    items = 4 if lax.axis_size("items") == 4 else 1
    span = here * half
    group_len = here * ways
    size = model // HEADS
    reach = (KERNEL - 1) // 2
    rows = chunks * here
    pieces = model // (half * LANES)
    place = lax.axis_index("heads")
    side = place // half
    where = jnp.stack(
        [place % 2, lax.axis_index("items") if items > 1 else 0 * place]
    ).astype(jnp.int32)
    always = place >= 0
    first = jnp.arange(chunks, dtype=jnp.int32)[:, None] * span + place % half * here
    position = first + jnp.arange(here, dtype=jnp.int32)[None]
    cosines, sines = rope_tables(position.reshape(-1), size)
    depth_rows = w_depth.astype(F32)
    gain = [gains[i : i + 1] for i in range(6)]
    counts = lax.dynamic_index_in_dim(bucket_counts[:, 0], side, 0, keepdims=False)
    wide_position = first - reach + jnp.arange(here + 2 * reach, dtype=jnp.int32)[None]
    seg_wide = segment_ids(wide_position, counts[0], counts[1], group_len)
    seg_own = seg_wide[:, reach : reach + here]

    def mine(value):
        return lax.dynamic_index_in_dim(value, side, 0, keepdims=False)

    def theirs(value):
        return lax.dynamic_index_in_dim(value, 1 - side, 0, keepdims=False)

    def begin(chunk, row, before=()):
        return front(
            chunk, row.reshape(1).astype(jnp.int32), gains, w_ffn1_in, w_ffn1_out, w_qkv,
            cosines, sines, half, chunks, size, before,
        )

    before, other_frames = fenced(
        always, (), lambda: (begin(frames, side), across(theirs(frames)))
    )
    stream_one, slope_one, hid_one, ent_one, ent_att, *sent = begin(
        other_frames[None], 1 - side, before
    )
    stream = gathered(mine(frames), other_frames, side)
    qkv = [exchange(sent[0])]
    kept, contexts = [], []
    for number in range(pieces):

        def attend_now():
            return attend_forward(qkv[number], counts, size)

        def beside():
            extra = []
            if number + 1 < pieces:
                extra.append(exchange(sent[number + 1]))
            if number > 0:
                extra.append(exchange(kept[number - 1][0]))
            return extra

        def early():
            if number == 0:
                return [other_core(part) for part in (hid_one, ent_one, ent_att)]
            return [across(theirs(cotangent))] if number == 1 else []

        made, extra, others = fenced(always, (), lambda: (attend_now(), beside(), early()))
        kept.append(made)
        if number == 0:
            hid_one, ent_one, ent_att = zip((hid_one, ent_one, ent_att), others)
        elif number == 1:
            cot_other = others[0]
        if number + 1 < pieces:
            qkv.append(extra.pop(0))
        if number > 0:
            contexts.append(extra.pop(0))
    contexts.append(exchange(kept[-1][0]))
    if pieces == 1:
        cot_other = across(theirs(cotangent))
    fulls = [made[1] for made in kept]
    lses = [made[2] for made in kept]
    contexts = [part.transpose(1, 2, 0, 3).reshape(rows, -1) for part in contexts]
    context = jnp.concatenate(contexts, 1)
    stream_two = stream_one
    for number, part in enumerate(contexts):
        wide = part.shape[1]
        stream_two = stream_two + dot(part, w_out[number * wide : (number + 1) * wide])
    shaped, conv_normed, conv_inverse = layer_norm(stream_two, gain[2])
    conv_entered = shaped.astype(BF16)
    pointwise = dot(conv_entered, w_point_in)
    linear = pointwise[:, :model]
    sigmoid_gate = jax.nn.sigmoid(pointwise[:, model:])
    gated_low = (linear * sigmoid_gate).astype(BF16).reshape(chunks, here, model)
    widened = edges(gated_low, reach)
    depth_out = jnp.zeros((chunks, here, model), F32)
    for offset in range(KERNEL):
        same = (seg_wide[:, offset : offset + here] == seg_own)[:, :, None]
        depth_out = depth_out + depth_rows[offset] * jnp.where(
            same, widened[:, offset : offset + here], 0.0
        )
    depth_out = depth_out.reshape(rows, model)
    depth_shaped, depth_normed, depth_inverse = layer_norm(depth_out, gain[3])
    mixed_low = (depth_shaped * jax.nn.sigmoid(depth_shaped)).astype(BF16)
    stream_three = stream_two + dot(mixed_low, w_point_out)
    layer_out, grad_four, gain_five, slope_two, hid_two, ent_two = ffn_forward(
        stream_three, gain[4], w_ffn2_in, w_ffn2_out, gain[5],
        gathered(mine(cotangent), cot_other, side),
    )
    (grad_three, gain_four, half_two, grad_pre_two), hid_other, ent_other = fenced(
        always,
        (),
        lambda: (
            ffn_backward(grad_four, stream_three, slope_two, gain[4], w_ffn2_in, w_ffn2_out),
            other_core(hid_two),
            other_core(ent_two),
        ),
    )
    half_other, grad_pre_other = other_core(half_two), other_core(grad_pre_two)
    grad_mix = grad_three.astype(BF16)
    grad_norm_in = dot(grad_mix, w_point_out, NT) * silu_slope(depth_shaped)
    grad_depth, gain_three = norm_back(grad_norm_in, depth_normed, depth_inverse, gain[3])
    grad_depth_low = grad_depth.astype(BF16).reshape(chunks, here, model)
    grad_widened = edges(grad_depth_low, reach)
    grad_gated = jnp.zeros((chunks, here, model), F32)
    for offset in range(KERNEL):
        mirror = 2 * reach - offset
        same_back = (seg_wide[:, mirror : mirror + here] == seg_own)[:, :, None]
        grad_gated = grad_gated + depth_rows[offset] * jnp.where(
            same_back, grad_widened[:, mirror : mirror + here], 0.0
        )
    grad_gated = grad_gated.reshape(rows, model)
    grad_a = (grad_gated * sigmoid_gate).astype(BF16)
    grad_b = (grad_gated * linear * sigmoid_gate * (1.0 - sigmoid_gate)).astype(BF16)
    through, gain_two = norm_back(
        dot(grad_a, w_point_in[:, :model], NT) + dot(grad_b, w_point_in[:, model:], NT),
        conv_normed, conv_inverse, gain[2],
    )
    grad_two = grad_three + through
    grad_attn_out = grad_two.astype(BF16)
    grad_heads = list(heads_gradient(grad_attn_out, w_out, half, chunks))
    lefts = (mixed_low, conv_entered, context)

    def ffn_grads():
        return (
            [other_core(part) for part in lefts + (grad_a, grad_b)],
            exchange(grad_heads[0]),
            out_grad((half_two, half_other), (hid_two, hid_other), ways, where, items),
            column_grads(
                [(ent_two, ent_other)], [(grad_pre_two, grad_pre_other)], ways, where, items
            ),
        )

    others, grad_heads[0], shares_out, shares_in = fenced(always, (), ffn_grads)
    two_out, two_in = Scatter(*shares_out), Scatter(*shares_in)
    out_own, out_theirs = parted(layer_out, side)
    grads, backs = [], []
    for number in range(pieces):
        last = number == pieces - 1

        def beside():
            extra = []
            if not last:
                extra.append(exchange(grad_heads[number + 1]))
            if number > 0:
                extra.append(exchange(grads[number - 1]))
            if number == 0:
                extra.append(across(out_theirs))
                extra += [other_core(grad_mix), other_core(grad_attn_out)]
            return extra

        def attend_now():
            return attend_backward(
                qkv[number], counts, size, fulls[number], lses[number], grad_heads[number]
            )

        moving = (two_out,) if number == 0 else (two_out, two_in) if number == 1 else ()
        made, extra = fenced(always, moving, lambda: (attend_now(), beside()))
        grads.append(made)
        if not last:
            grad_heads[number + 1] = extra.pop(0)
        if number > 0:
            backs.append(extra.pop(0))
        if number == 0:
            out_other, *late = extra
            two_out.second(second_sums(two_out)[0])
    two_in.second(second_sums(two_in)[0])

    def middle_part():
        back = exchange(grads[-1])
        scatter = copy.copy(two_in)
        moved(scatter)
        shares = column_grads(
            list(zip(lefts, others[:3])),
            [
                (grad_mix, late[0]),
                ((grad_a, others[3]), (grad_b, others[4])),
                (grad_attn_out, late[1]),
            ],
            ways, where, items,
        )
        return (back, shares, last_sum(two_out, scatter))

    back, shares, two_sum = fenced(always, (), middle_part)
    backs.append(back)
    middle = Scatter(*shares)

    def attention_part():
        two_grads = along_z(two_sum)
        scatter = copy.copy(middle)

        grad_proj, grad_one, half_one, gain_one = fenced(
            always,
            (scatter,),
            lambda: projection_backward(
                backs, cosines, sines, size, grad_two, stream_one, gain[1], w_qkv
            ),
        )
        first = scatter.got
        scatter.second(second_sums(scatter)[0])

        def qkv_part():
            half_other = other_core(half_one)
            right = (grad_proj, other_core(grad_proj))
            return (half_other, column_grads([ent_att], [right], ways, where, items))

        half_other, shares = fenced(always, (scatter,), qkv_part)
        attn = Scatter(*shares)

        def hidden_part():
            half_own, grad_pre = hidden_gradient(grad_one, slope_one, w_ffn1_out)
            shares = out_grad((half_own, half_other), hid_one, ways, where, items)
            return (grad_pre, shares)

        grad_pre, shares_out = fenced(always, (attn,), hidden_part)
        return (
            two_grads, first, scatter.got, (grad_one, gain_one), shares[:2], attn.got,
            grad_pre, shares_out,
        )

    two_grads, first, got, (grad_one, gain_one), shares, attn_got, grad_pre, shares_out = fenced(
        always, (), attention_part
    )
    middle.take(first)
    middle.take(got)
    attn = Scatter(*shares)
    attn.take(attn_got)
    attn.second(second_sums(attn)[0])
    one_out = Scatter(*shares_out)
    middle_columns = [w.shape[1] for w in (w_point_out, w_point_in, w_out)]
    middle_grad, shares, (grad_zero, _, gain_zero) = fenced(
        always,
        (one_out, attn),
        lambda: (
            along_z(last_sum(middle, columns=middle_columns)),
            column_grads([ent_one], [(grad_pre, other_core(grad_pre))], ways, where, items),
            stream_gradient(grad_one, stream, grad_pre, gain[0], w_ffn1_in, BF16),
        ),
    )
    one_in = Scatter(*shares)
    one_out.second(second_sums(one_out)[0])
    grad_own, grad_theirs = parted(grad_zero, side)
    attn_grad, grad_other = fenced(
        always, (one_in, one_out), lambda: (along_z(last_sum(attn)), across(grad_theirs))
    )
    one_in.second(second_sums(one_in)[0])

    hidden = w_ffn1_in.shape[1]

    def tap_sums_here():
        rows_of = []
        for offset in range(KERNEL):
            same = (seg_wide[:, offset : offset + here] == seg_own)[:, :, None]
            product = grad_depth_low.astype(F32) * widened[:, offset : offset + here]
            rows_of.append(jnp.sum(jnp.where(same, product, 0.0), (0, 1))[None])
        return rows_of

    def last_part():
        out_grads = along_z(last_sum(one_out))
        scatter = copy.copy(one_in)
        moved(scatter)
        small = sum_everywhere(
            jnp.concatenate(
                [gain_zero, gain_one, gain_two, gain_three, gain_four, gain_five]
                + tap_sums_here(),
                0,
            )
        )
        middle_parts = []
        start = 0
        for columns in middle_columns:
            each = columns // lax.axis_size("items")
            middle_parts.append(middle_grad[0][:, start : start + each].astype(F32))
            start += each
        ready = (
            gathered(out_own[None], out_other[None], side),
            gathered(grad_own[None], grad_other[None], side),
            attn_grad[0].astype(F32),
            middle_parts,
            two_grads[1].astype(F32),
            unfolded(two_grads[0], hidden // ways),
            unfolded(out_grads[0], hidden // ways),
        )
        return (along_z(last_sum(scatter)), small[:6], small[6:], ready)

    one_in_grad, gain_sums, tap_sums, ready = fenced(always, (), last_part)
    out, grad_in, attn_full, middle_parts, two_in_full, two_out_full, one_out_full = ready
    return (
        out,
        grad_in,
        gain_sums,
        one_in_grad[0].astype(F32),
        one_out_full,
        attn_full,
        middle_parts[2],
        middle_parts[1],
        tap_sums,
        middle_parts[0],
        two_in_full,
        two_out_full,
    )


def solution(mesh):
    split = P(None, EVERY, None)
    shares = P("heads", "items")
    in_specs = (split, split, P(None, "items", None)) + (P(),) * 10
    out_specs = (split, split, P(), shares, shares, shares, shares, shares, P()) + (shares,) * 3
    return jax.shard_map(body, mesh=mesh, in_specs=in_specs, out_specs=out_specs, check_vma=False)
```

```python
import copy
import functools

import jax
import jax.numpy as jnp
from jax import lax
from jax.experimental import pallas as pl
from jax.experimental.pallas import tpu as pltpu
from jax.sharding import PartitionSpec as P

HEADS = 16
KERNEL = 5
LONG = 1500
SHORT = 500
EPS = 1e-05
ROPE_BASE = 10000.0
BLOCK = 512
INNER_FWD = 1024
INNER_BWD = 512
TURNED = 512
LANES = 128
BIG = 1e30
VMEM_LIMIT = 56 << 20
F32 = jnp.float32
BF16 = jnp.bfloat16
NN = (((1,), (0,)), ((), ()))
NT = (((1,), (1,)), ((), ()))
EVERY = ("items", "heads")
FIRST = [("items", 1), ("items", 2)]


def dot(left, right, dims=NN):
    return lax.dot_general(left, right, dims, preferred_element_type=F32)


def silu_slope(field):
    gate_sig = jax.nn.sigmoid(field)
    return gate_sig * (1.0 + field * (1.0 - gate_sig))


def layer_norm(field, gain_row):
    centred = field - jnp.mean(field, -1, keepdims=True)
    inverse = lax.rsqrt(jnp.mean(centred * centred, -1, keepdims=True) + EPS)
    normed = centred * inverse
    return (normed * gain_row, normed, inverse)


def norm_back(upstream, normed, inverse, gain_row):
    scaled = upstream * gain_row
    through = inverse * (
        scaled
        - jnp.mean(scaled, -1, keepdims=True)
        - normed * jnp.mean(scaled * normed, -1, keepdims=True)
    )
    return (through, jnp.sum(upstream * normed, 0, keepdims=True))


def segment_ids(position, long_count, short_count, group_len):
    long_end = long_count * LONG
    short_end = long_end + short_count * SHORT
    segments = jnp.where(
        position < long_end, position // LONG, long_count + (position - long_end) // SHORT
    )
    segments = jnp.where(position < short_end, segments, long_count + short_count)
    return jnp.where((position < 0) | (position >= group_len), -1, segments)


def compiler_params():
    return pltpu.CompilerParams(vmem_limit_bytes=VMEM_LIMIT)


def whole(shape):
    return pl.BlockSpec(shape, lambda *_: (0,) * len(shape))


def cost(flops, bytes_accessed, transcendentals=0):
    return pl.CostEstimate(
        flops=flops, bytes_accessed=bytes_accessed, transcendentals=transcendentals
    )


def segment_bounds(counts, place, group):
    longs, shorts = counts
    long_end = longs * LONG
    short_end = long_end + shorts * SHORT
    start = jnp.where(place < longs, place * LONG, long_end + (place - longs) * SHORT)
    size = jnp.where(place < longs, LONG, SHORT)
    last = place == longs + shorts
    return (jnp.where(last, short_end, start), jnp.where(last, group, start + size), place <= longs + shorts)


def member_lanes(counts, first, rows, group, shift=0):
    shape = (rows, LANES)
    place = lax.broadcasted_iota(jnp.int32, (8, LANES), 1) - shift
    start, end, there = segment_bounds(counts, place, group)
    start = jnp.where(there & (place >= 0), start, group)
    start, end = start[:1], end[:1]
    frame = first + lax.broadcasted_iota(jnp.int32, shape, 0)
    return (frame >= start) & (frame < end)


def block_range(counts, step, group, inner):
    longs, shorts = counts
    long_end = longs * LONG
    short_end = long_end + shorts * SHORT

    def number(frame):
        place = jnp.where(frame < long_end, frame // LONG, longs + (frame - long_end) // SHORT)
        return jnp.where(frame < short_end, place, longs + shorts)

    first = segment_bounds(counts, number(step * BLOCK), group)[0]
    last = segment_bounds(counts, number(step * BLOCK + BLOCK - 1), group)[1]
    return (first // inner, (last + inner - 1) // inner)


def head_lanes(shape, head, size):
    lane = lax.broadcasted_iota(jnp.int32, shape, 1)
    return (lane >= head * size) & (lane < (head + 1) * size)


def split_three(v):
    hi = v.astype(BF16).astype(F32)
    rest = v - hi
    mid = rest.astype(BF16).astype(F32)
    return (hi, mid, rest - mid)


def spread_columns(columns, shape):
    lane = lax.broadcasted_iota(jnp.int32, shape, 1)
    out = jnp.zeros(shape, F32)
    for place, column in enumerate(columns):
        out = jnp.where(lane == place, column, out)
    return out


def chunk_rows(ref, lead, step):
    places, chunks, frames = ref.shape[0], ref.shape[-3], ref.shape[-2]
    per = BLOCK // frames
    steps = places // per
    at = (pl.ds(step % steps * per, per),) + lead + (step // steps,)
    return ref[at].reshape(BLOCK, LANES)


def attn_fwd_kernel(
    heads, size, group, counts_ref, qkv_ref, out_ref, full_ref, lse_ref, kcat, v_all, s_scr
):
    step = pl.program_id(0)
    counts = (counts_ref[0], counts_ref[1])

    @pl.when(step == 0)
    def _():
        chunks = qkv_ref.shape[2]
        span = group // chunks
        for chunk in range(chunks):
            rows = slice(chunk * span, (chunk + 1) * span)
            kcat[rows, :LANES] = qkv_ref[:, 1, chunk].reshape(span, LANES)
            v_all[rows, :] = qkv_ref[:, 2, chunk].reshape(span, LANES)
        kcat[:, LANES:] = jnp.where(member_lanes(counts, 0, group, group), 0.0, -BIG).astype(BF16)

    q = chunk_rows(qkv_ref, (0,), step).astype(F32) * (size ** -0.5)
    member = jnp.where(member_lanes(counts, step * BLOCK, BLOCK, group), 1.0, 0.0).astype(BF16)
    queries = []
    for head in range(heads):
        mine = jnp.where(head_lanes(q.shape, head, size), q, 0.0).astype(BF16)
        queries.append(jnp.concatenate([mine, member], 1))
    low, high = block_range(counts, step, group, INNER_FWD)

    def scores(j, tops):
        keys = kcat[pl.ds(pl.multiple_of(j * INNER_FWD, INNER_FWD), INNER_FWD), :]
        new = []
        for head in range(heads):
            s = dot(queries[head], keys, NT)
            s_scr[head, j] = s
            top = tops[head]
            for part in range(INNER_FWD // LANES):
                top = jnp.maximum(top, s[:, part * LANES : (part + 1) * LANES])
            new.append(top)
        return tuple(new)

    start = tuple(jnp.full((BLOCK, LANES), -BIG, F32) for _ in range(heads))
    tops = lax.fori_loop(low, high, scores, start)
    tops = [jnp.max(t, 1, keepdims=True) for t in tops]
    tops = [jnp.broadcast_to(t, (BLOCK, LANES)) for t in tops]

    def weigh(j, carried):
        sums, accs = carried
        values = v_all[pl.ds(pl.multiple_of(j * INNER_FWD, INNER_FWD), INNER_FWD), :]
        new_sums, new_accs = [], []
        for head in range(heads):
            total = sums[head]
            parts = []
            for part in range(INNER_FWD // LANES):
                p = jnp.exp(s_scr[head, j, :, part * LANES : (part + 1) * LANES] - tops[head])
                total = total + p
                parts.append(p.astype(BF16))
            new_sums.append(total)
            new_accs.append(accs[head] + dot(jnp.concatenate(parts, 1), values))
        return (tuple(new_sums), tuple(new_accs))

    zeros = tuple(jnp.zeros((BLOCK, LANES), F32) for _ in range(heads))
    sums, accs = lax.fori_loop(low, high, weigh, (zeros, zeros))
    result = None
    for head in range(heads):
        total = jnp.sum(sums[head], 1, keepdims=True)
        mine = accs[head] / total
        if result is None:
            result = mine
        else:
            result = jnp.where(head_lanes(mine.shape, head, size), mine, result)
        lse_ref[head] = tops[head] + jnp.log(jnp.broadcast_to(total, (BLOCK, LANES)))
    full_ref[...] = result
    out_ref[...] = result.astype(BF16).reshape(out_ref.shape)


def attend_forward(qkv, counts, size):
    places, _, chunks, frames, _ = qkv.shape
    group = places * chunks * frames
    heads = LANES // size
    per = BLOCK // frames
    each = places // per
    return pl.pallas_call(
        functools.partial(attn_fwd_kernel, heads, size, group),
        grid=(group // BLOCK,),
        in_specs=[pl.BlockSpec(memory_space=pltpu.SMEM), whole(qkv.shape)],
        out_specs=[
            pl.BlockSpec((per, 1, frames, LANES), lambda i: (i % each, i // each, 0, 0)),
            pl.BlockSpec((BLOCK, LANES), lambda i: (i, 0)),
            pl.BlockSpec((heads, BLOCK, LANES), lambda i: (0, i, 0)),
        ],
        out_shape=[
            jax.ShapeDtypeStruct((places, chunks, frames, LANES), BF16),
            jax.ShapeDtypeStruct((group, LANES), F32),
            jax.ShapeDtypeStruct((heads, group, LANES), F32),
        ],
        scratch_shapes=[
            pltpu.VMEM((group, 2 * LANES), BF16),
            pltpu.VMEM((group, LANES), BF16),
            pltpu.VMEM((heads, group // INNER_FWD, BLOCK, INNER_FWD), F32),
        ],
        compiler_params=compiler_params(),
        cost_estimate=cost(16 * group * group * LANES, 6 << 20, heads * group * group),
        name="attend_forward",
    )(counts, qkv)


def attn_bwd_kernel(
    heads, size, group, counts_ref, qkv_ref, full_ref, lse_ref, grad_ref, out_ref,
    qcat, gcat, k_turned, dq_turned,
):
    step = pl.program_id(0)
    counts = (counts_ref[0], counts_ref[1])
    blocks = group // BLOCK
    places, _, _, frames, _ = qkv_ref.shape
    per = BLOCK // frames
    each = places // per

    def put(part, j, value):
        out_ref[pl.ds(j % each * per, per), part, j // each] = value.astype(BF16).reshape(
            per, frames, LANES
        )

    @pl.when(step == 0)
    def _():
        dq_turned[...] = jnp.zeros_like(dq_turned)

        def prepare(j, _):
            rows = pl.ds(pl.multiple_of(j * BLOCK, BLOCK), BLOCK)
            lane = lax.broadcasted_iota(jnp.int32, (BLOCK, LANES), 1)
            q = chunk_rows(qkv_ref, (0,), j).astype(F32) * (size ** -0.5)
            g = chunk_rows(grad_ref, (), j).astype(F32)
            product = g * full_ref[rows, :]
            member = jnp.where(member_lanes(counts, j * BLOCK, BLOCK, group, 3), 1.0, 0.0)
            for head in range(heads):
                own = head_lanes((BLOCK, LANES), head, size)
                lse = lse_ref[head, rows, :]
                spread = spread_columns(split_three(lse), (BLOCK, LANES))
                delta = jnp.sum(jnp.where(own, product, 0.0), 1, keepdims=True)
                delta = jnp.broadcast_to(delta, (BLOCK, LANES))
                qcat[head, rows, :LANES] = jnp.where(own, q, 0.0).astype(BF16)
                qcat[head, rows, LANES:] = jnp.where(lane < 3, -spread, member).astype(BF16)
                gcat[head, rows, :LANES] = jnp.where(own, g, 0.0).astype(BF16)
                spread = spread_columns(split_three(delta), (BLOCK, LANES))
                gcat[head, rows, LANES:] = (-spread).astype(BF16)
            k = chunk_rows(qkv_ref, (1,), j).astype(F32)
            k_turned[j] = jnp.transpose(k).astype(BF16)
            return 0

        lax.fori_loop(0, blocks, prepare, 0)

    lane = lax.broadcasted_iota(jnp.int32, (BLOCK, LANES), 1)
    member = member_lanes(counts, step * BLOCK, BLOCK, group, 3)
    tail = jnp.where(lane < 3, 1.0, jnp.where(member, 0.0, -BIG)).astype(BF16)
    keys = jnp.concatenate([chunk_rows(qkv_ref, (1,), step), tail], 1)
    ones = jnp.where(lane < 3, 1.0, 0.0).astype(BF16)
    values = jnp.concatenate([chunk_rows(qkv_ref, (2,), step), ones], 1)

    def one(j, carried):
        dk, dv = carried
        cols = pl.ds(pl.multiple_of(j * INNER_BWD, INNER_BWD), INNER_BWD)
        for head in range(heads):
            qc = qcat[head, cols, :]
            gc = gcat[head, cols, :]
            p = jnp.exp(dot(keys, qc, NT))
            ds = (p * dot(values, gc, NT)).astype(BF16)
            dv = dv + dot(p.astype(BF16), gc[:, :LANES])
            dk = dk + dot(ds, qc[:, :LANES])
            mine = slice(head * size, (head + 1) * size)
            dq_turned[j, mine, :] += dot(k_turned[step, mine, :], ds)
        return (dk, dv)

    zero = jnp.zeros((BLOCK, LANES), F32)
    low, high = block_range(counts, step, group, INNER_BWD)
    dk, dv = lax.fori_loop(low, high, one, (zero, zero))
    put(1, step, dk)
    put(2, step, dv)

    @pl.when(step == blocks - 1)
    def _():
        def finish(j, _):
            put(0, j, jnp.transpose(dq_turned[j]) * (size ** -0.5))
            return 0

        lax.fori_loop(0, blocks, finish, 0)


def attend_backward(qkv, counts, size, full, lse, grad):
    places, _, chunks, frames, _ = qkv.shape
    group = places * chunks * frames
    heads = LANES // size
    steps = group // BLOCK
    return pl.pallas_call(
        functools.partial(attn_bwd_kernel, heads, size, group),
        grid=(steps,),
        in_specs=[
            pl.BlockSpec(memory_space=pltpu.SMEM),
            whole(qkv.shape),
            whole(full.shape),
            whole(lse.shape),
            whole(grad.shape),
        ],
        out_specs=whole(qkv.shape),
        out_shape=jax.ShapeDtypeStruct(qkv.shape, BF16),
        scratch_shapes=[
            pltpu.VMEM((heads, group, 2 * LANES), BF16),
            pltpu.VMEM((heads, group, 2 * LANES), BF16),
            pltpu.VMEM((steps, LANES, BLOCK), BF16),
            pltpu.VMEM((group // INNER_BWD, LANES, INNER_BWD), F32),
        ],
        compiler_params=compiler_params(),
        cost_estimate=cost(32 * group * group * LANES, 9 << 20, heads * group * group),
        name="attend_backward",
    )(counts, qkv, full, lse, grad)


def half_gate(field):
    return 0.5 * jnp.tanh(0.5 * field) + 0.5


def hidden_units(pre):
    gate = half_gate(pre)
    hidden = pre * gate
    return (hidden.astype(BF16), (gate + hidden * (1.0 - gate)).astype(BF16))


def ffn_fwd_kernel(
    x_ref, gain_ref, last_gain_ref, up_ref, win_ref, wout_ref,
    out_ref, down_ref, gain_grad_ref, slope_ref, hid_ref, entered_ref, total,
):
    step = pl.program_id(0)

    @pl.when(step == 0)
    def _():
        entered_ref[...] = layer_norm(x_ref[...], gain_ref[...])[0].astype(BF16)
        total[...] = jnp.zeros_like(total)

    hidden, slope = hidden_units(dot(entered_ref[...], win_ref[...]))
    slope_ref[...] = slope
    hid_ref[...] = hidden
    total[...] += dot(hidden, wout_ref[...])

    @pl.when(step == pl.num_programs(0) - 1)
    def _():
        gain = last_gain_ref[...]
        shaped, normed, inverse = layer_norm(x_ref[...] + 0.5 * total[...], gain)
        out_ref[...] = shaped.astype(BF16)
        through, grad_gain = norm_back(up_ref[...].astype(F32), normed, inverse, gain)
        down_ref[...] = through
        gain_grad_ref[...] = grad_gain


def ffn_forward(stream, gain_row, weight_in, weight_out, last_gain, upstream):
    rows, model = stream.shape
    units = weight_in.shape[1]
    wide = min(units, 1024)
    return pl.pallas_call(
        ffn_fwd_kernel,
        grid=(units // wide,),
        in_specs=[
            whole((rows, model)),
            whole((1, model)),
            whole((1, model)),
            whole((rows, model)),
            pl.BlockSpec((model, wide), lambda s: (0, s)),
            pl.BlockSpec((wide, model), lambda s: (s, 0)),
        ],
        out_specs=[whole((rows, model)), whole((rows, model)), whole((1, model))]
        + [pl.BlockSpec((rows, wide), lambda s: (0, s))] * 2
        + [whole((rows, model))],
        out_shape=[
            jax.ShapeDtypeStruct((rows, model), BF16),
            jax.ShapeDtypeStruct((rows, model), F32),
            jax.ShapeDtypeStruct((1, model), F32),
            jax.ShapeDtypeStruct((rows, units), BF16),
            jax.ShapeDtypeStruct((rows, units), BF16),
            jax.ShapeDtypeStruct((rows, model), BF16),
        ],
        scratch_shapes=[pltpu.VMEM((rows, model), F32)],
        compiler_params=compiler_params(),
        cost_estimate=cost(4 * rows * model * units, 4 * model * units + 4 * rows * units),
        name="ffn_forward",
    )(stream, gain_row, last_gain, upstream, weight_in, weight_out)


def ffn_bwd_kernel(
    x_ref, gain_ref, up_ref, slope_ref, win_ref, wout_ref,
    down_ref, gain_grad_ref, half_ref, grad_ref, total,
):
    step = pl.program_id(0)

    @pl.when(step == 0)
    def _():
        half_ref[...] = (0.5 * up_ref[...]).astype(BF16)
        total[...] = jnp.zeros_like(total)

    grad = (dot(half_ref[...], wout_ref[...], NT) * slope_ref[...].astype(F32)).astype(BF16)
    grad_ref[...] = grad
    total[...] += dot(grad, win_ref[...], NT)

    @pl.when(step == pl.num_programs(0) - 1)
    def _():
        gain = gain_ref[...]
        normed, inverse = layer_norm(x_ref[...].astype(F32), gain)[1:]
        through, grad_gain = norm_back(total[...], normed, inverse, gain)
        down_ref[...] = up_ref[...] + through
        gain_grad_ref[...] = grad_gain


def ffn_backward(upstream, stream, slope, gain_row, weight_in, weight_out):
    rows, model = stream.shape
    units = weight_in.shape[1]
    wide = min(units, 1024)
    return pl.pallas_call(
        ffn_bwd_kernel,
        grid=(units // wide,),
        in_specs=[
            whole((rows, model)),
            whole((1, model)),
            whole((rows, model)),
            pl.BlockSpec((rows, wide), lambda s: (0, s)),
            pl.BlockSpec((model, wide), lambda s: (0, s)),
            pl.BlockSpec((wide, model), lambda s: (s, 0)),
        ],
        out_specs=[
            whole((rows, model)),
            whole((1, model)),
            whole((rows, model)),
            pl.BlockSpec((rows, wide), lambda s: (0, s)),
        ],
        out_shape=[
            jax.ShapeDtypeStruct((rows, model), F32),
            jax.ShapeDtypeStruct((1, model), F32),
            jax.ShapeDtypeStruct((rows, model), BF16),
            jax.ShapeDtypeStruct((rows, units), BF16),
        ],
        scratch_shapes=[pltpu.VMEM((rows, model), F32)],
        compiler_params=compiler_params(),
        cost_estimate=cost(4 * rows * model * units, 4 * model * units + 6 * rows * units),
        name="ffn_backward",
    )(stream, gain_row, upstream, slope, weight_in, weight_out)


def hidden_kernel(up_ref, slope_ref, wout_ref, half_ref, grad_ref):
    @pl.when(pl.program_id(0) == 0)
    def _():
        half_ref[...] = (0.5 * up_ref[...]).astype(BF16)

    grad = dot(half_ref[...], wout_ref[...], NT) * slope_ref[...].astype(F32)
    grad_ref[...] = grad.astype(BF16)


def hidden_gradient(upstream, slope, weight_out):
    rows, model = upstream.shape
    units = weight_out.shape[0]
    wide = min(units, 1024)
    return pl.pallas_call(
        hidden_kernel,
        grid=(units // wide,),
        in_specs=[
            whole((rows, model)),
            pl.BlockSpec((rows, wide), lambda s: (0, s)),
            pl.BlockSpec((wide, model), lambda s: (s, 0)),
        ],
        out_specs=[whole((rows, model)), pl.BlockSpec((rows, wide), lambda s: (0, s))],
        out_shape=[
            jax.ShapeDtypeStruct((rows, model), BF16),
            jax.ShapeDtypeStruct((rows, units), BF16),
        ],
        compiler_params=compiler_params(),
        cost_estimate=cost(2 * rows * model * units, 2 * model * units + 6 * rows * units),
        name="hidden_gradient",
    )(upstream, slope, weight_out)


def down_kernel(
    x_ref, gain_ref, up_ref, grad_ref, weight_ref, down_ref, half_ref, gain_grad_ref, total
):
    step = pl.program_id(0)

    @pl.when(step == 0)
    def _():
        total[...] = jnp.zeros_like(total)

    total[...] += dot(grad_ref[...], weight_ref[...], NT)

    @pl.when(step == pl.num_programs(0) - 1)
    def _():
        gain = gain_ref[...]
        normed, inverse = layer_norm(x_ref[...].astype(F32), gain)[1:]
        through, grad_gain = norm_back(total[...], normed, inverse, gain)
        down = up_ref[...] + through
        down_ref[...] = down.astype(down_ref.dtype)
        half_ref[...] = (0.5 * down).astype(BF16)
        gain_grad_ref[...] = grad_gain


def stream_gradient(upstream, stream, grad, gain_row, weight, down_type):
    rows, model = stream.shape
    units = weight.shape[1]
    wide = min(units, 1024)
    return pl.pallas_call(
        down_kernel,
        grid=(units // wide,),
        in_specs=[
            whole((rows, model)),
            whole((1, model)),
            whole((rows, model)),
            pl.BlockSpec((rows, wide), lambda s: (0, s)),
            pl.BlockSpec((model, wide), lambda s: (0, s)),
        ],
        out_specs=[whole((rows, model)), whole((rows, model)), whole((1, model))],
        out_shape=[
            jax.ShapeDtypeStruct((rows, model), down_type),
            jax.ShapeDtypeStruct((rows, model), BF16),
            jax.ShapeDtypeStruct((1, model), F32),
        ],
        scratch_shapes=[pltpu.VMEM((rows, model), F32)],
        compiler_params=compiler_params(),
        cost_estimate=cost(2 * rows * model * units, 2 * model * units + 2 * rows * units),
        name="stream_gradient",
    )(stream, gain_row, upstream, grad, weight)


def turn(field, cosines, sines, size):
    repeats = field.shape[1] // cosines.shape[1]
    cosines = jnp.concatenate([cosines] * repeats, 1)
    sines = jnp.concatenate([sines] * repeats, 1)
    lane = lax.broadcasted_iota(jnp.int32, field.shape, 1)
    half = size // 2
    width = field.shape[1]
    swapped = jnp.where(
        lane % size < half,
        pltpu.roll(field, width - half, 1),
        pltpu.roll(field, half, 1),
    )
    return field * cosines + swapped * sines


def rope_tables(position, size):
    half = size // 2
    lane = jnp.arange(LANES, dtype=jnp.int32)
    freqs = jnp.exp(
        -jnp.log(jnp.float32(ROPE_BASE)) * (lane % half).astype(jnp.float32) / half
    )
    angles = position.astype(jnp.float32)[:, None] * freqs[None, :]
    signs = jnp.where(lane % size < half, -1.0, 1.0)
    return (jnp.cos(angles), jnp.sin(angles) * signs[None, :])


def front_kernel(
    size, ffn_steps, pieces, row_ref, x_ref, gain_ref, win_ref, wout_ref,
    wq_ref, wk_ref, wv_ref, cos_ref, sin_ref, *refs,
):
    refs = refs[-(6 + pieces) :]
    out_ref, slope_ref, hid_ref, entered_ref, next_ref = refs[:5]
    outs, total = refs[5:-1], refs[-1]
    step = pl.program_id(0)

    @pl.when(step == 0)
    def _():
        gain = gain_ref[0:1, :]
        entered_ref[...] = layer_norm(x_ref[0].astype(F32), gain)[0].astype(BF16)
        total[...] = jnp.zeros_like(total)

    @pl.when(step < ffn_steps)
    def _():
        hidden, slope = hidden_units(dot(entered_ref[...], win_ref[...]))
        slope_ref[...] = slope
        hid_ref[...] = hidden
        total[...] += dot(hidden, wout_ref[...])

    @pl.when(step == ffn_steps)
    def _():
        out = x_ref[0].astype(F32) + 0.5 * total[...]
        out_ref[...] = out
        next_ref[...] = layer_norm(out, gain_ref[1:2, :])[0].astype(BF16)

    each = (pl.num_programs(0) - ffn_steps) // pieces
    for piece, out in enumerate(outs):

        @pl.when((step >= ffn_steps) & ((step - ffn_steps) // each == piece))
        def _():
            for place, weight in enumerate((wq_ref, wk_ref, wv_ref)):
                made = dot(next_ref[...], weight[...])
                if place < 2:
                    made = turn(made, cos_ref[...], sin_ref[...], size)
                made = made.astype(BF16)
                for target in range(out.shape[0]):
                    out[target, place, 0] = made[:, target * LANES : (target + 1) * LANES]


def front(
    frames, row, gains, weight_in, weight_out, weight, cosines, sines,
    places, chunks, size, before=(),
):
    given, rows, model = frames.shape
    units = weight_in.shape[1]
    wide = min(units, 1024)
    ffn_steps = units // wide
    turned_wide = TURNED
    turns = model // turned_wide
    pieces = model // (places * LANES)
    each = turns // pieces
    piece = jax.ShapeDtypeStruct((places, 3, chunks, rows, LANES), BF16)

    def ffn_at(s, row):
        return jnp.minimum(s, ffn_steps - 1)

    def turn_at(s):
        return jnp.maximum(s - ffn_steps, 0)

    def piece_at(number):
        return lambda s, row: (
            jnp.clip(s - ffn_steps - number * each, 0, each - 1), 0, row[0], 0, 0
        )

    row_block = pl.BlockSpec((rows, model), lambda s, row: (row[0], 0))
    unit_block = pl.BlockSpec((rows, wide), lambda s, row: (row[0], ffn_at(s, row)))
    angle_block = pl.BlockSpec((rows, LANES), lambda s, row: (row[0], 0))
    out_shape = [
        jax.ShapeDtypeStruct((chunks * rows, model), F32),
        jax.ShapeDtypeStruct((chunks * rows, units), BF16),
        jax.ShapeDtypeStruct((chunks * rows, units), BF16),
        jax.ShapeDtypeStruct((chunks * rows, model), BF16),
        jax.ShapeDtypeStruct((chunks * rows, model), BF16),
    ] + [piece] * pieces
    in_specs = [
        pl.BlockSpec((1, rows, model), lambda s, row: (row[0] if given > 1 else 0, 0, 0)),
        whole(gains.shape),
        pl.BlockSpec((model, wide), lambda s, row: (0, ffn_at(s, row))),
        pl.BlockSpec((wide, model), lambda s, row: (ffn_at(s, row), 0)),
        pl.BlockSpec((model, turned_wide), lambda s, row: (0, turn_at(s))),
        pl.BlockSpec((model, turned_wide), lambda s, row: (0, turns + turn_at(s))),
        pl.BlockSpec((model, turned_wide), lambda s, row: (0, 2 * turns + turn_at(s))),
        angle_block,
        angle_block,
    ]
    grid_spec = pltpu.PrefetchScalarGridSpec(
        num_scalar_prefetch=1,
        grid=(ffn_steps + turns,),
        in_specs=in_specs + [pl.BlockSpec(memory_space=pl.ANY)] * len(before),
        out_specs=[row_block, unit_block, unit_block, row_block, row_block]
        + [
            pl.BlockSpec((turned_wide // LANES, 3, 1, rows, LANES), piece_at(number))
            for number in range(pieces)
        ],
        scratch_shapes=[pltpu.VMEM((rows, model), F32)],
    )
    return pl.pallas_call(
        functools.partial(front_kernel, size, ffn_steps, pieces),
        grid_spec=grid_spec,
        out_shape=out_shape,
        input_output_aliases={1 + len(in_specs) + i: i for i in range(len(before))},
        compiler_params=compiler_params(),
        cost_estimate=cost(
            4 * rows * model * units + 6 * rows * model * model,
            4 * model * units + 6 * model * model + 4 * rows * units + 16 * rows * model,
        ),
        name="front",
    )(
        row, frames, gains, weight_in, weight_out, weight, weight, weight,
        cosines, sines, *before,
    )


def projection_kernel(
    size, pieces, cos_ref, sin_ref, x_ref, gain_ref, up_ref, weight_ref, *refs
):
    backs, refs = refs[:pieces], refs[pieces:]
    grad_ref, down_ref, half_ref, gain_grad_ref, total = refs
    step = pl.program_id(0)

    @pl.when(step == 0)
    def _():
        total[...] = jnp.zeros_like(total)

    rotated = step < 2
    cosines = jnp.where(rotated, cos_ref[...], 1.0)
    sines = jnp.where(rotated, -sin_ref[...], 0.0)
    places, _, chunks, frames, _ = backs[0].shape
    per = TURNED // LANES
    for piece, back in enumerate(backs):
        for first in range(0, places, per):
            for chunk in range(chunks):
                rows = slice(chunk * frames, (chunk + 1) * frames)
                field = jnp.concatenate([back[first + i, 0, chunk] for i in range(per)], 1)
                made = turn(field.astype(F32), cosines[rows], sines[rows], size).astype(BF16)
                start = (piece * places + first) * LANES
                grad_ref[rows, start : start + TURNED] = made
    total[...] += dot(grad_ref[...], weight_ref[...], NT)

    @pl.when(step == pl.num_programs(0) - 1)
    def _():
        gain = gain_ref[...]
        normed, inverse = layer_norm(x_ref[...], gain)[1:]
        through, grad_gain = norm_back(total[...], normed, inverse, gain)
        down = up_ref[...] + through
        down_ref[...] = down
        half_ref[...] = (0.5 * down).astype(BF16)
        gain_grad_ref[...] = grad_gain


def projection_backward(backs, cosines, sines, size, upstream, stream, gain_row, weight):
    places, kinds, chunks, frames, _ = backs[0].shape
    pieces = len(backs)
    rows, model = stream.shape
    block = pl.BlockSpec((places, 1, chunks, frames, LANES), lambda s: (0, s, 0, 0, 0))
    return pl.pallas_call(
        functools.partial(projection_kernel, size, pieces),
        grid=(kinds,),
        in_specs=[
            whole(cosines.shape),
            whole(sines.shape),
            whole((rows, model)),
            whole((1, model)),
            whole((rows, model)),
            pl.BlockSpec((model, model), lambda s: (0, s)),
        ]
        + [block] * pieces,
        out_specs=[
            pl.BlockSpec((rows, model), lambda s: (0, s)),
            whole((rows, model)),
            whole((rows, model)),
            whole((1, model)),
        ],
        out_shape=[
            jax.ShapeDtypeStruct((rows, kinds * model), BF16),
            jax.ShapeDtypeStruct((rows, model), F32),
            jax.ShapeDtypeStruct((rows, model), BF16),
            jax.ShapeDtypeStruct((1, model), F32),
        ],
        scratch_shapes=[pltpu.VMEM((rows, model), F32)],
        compiler_params=compiler_params(),
        cost_estimate=cost(6 * rows * model * model, 6 * model * model + 22 * rows * model),
        name="projection_backward",
    )(cosines, sines, stream, gain_row, upstream, weight, *backs)


def flipped(axis_bit, count):
    axis, bit = axis_bit
    items, heads = count
    if axis == "items":
        return [(i * heads + h, (i ^ bit) * heads + h) for i in range(items) for h in range(heads)]
    return [(i * heads + h, i * heads + (h ^ bit)) for i in range(items) for h in range(heads)]


def swap(value, axis_bit):
    count = (lax.axis_size("items"), lax.axis_size("heads"))
    return lax.ppermute(value, EVERY, flipped(axis_bit, count))


def branched(always, work):
    def empty():
        return jax.tree.map(lambda leaf: jnp.zeros(leaf.shape, leaf.dtype), jax.eval_shape(work))

    return lax.optimization_barrier(lax.cond(always, work, empty))


def fenced(always, scatters, work):
    def run():
        moves = [scatter.move() for scatter in scatters]
        return (branched(always, work) if any(moves) else work(), moves)

    result, moves = branched(always, run)
    for scatter, parts in zip(scatters, moves):
        scatter.take(parts)
    return result


def moved(scatter):
    scatter.take(scatter.move())


def other_core(value):
    return swap(value, ("heads", 1))


def exchange(value):
    half = lax.axis_size("heads") // 2
    groups = [[side * half + i for i in range(half)] for side in range(2)]
    return lax.all_to_all(
        value, "heads", split_axis=0, concat_axis=0, tiled=True, axis_index_groups=groups
    )


def across(value):
    return swap(value, ("heads", lax.axis_size("heads") // 2))


def gathered(own, other, side):
    return jnp.concatenate([jnp.where(side == 0, own, other), jnp.where(side == 0, other, own)], 0)


def parted(value, side):
    low, high = jnp.split(value, 2, 0)
    return (jnp.where(side == 0, low, high), jnp.where(side == 0, high, low))


def own_rows(left_ref, heads, core, target, first):
    rows, model = left_ref.shape
    each = model // heads
    for place in range(heads // 2):
        if each % LANES == 0:
            start = pl.multiple_of((2 * place + core) * each, each)
            mine = jnp.transpose(left_ref[:, pl.ds(start, each)].astype(F32)).astype(BF16)
        else:
            pair = left_ref[:, 2 * place * each : 2 * (place + 1) * each]
            pair = jnp.transpose(pair.astype(F32))
            mine = jnp.where(core == 0, pair[:each], pair[each:]).astype(BF16)
        for half in range(2):
            start = (half * (heads // 2) + place) * (each // 2)
            target[start : start + each // 2, first : first + rows] = mine[
                half * (each // 2) : (half + 1) * (each // 2)
            ]


def turned_items(left, items, own, target, first):
    rows, model = left.shape
    each = model // items
    for item in range(items):
        part = jnp.transpose(left[:, item * each : (item + 1) * each].astype(F32)).astype(BF16)
        place = pl.multiple_of((own ^ item) * each, each)
        target[pl.ds(place, each), first : first + rows] = part


def share_shapes(items, heads, model, columns):
    lead = 2 if items > 1 else 1
    shape = (lead, heads // 2, model // heads // 2, columns // items)
    return [jax.ShapeDtypeStruct(shape, BF16)] * (4 if items > 1 else 2)


def out_grad_kernel(place_ref, up_own, up_other, hid_own, hid_other, *refs):
    targets, turned = refs[:-1], refs[-1]
    rows, model = up_own.shape
    items = 4 if len(targets) == 4 else 1

    @pl.when(pl.program_id(0) == 0)
    def _():
        turned_items(up_own[...], items, place_ref[1], turned, 0)
        turned_items(up_other[...], items, place_ref[1], turned, rows)

    hidden = jnp.concatenate([hid_own[...], hid_other[...]], 0)
    grad = dot(turned[...], hidden).astype(BF16)
    wide = grad.shape[1]
    each = targets[0].shape[2]
    parts = model // items // (2 * each)
    for r in range(items):
        for part in range(parts):
            for half in range(2):
                first = ((r * parts + part) * 2 + half) * each
                piece = grad[first : first + each]
                if half == 0:
                    target, at = targets[2 * (r % 2)], r // 2
                else:
                    target, at = targets[1 + 2 * (r // 2)], r % 2
                target[at, 0, :, part * wide : (part + 1) * wide] = piece


def out_grad(upstream, hidden, heads, place, items):
    rows, model = upstream[0].shape
    units = hidden[0].shape[1]
    wide = units // heads
    shapes = share_shapes(items, heads, model, units)
    block = (shapes[0].shape[0], 1) + shapes[0].shape[2:]
    hid_block = pl.BlockSpec((rows, wide), lambda s, place: (0, 2 * s + place[0]))
    grid_spec = pltpu.PrefetchScalarGridSpec(
        num_scalar_prefetch=1,
        grid=(heads // 2,),
        in_specs=[whole((rows, model))] * 2 + [hid_block] * 2,
        out_specs=[pl.BlockSpec(block, lambda s, place: (0, s, 0, 0))] * len(shapes),
        scratch_shapes=[pltpu.VMEM((model, 2 * rows), BF16)],
    )
    return pl.pallas_call(
        out_grad_kernel,
        grid_spec=grid_spec,
        out_shape=shapes,
        compiler_params=compiler_params(),
        cost_estimate=cost(2 * rows * model * units, 2 * model * units + 4 * rows * units),
        name="out_grad",
    )(place, *upstream, *hidden)


def column_grad_kernel(heads, items, split, place_ref, *refs):
    count = len(split)
    lefts, refs = refs[: 2 * count], refs[2 * count :]
    rights, refs = refs[: 2 * (count + sum(split))], refs[2 * (count + sum(split)) :]
    targets, turned = refs[:-count], refs[-count:]
    r = pl.program_id(0)
    rows = lefts[0].shape[0]

    @pl.when(r == 0)
    def _():
        for number in range(count):
            for other in range(2):
                own_rows(
                    lefts[2 * number + other], heads, place_ref[0], turned[number], other * rows
                )

    made = []
    at = 0
    for number in range(count):
        right = jnp.concatenate([rights[at][...], rights[at + 1][...]], 0)
        at += 2
        if split[number]:
            second = jnp.concatenate([rights[at][...], rights[at + 1][...]], 0)
            at += 2
            right = jnp.where((r ^ place_ref[1]) < items // 2, right, second)
        made.append(dot(turned[number][...], right).astype(BF16))
    made = made[0] if count == 1 else jnp.concatenate(made, 1)
    half = made.shape[0] // 2
    top, low = made[:half].reshape(targets[0].shape), made[half:].reshape(targets[0].shape)
    if len(targets) == 2:
        targets[0][...] = top
        targets[1][...] = low
        return

    @pl.when(r % 2 == 0)
    def _():
        targets[0][...] = top

    @pl.when(r % 2 == 1)
    def _():
        targets[2][...] = top

    @pl.when(r < 2)
    def _():
        targets[1][...] = low

    @pl.when(r >= 2)
    def _():
        targets[3][...] = low


def column_grads(lefts, rights, heads, place, items):
    if items == 1:
        flat = [
            (left, part)
            for left, right in zip(lefts, rights)
            for part in (right if isinstance(right[0], tuple) else (right,))
        ]
        lefts, rights = [left for left, _ in flat], [right for _, right in flat]
    split = [isinstance(right[0], tuple) for right in rights]
    rows, model = lefts[0][0].shape
    parts = []
    for right, two in zip(rights, split):
        parts += [part for pair in right for part in pair] if two else list(right)
    columns = sum(part.shape[1] for part in parts) // 2
    shapes = share_shapes(items, heads, model, columns)
    block = (1,) + shapes[0].shape[1:]
    right_specs = []
    for right, two in zip(rights, split):
        if two:
            share = pl.BlockSpec(
                (rows, right[0][0].shape[1] * 2 // items),
                lambda r, place: (0, (r ^ place[1]) % (items // 2)),
            )
            right_specs += [share] * 4
        else:
            share = pl.BlockSpec(
                (rows, right[0].shape[1] // items), lambda r, place: (0, r ^ place[1])
            )
            right_specs += [share] * 2
    maps = [
        lambda r, place: (r // 2, 0, 0, 0),
        lambda r, place: (jnp.minimum(r, 1), 0, 0, 0),
        lambda r, place: (r // 3, 0, 0, 0),
        lambda r, place: (r // 3, 0, 0, 0),
    ]
    grid_spec = pltpu.PrefetchScalarGridSpec(
        num_scalar_prefetch=1,
        grid=(items,),
        in_specs=[whole((rows, model))] * (2 * len(lefts)) + right_specs,
        out_specs=[pl.BlockSpec(block, index) for index in maps[: len(shapes)]],
        scratch_shapes=[pltpu.VMEM((model // 2, 2 * rows), BF16)] * len(lefts),
    )
    return pl.pallas_call(
        functools.partial(column_grad_kernel, heads, items, split),
        grid_spec=grid_spec,
        out_shape=shapes,
        compiler_params=compiler_params(),
        cost_estimate=cost(2 * rows * model * columns, 4 * model * columns),
        name="column_grads",
    )(place, *[part for left in lefts for part in left], *parts)


class Scatter:
    def __init__(self, keep_top, keep_low, *sends):
        self.keep = [keep_top, keep_low]
        self.got, self.early = [], []
        self.route(list(sends), FIRST[: len(sends)])

    def route(self, sends, routes):
        self.sends, self.routes = sends, routes

    def move(self):
        return [swap(send, route) for send, route in zip(self.sends, self.routes)]

    def take(self, moved):
        self.early, self.got = self.got, moved
        self.route([], [])

    def second(self, sends):
        self.route(sends, FIRST[::-1][: len(sends)])


def second_kernel(*refs):
    count = len(refs) // 3
    for number in range(count):
        keep, got, out = refs[2 * number], refs[2 * number + 1], refs[2 * count + number]
        out[...] = (keep[0].astype(F32) + got[0].astype(F32)).astype(BF16)


def second_sums(*scatters):
    terms = [
        part
        for scatter in scatters
        if scatter.got
        for keep, got in zip(scatter.keep, scatter.got)
        for part in (keep, got)
    ]
    if not terms:
        return [[] for _ in scatters]
    shape = terms[0].shape
    outs = []
    in_specs, out_specs = [], []
    for term in terms:
        in_specs.append(
            pl.BlockSpec((1, 2) + term.shape[2:], lambda g: (1, g, 0, 0))
        )
    for term in terms[::2]:
        out_specs.append(pl.BlockSpec((2,) + term.shape[2:], lambda g: (g, 0, 0)))
        outs.append(jax.ShapeDtypeStruct(term.shape[1:], BF16))
    made = pl.pallas_call(
        second_kernel,
        grid=(shape[1] // 2,),
        in_specs=in_specs,
        out_specs=out_specs,
        out_shape=outs,
        compiler_params=compiler_params(),
        cost_estimate=cost(0, 6 * sum(out.size for out in outs)),
        name="second_sums",
    )(*terms)
    return [list(made[2 * i : 2 * i + 2]) for i in range(len(scatters))]


def last_kernel(*refs):
    out = refs[-1]
    for number in range(out.shape[1]):
        for half in range(2):
            terms = refs[6 * number + 3 * half : 6 * number + 3 * half + 3]
            out[:, number, half] = (
                terms[0][0].astype(F32) + terms[1][0].astype(F32) + terms[2][...].astype(F32)
            ).astype(BF16)


def last_sum(*scatters, columns=None):
    if not scatters[0].got:
        items = lax.axis_size("items")
        values = []
        for scatter in scatters:
            value = jnp.stack([keep[0] for keep in scatter.keep], 1)
            if columns is not None:
                starts = [sum(columns[:i]) for i in range(len(columns))]
                parts = [
                    value[..., start : start + size].reshape(value.shape[:3] + (items, -1))
                    for start, size in zip(starts, columns)
                ]
                value = jnp.concatenate(parts, 4).reshape(value.shape)
            values.append(lax.psum_scatter(value, "items", scatter_dimension=3, tiled=True))
        return jnp.stack(values, 1)
    terms = [
        part
        for scatter in scatters
        for parts in zip(scatter.keep, scatter.early, scatter.got)
        for part in parts
    ]
    _, places, rows, wide = terms[0].shape
    held = pl.BlockSpec((1, 2, rows, wide), lambda g: (0, g, 0, 0))
    late = pl.BlockSpec((2, rows, wide), lambda g: (g, 0, 0))
    shape = (places, len(scatters), 2, rows, wide)
    return pl.pallas_call(
        last_kernel,
        grid=(places // 2,),
        in_specs=[held, held, late] * (2 * len(scatters)),
        out_specs=pl.BlockSpec((2,) + shape[1:], lambda g: (g, 0, 0, 0, 0)),
        out_shape=jax.ShapeDtypeStruct(shape, BF16),
        compiler_params=compiler_params(),
        cost_estimate=cost(0, 8 * places * len(scatters) * 2 * rows * wide),
        name="last_sum",
    )(*terms)


def along_z(value):
    heads = lax.axis_size("heads")
    groups = [[core + 2 * z for z in range(heads // 2)] for core in range(2)]
    made = lax.psum_scatter(
        value, "heads", scatter_dimension=0, tiled=False, axis_index_groups=groups
    )
    return [made[i].reshape(-1, made.shape[-1]) for i in range(made.shape[0])]


def unfold_kernel(share_ref, out_ref):
    each = share_ref.shape[0]
    span = out_ref.shape[0]
    for part in range(share_ref.shape[1] // span):
        turned = jnp.transpose(share_ref[:, part * span : (part + 1) * span].astype(F32))
        out_ref[:, part * each : (part + 1) * each] = turned


def unfolded(share, span):
    each, wide = share.shape
    shape = (span, each * wide // span)
    return pl.pallas_call(
        unfold_kernel,
        out_shape=jax.ShapeDtypeStruct(shape, F32),
        cost_estimate=cost(0, 6 * each * wide),
        name="unfolded",
    )(share)


def heads_kernel(grad_ref, weight_ref, *outs):
    step = pl.program_id(0)
    made = dot(grad_ref[...], weight_ref[...], NT).astype(BF16)
    for piece, out in enumerate(outs):

        @pl.when(step == piece)
        def _():
            places, chunks, frames, _ = out.shape
            for place in range(places):
                for chunk in range(chunks):
                    out[place, chunk] = made[
                        chunk * frames : (chunk + 1) * frames, place * LANES : (place + 1) * LANES
                    ]


def heads_gradient(grad, weight, places, chunks):
    rows, model = grad.shape
    wide = places * LANES
    pieces = model // wide
    shape = (places, chunks, rows // chunks, LANES)
    return pl.pallas_call(
        heads_kernel,
        grid=(pieces,),
        in_specs=[whole((rows, model)), pl.BlockSpec((wide, model), lambda s: (s, 0))],
        out_specs=[whole(shape)] * pieces,
        out_shape=[jax.ShapeDtypeStruct(shape, BF16)] * pieces,
        compiler_params=compiler_params(),
        cost_estimate=cost(2 * rows * model * model, 2 * model * model + 4 * rows * model),
        name="heads_gradient",
    )(grad, weight)


def sum_everywhere(value):
    for axis in EVERY:
        bit = 1
        while bit < lax.axis_size(axis):
            value = value + swap(value, (axis, bit))
            bit *= 2
    return value


def edges(block, width):
    ways = lax.axis_size("heads")
    half = ways // 2
    place = lax.axis_index("heads") % half
    ring = [(side * half + i, side * half + (i + 1) % half) for side in range(2) for i in range(half)]
    low = lax.ppermute(block[:, block.shape[1] - width :], "heads", ring)
    high = lax.ppermute(block[:, :width], "heads", [(to, at) for at, to in ring])
    low = jnp.where(place == 0, jnp.roll(low, 1, 0), low)
    high = jnp.where(place == half - 1, jnp.roll(high, -1, 0), high)
    return jnp.concatenate([low, block, high], axis=1)


def body(
    frames, cotangent, bucket_counts, gains, w_ffn1_in, w_ffn1_out, w_qkv, w_out,
    w_point_in, w_depth, w_point_out, w_ffn2_in, w_ffn2_out,
):
    chunks, here, model = frames.shape
    ways = lax.axis_size("heads")
    half = ways // 2
    items = 4 if lax.axis_size("items") == 4 else 1
    span = here * half
    group_len = here * ways
    size = model // HEADS
    reach = (KERNEL - 1) // 2
    rows = chunks * here
    pieces = model // (half * LANES)
    place = lax.axis_index("heads")
    side = place // half
    where = jnp.stack(
        [place % 2, lax.axis_index("items") if items > 1 else 0 * place]
    ).astype(jnp.int32)
    always = place >= 0
    first = jnp.arange(chunks, dtype=jnp.int32)[:, None] * span + place % half * here
    position = first + jnp.arange(here, dtype=jnp.int32)[None]
    cosines, sines = rope_tables(position.reshape(-1), size)
    depth_rows = w_depth.astype(F32)
    gain = [gains[i : i + 1] for i in range(6)]
    counts = lax.dynamic_index_in_dim(bucket_counts[:, 0], side, 0, keepdims=False)
    wide_position = first - reach + jnp.arange(here + 2 * reach, dtype=jnp.int32)[None]
    seg_wide = segment_ids(wide_position, counts[0], counts[1], group_len)
    seg_own = seg_wide[:, reach : reach + here]

    def mine(value):
        return lax.dynamic_index_in_dim(value, side, 0, keepdims=False)

    def theirs(value):
        return lax.dynamic_index_in_dim(value, 1 - side, 0, keepdims=False)

    def begin(chunk, row, before=()):
        return front(
            chunk, row.reshape(1).astype(jnp.int32), gains, w_ffn1_in, w_ffn1_out, w_qkv,
            cosines, sines, half, chunks, size, before,
        )

    before, other_frames = fenced(
        always, (), lambda: (begin(frames, side), across(theirs(frames)))
    )
    stream_one, slope_one, hid_one, ent_one, ent_att, *sent = begin(
        other_frames[None], 1 - side, before
    )
    stream = gathered(mine(frames), other_frames, side)
    qkv = [exchange(sent[0])]
    kept, contexts = [], []
    for number in range(pieces):

        def attend_now():
            return attend_forward(qkv[number], counts, size)

        def beside():
            extra = []
            if number + 1 < pieces:
                extra.append(exchange(sent[number + 1]))
            if number > 0:
                extra.append(exchange(kept[number - 1][0]))
            return extra

        def early():
            if number == 0:
                return [other_core(part) for part in (hid_one, ent_one, ent_att)]
            return [across(theirs(cotangent))] if number == 1 else []

        made, extra, others = fenced(always, (), lambda: (attend_now(), beside(), early()))
        kept.append(made)
        if number == 0:
            hid_one, ent_one, ent_att = zip((hid_one, ent_one, ent_att), others)
        elif number == 1:
            cot_other = others[0]
        if number + 1 < pieces:
            qkv.append(extra.pop(0))
        if number > 0:
            contexts.append(extra.pop(0))
    contexts.append(exchange(kept[-1][0]))
    if pieces == 1:
        cot_other = across(theirs(cotangent))
    fulls = [made[1] for made in kept]
    lses = [made[2] for made in kept]
    contexts = [part.transpose(1, 2, 0, 3).reshape(rows, -1) for part in contexts]
    context = jnp.concatenate(contexts, 1)
    stream_two = stream_one
    for number, part in enumerate(contexts):
        wide = part.shape[1]
        stream_two = stream_two + dot(part, w_out[number * wide : (number + 1) * wide])
    shaped, conv_normed, conv_inverse = layer_norm(stream_two, gain[2])
    conv_entered = shaped.astype(BF16)
    pointwise = dot(conv_entered, w_point_in)
    linear = pointwise[:, :model]
    sigmoid_gate = jax.nn.sigmoid(pointwise[:, model:])
    gated_low = (linear * sigmoid_gate).astype(BF16).reshape(chunks, here, model)
    widened = edges(gated_low, reach)
    depth_out = jnp.zeros((chunks, here, model), F32)
    for offset in range(KERNEL):
        same = (seg_wide[:, offset : offset + here] == seg_own)[:, :, None]
        depth_out = depth_out + depth_rows[offset] * jnp.where(
            same, widened[:, offset : offset + here], 0.0
        )
    depth_out = depth_out.reshape(rows, model)
    depth_shaped, depth_normed, depth_inverse = layer_norm(depth_out, gain[3])
    mixed_low = (depth_shaped * jax.nn.sigmoid(depth_shaped)).astype(BF16)
    stream_three = stream_two + dot(mixed_low, w_point_out)
    layer_out, grad_four, gain_five, slope_two, hid_two, ent_two = ffn_forward(
        stream_three, gain[4], w_ffn2_in, w_ffn2_out, gain[5],
        gathered(mine(cotangent), cot_other, side),
    )
    (grad_three, gain_four, half_two, grad_pre_two), hid_other, ent_other = fenced(
        always,
        (),
        lambda: (
            ffn_backward(grad_four, stream_three, slope_two, gain[4], w_ffn2_in, w_ffn2_out),
            other_core(hid_two),
            other_core(ent_two),
        ),
    )
    half_other, grad_pre_other = other_core(half_two), other_core(grad_pre_two)
    grad_mix = grad_three.astype(BF16)
    grad_norm_in = dot(grad_mix, w_point_out, NT) * silu_slope(depth_shaped)
    grad_depth, gain_three = norm_back(grad_norm_in, depth_normed, depth_inverse, gain[3])
    grad_depth_low = grad_depth.astype(BF16).reshape(chunks, here, model)
    grad_widened = edges(grad_depth_low, reach)
    grad_gated = jnp.zeros((chunks, here, model), F32)
    for offset in range(KERNEL):
        mirror = 2 * reach - offset
        same_back = (seg_wide[:, mirror : mirror + here] == seg_own)[:, :, None]
        grad_gated = grad_gated + depth_rows[offset] * jnp.where(
            same_back, grad_widened[:, mirror : mirror + here], 0.0
        )
    grad_gated = grad_gated.reshape(rows, model)
    grad_a = (grad_gated * sigmoid_gate).astype(BF16)
    grad_b = (grad_gated * linear * sigmoid_gate * (1.0 - sigmoid_gate)).astype(BF16)
    through, gain_two = norm_back(
        dot(grad_a, w_point_in[:, :model], NT) + dot(grad_b, w_point_in[:, model:], NT),
        conv_normed, conv_inverse, gain[2],
    )
    grad_two = grad_three + through
    grad_attn_out = grad_two.astype(BF16)
    grad_heads = list(heads_gradient(grad_attn_out, w_out, half, chunks))
    lefts = (mixed_low, conv_entered, context)

    def ffn_grads():
        return (
            [other_core(part) for part in lefts + (grad_a, grad_b)],
            exchange(grad_heads[0]),
            out_grad((half_two, half_other), (hid_two, hid_other), ways, where, items),
            column_grads(
                [(ent_two, ent_other)], [(grad_pre_two, grad_pre_other)], ways, where, items
            ),
        )

    others, grad_heads[0], shares_out, shares_in = fenced(always, (), ffn_grads)
    two_out, two_in = Scatter(*shares_out), Scatter(*shares_in)
    out_own, out_theirs = parted(layer_out, side)
    grads, backs = [], []
    for number in range(pieces):
        last = number == pieces - 1

        def beside():
            extra = []
            if not last:
                extra.append(exchange(grad_heads[number + 1]))
            if number > 0:
                extra.append(exchange(grads[number - 1]))
            if number == 0:
                extra.append(across(out_theirs))
                extra += [other_core(grad_mix), other_core(grad_attn_out)]
            return extra

        def attend_now():
            return attend_backward(
                qkv[number], counts, size, fulls[number], lses[number], grad_heads[number]
            )

        moving = (two_out,) if number == 0 else (two_out, two_in) if number == 1 else ()
        made, extra = fenced(always, moving, lambda: (attend_now(), beside()))
        grads.append(made)
        if not last:
            grad_heads[number + 1] = extra.pop(0)
        if number > 0:
            backs.append(extra.pop(0))
        if number == 0:
            out_other, *late = extra
            two_out.second(second_sums(two_out)[0])
    two_in.second(second_sums(two_in)[0])

    def middle_part():
        back = exchange(grads[-1])
        scatter = copy.copy(two_in)
        moved(scatter)
        shares = column_grads(
            list(zip(lefts, others[:3])),
            [
                (grad_mix, late[0]),
                ((grad_a, others[3]), (grad_b, others[4])),
                (grad_attn_out, late[1]),
            ],
            ways, where, items,
        )
        return (back, shares, last_sum(two_out, scatter))

    back, shares, two_sum = fenced(always, (), middle_part)
    backs.append(back)
    middle = Scatter(*shares)

    def attention_part():
        two_grads = along_z(two_sum)
        scatter = copy.copy(middle)

        def projection_part():
            grad_proj, *down = projection_backward(
                backs, cosines, sines, size, grad_two, stream_one, gain[1], w_qkv
            )
            return ((grad_proj, other_core(grad_proj)), down)

        grad_proj, (grad_one, half_one, gain_one) = fenced(always, (scatter,), projection_part)
        first = scatter.got
        scatter.second(second_sums(scatter)[0])

        def qkv_part():
            half_other = other_core(half_one)
            return (half_other, column_grads([ent_att], [grad_proj], ways, where, items))

        half_other, shares = fenced(always, (scatter,), qkv_part)
        attn = Scatter(*shares)

        def hidden_part():
            half_own, grad_pre = hidden_gradient(grad_one, slope_one, w_ffn1_out)
            shares = out_grad((half_own, half_other), hid_one, ways, where, items)
            return (grad_pre, shares)

        grad_pre, shares_out = fenced(always, (attn,), hidden_part)
        return (
            two_grads, first, scatter.got, (grad_one, gain_one), shares[:2], attn.got,
            grad_pre, shares_out,
        )

    two_grads, first, got, (grad_one, gain_one), shares, attn_got, grad_pre, shares_out = fenced(
        always, (), attention_part
    )
    middle.take(first)
    middle.take(got)
    attn = Scatter(*shares)
    attn.take(attn_got)
    attn.second(second_sums(attn)[0])
    one_out = Scatter(*shares_out)
    middle_columns = [w.shape[1] for w in (w_point_out, w_point_in, w_out)]
    middle_grad, shares, (grad_zero, _, gain_zero) = fenced(
        always,
        (one_out, attn),
        lambda: (
            along_z(last_sum(middle, columns=middle_columns)),
            column_grads([ent_one], [(grad_pre, other_core(grad_pre))], ways, where, items),
            stream_gradient(grad_one, stream, grad_pre, gain[0], w_ffn1_in, BF16),
        ),
    )
    one_in = Scatter(*shares)
    one_out.second(second_sums(one_out)[0])
    grad_own, grad_theirs = parted(grad_zero, side)
    attn_grad, grad_other = fenced(
        always, (one_in, one_out), lambda: (along_z(last_sum(attn)), across(grad_theirs))
    )
    one_in.second(second_sums(one_in)[0])

    hidden = w_ffn1_in.shape[1]

    def tap_sums_here():
        rows_of = []
        for offset in range(KERNEL):
            same = (seg_wide[:, offset : offset + here] == seg_own)[:, :, None]
            product = grad_depth_low.astype(F32) * widened[:, offset : offset + here]
            rows_of.append(jnp.sum(jnp.where(same, product, 0.0), (0, 1))[None])
        return rows_of

    def last_part():
        out_grads = along_z(last_sum(one_out))
        scatter = copy.copy(one_in)
        moved(scatter)
        small = sum_everywhere(
            jnp.concatenate(
                [gain_zero, gain_one, gain_two, gain_three, gain_four, gain_five]
                + tap_sums_here(),
                0,
            )
        )
        middle_parts = []
        start = 0
        for columns in middle_columns:
            each = columns // lax.axis_size("items")
            middle_parts.append(middle_grad[0][:, start : start + each].astype(F32))
            start += each
        ready = (
            gathered(out_own[None], out_other[None], side),
            gathered(grad_own[None], grad_other[None], side),
            attn_grad[0].astype(F32),
            middle_parts,
            two_grads[1].astype(F32),
            unfolded(two_grads[0], hidden // ways),
            unfolded(out_grads[0], hidden // ways),
        )
        return (along_z(last_sum(scatter)), small[:6], small[6:], ready)

    one_in_grad, gain_sums, tap_sums, ready = fenced(always, (), last_part)
    out, grad_in, attn_full, middle_parts, two_in_full, two_out_full, one_out_full = ready
    return (
        out,
        grad_in,
        gain_sums,
        one_in_grad[0].astype(F32),
        one_out_full,
        attn_full,
        middle_parts[2],
        middle_parts[1],
        tap_sums,
        middle_parts[0],
        two_in_full,
        two_out_full,
    )


def solution(mesh):
    split = P(None, EVERY, None)
    shares = P("heads", "items")
    in_specs = (split, split, P(None, "items", None)) + (P(),) * 10
    out_specs = (split, split, P(), shares, shares, shares, shares, shares, P()) + (shares,) * 3
    return jax.shard_map(body, mesh=mesh, in_specs=in_specs, out_specs=out_specs, check_vma=False)
```

```python
import copy
import functools

import jax
import jax.numpy as jnp
from jax import lax
from jax.experimental import pallas as pl
from jax.experimental.pallas import tpu as pltpu
from jax.sharding import PartitionSpec as P

HEADS = 16
KERNEL = 5
LONG = 1500
SHORT = 500
EPS = 1e-05
ROPE_BASE = 10000.0
BLOCK = 512
INNER_FWD = 1024
INNER_BWD = 512
TURNED = 512
LANES = 128
BIG = 1e30
VMEM_LIMIT = 56 << 20
F32 = jnp.float32
BF16 = jnp.bfloat16
NN = (((1,), (0,)), ((), ()))
NT = (((1,), (1,)), ((), ()))
EVERY = ("items", "heads")
FIRST = [("items", 1), ("items", 2)]


def dot(left, right, dims=NN):
    return lax.dot_general(left, right, dims, preferred_element_type=F32)


def silu_slope(field):
    gate_sig = jax.nn.sigmoid(field)
    return gate_sig * (1.0 + field * (1.0 - gate_sig))


def layer_norm(field, gain_row):
    centred = field - jnp.mean(field, -1, keepdims=True)
    inverse = lax.rsqrt(jnp.mean(centred * centred, -1, keepdims=True) + EPS)
    normed = centred * inverse
    return (normed * gain_row, normed, inverse)


def norm_back(upstream, normed, inverse, gain_row):
    scaled = upstream * gain_row
    through = inverse * (
        scaled
        - jnp.mean(scaled, -1, keepdims=True)
        - normed * jnp.mean(scaled * normed, -1, keepdims=True)
    )
    return (through, jnp.sum(upstream * normed, 0, keepdims=True))


def segment_ids(position, long_count, short_count, group_len):
    long_end = long_count * LONG
    short_end = long_end + short_count * SHORT
    segments = jnp.where(
        position < long_end, position // LONG, long_count + (position - long_end) // SHORT
    )
    segments = jnp.where(position < short_end, segments, long_count + short_count)
    return jnp.where((position < 0) | (position >= group_len), -1, segments)


def compiler_params():
    return pltpu.CompilerParams(vmem_limit_bytes=VMEM_LIMIT)


def whole(shape):
    return pl.BlockSpec(shape, lambda *_: (0,) * len(shape))


def cost(flops, bytes_accessed, transcendentals=0):
    return pl.CostEstimate(
        flops=flops, bytes_accessed=bytes_accessed, transcendentals=transcendentals
    )


def segment_bounds(counts, place, group):
    longs, shorts = counts
    long_end = longs * LONG
    short_end = long_end + shorts * SHORT
    start = jnp.where(place < longs, place * LONG, long_end + (place - longs) * SHORT)
    size = jnp.where(place < longs, LONG, SHORT)
    last = place == longs + shorts
    return (jnp.where(last, short_end, start), jnp.where(last, group, start + size), place <= longs + shorts)


def member_lanes(counts, first, rows, group, shift=0):
    shape = (rows, LANES)
    place = lax.broadcasted_iota(jnp.int32, (8, LANES), 1) - shift
    start, end, there = segment_bounds(counts, place, group)
    start = jnp.where(there & (place >= 0), start, group)
    start, end = start[:1], end[:1]
    frame = first + lax.broadcasted_iota(jnp.int32, shape, 0)
    return (frame >= start) & (frame < end)


def block_range(counts, step, group, inner):
    longs, shorts = counts
    long_end = longs * LONG
    short_end = long_end + shorts * SHORT

    def number(frame):
        place = jnp.where(frame < long_end, frame // LONG, longs + (frame - long_end) // SHORT)
        return jnp.where(frame < short_end, place, longs + shorts)

    first = segment_bounds(counts, number(step * BLOCK), group)[0]
    last = segment_bounds(counts, number(step * BLOCK + BLOCK - 1), group)[1]
    return (first // inner, (last + inner - 1) // inner)


def head_lanes(shape, head, size):
    lane = lax.broadcasted_iota(jnp.int32, shape, 1)
    return (lane >= head * size) & (lane < (head + 1) * size)


def split_three(v):
    hi = v.astype(BF16).astype(F32)
    rest = v - hi
    mid = rest.astype(BF16).astype(F32)
    return (hi, mid, rest - mid)


def spread_columns(columns, shape):
    lane = lax.broadcasted_iota(jnp.int32, shape, 1)
    out = jnp.zeros(shape, F32)
    for place, column in enumerate(columns):
        out = jnp.where(lane == place, column, out)
    return out


def chunk_rows(ref, lead, step):
    places, chunks, frames = ref.shape[0], ref.shape[-3], ref.shape[-2]
    per = BLOCK // frames
    steps = places // per
    at = (pl.ds(step % steps * per, per),) + lead + (step // steps,)
    return ref[at].reshape(BLOCK, LANES)


def attn_fwd_kernel(
    heads, size, group, counts_ref, qkv_ref, out_ref, full_ref, lse_ref, kcat, v_all, s_scr
):
    step = pl.program_id(0)
    counts = (counts_ref[0], counts_ref[1])

    @pl.when(step == 0)
    def _():
        chunks = qkv_ref.shape[2]
        span = group // chunks
        for chunk in range(chunks):
            rows = slice(chunk * span, (chunk + 1) * span)
            kcat[rows, :LANES] = qkv_ref[:, 1, chunk].reshape(span, LANES)
            v_all[rows, :] = qkv_ref[:, 2, chunk].reshape(span, LANES)
        kcat[:, LANES:] = jnp.where(member_lanes(counts, 0, group, group), 0.0, -BIG).astype(BF16)

    q = chunk_rows(qkv_ref, (0,), step).astype(F32) * (size ** -0.5)
    member = jnp.where(member_lanes(counts, step * BLOCK, BLOCK, group), 1.0, 0.0).astype(BF16)
    queries = []
    for head in range(heads):
        mine = jnp.where(head_lanes(q.shape, head, size), q, 0.0).astype(BF16)
        queries.append(jnp.concatenate([mine, member], 1))
    low, high = block_range(counts, step, group, INNER_FWD)

    def scores(j, tops):
        keys = kcat[pl.ds(pl.multiple_of(j * INNER_FWD, INNER_FWD), INNER_FWD), :]
        new = []
        for head in range(heads):
            s = dot(queries[head], keys, NT)
            s_scr[head, j] = s
            top = tops[head]
            for part in range(INNER_FWD // LANES):
                top = jnp.maximum(top, s[:, part * LANES : (part + 1) * LANES])
            new.append(top)
        return tuple(new)

    start = tuple(jnp.full((BLOCK, LANES), -BIG, F32) for _ in range(heads))
    tops = lax.fori_loop(low, high, scores, start)
    tops = [jnp.max(t, 1, keepdims=True) for t in tops]
    tops = [jnp.broadcast_to(t, (BLOCK, LANES)) for t in tops]

    def weigh(j, carried):
        sums, accs = carried
        values = v_all[pl.ds(pl.multiple_of(j * INNER_FWD, INNER_FWD), INNER_FWD), :]
        new_sums, new_accs = [], []
        for head in range(heads):
            total = sums[head]
            parts = []
            for part in range(INNER_FWD // LANES):
                p = jnp.exp(s_scr[head, j, :, part * LANES : (part + 1) * LANES] - tops[head])
                total = total + p
                parts.append(p.astype(BF16))
            new_sums.append(total)
            new_accs.append(accs[head] + dot(jnp.concatenate(parts, 1), values))
        return (tuple(new_sums), tuple(new_accs))

    zeros = tuple(jnp.zeros((BLOCK, LANES), F32) for _ in range(heads))
    sums, accs = lax.fori_loop(low, high, weigh, (zeros, zeros))
    result = None
    for head in range(heads):
        total = jnp.sum(sums[head], 1, keepdims=True)
        mine = accs[head] / total
        if result is None:
            result = mine
        else:
            result = jnp.where(head_lanes(mine.shape, head, size), mine, result)
        lse_ref[head] = tops[head] + jnp.log(jnp.broadcast_to(total, (BLOCK, LANES)))
    full_ref[...] = result
    out_ref[...] = result.astype(BF16).reshape(out_ref.shape)


def attend_forward(qkv, counts, size):
    places, _, chunks, frames, _ = qkv.shape
    group = places * chunks * frames
    heads = LANES // size
    per = BLOCK // frames
    each = places // per
    return pl.pallas_call(
        functools.partial(attn_fwd_kernel, heads, size, group),
        grid=(group // BLOCK,),
        in_specs=[pl.BlockSpec(memory_space=pltpu.SMEM), whole(qkv.shape)],
        out_specs=[
            pl.BlockSpec((per, 1, frames, LANES), lambda i: (i % each, i // each, 0, 0)),
            pl.BlockSpec((BLOCK, LANES), lambda i: (i, 0)),
            pl.BlockSpec((heads, BLOCK, LANES), lambda i: (0, i, 0)),
        ],
        out_shape=[
            jax.ShapeDtypeStruct((places, chunks, frames, LANES), BF16),
            jax.ShapeDtypeStruct((group, LANES), F32),
            jax.ShapeDtypeStruct((heads, group, LANES), F32),
        ],
        scratch_shapes=[
            pltpu.VMEM((group, 2 * LANES), BF16),
            pltpu.VMEM((group, LANES), BF16),
            pltpu.VMEM((heads, group // INNER_FWD, BLOCK, INNER_FWD), F32),
        ],
        compiler_params=compiler_params(),
        cost_estimate=cost(16 * group * group * LANES, 6 << 20, heads * group * group),
        name="attend_forward",
    )(counts, qkv)


def attn_bwd_kernel(
    heads, size, group, counts_ref, qkv_ref, full_ref, lse_ref, grad_ref, out_ref,
    qcat, gcat, k_turned, dq_turned,
):
    step = pl.program_id(0)
    counts = (counts_ref[0], counts_ref[1])
    blocks = group // BLOCK
    places, _, _, frames, _ = qkv_ref.shape
    per = BLOCK // frames
    each = places // per

    def put(part, j, value):
        out_ref[pl.ds(j % each * per, per), part, j // each] = value.astype(BF16).reshape(
            per, frames, LANES
        )

    @pl.when(step == 0)
    def _():
        dq_turned[...] = jnp.zeros_like(dq_turned)

        def prepare(j, _):
            rows = pl.ds(pl.multiple_of(j * BLOCK, BLOCK), BLOCK)
            lane = lax.broadcasted_iota(jnp.int32, (BLOCK, LANES), 1)
            q = chunk_rows(qkv_ref, (0,), j).astype(F32) * (size ** -0.5)
            g = chunk_rows(grad_ref, (), j).astype(F32)
            product = g * full_ref[rows, :]
            member = jnp.where(member_lanes(counts, j * BLOCK, BLOCK, group, 3), 1.0, 0.0)
            for head in range(heads):
                own = head_lanes((BLOCK, LANES), head, size)
                lse = lse_ref[head, rows, :]
                spread = spread_columns(split_three(lse), (BLOCK, LANES))
                delta = jnp.sum(jnp.where(own, product, 0.0), 1, keepdims=True)
                delta = jnp.broadcast_to(delta, (BLOCK, LANES))
                qcat[head, rows, :LANES] = jnp.where(own, q, 0.0).astype(BF16)
                qcat[head, rows, LANES:] = jnp.where(lane < 3, -spread, member).astype(BF16)
                gcat[head, rows, :LANES] = jnp.where(own, g, 0.0).astype(BF16)
                spread = spread_columns(split_three(delta), (BLOCK, LANES))
                gcat[head, rows, LANES:] = (-spread).astype(BF16)
            k = chunk_rows(qkv_ref, (1,), j).astype(F32)
            k_turned[j] = jnp.transpose(k).astype(BF16)
            return 0

        lax.fori_loop(0, blocks, prepare, 0)

    lane = lax.broadcasted_iota(jnp.int32, (BLOCK, LANES), 1)
    member = member_lanes(counts, step * BLOCK, BLOCK, group, 3)
    tail = jnp.where(lane < 3, 1.0, jnp.where(member, 0.0, -BIG)).astype(BF16)
    keys = jnp.concatenate([chunk_rows(qkv_ref, (1,), step), tail], 1)
    ones = jnp.where(lane < 3, 1.0, 0.0).astype(BF16)
    values = jnp.concatenate([chunk_rows(qkv_ref, (2,), step), ones], 1)

    def one(j, carried):
        dk, dv = carried
        cols = pl.ds(pl.multiple_of(j * INNER_BWD, INNER_BWD), INNER_BWD)
        for head in range(heads):
            qc = qcat[head, cols, :]
            gc = gcat[head, cols, :]
            p = jnp.exp(dot(keys, qc, NT))
            ds = (p * dot(values, gc, NT)).astype(BF16)
            dv = dv + dot(p.astype(BF16), gc[:, :LANES])
            dk = dk + dot(ds, qc[:, :LANES])
            mine = slice(head * size, (head + 1) * size)
            dq_turned[j, mine, :] += dot(k_turned[step, mine, :], ds)
        return (dk, dv)

    zero = jnp.zeros((BLOCK, LANES), F32)
    low, high = block_range(counts, step, group, INNER_BWD)
    dk, dv = lax.fori_loop(low, high, one, (zero, zero))
    put(1, step, dk)
    put(2, step, dv)

    @pl.when(step == blocks - 1)
    def _():
        def finish(j, _):
            put(0, j, jnp.transpose(dq_turned[j]) * (size ** -0.5))
            return 0

        lax.fori_loop(0, blocks, finish, 0)


def attend_backward(qkv, counts, size, full, lse, grad):
    places, _, chunks, frames, _ = qkv.shape
    group = places * chunks * frames
    heads = LANES // size
    steps = group // BLOCK
    return pl.pallas_call(
        functools.partial(attn_bwd_kernel, heads, size, group),
        grid=(steps,),
        in_specs=[
            pl.BlockSpec(memory_space=pltpu.SMEM),
            whole(qkv.shape),
            whole(full.shape),
            whole(lse.shape),
            whole(grad.shape),
        ],
        out_specs=whole(qkv.shape),
        out_shape=jax.ShapeDtypeStruct(qkv.shape, BF16),
        scratch_shapes=[
            pltpu.VMEM((heads, group, 2 * LANES), BF16),
            pltpu.VMEM((heads, group, 2 * LANES), BF16),
            pltpu.VMEM((steps, LANES, BLOCK), BF16),
            pltpu.VMEM((group // INNER_BWD, LANES, INNER_BWD), F32),
        ],
        compiler_params=compiler_params(),
        cost_estimate=cost(32 * group * group * LANES, 9 << 20, heads * group * group),
        name="attend_backward",
    )(counts, qkv, full, lse, grad)


def half_gate(field):
    return 0.5 * jnp.tanh(0.5 * field) + 0.5


def hidden_units(pre):
    gate = half_gate(pre)
    hidden = pre * gate
    return (hidden.astype(BF16), (gate + hidden * (1.0 - gate)).astype(BF16))


def ffn_fwd_kernel(
    x_ref, gain_ref, last_gain_ref, up_ref, win_ref, wout_ref,
    out_ref, down_ref, gain_grad_ref, slope_ref, hid_ref, entered_ref, total,
):
    step = pl.program_id(0)

    @pl.when(step == 0)
    def _():
        entered_ref[...] = layer_norm(x_ref[...], gain_ref[...])[0].astype(BF16)
        total[...] = jnp.zeros_like(total)

    hidden, slope = hidden_units(dot(entered_ref[...], win_ref[...]))
    slope_ref[...] = slope
    hid_ref[...] = hidden
    total[...] += dot(hidden, wout_ref[...])

    @pl.when(step == pl.num_programs(0) - 1)
    def _():
        gain = last_gain_ref[...]
        shaped, normed, inverse = layer_norm(x_ref[...] + 0.5 * total[...], gain)
        out_ref[...] = shaped.astype(BF16)
        through, grad_gain = norm_back(up_ref[...].astype(F32), normed, inverse, gain)
        down_ref[...] = through
        gain_grad_ref[...] = grad_gain


def ffn_forward(stream, gain_row, weight_in, weight_out, last_gain, upstream):
    rows, model = stream.shape
    units = weight_in.shape[1]
    wide = min(units, 1024)
    return pl.pallas_call(
        ffn_fwd_kernel,
        grid=(units // wide,),
        in_specs=[
            whole((rows, model)),
            whole((1, model)),
            whole((1, model)),
            whole((rows, model)),
            pl.BlockSpec((model, wide), lambda s: (0, s)),
            pl.BlockSpec((wide, model), lambda s: (s, 0)),
        ],
        out_specs=[whole((rows, model)), whole((rows, model)), whole((1, model))]
        + [pl.BlockSpec((rows, wide), lambda s: (0, s))] * 2
        + [whole((rows, model))],
        out_shape=[
            jax.ShapeDtypeStruct((rows, model), BF16),
            jax.ShapeDtypeStruct((rows, model), F32),
            jax.ShapeDtypeStruct((1, model), F32),
            jax.ShapeDtypeStruct((rows, units), BF16),
            jax.ShapeDtypeStruct((rows, units), BF16),
            jax.ShapeDtypeStruct((rows, model), BF16),
        ],
        scratch_shapes=[pltpu.VMEM((rows, model), F32)],
        compiler_params=compiler_params(),
        cost_estimate=cost(4 * rows * model * units, 4 * model * units + 4 * rows * units),
        name="ffn_forward",
    )(stream, gain_row, last_gain, upstream, weight_in, weight_out)


def ffn_bwd_kernel(
    x_ref, gain_ref, up_ref, slope_ref, win_ref, wout_ref,
    down_ref, gain_grad_ref, half_ref, grad_ref, total,
):
    step = pl.program_id(0)

    @pl.when(step == 0)
    def _():
        half_ref[...] = (0.5 * up_ref[...]).astype(BF16)
        total[...] = jnp.zeros_like(total)

    grad = (dot(half_ref[...], wout_ref[...], NT) * slope_ref[...].astype(F32)).astype(BF16)
    grad_ref[...] = grad
    total[...] += dot(grad, win_ref[...], NT)

    @pl.when(step == pl.num_programs(0) - 1)
    def _():
        gain = gain_ref[...]
        normed, inverse = layer_norm(x_ref[...].astype(F32), gain)[1:]
        through, grad_gain = norm_back(total[...], normed, inverse, gain)
        down_ref[...] = up_ref[...] + through
        gain_grad_ref[...] = grad_gain


def ffn_backward(upstream, stream, slope, gain_row, weight_in, weight_out):
    rows, model = stream.shape
    units = weight_in.shape[1]
    wide = min(units, 1024)
    return pl.pallas_call(
        ffn_bwd_kernel,
        grid=(units // wide,),
        in_specs=[
            whole((rows, model)),
            whole((1, model)),
            whole((rows, model)),
            pl.BlockSpec((rows, wide), lambda s: (0, s)),
            pl.BlockSpec((model, wide), lambda s: (0, s)),
            pl.BlockSpec((wide, model), lambda s: (s, 0)),
        ],
        out_specs=[
            whole((rows, model)),
            whole((1, model)),
            whole((rows, model)),
            pl.BlockSpec((rows, wide), lambda s: (0, s)),
        ],
        out_shape=[
            jax.ShapeDtypeStruct((rows, model), F32),
            jax.ShapeDtypeStruct((1, model), F32),
            jax.ShapeDtypeStruct((rows, model), BF16),
            jax.ShapeDtypeStruct((rows, units), BF16),
        ],
        scratch_shapes=[pltpu.VMEM((rows, model), F32)],
        compiler_params=compiler_params(),
        cost_estimate=cost(4 * rows * model * units, 4 * model * units + 6 * rows * units),
        name="ffn_backward",
    )(stream, gain_row, upstream, slope, weight_in, weight_out)


def hidden_kernel(up_ref, slope_ref, wout_ref, half_ref, grad_ref):
    @pl.when(pl.program_id(0) == 0)
    def _():
        half_ref[...] = (0.5 * up_ref[...]).astype(BF16)

    grad = dot(half_ref[...], wout_ref[...], NT) * slope_ref[...].astype(F32)
    grad_ref[...] = grad.astype(BF16)


def hidden_gradient(upstream, slope, weight_out):
    rows, model = upstream.shape
    units = weight_out.shape[0]
    wide = min(units, 1024)
    return pl.pallas_call(
        hidden_kernel,
        grid=(units // wide,),
        in_specs=[
            whole((rows, model)),
            pl.BlockSpec((rows, wide), lambda s: (0, s)),
            pl.BlockSpec((wide, model), lambda s: (s, 0)),
        ],
        out_specs=[whole((rows, model)), pl.BlockSpec((rows, wide), lambda s: (0, s))],
        out_shape=[
            jax.ShapeDtypeStruct((rows, model), BF16),
            jax.ShapeDtypeStruct((rows, units), BF16),
        ],
        compiler_params=compiler_params(),
        cost_estimate=cost(2 * rows * model * units, 2 * model * units + 6 * rows * units),
        name="hidden_gradient",
    )(upstream, slope, weight_out)


def down_kernel(
    x_ref, gain_ref, up_ref, grad_ref, weight_ref, down_ref, half_ref, gain_grad_ref, total
):
    step = pl.program_id(0)

    @pl.when(step == 0)
    def _():
        total[...] = jnp.zeros_like(total)

    total[...] += dot(grad_ref[...], weight_ref[...], NT)

    @pl.when(step == pl.num_programs(0) - 1)
    def _():
        gain = gain_ref[...]
        normed, inverse = layer_norm(x_ref[...].astype(F32), gain)[1:]
        through, grad_gain = norm_back(total[...], normed, inverse, gain)
        down = up_ref[...] + through
        down_ref[...] = down.astype(down_ref.dtype)
        half_ref[...] = (0.5 * down).astype(BF16)
        gain_grad_ref[...] = grad_gain


def stream_gradient(upstream, stream, grad, gain_row, weight, down_type):
    rows, model = stream.shape
    units = weight.shape[1]
    wide = min(units, 1024)
    return pl.pallas_call(
        down_kernel,
        grid=(units // wide,),
        in_specs=[
            whole((rows, model)),
            whole((1, model)),
            whole((rows, model)),
            pl.BlockSpec((rows, wide), lambda s: (0, s)),
            pl.BlockSpec((model, wide), lambda s: (0, s)),
        ],
        out_specs=[whole((rows, model)), whole((rows, model)), whole((1, model))],
        out_shape=[
            jax.ShapeDtypeStruct((rows, model), down_type),
            jax.ShapeDtypeStruct((rows, model), BF16),
            jax.ShapeDtypeStruct((1, model), F32),
        ],
        scratch_shapes=[pltpu.VMEM((rows, model), F32)],
        compiler_params=compiler_params(),
        cost_estimate=cost(2 * rows * model * units, 2 * model * units + 2 * rows * units),
        name="stream_gradient",
    )(stream, gain_row, upstream, grad, weight)


def turn(field, cosines, sines, size):
    repeats = field.shape[1] // cosines.shape[1]
    cosines = jnp.concatenate([cosines] * repeats, 1)
    sines = jnp.concatenate([sines] * repeats, 1)
    lane = lax.broadcasted_iota(jnp.int32, field.shape, 1)
    half = size // 2
    width = field.shape[1]
    swapped = jnp.where(
        lane % size < half,
        pltpu.roll(field, width - half, 1),
        pltpu.roll(field, half, 1),
    )
    return field * cosines + swapped * sines


def rope_tables(position, size):
    half = size // 2
    lane = jnp.arange(LANES, dtype=jnp.int32)
    freqs = jnp.exp(
        -jnp.log(jnp.float32(ROPE_BASE)) * (lane % half).astype(jnp.float32) / half
    )
    angles = position.astype(jnp.float32)[:, None] * freqs[None, :]
    signs = jnp.where(lane % size < half, -1.0, 1.0)
    return (jnp.cos(angles), jnp.sin(angles) * signs[None, :])


def front_kernel(
    size, ffn_steps, pieces, row_ref, x_ref, gain_ref, win_ref, wout_ref,
    wq_ref, wk_ref, wv_ref, cos_ref, sin_ref, *refs,
):
    refs = refs[-(6 + pieces) :]
    out_ref, slope_ref, hid_ref, entered_ref, next_ref = refs[:5]
    outs, total = refs[5:-1], refs[-1]
    step = pl.program_id(0)

    @pl.when(step == 0)
    def _():
        gain = gain_ref[0:1, :]
        entered_ref[...] = layer_norm(x_ref[0].astype(F32), gain)[0].astype(BF16)
        total[...] = jnp.zeros_like(total)

    @pl.when(step < ffn_steps)
    def _():
        hidden, slope = hidden_units(dot(entered_ref[...], win_ref[...]))
        slope_ref[...] = slope
        hid_ref[...] = hidden
        total[...] += dot(hidden, wout_ref[...])

    @pl.when(step == ffn_steps)
    def _():
        out = x_ref[0].astype(F32) + 0.5 * total[...]
        out_ref[...] = out
        next_ref[...] = layer_norm(out, gain_ref[1:2, :])[0].astype(BF16)

    each = (pl.num_programs(0) - ffn_steps) // pieces
    for piece, out in enumerate(outs):

        @pl.when((step >= ffn_steps) & ((step - ffn_steps) // each == piece))
        def _():
            for place, weight in enumerate((wq_ref, wk_ref, wv_ref)):
                made = dot(next_ref[...], weight[...])
                if place < 2:
                    made = turn(made, cos_ref[...], sin_ref[...], size)
                made = made.astype(BF16)
                for target in range(out.shape[0]):
                    out[target, place, 0] = made[:, target * LANES : (target + 1) * LANES]


def front(
    frames, row, gains, weight_in, weight_out, weight, cosines, sines,
    places, chunks, size, before=(),
):
    given, rows, model = frames.shape
    units = weight_in.shape[1]
    wide = min(units, 1024)
    ffn_steps = units // wide
    turned_wide = TURNED
    turns = model // turned_wide
    pieces = model // (places * LANES)
    each = turns // pieces
    piece = jax.ShapeDtypeStruct((places, 3, chunks, rows, LANES), BF16)

    def ffn_at(s, row):
        return jnp.minimum(s, ffn_steps - 1)

    def turn_at(s):
        return jnp.maximum(s - ffn_steps, 0)

    def piece_at(number):
        return lambda s, row: (
            jnp.clip(s - ffn_steps - number * each, 0, each - 1), 0, row[0], 0, 0
        )

    row_block = pl.BlockSpec((rows, model), lambda s, row: (row[0], 0))
    unit_block = pl.BlockSpec((rows, wide), lambda s, row: (row[0], ffn_at(s, row)))
    angle_block = pl.BlockSpec((rows, LANES), lambda s, row: (row[0], 0))
    out_shape = [
        jax.ShapeDtypeStruct((chunks * rows, model), F32),
        jax.ShapeDtypeStruct((chunks * rows, units), BF16),
        jax.ShapeDtypeStruct((chunks * rows, units), BF16),
        jax.ShapeDtypeStruct((chunks * rows, model), BF16),
        jax.ShapeDtypeStruct((chunks * rows, model), BF16),
    ] + [piece] * pieces
    in_specs = [
        pl.BlockSpec((1, rows, model), lambda s, row: (row[0] if given > 1 else 0, 0, 0)),
        whole(gains.shape),
        pl.BlockSpec((model, wide), lambda s, row: (0, ffn_at(s, row))),
        pl.BlockSpec((wide, model), lambda s, row: (ffn_at(s, row), 0)),
        pl.BlockSpec((model, turned_wide), lambda s, row: (0, turn_at(s))),
        pl.BlockSpec((model, turned_wide), lambda s, row: (0, turns + turn_at(s))),
        pl.BlockSpec((model, turned_wide), lambda s, row: (0, 2 * turns + turn_at(s))),
        angle_block,
        angle_block,
    ]
    grid_spec = pltpu.PrefetchScalarGridSpec(
        num_scalar_prefetch=1,
        grid=(ffn_steps + turns,),
        in_specs=in_specs + [pl.BlockSpec(memory_space=pl.ANY)] * len(before),
        out_specs=[row_block, unit_block, unit_block, row_block, row_block]
        + [
            pl.BlockSpec((turned_wide // LANES, 3, 1, rows, LANES), piece_at(number))
            for number in range(pieces)
        ],
        scratch_shapes=[pltpu.VMEM((rows, model), F32)],
    )
    return pl.pallas_call(
        functools.partial(front_kernel, size, ffn_steps, pieces),
        grid_spec=grid_spec,
        out_shape=out_shape,
        input_output_aliases={1 + len(in_specs) + i: i for i in range(len(before))},
        compiler_params=compiler_params(),
        cost_estimate=cost(
            4 * rows * model * units + 6 * rows * model * model,
            4 * model * units + 6 * model * model + 4 * rows * units + 16 * rows * model,
        ),
        name="front",
    )(
        row, frames, gains, weight_in, weight_out, weight, weight, weight,
        cosines, sines, *before,
    )


def projection_kernel(
    size, pieces, cos_ref, sin_ref, x_ref, gain_ref, up_ref, weight_ref, *refs
):
    backs, refs = refs[:pieces], refs[pieces:]
    grad_ref, down_ref, half_ref, gain_grad_ref, total = refs
    step = pl.program_id(0)

    @pl.when(step == 0)
    def _():
        total[...] = jnp.zeros_like(total)

    rotated = step < 2
    cosines = jnp.where(rotated, cos_ref[...], 1.0)
    sines = jnp.where(rotated, -sin_ref[...], 0.0)
    places, _, chunks, frames, _ = backs[0].shape
    per = TURNED // LANES
    for piece, back in enumerate(backs):
        for first in range(0, places, per):
            for chunk in range(chunks):
                rows = slice(chunk * frames, (chunk + 1) * frames)
                field = jnp.concatenate([back[first + i, 0, chunk] for i in range(per)], 1)
                made = turn(field.astype(F32), cosines[rows], sines[rows], size).astype(BF16)
                start = (piece * places + first) * LANES
                grad_ref[rows, start : start + TURNED] = made
    total[...] += dot(grad_ref[...], weight_ref[...], NT)

    @pl.when(step == pl.num_programs(0) - 1)
    def _():
        gain = gain_ref[...]
        normed, inverse = layer_norm(x_ref[...], gain)[1:]
        through, grad_gain = norm_back(total[...], normed, inverse, gain)
        down = up_ref[...] + through
        down_ref[...] = down
        half_ref[...] = (0.5 * down).astype(BF16)
        gain_grad_ref[...] = grad_gain


def projection_backward(backs, cosines, sines, size, upstream, stream, gain_row, weight):
    places, kinds, chunks, frames, _ = backs[0].shape
    pieces = len(backs)
    rows, model = stream.shape
    block = pl.BlockSpec((places, 1, chunks, frames, LANES), lambda s: (0, s, 0, 0, 0))
    return pl.pallas_call(
        functools.partial(projection_kernel, size, pieces),
        grid=(kinds,),
        in_specs=[
            whole(cosines.shape),
            whole(sines.shape),
            whole((rows, model)),
            whole((1, model)),
            whole((rows, model)),
            pl.BlockSpec((model, model), lambda s: (0, s)),
        ]
        + [block] * pieces,
        out_specs=[
            pl.BlockSpec((rows, model), lambda s: (0, s)),
            whole((rows, model)),
            whole((rows, model)),
            whole((1, model)),
        ],
        out_shape=[
            jax.ShapeDtypeStruct((rows, kinds * model), BF16),
            jax.ShapeDtypeStruct((rows, model), F32),
            jax.ShapeDtypeStruct((rows, model), BF16),
            jax.ShapeDtypeStruct((1, model), F32),
        ],
        scratch_shapes=[pltpu.VMEM((rows, model), F32)],
        compiler_params=compiler_params(),
        cost_estimate=cost(6 * rows * model * model, 6 * model * model + 22 * rows * model),
        name="projection_backward",
    )(cosines, sines, stream, gain_row, upstream, weight, *backs)


def flipped(axis_bit, count):
    axis, bit = axis_bit
    items, heads = count
    if axis == "items":
        return [(i * heads + h, (i ^ bit) * heads + h) for i in range(items) for h in range(heads)]
    return [(i * heads + h, i * heads + (h ^ bit)) for i in range(items) for h in range(heads)]


def swap(value, axis_bit):
    count = (lax.axis_size("items"), lax.axis_size("heads"))
    return lax.ppermute(value, EVERY, flipped(axis_bit, count))


def branched(always, work):
    def empty():
        return jax.tree.map(lambda leaf: jnp.zeros(leaf.shape, leaf.dtype), jax.eval_shape(work))

    return lax.optimization_barrier(lax.cond(always, work, empty))


def fenced(always, scatters, work):
    def run():
        moves = [scatter.move() for scatter in scatters]
        return (branched(always, work) if any(moves) else work(), moves)

    result, moves = branched(always, run)
    for scatter, parts in zip(scatters, moves):
        scatter.take(parts)
    return result


def moved(scatter):
    scatter.take(scatter.move())


def other_core(value):
    return swap(value, ("heads", 1))


def exchange(value):
    half = lax.axis_size("heads") // 2
    groups = [[side * half + i for i in range(half)] for side in range(2)]
    return lax.all_to_all(
        value, "heads", split_axis=0, concat_axis=0, tiled=True, axis_index_groups=groups
    )


def across(value):
    return swap(value, ("heads", lax.axis_size("heads") // 2))


def gathered(own, other, side):
    return jnp.concatenate([jnp.where(side == 0, own, other), jnp.where(side == 0, other, own)], 0)


def parted(value, side):
    low, high = jnp.split(value, 2, 0)
    return (jnp.where(side == 0, low, high), jnp.where(side == 0, high, low))


def own_rows(left_ref, heads, core, target, first):
    rows, model = left_ref.shape
    each = model // heads
    for place in range(heads // 2):
        if each % LANES == 0:
            start = pl.multiple_of((2 * place + core) * each, each)
            mine = jnp.transpose(left_ref[:, pl.ds(start, each)].astype(F32)).astype(BF16)
        else:
            pair = left_ref[:, 2 * place * each : 2 * (place + 1) * each]
            pair = jnp.transpose(pair.astype(F32))
            mine = jnp.where(core == 0, pair[:each], pair[each:]).astype(BF16)
        for half in range(2):
            start = (half * (heads // 2) + place) * (each // 2)
            target[start : start + each // 2, first : first + rows] = mine[
                half * (each // 2) : (half + 1) * (each // 2)
            ]


def turned_items(left, items, own, target, first):
    rows, model = left.shape
    each = model // items
    for item in range(items):
        part = jnp.transpose(left[:, item * each : (item + 1) * each].astype(F32)).astype(BF16)
        place = pl.multiple_of((own ^ item) * each, each)
        target[pl.ds(place, each), first : first + rows] = part


def share_shapes(items, heads, model, columns):
    lead = 2 if items > 1 else 1
    shape = (lead, heads // 2, model // heads // 2, columns // items)
    return [jax.ShapeDtypeStruct(shape, BF16)] * (4 if items > 1 else 2)


def out_grad_kernel(place_ref, up_own, up_other, hid_own, hid_other, *refs):
    targets, turned = refs[:-1], refs[-1]
    rows, model = up_own.shape
    items = 4 if len(targets) == 4 else 1

    @pl.when(pl.program_id(0) == 0)
    def _():
        turned_items(up_own[...], items, place_ref[1], turned, 0)
        turned_items(up_other[...], items, place_ref[1], turned, rows)

    hidden = jnp.concatenate([hid_own[...], hid_other[...]], 0)
    grad = dot(turned[...], hidden).astype(BF16)
    wide = grad.shape[1]
    each = targets[0].shape[2]
    parts = model // items // (2 * each)
    for r in range(items):
        for part in range(parts):
            for half in range(2):
                first = ((r * parts + part) * 2 + half) * each
                piece = grad[first : first + each]
                if half == 0:
                    target, at = targets[2 * (r % 2)], r // 2
                else:
                    target, at = targets[1 + 2 * (r // 2)], r % 2
                target[at, 0, :, part * wide : (part + 1) * wide] = piece


def out_grad(upstream, hidden, heads, place, items):
    rows, model = upstream[0].shape
    units = hidden[0].shape[1]
    wide = units // heads
    shapes = share_shapes(items, heads, model, units)
    block = (shapes[0].shape[0], 1) + shapes[0].shape[2:]
    hid_block = pl.BlockSpec((rows, wide), lambda s, place: (0, 2 * s + place[0]))
    grid_spec = pltpu.PrefetchScalarGridSpec(
        num_scalar_prefetch=1,
        grid=(heads // 2,),
        in_specs=[whole((rows, model))] * 2 + [hid_block] * 2,
        out_specs=[pl.BlockSpec(block, lambda s, place: (0, s, 0, 0))] * len(shapes),
        scratch_shapes=[pltpu.VMEM((model, 2 * rows), BF16)],
    )
    return pl.pallas_call(
        out_grad_kernel,
        grid_spec=grid_spec,
        out_shape=shapes,
        compiler_params=compiler_params(),
        cost_estimate=cost(2 * rows * model * units, 2 * model * units + 4 * rows * units),
        name="out_grad",
    )(place, *upstream, *hidden)


def column_grad_kernel(heads, items, split, place_ref, *refs):
    count = len(split)
    lefts, refs = refs[: 2 * count], refs[2 * count :]
    rights, refs = refs[: 2 * (count + sum(split))], refs[2 * (count + sum(split)) :]
    targets, turned = refs[:-count], refs[-count:]
    r = pl.program_id(0)
    rows = lefts[0].shape[0]

    @pl.when(r == 0)
    def _():
        for number in range(count):
            for other in range(2):
                own_rows(
                    lefts[2 * number + other], heads, place_ref[0], turned[number], other * rows
                )

    made = []
    at = 0
    for number in range(count):
        right = jnp.concatenate([rights[at][...], rights[at + 1][...]], 0)
        at += 2
        if split[number]:
            second = jnp.concatenate([rights[at][...], rights[at + 1][...]], 0)
            at += 2
            right = jnp.where((r ^ place_ref[1]) < items // 2, right, second)
        made.append(dot(turned[number][...], right).astype(BF16))
    made = made[0] if count == 1 else jnp.concatenate(made, 1)
    half = made.shape[0] // 2
    top, low = made[:half].reshape(targets[0].shape), made[half:].reshape(targets[0].shape)
    if len(targets) == 2:
        targets[0][...] = top
        targets[1][...] = low
        return

    @pl.when(r % 2 == 0)
    def _():
        targets[0][...] = top

    @pl.when(r % 2 == 1)
    def _():
        targets[2][...] = top

    @pl.when(r < 2)
    def _():
        targets[1][...] = low

    @pl.when(r >= 2)
    def _():
        targets[3][...] = low


def column_grads(lefts, rights, heads, place, items):
    if items == 1:
        flat = [
            (left, part)
            for left, right in zip(lefts, rights)
            for part in (right if isinstance(right[0], tuple) else (right,))
        ]
        lefts, rights = [left for left, _ in flat], [right for _, right in flat]
    split = [isinstance(right[0], tuple) for right in rights]
    rows, model = lefts[0][0].shape
    parts = []
    for right, two in zip(rights, split):
        parts += [part for pair in right for part in pair] if two else list(right)
    columns = sum(part.shape[1] for part in parts) // 2
    shapes = share_shapes(items, heads, model, columns)
    block = (1,) + shapes[0].shape[1:]
    right_specs = []
    for right, two in zip(rights, split):
        if two:
            share = pl.BlockSpec(
                (rows, right[0][0].shape[1] * 2 // items),
                lambda r, place: (0, (r ^ place[1]) % (items // 2)),
            )
            right_specs += [share] * 4
        else:
            share = pl.BlockSpec(
                (rows, right[0].shape[1] // items), lambda r, place: (0, r ^ place[1])
            )
            right_specs += [share] * 2
    maps = [
        lambda r, place: (r // 2, 0, 0, 0),
        lambda r, place: (jnp.minimum(r, 1), 0, 0, 0),
        lambda r, place: (r // 3, 0, 0, 0),
        lambda r, place: (r // 3, 0, 0, 0),
    ]
    grid_spec = pltpu.PrefetchScalarGridSpec(
        num_scalar_prefetch=1,
        grid=(items,),
        in_specs=[whole((rows, model))] * (2 * len(lefts)) + right_specs,
        out_specs=[pl.BlockSpec(block, index) for index in maps[: len(shapes)]],
        scratch_shapes=[pltpu.VMEM((model // 2, 2 * rows), BF16)] * len(lefts),
    )
    return pl.pallas_call(
        functools.partial(column_grad_kernel, heads, items, split),
        grid_spec=grid_spec,
        out_shape=shapes,
        compiler_params=compiler_params(),
        cost_estimate=cost(2 * rows * model * columns, 4 * model * columns),
        name="column_grads",
    )(place, *[part for left in lefts for part in left], *parts)


class Scatter:
    def __init__(self, keep_top, keep_low, *sends):
        self.keep = [keep_top, keep_low]
        self.got, self.early = [], []
        self.route(list(sends), FIRST[: len(sends)])

    def route(self, sends, routes):
        self.sends, self.routes = sends, routes

    def move(self):
        return [swap(send, route) for send, route in zip(self.sends, self.routes)]

    def take(self, moved):
        self.early, self.got = self.got, moved
        self.route([], [])

    def second(self, sends):
        self.route(sends, FIRST[::-1][: len(sends)])


def second_kernel(*refs):
    count = len(refs) // 3
    for number in range(count):
        keep, got, out = refs[2 * number], refs[2 * number + 1], refs[2 * count + number]
        out[...] = (keep[0].astype(F32) + got[0].astype(F32)).astype(BF16)


def second_sums(*scatters):
    terms = [
        part
        for scatter in scatters
        if scatter.got
        for keep, got in zip(scatter.keep, scatter.got)
        for part in (keep, got)
    ]
    if not terms:
        return [[] for _ in scatters]
    shape = terms[0].shape
    outs = []
    in_specs, out_specs = [], []
    for term in terms:
        in_specs.append(
            pl.BlockSpec((1, 2) + term.shape[2:], lambda g: (1, g, 0, 0))
        )
    for term in terms[::2]:
        out_specs.append(pl.BlockSpec((2,) + term.shape[2:], lambda g: (g, 0, 0)))
        outs.append(jax.ShapeDtypeStruct(term.shape[1:], BF16))
    made = pl.pallas_call(
        second_kernel,
        grid=(shape[1] // 2,),
        in_specs=in_specs,
        out_specs=out_specs,
        out_shape=outs,
        compiler_params=compiler_params(),
        cost_estimate=cost(0, 6 * sum(out.size for out in outs)),
        name="second_sums",
    )(*terms)
    return [list(made[2 * i : 2 * i + 2]) for i in range(len(scatters))]


def last_kernel(*refs):
    out = refs[-1]
    for number in range(out.shape[1]):
        for half in range(2):
            terms = refs[6 * number + 3 * half : 6 * number + 3 * half + 3]
            out[:, number, half] = (
                terms[0][0].astype(F32) + terms[1][0].astype(F32) + terms[2][...].astype(F32)
            ).astype(BF16)


def last_sum(*scatters, columns=None):
    if not scatters[0].got:
        items = lax.axis_size("items")
        values = []
        for scatter in scatters:
            value = jnp.stack([keep[0] for keep in scatter.keep], 1)
            if columns is not None:
                starts = [sum(columns[:i]) for i in range(len(columns))]
                parts = [
                    value[..., start : start + size].reshape(value.shape[:3] + (items, -1))
                    for start, size in zip(starts, columns)
                ]
                value = jnp.concatenate(parts, 4).reshape(value.shape)
            values.append(lax.psum_scatter(value, "items", scatter_dimension=3, tiled=True))
        return jnp.stack(values, 1)
    terms = [
        part
        for scatter in scatters
        for parts in zip(scatter.keep, scatter.early, scatter.got)
        for part in parts
    ]
    _, places, rows, wide = terms[0].shape
    held = pl.BlockSpec((1, 2, rows, wide), lambda g: (0, g, 0, 0))
    late = pl.BlockSpec((2, rows, wide), lambda g: (g, 0, 0))
    shape = (places, len(scatters), 2, rows, wide)
    return pl.pallas_call(
        last_kernel,
        grid=(places // 2,),
        in_specs=[held, held, late] * (2 * len(scatters)),
        out_specs=pl.BlockSpec((2,) + shape[1:], lambda g: (g, 0, 0, 0, 0)),
        out_shape=jax.ShapeDtypeStruct(shape, BF16),
        compiler_params=compiler_params(),
        cost_estimate=cost(0, 8 * places * len(scatters) * 2 * rows * wide),
        name="last_sum",
    )(*terms)


def along_z(value):
    heads = lax.axis_size("heads")
    groups = [[core + 2 * z for z in range(heads // 2)] for core in range(2)]
    made = lax.psum_scatter(
        value, "heads", scatter_dimension=0, tiled=False, axis_index_groups=groups
    )
    return [made[i].reshape(-1, made.shape[-1]) for i in range(made.shape[0])]


def unfold_kernel(share_ref, out_ref):
    each = share_ref.shape[0]
    span = out_ref.shape[0]
    for part in range(share_ref.shape[1] // span):
        turned = jnp.transpose(share_ref[:, part * span : (part + 1) * span].astype(F32))
        out_ref[:, part * each : (part + 1) * each] = turned


def unfolded(share, span):
    each, wide = share.shape
    shape = (span, each * wide // span)
    return pl.pallas_call(
        unfold_kernel,
        out_shape=jax.ShapeDtypeStruct(shape, F32),
        cost_estimate=cost(0, 6 * each * wide),
        name="unfolded",
    )(share)


def heads_kernel(grad_ref, weight_ref, *outs):
    step = pl.program_id(0)
    made = dot(grad_ref[...], weight_ref[...], NT).astype(BF16)
    for piece, out in enumerate(outs):

        @pl.when(step == piece)
        def _():
            places, chunks, frames, _ = out.shape
            for place in range(places):
                for chunk in range(chunks):
                    out[place, chunk] = made[
                        chunk * frames : (chunk + 1) * frames, place * LANES : (place + 1) * LANES
                    ]


def heads_gradient(grad, weight, places, chunks):
    rows, model = grad.shape
    wide = places * LANES
    pieces = model // wide
    shape = (places, chunks, rows // chunks, LANES)
    return pl.pallas_call(
        heads_kernel,
        grid=(pieces,),
        in_specs=[whole((rows, model)), pl.BlockSpec((wide, model), lambda s: (s, 0))],
        out_specs=[whole(shape)] * pieces,
        out_shape=[jax.ShapeDtypeStruct(shape, BF16)] * pieces,
        compiler_params=compiler_params(),
        cost_estimate=cost(2 * rows * model * model, 2 * model * model + 4 * rows * model),
        name="heads_gradient",
    )(grad, weight)


def sum_everywhere(value):
    for axis in EVERY:
        bit = 1
        while bit < lax.axis_size(axis):
            value = value + swap(value, (axis, bit))
            bit *= 2
    return value


def edges(block, width):
    ways = lax.axis_size("heads")
    half = ways // 2
    place = lax.axis_index("heads") % half
    ring = [(side * half + i, side * half + (i + 1) % half) for side in range(2) for i in range(half)]
    low = lax.ppermute(block[:, block.shape[1] - width :], "heads", ring)
    high = lax.ppermute(block[:, :width], "heads", [(to, at) for at, to in ring])
    low = jnp.where(place == 0, jnp.roll(low, 1, 0), low)
    high = jnp.where(place == half - 1, jnp.roll(high, -1, 0), high)
    return jnp.concatenate([low, block, high], axis=1)


def body(
    frames, cotangent, bucket_counts, gains, w_ffn1_in, w_ffn1_out, w_qkv, w_out,
    w_point_in, w_depth, w_point_out, w_ffn2_in, w_ffn2_out,
):
    chunks, here, model = frames.shape
    ways = lax.axis_size("heads")
    half = ways // 2
    items = 4 if lax.axis_size("items") == 4 else 1
    span = here * half
    group_len = here * ways
    size = model // HEADS
    reach = (KERNEL - 1) // 2
    rows = chunks * here
    pieces = model // (half * LANES)
    place = lax.axis_index("heads")
    side = place // half
    where = jnp.stack(
        [place % 2, lax.axis_index("items") if items > 1 else 0 * place]
    ).astype(jnp.int32)
    always = place >= 0
    first = jnp.arange(chunks, dtype=jnp.int32)[:, None] * span + place % half * here
    position = first + jnp.arange(here, dtype=jnp.int32)[None]
    cosines, sines = rope_tables(position.reshape(-1), size)
    depth_rows = w_depth.astype(F32)
    gain = [gains[i : i + 1] for i in range(6)]
    counts = lax.dynamic_index_in_dim(bucket_counts[:, 0], side, 0, keepdims=False)
    wide_position = first - reach + jnp.arange(here + 2 * reach, dtype=jnp.int32)[None]
    seg_wide = segment_ids(wide_position, counts[0], counts[1], group_len)
    seg_own = seg_wide[:, reach : reach + here]

    def mine(value):
        return lax.dynamic_index_in_dim(value, side, 0, keepdims=False)

    def theirs(value):
        return lax.dynamic_index_in_dim(value, 1 - side, 0, keepdims=False)

    def begin(chunk, row, before=()):
        return front(
            chunk, row.reshape(1).astype(jnp.int32), gains, w_ffn1_in, w_ffn1_out, w_qkv,
            cosines, sines, half, chunks, size, before,
        )

    before, other_frames = fenced(
        always, (), lambda: (begin(frames, side), across(theirs(frames)))
    )
    stream_one, slope_one, hid_one, ent_one, ent_att, *sent = begin(
        other_frames[None], 1 - side, before
    )
    stream = gathered(mine(frames), other_frames, side)
    qkv = [exchange(sent[0])]
    kept, contexts = [], []
    for number in range(pieces):

        def attend_now():
            return attend_forward(qkv[number], counts, size)

        def beside():
            extra = []
            if number + 1 < pieces:
                extra.append(exchange(sent[number + 1]))
            if number > 0:
                extra.append(exchange(kept[number - 1][0]))
            return extra

        def early():
            if number == 0:
                return [other_core(part) for part in (hid_one, ent_one, ent_att)]
            return [across(theirs(cotangent))] if number == 1 else []

        made, extra, others = fenced(always, (), lambda: (attend_now(), beside(), early()))
        kept.append(made)
        if number == 0:
            hid_one, ent_one, ent_att = zip((hid_one, ent_one, ent_att), others)
        elif number == 1:
            cot_other = others[0]
        if number + 1 < pieces:
            qkv.append(extra.pop(0))
        if number > 0:
            contexts.append(extra.pop(0))
    contexts.append(exchange(kept[-1][0]))
    if pieces == 1:
        cot_other = across(theirs(cotangent))
    fulls = [made[1] for made in kept]
    lses = [made[2] for made in kept]
    contexts = [part.transpose(1, 2, 0, 3).reshape(rows, -1) for part in contexts]
    context = jnp.concatenate(contexts, 1)
    stream_two = stream_one
    for number, part in enumerate(contexts):
        wide = part.shape[1]
        stream_two = stream_two + dot(part, w_out[number * wide : (number + 1) * wide])
    shaped, conv_normed, conv_inverse = layer_norm(stream_two, gain[2])
    conv_entered = shaped.astype(BF16)
    pointwise = dot(conv_entered, w_point_in)
    linear = pointwise[:, :model]
    sigmoid_gate = jax.nn.sigmoid(pointwise[:, model:])
    gated_low = (linear * sigmoid_gate).astype(BF16).reshape(chunks, here, model)
    widened = edges(gated_low, reach)
    depth_out = jnp.zeros((chunks, here, model), F32)
    for offset in range(KERNEL):
        same = (seg_wide[:, offset : offset + here] == seg_own)[:, :, None]
        depth_out = depth_out + depth_rows[offset] * jnp.where(
            same, widened[:, offset : offset + here], 0.0
        )
    depth_out = depth_out.reshape(rows, model)
    depth_shaped, depth_normed, depth_inverse = layer_norm(depth_out, gain[3])
    mixed_low = (depth_shaped * jax.nn.sigmoid(depth_shaped)).astype(BF16)
    stream_three = stream_two + dot(mixed_low, w_point_out)
    layer_out, grad_four, gain_five, slope_two, hid_two, ent_two = ffn_forward(
        stream_three, gain[4], w_ffn2_in, w_ffn2_out, gain[5],
        gathered(mine(cotangent), cot_other, side),
    )
    (grad_three, gain_four, half_two, grad_pre_two), hid_other, ent_other = fenced(
        always,
        (),
        lambda: (
            ffn_backward(grad_four, stream_three, slope_two, gain[4], w_ffn2_in, w_ffn2_out),
            other_core(hid_two),
            other_core(ent_two),
        ),
    )
    half_other, grad_pre_other = other_core(half_two), other_core(grad_pre_two)
    grad_mix = grad_three.astype(BF16)
    grad_norm_in = dot(grad_mix, w_point_out, NT) * silu_slope(depth_shaped)
    grad_depth, gain_three = norm_back(grad_norm_in, depth_normed, depth_inverse, gain[3])
    grad_depth_low = grad_depth.astype(BF16).reshape(chunks, here, model)
    grad_widened = edges(grad_depth_low, reach)
    grad_gated = jnp.zeros((chunks, here, model), F32)
    for offset in range(KERNEL):
        mirror = 2 * reach - offset
        same_back = (seg_wide[:, mirror : mirror + here] == seg_own)[:, :, None]
        grad_gated = grad_gated + depth_rows[offset] * jnp.where(
            same_back, grad_widened[:, mirror : mirror + here], 0.0
        )
    grad_gated = grad_gated.reshape(rows, model)
    grad_a = (grad_gated * sigmoid_gate).astype(BF16)
    grad_b = (grad_gated * linear * sigmoid_gate * (1.0 - sigmoid_gate)).astype(BF16)
    through, gain_two = norm_back(
        dot(grad_a, w_point_in[:, :model], NT) + dot(grad_b, w_point_in[:, model:], NT),
        conv_normed, conv_inverse, gain[2],
    )
    grad_two = grad_three + through
    grad_attn_out = grad_two.astype(BF16)
    grad_heads = list(heads_gradient(grad_attn_out, w_out, half, chunks))
    lefts = (mixed_low, conv_entered, context)

    def ffn_grads():
        return (
            [other_core(part) for part in lefts + (grad_a, grad_b)],
            exchange(grad_heads[0]),
            out_grad((half_two, half_other), (hid_two, hid_other), ways, where, items),
            column_grads(
                [(ent_two, ent_other)], [(grad_pre_two, grad_pre_other)], ways, where, items
            ),
        )

    others, grad_heads[0], shares_out, shares_in = fenced(always, (), ffn_grads)
    two_out, two_in = Scatter(*shares_out), Scatter(*shares_in)
    out_own, out_theirs = parted(layer_out, side)
    grads, backs = [], []
    for number in range(pieces):
        last = number == pieces - 1

        def beside():
            extra = []
            if not last:
                extra.append(exchange(grad_heads[number + 1]))
            if number > 0:
                extra.append(exchange(grads[number - 1]))
            if number == 0:
                extra.append(across(out_theirs))
                extra += [other_core(grad_mix), other_core(grad_attn_out)]
            return extra

        def attend_now():
            return attend_backward(
                qkv[number], counts, size, fulls[number], lses[number], grad_heads[number]
            )

        moving = (two_out,) if number == 0 else (two_out, two_in) if number == 1 else ()
        made, extra = fenced(always, moving, lambda: (attend_now(), beside()))
        grads.append(made)
        if not last:
            grad_heads[number + 1] = extra.pop(0)
        if number > 0:
            backs.append(extra.pop(0))
        if number == 0:
            out_other, *late = extra
            two_out.second(second_sums(two_out)[0])
    two_in.second(second_sums(two_in)[0])

    def middle_part():
        back = exchange(grads[-1])
        scatter = copy.copy(two_in)
        moved(scatter)
        shares = column_grads(
            list(zip(lefts, others[:3])),
            [
                (grad_mix, late[0]),
                ((grad_a, others[3]), (grad_b, others[4])),
                (grad_attn_out, late[1]),
            ],
            ways, where, items,
        )
        return (back, shares, last_sum(two_out, scatter))

    back, shares, two_sum = fenced(always, (), middle_part)
    backs.append(back)
    middle = Scatter(*shares)

    def attention_part():
        two_grads = along_z(two_sum)
        scatter = copy.copy(middle)

        def projection_part():
            grad_proj, *down = projection_backward(
                backs, cosines, sines, size, grad_two, stream_one, gain[1], w_qkv
            )
            return ((grad_proj, other_core(grad_proj)), down)

        grad_proj, (grad_one, half_one, gain_one) = fenced(always, (scatter,), projection_part)
        first = scatter.got
        scatter.second(second_sums(scatter)[0])

        def qkv_part():
            half_other = other_core(half_one)
            return (half_other, column_grads([ent_att], [grad_proj], ways, where, items))

        half_other, shares = fenced(always, (scatter,), qkv_part)
        attn = Scatter(*shares)

        def hidden_part():
            half_own, grad_pre = hidden_gradient(grad_one, slope_one, w_ffn1_out)
            shares = out_grad((half_own, half_other), hid_one, ways, where, items)
            return (grad_pre, shares)

        grad_pre, shares_out = fenced(always, (attn,), hidden_part)
        return (
            two_grads, first, scatter.got, (grad_one, gain_one), shares[:2], attn.got,
            grad_pre, shares_out,
        )

    two_grads, first, got, (grad_one, gain_one), shares, attn_got, grad_pre, shares_out = fenced(
        always, (), attention_part
    )
    middle.take(first)
    middle.take(got)
    attn = Scatter(*shares)
    attn.take(attn_got)
    attn.second(second_sums(attn)[0])
    one_out = Scatter(*shares_out)
    middle_columns = [w.shape[1] for w in (w_point_out, w_point_in, w_out)]
    def input_part():
        middle_grad = along_z(last_sum(middle, columns=middle_columns))
        grad_zero, _, gain_zero = stream_gradient(
            grad_one, stream, grad_pre, gain[0], w_ffn1_in, BF16
        )
        shares = column_grads([ent_one], [(grad_pre, other_core(grad_pre))], ways, where, items)
        return (middle_grad, shares, parted(grad_zero, side), gain_zero)

    middle_grad, shares, (grad_own, grad_theirs), gain_zero = fenced(
        always, (one_out, attn), input_part
    )
    one_in = Scatter(*shares)
    one_out.second(second_sums(one_out)[0])
    hidden = w_ffn1_in.shape[1]

    def tap_sums_here():
        rows_of = []
        for offset in range(KERNEL):
            same = (seg_wide[:, offset : offset + here] == seg_own)[:, :, None]
            product = grad_depth_low.astype(F32) * widened[:, offset : offset + here]
            rows_of.append(jnp.sum(jnp.where(same, product, 0.0), (0, 1))[None])
        return rows_of

    def last_part():
        grad_other = across(grad_theirs)
        attn_grad = along_z(last_sum(attn))
        out, scatter = copy.copy(one_out), copy.copy(one_in)
        fenced(always, (out,), lambda: ())
        out_grads = along_z(last_sum(out))
        fenced(always, (scatter,), lambda: ())
        scatter.second(second_sums(scatter)[0])
        fenced(always, (scatter,), lambda: ())
        last, grad_other = branched(
            always,
            lambda: (last_sum(scatter), grad_other),
        )
        small = sum_everywhere(
            jnp.concatenate(
                [gain_zero, gain_one, gain_two, gain_three, gain_four, gain_five]
                + tap_sums_here(),
                0,
            )
        )
        middle_parts = []
        start = 0
        for columns in middle_columns:
            each = columns // lax.axis_size("items")
            middle_parts.append(middle_grad[0][:, start : start + each].astype(F32))
            start += each
        ready = (
            gathered(out_own[None], out_other[None], side),
            gathered(grad_own[None], grad_other[None], side),
            attn_grad[0].astype(F32),
            middle_parts,
            two_grads[1].astype(F32),
            unfolded(two_grads[0], hidden // ways),
            unfolded(out_grads[0], hidden // ways),
        )
        return (along_z(last), small[:6], small[6:], ready)

    one_in_grad, gain_sums, tap_sums, ready = fenced(always, (), last_part)
    out, grad_in, attn_full, middle_parts, two_in_full, two_out_full, one_out_full = ready
    return (
        out,
        grad_in,
        gain_sums,
        one_in_grad[0].astype(F32),
        one_out_full,
        attn_full,
        middle_parts[2],
        middle_parts[1],
        tap_sums,
        middle_parts[0],
        two_in_full,
        two_out_full,
    )


def solution(mesh):
    split = P(None, EVERY, None)
    shares = P("heads", "items")
    in_specs = (split, split, P(None, "items", None)) + (P(),) * 10
    out_specs = (split, split, P(), shares, shares, shares, shares, shares, P()) + (shares,) * 3
    return jax.shard_map(body, mesh=mesh, in_specs=in_specs, out_specs=out_specs, check_vma=False)
```

```python
import copy
import functools

import jax
import jax.numpy as jnp
from jax import lax
from jax.experimental import pallas as pl
from jax.experimental.pallas import tpu as pltpu
from jax.sharding import PartitionSpec as P

HEADS = 16
KERNEL = 5
LONG = 1500
SHORT = 500
EPS = 1e-05
ROPE_BASE = 10000.0
BLOCK = 512
INNER_FWD = 1024
INNER_BWD = 512
TURNED = 512
LANES = 128
BIG = 1e30
VMEM_LIMIT = 56 << 20
F32 = jnp.float32
BF16 = jnp.bfloat16
NN = (((1,), (0,)), ((), ()))
NT = (((1,), (1,)), ((), ()))
EVERY = ("items", "heads")
FIRST = [("items", 1), ("items", 2)]


def dot(left, right, dims=NN):
    return lax.dot_general(left, right, dims, preferred_element_type=F32)


def silu_slope(field):
    gate_sig = jax.nn.sigmoid(field)
    return gate_sig * (1.0 + field * (1.0 - gate_sig))


def layer_norm(field, gain_row):
    centred = field - jnp.mean(field, -1, keepdims=True)
    inverse = lax.rsqrt(jnp.mean(centred * centred, -1, keepdims=True) + EPS)
    normed = centred * inverse
    return (normed * gain_row, normed, inverse)


def norm_back(upstream, normed, inverse, gain_row):
    scaled = upstream * gain_row
    through = inverse * (
        scaled
        - jnp.mean(scaled, -1, keepdims=True)
        - normed * jnp.mean(scaled * normed, -1, keepdims=True)
    )
    return (through, jnp.sum(upstream * normed, 0, keepdims=True))


def segment_ids(position, long_count, short_count, group_len):
    long_end = long_count * LONG
    short_end = long_end + short_count * SHORT
    segments = jnp.where(
        position < long_end, position // LONG, long_count + (position - long_end) // SHORT
    )
    segments = jnp.where(position < short_end, segments, long_count + short_count)
    return jnp.where((position < 0) | (position >= group_len), -1, segments)


def compiler_params():
    return pltpu.CompilerParams(vmem_limit_bytes=VMEM_LIMIT)


def whole(shape):
    return pl.BlockSpec(shape, lambda *_: (0,) * len(shape))


def cost(flops, bytes_accessed, transcendentals=0):
    return pl.CostEstimate(
        flops=flops, bytes_accessed=bytes_accessed, transcendentals=transcendentals
    )


def segment_bounds(counts, place, group):
    longs, shorts = counts
    long_end = longs * LONG
    short_end = long_end + shorts * SHORT
    start = jnp.where(place < longs, place * LONG, long_end + (place - longs) * SHORT)
    size = jnp.where(place < longs, LONG, SHORT)
    last = place == longs + shorts
    return (jnp.where(last, short_end, start), jnp.where(last, group, start + size), place <= longs + shorts)


def member_lanes(counts, first, rows, group, shift=0):
    shape = (rows, LANES)
    place = lax.broadcasted_iota(jnp.int32, (8, LANES), 1) - shift
    start, end, there = segment_bounds(counts, place, group)
    start = jnp.where(there & (place >= 0), start, group)
    start, end = start[:1], end[:1]
    frame = first + lax.broadcasted_iota(jnp.int32, shape, 0)
    return (frame >= start) & (frame < end)


def block_range(counts, step, group, inner):
    longs, shorts = counts
    long_end = longs * LONG
    short_end = long_end + shorts * SHORT

    def number(frame):
        place = jnp.where(frame < long_end, frame // LONG, longs + (frame - long_end) // SHORT)
        return jnp.where(frame < short_end, place, longs + shorts)

    first = segment_bounds(counts, number(step * BLOCK), group)[0]
    last = segment_bounds(counts, number(step * BLOCK + BLOCK - 1), group)[1]
    return (first // inner, (last + inner - 1) // inner)


def head_lanes(shape, head, size):
    lane = lax.broadcasted_iota(jnp.int32, shape, 1)
    return (lane >= head * size) & (lane < (head + 1) * size)


def split_three(v):
    hi = v.astype(BF16).astype(F32)
    rest = v - hi
    mid = rest.astype(BF16).astype(F32)
    return (hi, mid, rest - mid)


def spread_columns(columns, shape):
    lane = lax.broadcasted_iota(jnp.int32, shape, 1)
    out = jnp.zeros(shape, F32)
    for place, column in enumerate(columns):
        out = jnp.where(lane == place, column, out)
    return out


def chunk_rows(ref, lead, step):
    places, chunks, frames = ref.shape[0], ref.shape[-3], ref.shape[-2]
    per = BLOCK // frames
    steps = places // per
    at = (pl.ds(step % steps * per, per),) + lead + (step // steps,)
    return ref[at].reshape(BLOCK, LANES)


def attn_fwd_kernel(
    heads, size, group, counts_ref, qkv_ref, out_ref, full_ref, lse_ref, kcat, v_all, s_scr
):
    step = pl.program_id(0)
    counts = (counts_ref[0], counts_ref[1])

    @pl.when(step == 0)
    def _():
        chunks = qkv_ref.shape[2]
        span = group // chunks
        for chunk in range(chunks):
            rows = slice(chunk * span, (chunk + 1) * span)
            kcat[rows, :LANES] = qkv_ref[:, 1, chunk].reshape(span, LANES)
            v_all[rows, :] = qkv_ref[:, 2, chunk].reshape(span, LANES)
        kcat[:, LANES:] = jnp.where(member_lanes(counts, 0, group, group), 0.0, -BIG).astype(BF16)

    q = chunk_rows(qkv_ref, (0,), step).astype(F32) * (size ** -0.5)
    member = jnp.where(member_lanes(counts, step * BLOCK, BLOCK, group), 1.0, 0.0).astype(BF16)
    queries = []
    for head in range(heads):
        mine = jnp.where(head_lanes(q.shape, head, size), q, 0.0).astype(BF16)
        queries.append(jnp.concatenate([mine, member], 1))
    low, high = block_range(counts, step, group, INNER_FWD)

    def scores(j, tops):
        keys = kcat[pl.ds(pl.multiple_of(j * INNER_FWD, INNER_FWD), INNER_FWD), :]
        new = []
        for head in range(heads):
            s = dot(queries[head], keys, NT)
            s_scr[head, j] = s
            top = tops[head]
            for part in range(INNER_FWD // LANES):
                top = jnp.maximum(top, s[:, part * LANES : (part + 1) * LANES])
            new.append(top)
        return tuple(new)

    start = tuple(jnp.full((BLOCK, LANES), -BIG, F32) for _ in range(heads))
    tops = lax.fori_loop(low, high, scores, start)
    tops = [jnp.max(t, 1, keepdims=True) for t in tops]
    tops = [jnp.broadcast_to(t, (BLOCK, LANES)) for t in tops]

    def weigh(j, carried):
        sums, accs = carried
        values = v_all[pl.ds(pl.multiple_of(j * INNER_FWD, INNER_FWD), INNER_FWD), :]
        new_sums, new_accs = [], []
        for head in range(heads):
            total = sums[head]
            parts = []
            for part in range(INNER_FWD // LANES):
                p = jnp.exp(s_scr[head, j, :, part * LANES : (part + 1) * LANES] - tops[head])
                total = total + p
                parts.append(p.astype(BF16))
            new_sums.append(total)
            new_accs.append(accs[head] + dot(jnp.concatenate(parts, 1), values))
        return (tuple(new_sums), tuple(new_accs))

    zeros = tuple(jnp.zeros((BLOCK, LANES), F32) for _ in range(heads))
    sums, accs = lax.fori_loop(low, high, weigh, (zeros, zeros))
    result = None
    lane = lax.broadcasted_iota(jnp.int32, (BLOCK, LANES), 1)
    shifted = jnp.where(member_lanes(counts, step * BLOCK, BLOCK, group, 3), 1.0, 0.0)
    for head in range(heads):
        total = jnp.sum(sums[head], 1, keepdims=True)
        mine = accs[head] / total
        if result is None:
            result = mine
        else:
            result = jnp.where(head_lanes(mine.shape, head, size), mine, result)
        lse = tops[head] + jnp.log(jnp.broadcast_to(total, (BLOCK, LANES)))
        spread = spread_columns(split_three(lse), (BLOCK, LANES))
        lse_ref[head] = jnp.where(lane < 3, -spread, shifted).astype(BF16)
    full_ref[...] = result
    out_ref[...] = result.astype(BF16).reshape(out_ref.shape)


def attend_forward(qkv, counts, size):
    places, _, chunks, frames, _ = qkv.shape
    group = places * chunks * frames
    heads = LANES // size
    per = BLOCK // frames
    each = places // per
    return pl.pallas_call(
        functools.partial(attn_fwd_kernel, heads, size, group),
        grid=(group // BLOCK,),
        in_specs=[pl.BlockSpec(memory_space=pltpu.SMEM), whole(qkv.shape)],
        out_specs=[
            pl.BlockSpec((per, 1, frames, LANES), lambda i: (i % each, i // each, 0, 0)),
            pl.BlockSpec((BLOCK, LANES), lambda i: (i, 0)),
            pl.BlockSpec((heads, BLOCK, LANES), lambda i: (0, i, 0)),
        ],
        out_shape=[
            jax.ShapeDtypeStruct((places, chunks, frames, LANES), BF16),
            jax.ShapeDtypeStruct((group, LANES), F32),
            jax.ShapeDtypeStruct((heads, group, LANES), BF16),
        ],
        scratch_shapes=[
            pltpu.VMEM((group, 2 * LANES), BF16),
            pltpu.VMEM((group, LANES), BF16),
            pltpu.VMEM((heads, group // INNER_FWD, BLOCK, INNER_FWD), F32),
        ],
        compiler_params=compiler_params(),
        cost_estimate=cost(16 * group * group * LANES, 6 << 20, heads * group * group),
        name="attend_forward",
    )(counts, qkv)


def attn_bwd_kernel(
    heads, size, group, counts_ref, qkv_ref, full_ref, lse_ref, grad_ref, out_ref,
    qcat, gcat, k_turned, dq_turned,
):
    step = pl.program_id(0)
    counts = (counts_ref[0], counts_ref[1])
    blocks = group // BLOCK
    places, _, _, frames, _ = qkv_ref.shape
    per = BLOCK // frames
    each = places // per

    def put(part, j, value):
        out_ref[pl.ds(j % each * per, per), part, j // each] = value.astype(BF16).reshape(
            per, frames, LANES
        )

    @pl.when(step == 0)
    def _():
        dq_turned[...] = jnp.zeros_like(dq_turned)

        def prepare(j, _):
            rows = pl.ds(pl.multiple_of(j * BLOCK, BLOCK), BLOCK)
            q = chunk_rows(qkv_ref, (0,), j).astype(F32) * (size ** -0.5)
            g = chunk_rows(grad_ref, (), j).astype(F32)
            product = g * full_ref[rows, :]
            for head in range(heads):
                own = head_lanes((BLOCK, LANES), head, size)
                delta = jnp.sum(jnp.where(own, product, 0.0), 1, keepdims=True)
                delta = jnp.broadcast_to(delta, (BLOCK, LANES))
                qcat[head, rows, :LANES] = jnp.where(own, q, 0.0).astype(BF16)
                qcat[head, rows, LANES:] = lse_ref[head, rows, :]
                gcat[head, rows, :LANES] = jnp.where(own, g, 0.0).astype(BF16)
                spread = spread_columns(split_three(delta), (BLOCK, LANES))
                gcat[head, rows, LANES:] = (-spread).astype(BF16)
            k = chunk_rows(qkv_ref, (1,), j).astype(F32)
            k_turned[j] = jnp.transpose(k).astype(BF16)
            return 0

        lax.fori_loop(0, blocks, prepare, 0)

    lane = lax.broadcasted_iota(jnp.int32, (BLOCK, LANES), 1)
    member = member_lanes(counts, step * BLOCK, BLOCK, group, 3)
    tail = jnp.where(lane < 3, 1.0, jnp.where(member, 0.0, -BIG)).astype(BF16)
    keys = jnp.concatenate([chunk_rows(qkv_ref, (1,), step), tail], 1)
    ones = jnp.where(lane < 3, 1.0, 0.0).astype(BF16)
    values = jnp.concatenate([chunk_rows(qkv_ref, (2,), step), ones], 1)

    def one(j, carried):
        dk, dv = carried
        cols = pl.ds(pl.multiple_of(j * INNER_BWD, INNER_BWD), INNER_BWD)
        for head in range(heads):
            qc = qcat[head, cols, :]
            gc = gcat[head, cols, :]
            p = jnp.exp(dot(keys, qc, NT))
            ds = (p * dot(values, gc, NT)).astype(BF16)
            dv = dv + dot(p.astype(BF16), gc[:, :LANES])
            dk = dk + dot(ds, qc[:, :LANES])
            mine = slice(head * size, (head + 1) * size)
            dq_turned[j, mine, :] += dot(k_turned[step, mine, :], ds)
        return (dk, dv)

    zero = jnp.zeros((BLOCK, LANES), F32)
    low, high = block_range(counts, step, group, INNER_BWD)
    dk, dv = lax.fori_loop(low, high, one, (zero, zero))
    put(1, step, dk)
    put(2, step, dv)

    @pl.when(step == blocks - 1)
    def _():
        def finish(j, _):
            put(0, j, jnp.transpose(dq_turned[j]) * (size ** -0.5))
            return 0

        lax.fori_loop(0, blocks, finish, 0)


def attend_backward(qkv, counts, size, full, lse, grad):
    places, _, chunks, frames, _ = qkv.shape
    group = places * chunks * frames
    heads = LANES // size
    steps = group // BLOCK
    return pl.pallas_call(
        functools.partial(attn_bwd_kernel, heads, size, group),
        grid=(steps,),
        in_specs=[
            pl.BlockSpec(memory_space=pltpu.SMEM),
            whole(qkv.shape),
            whole(full.shape),
            whole(lse.shape),
            whole(grad.shape),
        ],
        out_specs=whole(qkv.shape),
        out_shape=jax.ShapeDtypeStruct(qkv.shape, BF16),
        scratch_shapes=[
            pltpu.VMEM((heads, group, 2 * LANES), BF16),
            pltpu.VMEM((heads, group, 2 * LANES), BF16),
            pltpu.VMEM((steps, LANES, BLOCK), BF16),
            pltpu.VMEM((group // INNER_BWD, LANES, INNER_BWD), F32),
        ],
        compiler_params=compiler_params(),
        cost_estimate=cost(32 * group * group * LANES, 9 << 20, heads * group * group),
        name="attend_backward",
    )(counts, qkv, full, lse, grad)


def half_gate(field):
    return 0.5 * jnp.tanh(0.5 * field) + 0.5


def hidden_units(pre):
    gate = half_gate(pre)
    hidden = pre * gate
    return (hidden.astype(BF16), (gate + hidden * (1.0 - gate)).astype(BF16))


def ffn_fwd_kernel(
    x_ref, gain_ref, last_gain_ref, up_ref, win_ref, wout_ref,
    out_ref, down_ref, gain_grad_ref, slope_ref, hid_ref, entered_ref, total,
):
    step = pl.program_id(0)

    @pl.when(step == 0)
    def _():
        entered_ref[...] = layer_norm(x_ref[...], gain_ref[...])[0].astype(BF16)
        total[...] = jnp.zeros_like(total)

    hidden, slope = hidden_units(dot(entered_ref[...], win_ref[...]))
    slope_ref[...] = slope
    hid_ref[...] = hidden
    total[...] += dot(hidden, wout_ref[...])

    @pl.when(step == pl.num_programs(0) - 1)
    def _():
        gain = last_gain_ref[...]
        shaped, normed, inverse = layer_norm(x_ref[...] + 0.5 * total[...], gain)
        out_ref[...] = shaped.astype(BF16)
        through, grad_gain = norm_back(up_ref[...].astype(F32), normed, inverse, gain)
        down_ref[...] = through
        gain_grad_ref[...] = grad_gain


def ffn_forward(stream, gain_row, weight_in, weight_out, last_gain, upstream):
    rows, model = stream.shape
    units = weight_in.shape[1]
    wide = min(units, 1024)
    return pl.pallas_call(
        ffn_fwd_kernel,
        grid=(units // wide,),
        in_specs=[
            whole((rows, model)),
            whole((1, model)),
            whole((1, model)),
            whole((rows, model)),
            pl.BlockSpec((model, wide), lambda s: (0, s)),
            pl.BlockSpec((wide, model), lambda s: (s, 0)),
        ],
        out_specs=[whole((rows, model)), whole((rows, model)), whole((1, model))]
        + [pl.BlockSpec((rows, wide), lambda s: (0, s))] * 2
        + [whole((rows, model))],
        out_shape=[
            jax.ShapeDtypeStruct((rows, model), BF16),
            jax.ShapeDtypeStruct((rows, model), F32),
            jax.ShapeDtypeStruct((1, model), F32),
            jax.ShapeDtypeStruct((rows, units), BF16),
            jax.ShapeDtypeStruct((rows, units), BF16),
            jax.ShapeDtypeStruct((rows, model), BF16),
        ],
        scratch_shapes=[pltpu.VMEM((rows, model), F32)],
        compiler_params=compiler_params(),
        cost_estimate=cost(4 * rows * model * units, 4 * model * units + 4 * rows * units),
        name="ffn_forward",
    )(stream, gain_row, last_gain, upstream, weight_in, weight_out)


def ffn_bwd_kernel(
    x_ref, gain_ref, up_ref, slope_ref, win_ref, wout_ref,
    down_ref, gain_grad_ref, half_ref, grad_ref, total,
):
    step = pl.program_id(0)

    @pl.when(step == 0)
    def _():
        half_ref[...] = (0.5 * up_ref[...]).astype(BF16)
        total[...] = jnp.zeros_like(total)

    grad = (dot(half_ref[...], wout_ref[...], NT) * slope_ref[...].astype(F32)).astype(BF16)
    grad_ref[...] = grad
    total[...] += dot(grad, win_ref[...], NT)

    @pl.when(step == pl.num_programs(0) - 1)
    def _():
        gain = gain_ref[...]
        normed, inverse = layer_norm(x_ref[...].astype(F32), gain)[1:]
        through, grad_gain = norm_back(total[...], normed, inverse, gain)
        down_ref[...] = up_ref[...] + through
        gain_grad_ref[...] = grad_gain


def ffn_backward(upstream, stream, slope, gain_row, weight_in, weight_out):
    rows, model = stream.shape
    units = weight_in.shape[1]
    wide = min(units, 1024)
    return pl.pallas_call(
        ffn_bwd_kernel,
        grid=(units // wide,),
        in_specs=[
            whole((rows, model)),
            whole((1, model)),
            whole((rows, model)),
            pl.BlockSpec((rows, wide), lambda s: (0, s)),
            pl.BlockSpec((model, wide), lambda s: (0, s)),
            pl.BlockSpec((wide, model), lambda s: (s, 0)),
        ],
        out_specs=[
            whole((rows, model)),
            whole((1, model)),
            whole((rows, model)),
            pl.BlockSpec((rows, wide), lambda s: (0, s)),
        ],
        out_shape=[
            jax.ShapeDtypeStruct((rows, model), F32),
            jax.ShapeDtypeStruct((1, model), F32),
            jax.ShapeDtypeStruct((rows, model), BF16),
            jax.ShapeDtypeStruct((rows, units), BF16),
        ],
        scratch_shapes=[pltpu.VMEM((rows, model), F32)],
        compiler_params=compiler_params(),
        cost_estimate=cost(4 * rows * model * units, 4 * model * units + 6 * rows * units),
        name="ffn_backward",
    )(stream, gain_row, upstream, slope, weight_in, weight_out)


def hidden_kernel(up_ref, slope_ref, wout_ref, half_ref, grad_ref):
    @pl.when(pl.program_id(0) == 0)
    def _():
        half_ref[...] = (0.5 * up_ref[...]).astype(BF16)

    grad = dot(half_ref[...], wout_ref[...], NT) * slope_ref[...].astype(F32)
    grad_ref[...] = grad.astype(BF16)


def hidden_gradient(upstream, slope, weight_out):
    rows, model = upstream.shape
    units = weight_out.shape[0]
    wide = min(units, 1024)
    return pl.pallas_call(
        hidden_kernel,
        grid=(units // wide,),
        in_specs=[
            whole((rows, model)),
            pl.BlockSpec((rows, wide), lambda s: (0, s)),
            pl.BlockSpec((wide, model), lambda s: (s, 0)),
        ],
        out_specs=[whole((rows, model)), pl.BlockSpec((rows, wide), lambda s: (0, s))],
        out_shape=[
            jax.ShapeDtypeStruct((rows, model), BF16),
            jax.ShapeDtypeStruct((rows, units), BF16),
        ],
        compiler_params=compiler_params(),
        cost_estimate=cost(2 * rows * model * units, 2 * model * units + 6 * rows * units),
        name="hidden_gradient",
    )(upstream, slope, weight_out)


def down_kernel(
    x_ref, gain_ref, up_ref, grad_ref, weight_ref, down_ref, half_ref, gain_grad_ref, total
):
    step = pl.program_id(0)

    @pl.when(step == 0)
    def _():
        total[...] = jnp.zeros_like(total)

    total[...] += dot(grad_ref[...], weight_ref[...], NT)

    @pl.when(step == pl.num_programs(0) - 1)
    def _():
        gain = gain_ref[...]
        normed, inverse = layer_norm(x_ref[...].astype(F32), gain)[1:]
        through, grad_gain = norm_back(total[...], normed, inverse, gain)
        down = up_ref[...] + through
        down_ref[...] = down.astype(down_ref.dtype)
        half_ref[...] = (0.5 * down).astype(BF16)
        gain_grad_ref[...] = grad_gain


def stream_gradient(upstream, stream, grad, gain_row, weight, down_type):
    rows, model = stream.shape
    units = weight.shape[1]
    wide = min(units, 1024)
    return pl.pallas_call(
        down_kernel,
        grid=(units // wide,),
        in_specs=[
            whole((rows, model)),
            whole((1, model)),
            whole((rows, model)),
            pl.BlockSpec((rows, wide), lambda s: (0, s)),
            pl.BlockSpec((model, wide), lambda s: (0, s)),
        ],
        out_specs=[whole((rows, model)), whole((rows, model)), whole((1, model))],
        out_shape=[
            jax.ShapeDtypeStruct((rows, model), down_type),
            jax.ShapeDtypeStruct((rows, model), BF16),
            jax.ShapeDtypeStruct((1, model), F32),
        ],
        scratch_shapes=[pltpu.VMEM((rows, model), F32)],
        compiler_params=compiler_params(),
        cost_estimate=cost(2 * rows * model * units, 2 * model * units + 2 * rows * units),
        name="stream_gradient",
    )(stream, gain_row, upstream, grad, weight)


def turn(field, cosines, sines, size):
    repeats = field.shape[1] // cosines.shape[1]
    cosines = jnp.concatenate([cosines] * repeats, 1)
    sines = jnp.concatenate([sines] * repeats, 1)
    lane = lax.broadcasted_iota(jnp.int32, field.shape, 1)
    half = size // 2
    width = field.shape[1]
    swapped = jnp.where(
        lane % size < half,
        pltpu.roll(field, width - half, 1),
        pltpu.roll(field, half, 1),
    )
    return field * cosines + swapped * sines


def rope_tables(position, size):
    half = size // 2
    lane = jnp.arange(LANES, dtype=jnp.int32)
    freqs = jnp.exp(
        -jnp.log(jnp.float32(ROPE_BASE)) * (lane % half).astype(jnp.float32) / half
    )
    angles = position.astype(jnp.float32)[:, None] * freqs[None, :]
    signs = jnp.where(lane % size < half, -1.0, 1.0)
    return (jnp.cos(angles), jnp.sin(angles) * signs[None, :])


def front_kernel(
    size, ffn_steps, pieces, row_ref, x_ref, gain_ref, win_ref, wout_ref,
    wq_ref, wk_ref, wv_ref, cos_ref, sin_ref, *refs,
):
    refs = refs[-(6 + pieces) :]
    out_ref, slope_ref, hid_ref, entered_ref, next_ref = refs[:5]
    outs, total = refs[5:-1], refs[-1]
    step = pl.program_id(0)

    @pl.when(step == 0)
    def _():
        gain = gain_ref[0:1, :]
        entered_ref[...] = layer_norm(x_ref[0].astype(F32), gain)[0].astype(BF16)
        total[...] = jnp.zeros_like(total)

    @pl.when(step < ffn_steps)
    def _():
        hidden, slope = hidden_units(dot(entered_ref[...], win_ref[...]))
        slope_ref[...] = slope
        hid_ref[...] = hidden
        total[...] += dot(hidden, wout_ref[...])

    @pl.when(step == ffn_steps)
    def _():
        out = x_ref[0].astype(F32) + 0.5 * total[...]
        out_ref[...] = out
        next_ref[...] = layer_norm(out, gain_ref[1:2, :])[0].astype(BF16)

    each = (pl.num_programs(0) - ffn_steps) // pieces
    for piece, out in enumerate(outs):

        @pl.when((step >= ffn_steps) & ((step - ffn_steps) // each == piece))
        def _():
            for place, weight in enumerate((wq_ref, wk_ref, wv_ref)):
                made = dot(next_ref[...], weight[...])
                if place < 2:
                    made = turn(made, cos_ref[...], sin_ref[...], size)
                made = made.astype(BF16)
                for target in range(out.shape[0]):
                    out[target, place, 0] = made[:, target * LANES : (target + 1) * LANES]


def front(
    frames, row, gains, weight_in, weight_out, weight, cosines, sines,
    places, chunks, size, before=(),
):
    given, rows, model = frames.shape
    units = weight_in.shape[1]
    wide = min(units, 1024)
    ffn_steps = units // wide
    turned_wide = TURNED
    turns = model // turned_wide
    pieces = model // (places * LANES)
    each = turns // pieces
    piece = jax.ShapeDtypeStruct((places, 3, chunks, rows, LANES), BF16)

    def ffn_at(s, row):
        return jnp.minimum(s, ffn_steps - 1)

    def turn_at(s):
        return jnp.maximum(s - ffn_steps, 0)

    def piece_at(number):
        return lambda s, row: (
            jnp.clip(s - ffn_steps - number * each, 0, each - 1), 0, row[0], 0, 0
        )

    row_block = pl.BlockSpec((rows, model), lambda s, row: (row[0], 0))
    unit_block = pl.BlockSpec((rows, wide), lambda s, row: (row[0], ffn_at(s, row)))
    angle_block = pl.BlockSpec((rows, LANES), lambda s, row: (row[0], 0))
    out_shape = [
        jax.ShapeDtypeStruct((chunks * rows, model), F32),
        jax.ShapeDtypeStruct((chunks * rows, units), BF16),
        jax.ShapeDtypeStruct((chunks * rows, units), BF16),
        jax.ShapeDtypeStruct((chunks * rows, model), BF16),
        jax.ShapeDtypeStruct((chunks * rows, model), BF16),
    ] + [piece] * pieces
    in_specs = [
        pl.BlockSpec((1, rows, model), lambda s, row: (row[0] if given > 1 else 0, 0, 0)),
        whole(gains.shape),
        pl.BlockSpec((model, wide), lambda s, row: (0, ffn_at(s, row))),
        pl.BlockSpec((wide, model), lambda s, row: (ffn_at(s, row), 0)),
        pl.BlockSpec((model, turned_wide), lambda s, row: (0, turn_at(s))),
        pl.BlockSpec((model, turned_wide), lambda s, row: (0, turns + turn_at(s))),
        pl.BlockSpec((model, turned_wide), lambda s, row: (0, 2 * turns + turn_at(s))),
        angle_block,
        angle_block,
    ]
    grid_spec = pltpu.PrefetchScalarGridSpec(
        num_scalar_prefetch=1,
        grid=(ffn_steps + turns,),
        in_specs=in_specs + [pl.BlockSpec(memory_space=pl.ANY)] * len(before),
        out_specs=[row_block, unit_block, unit_block, row_block, row_block]
        + [
            pl.BlockSpec((turned_wide // LANES, 3, 1, rows, LANES), piece_at(number))
            for number in range(pieces)
        ],
        scratch_shapes=[pltpu.VMEM((rows, model), F32)],
    )
    return pl.pallas_call(
        functools.partial(front_kernel, size, ffn_steps, pieces),
        grid_spec=grid_spec,
        out_shape=out_shape,
        input_output_aliases={1 + len(in_specs) + i: i for i in range(len(before))},
        compiler_params=compiler_params(),
        cost_estimate=cost(
            4 * rows * model * units + 6 * rows * model * model,
            4 * model * units + 6 * model * model + 4 * rows * units + 16 * rows * model,
        ),
        name="front",
    )(
        row, frames, gains, weight_in, weight_out, weight, weight, weight,
        cosines, sines, *before,
    )


def projection_kernel(
    size, pieces, cos_ref, sin_ref, x_ref, gain_ref, up_ref, weight_ref, *refs
):
    backs, refs = refs[:pieces], refs[pieces:]
    grad_ref, down_ref, half_ref, gain_grad_ref, total = refs
    step = pl.program_id(0)

    @pl.when(step == 0)
    def _():
        total[...] = jnp.zeros_like(total)

    rotated = step < 2
    cosines = jnp.where(rotated, cos_ref[...], 1.0)
    sines = jnp.where(rotated, -sin_ref[...], 0.0)
    places, _, chunks, frames, _ = backs[0].shape
    per = TURNED // LANES
    for piece, back in enumerate(backs):
        for first in range(0, places, per):
            for chunk in range(chunks):
                rows = slice(chunk * frames, (chunk + 1) * frames)
                field = jnp.concatenate([back[first + i, 0, chunk] for i in range(per)], 1)
                made = turn(field.astype(F32), cosines[rows], sines[rows], size).astype(BF16)
                start = (piece * places + first) * LANES
                grad_ref[rows, start : start + TURNED] = made
    total[...] += dot(grad_ref[...], weight_ref[...], NT)

    @pl.when(step == pl.num_programs(0) - 1)
    def _():
        gain = gain_ref[...]
        normed, inverse = layer_norm(x_ref[...], gain)[1:]
        through, grad_gain = norm_back(total[...], normed, inverse, gain)
        down = up_ref[...] + through
        down_ref[...] = down
        half_ref[...] = (0.5 * down).astype(BF16)
        gain_grad_ref[...] = grad_gain


def projection_backward(backs, cosines, sines, size, upstream, stream, gain_row, weight):
    places, kinds, chunks, frames, _ = backs[0].shape
    pieces = len(backs)
    rows, model = stream.shape
    block = pl.BlockSpec((places, 1, chunks, frames, LANES), lambda s: (0, s, 0, 0, 0))
    return pl.pallas_call(
        functools.partial(projection_kernel, size, pieces),
        grid=(kinds,),
        in_specs=[
            whole(cosines.shape),
            whole(sines.shape),
            whole((rows, model)),
            whole((1, model)),
            whole((rows, model)),
            pl.BlockSpec((model, model), lambda s: (0, s)),
        ]
        + [block] * pieces,
        out_specs=[
            pl.BlockSpec((rows, model), lambda s: (0, s)),
            whole((rows, model)),
            whole((rows, model)),
            whole((1, model)),
        ],
        out_shape=[
            jax.ShapeDtypeStruct((rows, kinds * model), BF16),
            jax.ShapeDtypeStruct((rows, model), F32),
            jax.ShapeDtypeStruct((rows, model), BF16),
            jax.ShapeDtypeStruct((1, model), F32),
        ],
        scratch_shapes=[pltpu.VMEM((rows, model), F32)],
        compiler_params=compiler_params(),
        cost_estimate=cost(6 * rows * model * model, 6 * model * model + 22 * rows * model),
        name="projection_backward",
    )(cosines, sines, stream, gain_row, upstream, weight, *backs)


def flipped(axis_bit, count):
    axis, bit = axis_bit
    items, heads = count
    if axis == "items":
        return [(i * heads + h, (i ^ bit) * heads + h) for i in range(items) for h in range(heads)]
    return [(i * heads + h, i * heads + (h ^ bit)) for i in range(items) for h in range(heads)]


def swap(value, axis_bit):
    count = (lax.axis_size("items"), lax.axis_size("heads"))
    return lax.ppermute(value, EVERY, flipped(axis_bit, count))


def branched(always, work):
    def empty():
        return jax.tree.map(lambda leaf: jnp.zeros(leaf.shape, leaf.dtype), jax.eval_shape(work))

    return lax.optimization_barrier(lax.cond(always, work, empty))


def fenced(always, scatters, work):
    def run():
        moves = [scatter.move() for scatter in scatters]
        return (branched(always, work) if any(moves) else work(), moves)

    result, moves = branched(always, run)
    for scatter, parts in zip(scatters, moves):
        scatter.take(parts)
    return result


def moved(scatter):
    scatter.take(scatter.move())


def other_core(value):
    return swap(value, ("heads", 1))


def exchange(value):
    half = lax.axis_size("heads") // 2
    groups = [[side * half + i for i in range(half)] for side in range(2)]
    return lax.all_to_all(
        value, "heads", split_axis=0, concat_axis=0, tiled=True, axis_index_groups=groups
    )


def across(value):
    return swap(value, ("heads", lax.axis_size("heads") // 2))


def gathered(own, other, side):
    return jnp.concatenate([jnp.where(side == 0, own, other), jnp.where(side == 0, other, own)], 0)


def parted(value, side):
    low, high = jnp.split(value, 2, 0)
    return (jnp.where(side == 0, low, high), jnp.where(side == 0, high, low))


def own_rows(left_ref, heads, core, target, first):
    rows, model = left_ref.shape
    each = model // heads
    for place in range(heads // 2):
        if each % LANES == 0:
            start = pl.multiple_of((2 * place + core) * each, each)
            mine = jnp.transpose(left_ref[:, pl.ds(start, each)].astype(F32)).astype(BF16)
        else:
            pair = left_ref[:, 2 * place * each : 2 * (place + 1) * each]
            pair = jnp.transpose(pair.astype(F32))
            mine = jnp.where(core == 0, pair[:each], pair[each:]).astype(BF16)
        for half in range(2):
            start = (half * (heads // 2) + place) * (each // 2)
            target[start : start + each // 2, first : first + rows] = mine[
                half * (each // 2) : (half + 1) * (each // 2)
            ]


def turned_items(left, items, own, target, first):
    rows, model = left.shape
    each = model // items
    for item in range(items):
        part = jnp.transpose(left[:, item * each : (item + 1) * each].astype(F32)).astype(BF16)
        place = pl.multiple_of((own ^ item) * each, each)
        target[pl.ds(place, each), first : first + rows] = part


def share_shapes(items, heads, model, columns):
    lead = 2 if items > 1 else 1
    shape = (lead, heads // 2, model // heads // 2, columns // items)
    return [jax.ShapeDtypeStruct(shape, BF16)] * (4 if items > 1 else 2)


def out_grad_kernel(place_ref, up_own, up_other, hid_own, hid_other, *refs):
    targets, turned = refs[:-1], refs[-1]
    rows, model = up_own.shape
    items = 4 if len(targets) == 4 else 1

    @pl.when(pl.program_id(0) == 0)
    def _():
        turned_items(up_own[...], items, place_ref[1], turned, 0)
        turned_items(up_other[...], items, place_ref[1], turned, rows)

    hidden = jnp.concatenate([hid_own[...], hid_other[...]], 0)
    grad = dot(turned[...], hidden).astype(BF16)
    wide = grad.shape[1]
    each = targets[0].shape[2]
    parts = model // items // (2 * each)
    for r in range(items):
        for part in range(parts):
            for half in range(2):
                first = ((r * parts + part) * 2 + half) * each
                piece = grad[first : first + each]
                if half == 0:
                    target, at = targets[2 * (r % 2)], r // 2
                else:
                    target, at = targets[1 + 2 * (r // 2)], r % 2
                target[at, 0, :, part * wide : (part + 1) * wide] = piece


def out_grad(upstream, hidden, heads, place, items):
    rows, model = upstream[0].shape
    units = hidden[0].shape[1]
    wide = units // heads
    shapes = share_shapes(items, heads, model, units)
    block = (shapes[0].shape[0], 1) + shapes[0].shape[2:]
    hid_block = pl.BlockSpec((rows, wide), lambda s, place: (0, 2 * s + place[0]))
    grid_spec = pltpu.PrefetchScalarGridSpec(
        num_scalar_prefetch=1,
        grid=(heads // 2,),
        in_specs=[whole((rows, model))] * 2 + [hid_block] * 2,
        out_specs=[pl.BlockSpec(block, lambda s, place: (0, s, 0, 0))] * len(shapes),
        scratch_shapes=[pltpu.VMEM((model, 2 * rows), BF16)],
    )
    return pl.pallas_call(
        out_grad_kernel,
        grid_spec=grid_spec,
        out_shape=shapes,
        compiler_params=compiler_params(),
        cost_estimate=cost(2 * rows * model * units, 2 * model * units + 4 * rows * units),
        name="out_grad",
    )(place, *upstream, *hidden)


def column_grad_kernel(heads, items, split, place_ref, *refs):
    count = len(split)
    lefts, refs = refs[: 2 * count], refs[2 * count :]
    rights, refs = refs[: 2 * (count + sum(split))], refs[2 * (count + sum(split)) :]
    targets, turned = refs[:-count], refs[-count:]
    r = pl.program_id(0)
    rows = lefts[0].shape[0]

    @pl.when(r == 0)
    def _():
        for number in range(count):
            for other in range(2):
                own_rows(
                    lefts[2 * number + other], heads, place_ref[0], turned[number], other * rows
                )

    made = []
    at = 0
    for number in range(count):
        right = jnp.concatenate([rights[at][...], rights[at + 1][...]], 0)
        at += 2
        if split[number]:
            second = jnp.concatenate([rights[at][...], rights[at + 1][...]], 0)
            at += 2
            right = jnp.where((r ^ place_ref[1]) < items // 2, right, second)
        made.append(dot(turned[number][...], right).astype(BF16))
    made = made[0] if count == 1 else jnp.concatenate(made, 1)
    half = made.shape[0] // 2
    top, low = made[:half].reshape(targets[0].shape), made[half:].reshape(targets[0].shape)
    if len(targets) == 2:
        targets[0][...] = top
        targets[1][...] = low
        return

    @pl.when(r % 2 == 0)
    def _():
        targets[0][...] = top

    @pl.when(r % 2 == 1)
    def _():
        targets[2][...] = top

    @pl.when(r < 2)
    def _():
        targets[1][...] = low

    @pl.when(r >= 2)
    def _():
        targets[3][...] = low


def column_grads(lefts, rights, heads, place, items):
    if items == 1:
        flat = [
            (left, part)
            for left, right in zip(lefts, rights)
            for part in (right if isinstance(right[0], tuple) else (right,))
        ]
        lefts, rights = [left for left, _ in flat], [right for _, right in flat]
    split = [isinstance(right[0], tuple) for right in rights]
    rows, model = lefts[0][0].shape
    parts = []
    for right, two in zip(rights, split):
        parts += [part for pair in right for part in pair] if two else list(right)
    columns = sum(part.shape[1] for part in parts) // 2
    shapes = share_shapes(items, heads, model, columns)
    block = (1,) + shapes[0].shape[1:]
    right_specs = []
    for right, two in zip(rights, split):
        if two:
            share = pl.BlockSpec(
                (rows, right[0][0].shape[1] * 2 // items),
                lambda r, place: (0, (r ^ place[1]) % (items // 2)),
            )
            right_specs += [share] * 4
        else:
            share = pl.BlockSpec(
                (rows, right[0].shape[1] // items), lambda r, place: (0, r ^ place[1])
            )
            right_specs += [share] * 2
    maps = [
        lambda r, place: (r // 2, 0, 0, 0),
        lambda r, place: (jnp.minimum(r, 1), 0, 0, 0),
        lambda r, place: (r // 3, 0, 0, 0),
        lambda r, place: (r // 3, 0, 0, 0),
    ]
    grid_spec = pltpu.PrefetchScalarGridSpec(
        num_scalar_prefetch=1,
        grid=(items,),
        in_specs=[whole((rows, model))] * (2 * len(lefts)) + right_specs,
        out_specs=[pl.BlockSpec(block, index) for index in maps[: len(shapes)]],
        scratch_shapes=[pltpu.VMEM((model // 2, 2 * rows), BF16)] * len(lefts),
    )
    return pl.pallas_call(
        functools.partial(column_grad_kernel, heads, items, split),
        grid_spec=grid_spec,
        out_shape=shapes,
        compiler_params=compiler_params(),
        cost_estimate=cost(2 * rows * model * columns, 4 * model * columns),
        name="column_grads",
    )(place, *[part for left in lefts for part in left], *parts)


class Scatter:
    def __init__(self, keep_top, keep_low, *sends):
        self.keep = [keep_top, keep_low]
        self.got, self.early = [], []
        self.route(list(sends), FIRST[: len(sends)])

    def route(self, sends, routes):
        self.sends, self.routes = sends, routes

    def move(self):
        return [swap(send, route) for send, route in zip(self.sends, self.routes)]

    def take(self, moved):
        self.early, self.got = self.got, moved
        self.route([], [])

    def second(self, sends):
        self.route(sends, FIRST[::-1][: len(sends)])


def second_kernel(*refs):
    count = len(refs) // 3
    for number in range(count):
        keep, got, out = refs[2 * number], refs[2 * number + 1], refs[2 * count + number]
        out[...] = (keep[0].astype(F32) + got[0].astype(F32)).astype(BF16)


def second_sums(*scatters):
    terms = [
        part
        for scatter in scatters
        if scatter.got
        for keep, got in zip(scatter.keep, scatter.got)
        for part in (keep, got)
    ]
    if not terms:
        return [[] for _ in scatters]
    shape = terms[0].shape
    outs = []
    in_specs, out_specs = [], []
    for term in terms:
        in_specs.append(
            pl.BlockSpec((1, 2) + term.shape[2:], lambda g: (1, g, 0, 0))
        )
    for term in terms[::2]:
        out_specs.append(pl.BlockSpec((2,) + term.shape[2:], lambda g: (g, 0, 0)))
        outs.append(jax.ShapeDtypeStruct(term.shape[1:], BF16))
    made = pl.pallas_call(
        second_kernel,
        grid=(shape[1] // 2,),
        in_specs=in_specs,
        out_specs=out_specs,
        out_shape=outs,
        compiler_params=compiler_params(),
        cost_estimate=cost(0, 6 * sum(out.size for out in outs)),
        name="second_sums",
    )(*terms)
    return [list(made[2 * i : 2 * i + 2]) for i in range(len(scatters))]


def last_kernel(*refs):
    out = refs[-1]
    for number in range(out.shape[1]):
        for half in range(2):
            terms = refs[6 * number + 3 * half : 6 * number + 3 * half + 3]
            out[:, number, half] = (
                terms[0][0].astype(F32) + terms[1][0].astype(F32) + terms[2][...].astype(F32)
            ).astype(BF16)


def last_sum(*scatters, columns=None):
    if not scatters[0].got:
        items = lax.axis_size("items")
        values = []
        for scatter in scatters:
            value = jnp.stack([keep[0] for keep in scatter.keep], 1)
            if columns is not None:
                starts = [sum(columns[:i]) for i in range(len(columns))]
                parts = [
                    value[..., start : start + size].reshape(value.shape[:3] + (items, -1))
                    for start, size in zip(starts, columns)
                ]
                value = jnp.concatenate(parts, 4).reshape(value.shape)
            values.append(lax.psum_scatter(value, "items", scatter_dimension=3, tiled=True))
        return jnp.stack(values, 1)
    terms = [
        part
        for scatter in scatters
        for parts in zip(scatter.keep, scatter.early, scatter.got)
        for part in parts
    ]
    _, places, rows, wide = terms[0].shape
    held = pl.BlockSpec((1, 2, rows, wide), lambda g: (0, g, 0, 0))
    late = pl.BlockSpec((2, rows, wide), lambda g: (g, 0, 0))
    shape = (places, len(scatters), 2, rows, wide)
    return pl.pallas_call(
        last_kernel,
        grid=(places // 2,),
        in_specs=[held, held, late] * (2 * len(scatters)),
        out_specs=pl.BlockSpec((2,) + shape[1:], lambda g: (g, 0, 0, 0, 0)),
        out_shape=jax.ShapeDtypeStruct(shape, BF16),
        compiler_params=compiler_params(),
        cost_estimate=cost(0, 8 * places * len(scatters) * 2 * rows * wide),
        name="last_sum",
    )(*terms)


def along_z(value):
    heads = lax.axis_size("heads")
    groups = [[core + 2 * z for z in range(heads // 2)] for core in range(2)]
    made = lax.psum_scatter(
        value, "heads", scatter_dimension=0, tiled=False, axis_index_groups=groups
    )
    return [made[i].reshape(-1, made.shape[-1]) for i in range(made.shape[0])]


def unfold_kernel(share_ref, out_ref):
    each = share_ref.shape[0]
    span = out_ref.shape[0]
    for part in range(share_ref.shape[1] // span):
        turned = jnp.transpose(share_ref[:, part * span : (part + 1) * span].astype(F32))
        out_ref[:, part * each : (part + 1) * each] = turned


def unfolded(share, span):
    each, wide = share.shape
    shape = (span, each * wide // span)
    return pl.pallas_call(
        unfold_kernel,
        out_shape=jax.ShapeDtypeStruct(shape, F32),
        cost_estimate=cost(0, 6 * each * wide),
        name="unfolded",
    )(share)


def heads_kernel(grad_ref, weight_ref, *outs):
    step = pl.program_id(0)
    made = dot(grad_ref[...], weight_ref[...], NT).astype(BF16)
    for piece, out in enumerate(outs):

        @pl.when(step == piece)
        def _():
            places, chunks, frames, _ = out.shape
            for place in range(places):
                for chunk in range(chunks):
                    out[place, chunk] = made[
                        chunk * frames : (chunk + 1) * frames, place * LANES : (place + 1) * LANES
                    ]


def heads_gradient(grad, weight, places, chunks):
    rows, model = grad.shape
    wide = places * LANES
    pieces = model // wide
    shape = (places, chunks, rows // chunks, LANES)
    return pl.pallas_call(
        heads_kernel,
        grid=(pieces,),
        in_specs=[whole((rows, model)), pl.BlockSpec((wide, model), lambda s: (s, 0))],
        out_specs=[whole(shape)] * pieces,
        out_shape=[jax.ShapeDtypeStruct(shape, BF16)] * pieces,
        compiler_params=compiler_params(),
        cost_estimate=cost(2 * rows * model * model, 2 * model * model + 4 * rows * model),
        name="heads_gradient",
    )(grad, weight)


def sum_everywhere(value):
    for axis in EVERY:
        bit = 1
        while bit < lax.axis_size(axis):
            value = value + swap(value, (axis, bit))
            bit *= 2
    return value


def edges(block, width):
    ways = lax.axis_size("heads")
    half = ways // 2
    place = lax.axis_index("heads") % half
    ring = [(side * half + i, side * half + (i + 1) % half) for side in range(2) for i in range(half)]
    low = lax.ppermute(block[:, block.shape[1] - width :], "heads", ring)
    high = lax.ppermute(block[:, :width], "heads", [(to, at) for at, to in ring])
    low = jnp.where(place == 0, jnp.roll(low, 1, 0), low)
    high = jnp.where(place == half - 1, jnp.roll(high, -1, 0), high)
    return jnp.concatenate([low, block, high], axis=1)


def body(
    frames, cotangent, bucket_counts, gains, w_ffn1_in, w_ffn1_out, w_qkv, w_out,
    w_point_in, w_depth, w_point_out, w_ffn2_in, w_ffn2_out,
):
    chunks, here, model = frames.shape
    ways = lax.axis_size("heads")
    half = ways // 2
    items = 4 if lax.axis_size("items") == 4 else 1
    span = here * half
    group_len = here * ways
    size = model // HEADS
    reach = (KERNEL - 1) // 2
    rows = chunks * here
    pieces = model // (half * LANES)
    place = lax.axis_index("heads")
    side = place // half
    where = jnp.stack(
        [place % 2, lax.axis_index("items") if items > 1 else 0 * place]
    ).astype(jnp.int32)
    always = place >= 0
    first = jnp.arange(chunks, dtype=jnp.int32)[:, None] * span + place % half * here
    position = first + jnp.arange(here, dtype=jnp.int32)[None]
    cosines, sines = rope_tables(position.reshape(-1), size)
    depth_rows = w_depth.astype(F32)
    gain = [gains[i : i + 1] for i in range(6)]
    counts = lax.dynamic_index_in_dim(bucket_counts[:, 0], side, 0, keepdims=False)
    wide_position = first - reach + jnp.arange(here + 2 * reach, dtype=jnp.int32)[None]
    seg_wide = segment_ids(wide_position, counts[0], counts[1], group_len)
    seg_own = seg_wide[:, reach : reach + here]

    def mine(value):
        return lax.dynamic_index_in_dim(value, side, 0, keepdims=False)

    def theirs(value):
        return lax.dynamic_index_in_dim(value, 1 - side, 0, keepdims=False)

    def begin(chunk, row, before=()):
        return front(
            chunk, row.reshape(1).astype(jnp.int32), gains, w_ffn1_in, w_ffn1_out, w_qkv,
            cosines, sines, half, chunks, size, before,
        )

    before, other_frames = fenced(
        always, (), lambda: (begin(frames, side), across(theirs(frames)))
    )
    stream_one, slope_one, hid_one, ent_one, ent_att, *sent = begin(
        other_frames[None], 1 - side, before
    )
    stream = gathered(mine(frames), other_frames, side)
    qkv = [exchange(sent[0])]
    kept, contexts = [], []
    for number in range(pieces):

        def attend_now():
            return attend_forward(qkv[number], counts, size)

        def beside():
            extra = []
            if number + 1 < pieces:
                extra.append(exchange(sent[number + 1]))
            if number > 0:
                extra.append(exchange(kept[number - 1][0]))
            return extra

        def early():
            if number == 0:
                return [other_core(part) for part in (hid_one, ent_one, ent_att)]
            return [across(theirs(cotangent))] if number == 1 else []

        made, extra, others = fenced(always, (), lambda: (attend_now(), beside(), early()))
        kept.append(made)
        if number == 0:
            hid_one, ent_one, ent_att = zip((hid_one, ent_one, ent_att), others)
        elif number == 1:
            cot_other = others[0]
        if number + 1 < pieces:
            qkv.append(extra.pop(0))
        if number > 0:
            contexts.append(extra.pop(0))
    contexts.append(exchange(kept[-1][0]))
    if pieces == 1:
        cot_other = across(theirs(cotangent))
    fulls = [made[1] for made in kept]
    lses = [made[2] for made in kept]
    contexts = [part.transpose(1, 2, 0, 3).reshape(rows, -1) for part in contexts]
    context = jnp.concatenate(contexts, 1)
    stream_two = stream_one
    for number, part in enumerate(contexts):
        wide = part.shape[1]
        stream_two = stream_two + dot(part, w_out[number * wide : (number + 1) * wide])
    shaped, conv_normed, conv_inverse = layer_norm(stream_two, gain[2])
    conv_entered = shaped.astype(BF16)
    pointwise = dot(conv_entered, w_point_in)
    linear = pointwise[:, :model]
    sigmoid_gate = jax.nn.sigmoid(pointwise[:, model:])
    gated_low = (linear * sigmoid_gate).astype(BF16).reshape(chunks, here, model)
    widened = edges(gated_low, reach)
    depth_out = jnp.zeros((chunks, here, model), F32)
    for offset in range(KERNEL):
        same = (seg_wide[:, offset : offset + here] == seg_own)[:, :, None]
        depth_out = depth_out + depth_rows[offset] * jnp.where(
            same, widened[:, offset : offset + here], 0.0
        )
    depth_out = depth_out.reshape(rows, model)
    depth_shaped, depth_normed, depth_inverse = layer_norm(depth_out, gain[3])
    mixed_low = (depth_shaped * jax.nn.sigmoid(depth_shaped)).astype(BF16)
    stream_three = stream_two + dot(mixed_low, w_point_out)
    layer_out, grad_four, gain_five, slope_two, hid_two, ent_two = ffn_forward(
        stream_three, gain[4], w_ffn2_in, w_ffn2_out, gain[5],
        gathered(mine(cotangent), cot_other, side),
    )
    (grad_three, gain_four, half_two, grad_pre_two), hid_other, ent_other = fenced(
        always,
        (),
        lambda: (
            ffn_backward(grad_four, stream_three, slope_two, gain[4], w_ffn2_in, w_ffn2_out),
            other_core(hid_two),
            other_core(ent_two),
        ),
    )
    half_other, grad_pre_other = other_core(half_two), other_core(grad_pre_two)
    grad_mix = grad_three.astype(BF16)
    grad_norm_in = dot(grad_mix, w_point_out, NT) * silu_slope(depth_shaped)
    grad_depth, gain_three = norm_back(grad_norm_in, depth_normed, depth_inverse, gain[3])
    grad_depth_low = grad_depth.astype(BF16).reshape(chunks, here, model)
    grad_widened = edges(grad_depth_low, reach)
    grad_gated = jnp.zeros((chunks, here, model), F32)
    for offset in range(KERNEL):
        mirror = 2 * reach - offset
        same_back = (seg_wide[:, mirror : mirror + here] == seg_own)[:, :, None]
        grad_gated = grad_gated + depth_rows[offset] * jnp.where(
            same_back, grad_widened[:, mirror : mirror + here], 0.0
        )
    grad_gated = grad_gated.reshape(rows, model)
    grad_a = (grad_gated * sigmoid_gate).astype(BF16)
    grad_b = (grad_gated * linear * sigmoid_gate * (1.0 - sigmoid_gate)).astype(BF16)
    through, gain_two = norm_back(
        dot(grad_a, w_point_in[:, :model], NT) + dot(grad_b, w_point_in[:, model:], NT),
        conv_normed, conv_inverse, gain[2],
    )
    grad_two = grad_three + through
    grad_attn_out = grad_two.astype(BF16)
    grad_heads = list(heads_gradient(grad_attn_out, w_out, half, chunks))
    lefts = (mixed_low, conv_entered, context)

    def ffn_grads():
        return (
            [other_core(part) for part in lefts + (grad_a, grad_b)],
            exchange(grad_heads[0]),
            out_grad((half_two, half_other), (hid_two, hid_other), ways, where, items),
            column_grads(
                [(ent_two, ent_other)], [(grad_pre_two, grad_pre_other)], ways, where, items
            ),
        )

    others, grad_heads[0], shares_out, shares_in = fenced(always, (), ffn_grads)
    two_out, two_in = Scatter(*shares_out), Scatter(*shares_in)
    out_own, out_theirs = parted(layer_out, side)
    grads, backs = [], []
    for number in range(pieces):
        last = number == pieces - 1

        def beside():
            extra = []
            if not last:
                extra.append(exchange(grad_heads[number + 1]))
            if number > 0:
                extra.append(exchange(grads[number - 1]))
            if number == 0:
                extra.append(across(out_theirs))
                extra += [other_core(grad_mix), other_core(grad_attn_out)]
            return extra

        def attend_now():
            return attend_backward(
                qkv[number], counts, size, fulls[number], lses[number], grad_heads[number]
            )

        moving = (two_out,) if number == 0 else (two_out, two_in) if number == 1 else ()
        made, extra = fenced(always, moving, lambda: (attend_now(), beside()))
        grads.append(made)
        if not last:
            grad_heads[number + 1] = extra.pop(0)
        if number > 0:
            backs.append(extra.pop(0))
        if number == 0:
            out_other, *late = extra
            two_out.second(second_sums(two_out)[0])
    two_in.second(second_sums(two_in)[0])

    def middle_part():
        back = exchange(grads[-1])
        scatter = copy.copy(two_in)
        moved(scatter)
        shares = column_grads(
            list(zip(lefts, others[:3])),
            [
                (grad_mix, late[0]),
                ((grad_a, others[3]), (grad_b, others[4])),
                (grad_attn_out, late[1]),
            ],
            ways, where, items,
        )
        return (back, shares, last_sum(two_out, scatter))

    back, shares, two_sum = fenced(always, (), middle_part)
    backs.append(back)
    middle = Scatter(*shares)

    def attention_part():
        two_grads = along_z(two_sum)
        scatter = copy.copy(middle)

        def projection_part():
            grad_proj, *down = projection_backward(
                backs, cosines, sines, size, grad_two, stream_one, gain[1], w_qkv
            )
            return ((grad_proj, other_core(grad_proj)), down)

        grad_proj, (grad_one, half_one, gain_one) = fenced(always, (scatter,), projection_part)
        first = scatter.got
        scatter.second(second_sums(scatter)[0])

        def qkv_part():
            half_other = other_core(half_one)
            return (half_other, column_grads([ent_att], [grad_proj], ways, where, items))

        half_other, shares = fenced(always, (scatter,), qkv_part)
        attn = Scatter(*shares)

        def hidden_part():
            half_own, grad_pre = hidden_gradient(grad_one, slope_one, w_ffn1_out)
            shares = out_grad((half_own, half_other), hid_one, ways, where, items)
            return (grad_pre, shares)

        grad_pre, shares_out = fenced(always, (attn,), hidden_part)
        return (
            two_grads, first, scatter.got, (grad_one, gain_one), shares[:2], attn.got,
            grad_pre, shares_out,
        )

    two_grads, first, got, (grad_one, gain_one), shares, attn_got, grad_pre, shares_out = fenced(
        always, (), attention_part
    )
    middle.take(first)
    middle.take(got)
    attn = Scatter(*shares)
    attn.take(attn_got)
    attn.second(second_sums(attn)[0])
    one_out = Scatter(*shares_out)
    middle_columns = [w.shape[1] for w in (w_point_out, w_point_in, w_out)]
    def input_part():
        middle_grad = along_z(last_sum(middle, columns=middle_columns))
        grad_zero, _, gain_zero = stream_gradient(
            grad_one, stream, grad_pre, gain[0], w_ffn1_in, BF16
        )
        shares = column_grads([ent_one], [(grad_pre, other_core(grad_pre))], ways, where, items)
        return (middle_grad, shares, parted(grad_zero, side), gain_zero)

    middle_grad, shares, (grad_own, grad_theirs), gain_zero = fenced(
        always, (one_out, attn), input_part
    )
    one_in = Scatter(*shares)
    one_out.second(second_sums(one_out)[0])
    hidden = w_ffn1_in.shape[1]

    def tap_sums_here():
        rows_of = []
        for offset in range(KERNEL):
            same = (seg_wide[:, offset : offset + here] == seg_own)[:, :, None]
            product = grad_depth_low.astype(F32) * widened[:, offset : offset + here]
            rows_of.append(jnp.sum(jnp.where(same, product, 0.0), (0, 1))[None])
        return rows_of

    def last_part():
        grad_other = across(grad_theirs)
        attn_grad = along_z(last_sum(attn))
        out, scatter = copy.copy(one_out), copy.copy(one_in)
        fenced(always, (out,), lambda: ())
        out_grads = along_z(last_sum(out))
        fenced(always, (scatter,), lambda: ())
        scatter.second(second_sums(scatter)[0])
        fenced(always, (scatter,), lambda: ())
        last, grad_other = branched(
            always,
            lambda: (last_sum(scatter), grad_other),
        )
        small = sum_everywhere(
            jnp.concatenate(
                [gain_zero, gain_one, gain_two, gain_three, gain_four, gain_five]
                + tap_sums_here(),
                0,
            )
        )
        middle_parts = []
        start = 0
        for columns in middle_columns:
            each = columns // lax.axis_size("items")
            middle_parts.append(middle_grad[0][:, start : start + each].astype(F32))
            start += each
        ready = (
            gathered(out_own[None], out_other[None], side),
            gathered(grad_own[None], grad_other[None], side),
            attn_grad[0].astype(F32),
            middle_parts,
            two_grads[1].astype(F32),
            unfolded(two_grads[0], hidden // ways),
            unfolded(out_grads[0], hidden // ways),
        )
        return (along_z(last), small[:6], small[6:], ready)

    one_in_grad, gain_sums, tap_sums, ready = fenced(always, (), last_part)
    out, grad_in, attn_full, middle_parts, two_in_full, two_out_full, one_out_full = ready
    return (
        out,
        grad_in,
        gain_sums,
        one_in_grad[0].astype(F32),
        one_out_full,
        attn_full,
        middle_parts[2],
        middle_parts[1],
        tap_sums,
        middle_parts[0],
        two_in_full,
        two_out_full,
    )


def solution(mesh):
    split = P(None, EVERY, None)
    shares = P("heads", "items")
    in_specs = (split, split, P(None, "items", None)) + (P(),) * 10
    out_specs = (split, split, P(), shares, shares, shares, shares, shares, P()) + (shares,) * 3
    return jax.shard_map(body, mesh=mesh, in_specs=in_specs, out_specs=out_specs, check_vma=False)
```

```python
import copy
import functools

import jax
import jax.numpy as jnp
from jax import lax
from jax.experimental import pallas as pl
from jax.experimental.pallas import tpu as pltpu
from jax.sharding import PartitionSpec as P

HEADS = 16
KERNEL = 5
LONG = 1500
SHORT = 500
EPS = 1e-05
ROPE_BASE = 10000.0
BLOCK = 512
INNER_FWD = 1024
INNER_BWD = 512
TURNED = 512
LANES = 128
BIG = 1e30
VMEM_LIMIT = 56 << 20
F32 = jnp.float32
BF16 = jnp.bfloat16
NN = (((1,), (0,)), ((), ()))
NT = (((1,), (1,)), ((), ()))
EVERY = ("items", "heads")
FIRST = [("items", 1), ("items", 2)]


def dot(left, right, dims=NN):
    return lax.dot_general(left, right, dims, preferred_element_type=F32)


def silu_slope(field):
    gate_sig = jax.nn.sigmoid(field)
    return gate_sig * (1.0 + field * (1.0 - gate_sig))


def layer_norm(field, gain_row):
    centred = field - jnp.mean(field, -1, keepdims=True)
    inverse = lax.rsqrt(jnp.mean(centred * centred, -1, keepdims=True) + EPS)
    normed = centred * inverse
    return (normed * gain_row, normed, inverse)


def norm_back(upstream, normed, inverse, gain_row):
    scaled = upstream * gain_row
    through = inverse * (
        scaled
        - jnp.mean(scaled, -1, keepdims=True)
        - normed * jnp.mean(scaled * normed, -1, keepdims=True)
    )
    return (through, jnp.sum(upstream * normed, 0, keepdims=True))


def segment_ids(position, long_count, short_count, group_len):
    long_end = long_count * LONG
    short_end = long_end + short_count * SHORT
    segments = jnp.where(
        position < long_end, position // LONG, long_count + (position - long_end) // SHORT
    )
    segments = jnp.where(position < short_end, segments, long_count + short_count)
    return jnp.where((position < 0) | (position >= group_len), -1, segments)


def compiler_params():
    return pltpu.CompilerParams(vmem_limit_bytes=VMEM_LIMIT)


def whole(shape):
    return pl.BlockSpec(shape, lambda *_: (0,) * len(shape))


def cost(flops, bytes_accessed, transcendentals=0):
    return pl.CostEstimate(
        flops=flops, bytes_accessed=bytes_accessed, transcendentals=transcendentals
    )


def segment_bounds(counts, place, group):
    longs, shorts = counts
    long_end = longs * LONG
    short_end = long_end + shorts * SHORT
    start = jnp.where(place < longs, place * LONG, long_end + (place - longs) * SHORT)
    size = jnp.where(place < longs, LONG, SHORT)
    last = place == longs + shorts
    return (jnp.where(last, short_end, start), jnp.where(last, group, start + size), place <= longs + shorts)


def member_lanes(counts, first, rows, group, shift=0):
    shape = (rows, LANES)
    place = lax.broadcasted_iota(jnp.int32, (8, LANES), 1) - shift
    start, end, there = segment_bounds(counts, place, group)
    start = jnp.where(there & (place >= 0), start, group)
    start, end = start[:1], end[:1]
    frame = first + lax.broadcasted_iota(jnp.int32, shape, 0)
    return (frame >= start) & (frame < end)


def block_range(counts, step, group, inner):
    longs, shorts = counts
    long_end = longs * LONG
    short_end = long_end + shorts * SHORT

    def number(frame):
        place = jnp.where(frame < long_end, frame // LONG, longs + (frame - long_end) // SHORT)
        return jnp.where(frame < short_end, place, longs + shorts)

    first = segment_bounds(counts, number(step * BLOCK), group)[0]
    last = segment_bounds(counts, number(step * BLOCK + BLOCK - 1), group)[1]
    return (first // inner, (last + inner - 1) // inner)


def head_lanes(shape, head, size):
    lane = lax.broadcasted_iota(jnp.int32, shape, 1)
    return (lane >= head * size) & (lane < (head + 1) * size)


def split_three(v):
    hi = v.astype(BF16).astype(F32)
    rest = v - hi
    mid = rest.astype(BF16).astype(F32)
    return (hi, mid, rest - mid)


def spread_columns(columns, shape):
    lane = lax.broadcasted_iota(jnp.int32, shape, 1)
    out = jnp.zeros(shape, F32)
    for place, column in enumerate(columns):
        out = jnp.where(lane == place, column, out)
    return out


def chunk_rows(ref, lead, step):
    places, chunks, frames = ref.shape[0], ref.shape[-3], ref.shape[-2]
    per = BLOCK // frames
    steps = places // per
    at = (pl.ds(step % steps * per, per),) + lead + (step // steps,)
    return ref[at].reshape(BLOCK, LANES)


def attn_fwd_kernel(
    heads, size, group, counts_ref, qkv_ref, out_ref, full_ref, lse_ref, kcat, v_all, s_scr
):
    step = pl.program_id(0)
    counts = (counts_ref[0], counts_ref[1])

    @pl.when(step == 0)
    def _():
        chunks = qkv_ref.shape[2]
        span = group // chunks
        for chunk in range(chunks):
            rows = slice(chunk * span, (chunk + 1) * span)
            kcat[rows, :LANES] = qkv_ref[:, 1, chunk].reshape(span, LANES)
            v_all[rows, :] = qkv_ref[:, 2, chunk].reshape(span, LANES)
        kcat[:, LANES:] = jnp.where(member_lanes(counts, 0, group, group), 0.0, -BIG).astype(BF16)

    q = chunk_rows(qkv_ref, (0,), step).astype(F32) * (size ** -0.5)
    member = jnp.where(member_lanes(counts, step * BLOCK, BLOCK, group), 1.0, 0.0).astype(BF16)
    queries = []
    for head in range(heads):
        mine = jnp.where(head_lanes(q.shape, head, size), q, 0.0).astype(BF16)
        queries.append(jnp.concatenate([mine, member], 1))
    low, high = block_range(counts, step, group, INNER_FWD)

    def scores(j, tops):
        keys = kcat[pl.ds(pl.multiple_of(j * INNER_FWD, INNER_FWD), INNER_FWD), :]
        new = []
        for head in range(heads):
            s = dot(queries[head], keys, NT)
            s_scr[head, j] = s
            top = tops[head]
            for part in range(INNER_FWD // LANES):
                top = jnp.maximum(top, s[:, part * LANES : (part + 1) * LANES])
            new.append(top)
        return tuple(new)

    start = tuple(jnp.full((BLOCK, LANES), -BIG, F32) for _ in range(heads))
    tops = lax.fori_loop(low, high, scores, start)
    tops = [jnp.max(t, 1, keepdims=True) for t in tops]
    tops = [jnp.broadcast_to(t, (BLOCK, LANES)) for t in tops]

    def weigh(j, carried):
        sums, accs = carried
        values = v_all[pl.ds(pl.multiple_of(j * INNER_FWD, INNER_FWD), INNER_FWD), :]
        new_sums, new_accs = [], []
        for head in range(heads):
            total = sums[head]
            parts = []
            for part in range(INNER_FWD // LANES):
                p = jnp.exp(s_scr[head, j, :, part * LANES : (part + 1) * LANES] - tops[head])
                total = total + p
                parts.append(p.astype(BF16))
            new_sums.append(total)
            new_accs.append(accs[head] + dot(jnp.concatenate(parts, 1), values))
        return (tuple(new_sums), tuple(new_accs))

    zeros = tuple(jnp.zeros((BLOCK, LANES), F32) for _ in range(heads))
    sums, accs = lax.fori_loop(low, high, weigh, (zeros, zeros))
    result = None
    lane = lax.broadcasted_iota(jnp.int32, (BLOCK, LANES), 1)
    shifted = jnp.where(member_lanes(counts, step * BLOCK, BLOCK, group, 3), 1.0, 0.0)
    for head in range(heads):
        total = jnp.sum(sums[head], 1, keepdims=True)
        mine = accs[head] / total
        if result is None:
            result = mine
        else:
            result = jnp.where(head_lanes(mine.shape, head, size), mine, result)
        lse = tops[head] + jnp.log(jnp.broadcast_to(total, (BLOCK, LANES)))
        spread = spread_columns(split_three(lse), (BLOCK, LANES))
        lse_ref[head, :, :LANES] = queries[head][:, :LANES]
        lse_ref[head, :, LANES:] = jnp.where(lane < 3, -spread, shifted).astype(BF16)
    full_ref[...] = result
    out_ref[...] = result.astype(BF16).reshape(out_ref.shape)


def attend_forward(qkv, counts, size):
    places, _, chunks, frames, _ = qkv.shape
    group = places * chunks * frames
    heads = LANES // size
    per = BLOCK // frames
    each = places // per
    return pl.pallas_call(
        functools.partial(attn_fwd_kernel, heads, size, group),
        grid=(group // BLOCK,),
        in_specs=[pl.BlockSpec(memory_space=pltpu.SMEM), whole(qkv.shape)],
        out_specs=[
            pl.BlockSpec((per, 1, frames, LANES), lambda i: (i % each, i // each, 0, 0)),
            pl.BlockSpec((BLOCK, LANES), lambda i: (i, 0)),
            pl.BlockSpec((heads, BLOCK, 2 * LANES), lambda i: (0, i, 0)),
        ],
        out_shape=[
            jax.ShapeDtypeStruct((places, chunks, frames, LANES), BF16),
            jax.ShapeDtypeStruct((group, LANES), F32),
            jax.ShapeDtypeStruct((heads, group, 2 * LANES), BF16),
        ],
        scratch_shapes=[
            pltpu.VMEM((group, 2 * LANES), BF16),
            pltpu.VMEM((group, LANES), BF16),
            pltpu.VMEM((heads, group // INNER_FWD, BLOCK, INNER_FWD), F32),
        ],
        compiler_params=compiler_params(),
        cost_estimate=cost(16 * group * group * LANES, 6 << 20, heads * group * group),
        name="attend_forward",
    )(counts, qkv)


def attn_bwd_kernel(
    heads, size, group, counts_ref, qkv_ref, full_ref, qcat, grad_ref, out_ref,
    gcat, k_turned, dq_turned,
):
    step = pl.program_id(0)
    counts = (counts_ref[0], counts_ref[1])
    blocks = group // BLOCK
    places, _, _, frames, _ = qkv_ref.shape
    per = BLOCK // frames
    each = places // per

    def put(part, j, value):
        out_ref[pl.ds(j % each * per, per), part, j // each] = value.astype(BF16).reshape(
            per, frames, LANES
        )

    @pl.when(step == 0)
    def _():
        dq_turned[...] = jnp.zeros_like(dq_turned)

        def prepare(j, _):
            rows = pl.ds(pl.multiple_of(j * BLOCK, BLOCK), BLOCK)
            g = chunk_rows(grad_ref, (), j).astype(F32)
            product = g * full_ref[rows, :]
            for head in range(heads):
                own = head_lanes((BLOCK, LANES), head, size)
                delta = jnp.sum(jnp.where(own, product, 0.0), 1, keepdims=True)
                delta = jnp.broadcast_to(delta, (BLOCK, LANES))
                gcat[head, rows, :LANES] = jnp.where(own, g, 0.0).astype(BF16)
                spread = spread_columns(split_three(delta), (BLOCK, LANES))
                gcat[head, rows, LANES:] = (-spread).astype(BF16)
            k = chunk_rows(qkv_ref, (1,), j).astype(F32)
            k_turned[j] = jnp.transpose(k).astype(BF16)
            return 0

        lax.fori_loop(0, blocks, prepare, 0)

    lane = lax.broadcasted_iota(jnp.int32, (BLOCK, LANES), 1)
    member = member_lanes(counts, step * BLOCK, BLOCK, group, 3)
    tail = jnp.where(lane < 3, 1.0, jnp.where(member, 0.0, -BIG)).astype(BF16)
    keys = jnp.concatenate([chunk_rows(qkv_ref, (1,), step), tail], 1)
    ones = jnp.where(lane < 3, 1.0, 0.0).astype(BF16)
    values = jnp.concatenate([chunk_rows(qkv_ref, (2,), step), ones], 1)

    def one(j, carried):
        dk, dv = carried
        cols = pl.ds(pl.multiple_of(j * INNER_BWD, INNER_BWD), INNER_BWD)
        for head in range(heads):
            qc = qcat[head, cols, :]
            gc = gcat[head, cols, :]
            p = jnp.exp(dot(keys, qc, NT))
            ds = (p * dot(values, gc, NT)).astype(BF16)
            dv = dv + dot(p.astype(BF16), gc[:, :LANES])
            dk = dk + dot(ds, qc[:, :LANES])
            mine = slice(head * size, (head + 1) * size)
            dq_turned[j, mine, :] += dot(k_turned[step, mine, :], ds)
        return (dk, dv)

    zero = jnp.zeros((BLOCK, LANES), F32)
    low, high = block_range(counts, step, group, INNER_BWD)
    dk, dv = lax.fori_loop(low, high, one, (zero, zero))
    put(1, step, dk)
    put(2, step, dv)

    @pl.when(step == blocks - 1)
    def _():
        def finish(j, _):
            put(0, j, jnp.transpose(dq_turned[j]) * (size ** -0.5))
            return 0

        lax.fori_loop(0, blocks, finish, 0)


def attend_backward(qkv, counts, size, full, lse, grad):
    places, _, chunks, frames, _ = qkv.shape
    group = places * chunks * frames
    heads = LANES // size
    steps = group // BLOCK
    return pl.pallas_call(
        functools.partial(attn_bwd_kernel, heads, size, group),
        grid=(steps,),
        in_specs=[
            pl.BlockSpec(memory_space=pltpu.SMEM),
            whole(qkv.shape),
            whole(full.shape),
            whole(lse.shape),
            whole(grad.shape),
        ],
        out_specs=whole(qkv.shape),
        out_shape=jax.ShapeDtypeStruct(qkv.shape, BF16),
        scratch_shapes=[
            pltpu.VMEM((heads, group, 2 * LANES), BF16),
            pltpu.VMEM((steps, LANES, BLOCK), BF16),
            pltpu.VMEM((group // INNER_BWD, LANES, INNER_BWD), F32),
        ],
        compiler_params=compiler_params(),
        cost_estimate=cost(32 * group * group * LANES, 9 << 20, heads * group * group),
        name="attend_backward",
    )(counts, qkv, full, lse, grad)


def half_gate(field):
    return 0.5 * jnp.tanh(0.5 * field) + 0.5


def hidden_units(pre):
    gate = half_gate(pre)
    hidden = pre * gate
    return (hidden.astype(BF16), (gate + hidden * (1.0 - gate)).astype(BF16))


def ffn_fwd_kernel(
    x_ref, gain_ref, last_gain_ref, up_ref, win_ref, wout_ref,
    out_ref, down_ref, gain_grad_ref, slope_ref, hid_ref, entered_ref, total,
):
    step = pl.program_id(0)

    @pl.when(step == 0)
    def _():
        entered_ref[...] = layer_norm(x_ref[...], gain_ref[...])[0].astype(BF16)
        total[...] = jnp.zeros_like(total)

    hidden, slope = hidden_units(dot(entered_ref[...], win_ref[...]))
    slope_ref[...] = slope
    hid_ref[...] = hidden
    total[...] += dot(hidden, wout_ref[...])

    @pl.when(step == pl.num_programs(0) - 1)
    def _():
        gain = last_gain_ref[...]
        shaped, normed, inverse = layer_norm(x_ref[...] + 0.5 * total[...], gain)
        out_ref[...] = shaped.astype(BF16)
        through, grad_gain = norm_back(up_ref[...].astype(F32), normed, inverse, gain)
        down_ref[...] = through
        gain_grad_ref[...] = grad_gain


def ffn_forward(stream, gain_row, weight_in, weight_out, last_gain, upstream):
    rows, model = stream.shape
    units = weight_in.shape[1]
    wide = min(units, 1024)
    return pl.pallas_call(
        ffn_fwd_kernel,
        grid=(units // wide,),
        in_specs=[
            whole((rows, model)),
            whole((1, model)),
            whole((1, model)),
            whole((rows, model)),
            pl.BlockSpec((model, wide), lambda s: (0, s)),
            pl.BlockSpec((wide, model), lambda s: (s, 0)),
        ],
        out_specs=[whole((rows, model)), whole((rows, model)), whole((1, model))]
        + [pl.BlockSpec((rows, wide), lambda s: (0, s))] * 2
        + [whole((rows, model))],
        out_shape=[
            jax.ShapeDtypeStruct((rows, model), BF16),
            jax.ShapeDtypeStruct((rows, model), F32),
            jax.ShapeDtypeStruct((1, model), F32),
            jax.ShapeDtypeStruct((rows, units), BF16),
            jax.ShapeDtypeStruct((rows, units), BF16),
            jax.ShapeDtypeStruct((rows, model), BF16),
        ],
        scratch_shapes=[pltpu.VMEM((rows, model), F32)],
        compiler_params=compiler_params(),
        cost_estimate=cost(4 * rows * model * units, 4 * model * units + 4 * rows * units),
        name="ffn_forward",
    )(stream, gain_row, last_gain, upstream, weight_in, weight_out)


def ffn_bwd_kernel(
    x_ref, gain_ref, up_ref, slope_ref, win_ref, wout_ref,
    down_ref, gain_grad_ref, half_ref, grad_ref, total,
):
    step = pl.program_id(0)

    @pl.when(step == 0)
    def _():
        half_ref[...] = (0.5 * up_ref[...]).astype(BF16)
        total[...] = jnp.zeros_like(total)

    grad = (dot(half_ref[...], wout_ref[...], NT) * slope_ref[...].astype(F32)).astype(BF16)
    grad_ref[...] = grad
    total[...] += dot(grad, win_ref[...], NT)

    @pl.when(step == pl.num_programs(0) - 1)
    def _():
        gain = gain_ref[...]
        normed, inverse = layer_norm(x_ref[...].astype(F32), gain)[1:]
        through, grad_gain = norm_back(total[...], normed, inverse, gain)
        down_ref[...] = up_ref[...] + through
        gain_grad_ref[...] = grad_gain


def ffn_backward(upstream, stream, slope, gain_row, weight_in, weight_out):
    rows, model = stream.shape
    units = weight_in.shape[1]
    wide = min(units, 1024)
    return pl.pallas_call(
        ffn_bwd_kernel,
        grid=(units // wide,),
        in_specs=[
            whole((rows, model)),
            whole((1, model)),
            whole((rows, model)),
            pl.BlockSpec((rows, wide), lambda s: (0, s)),
            pl.BlockSpec((model, wide), lambda s: (0, s)),
            pl.BlockSpec((wide, model), lambda s: (s, 0)),
        ],
        out_specs=[
            whole((rows, model)),
            whole((1, model)),
            whole((rows, model)),
            pl.BlockSpec((rows, wide), lambda s: (0, s)),
        ],
        out_shape=[
            jax.ShapeDtypeStruct((rows, model), F32),
            jax.ShapeDtypeStruct((1, model), F32),
            jax.ShapeDtypeStruct((rows, model), BF16),
            jax.ShapeDtypeStruct((rows, units), BF16),
        ],
        scratch_shapes=[pltpu.VMEM((rows, model), F32)],
        compiler_params=compiler_params(),
        cost_estimate=cost(4 * rows * model * units, 4 * model * units + 6 * rows * units),
        name="ffn_backward",
    )(stream, gain_row, upstream, slope, weight_in, weight_out)


def hidden_kernel(up_ref, slope_ref, wout_ref, half_ref, grad_ref):
    @pl.when(pl.program_id(0) == 0)
    def _():
        half_ref[...] = (0.5 * up_ref[...]).astype(BF16)

    grad = dot(half_ref[...], wout_ref[...], NT) * slope_ref[...].astype(F32)
    grad_ref[...] = grad.astype(BF16)


def hidden_gradient(upstream, slope, weight_out):
    rows, model = upstream.shape
    units = weight_out.shape[0]
    wide = min(units, 1024)
    return pl.pallas_call(
        hidden_kernel,
        grid=(units // wide,),
        in_specs=[
            whole((rows, model)),
            pl.BlockSpec((rows, wide), lambda s: (0, s)),
            pl.BlockSpec((wide, model), lambda s: (s, 0)),
        ],
        out_specs=[whole((rows, model)), pl.BlockSpec((rows, wide), lambda s: (0, s))],
        out_shape=[
            jax.ShapeDtypeStruct((rows, model), BF16),
            jax.ShapeDtypeStruct((rows, units), BF16),
        ],
        compiler_params=compiler_params(),
        cost_estimate=cost(2 * rows * model * units, 2 * model * units + 6 * rows * units),
        name="hidden_gradient",
    )(upstream, slope, weight_out)


def down_kernel(
    x_ref, gain_ref, up_ref, grad_ref, weight_ref, down_ref, half_ref, gain_grad_ref, total
):
    step = pl.program_id(0)

    @pl.when(step == 0)
    def _():
        total[...] = jnp.zeros_like(total)

    total[...] += dot(grad_ref[...], weight_ref[...], NT)

    @pl.when(step == pl.num_programs(0) - 1)
    def _():
        gain = gain_ref[...]
        normed, inverse = layer_norm(x_ref[...].astype(F32), gain)[1:]
        through, grad_gain = norm_back(total[...], normed, inverse, gain)
        down = up_ref[...] + through
        down_ref[...] = down.astype(down_ref.dtype)
        half_ref[...] = (0.5 * down).astype(BF16)
        gain_grad_ref[...] = grad_gain


def stream_gradient(upstream, stream, grad, gain_row, weight, down_type):
    rows, model = stream.shape
    units = weight.shape[1]
    wide = min(units, 1024)
    return pl.pallas_call(
        down_kernel,
        grid=(units // wide,),
        in_specs=[
            whole((rows, model)),
            whole((1, model)),
            whole((rows, model)),
            pl.BlockSpec((rows, wide), lambda s: (0, s)),
            pl.BlockSpec((model, wide), lambda s: (0, s)),
        ],
        out_specs=[whole((rows, model)), whole((rows, model)), whole((1, model))],
        out_shape=[
            jax.ShapeDtypeStruct((rows, model), down_type),
            jax.ShapeDtypeStruct((rows, model), BF16),
            jax.ShapeDtypeStruct((1, model), F32),
        ],
        scratch_shapes=[pltpu.VMEM((rows, model), F32)],
        compiler_params=compiler_params(),
        cost_estimate=cost(2 * rows * model * units, 2 * model * units + 2 * rows * units),
        name="stream_gradient",
    )(stream, gain_row, upstream, grad, weight)


def turn(field, cosines, sines, size):
    repeats = field.shape[1] // cosines.shape[1]
    cosines = jnp.concatenate([cosines] * repeats, 1)
    sines = jnp.concatenate([sines] * repeats, 1)
    lane = lax.broadcasted_iota(jnp.int32, field.shape, 1)
    half = size // 2
    width = field.shape[1]
    swapped = jnp.where(
        lane % size < half,
        pltpu.roll(field, width - half, 1),
        pltpu.roll(field, half, 1),
    )
    return field * cosines + swapped * sines


def rope_tables(position, size):
    half = size // 2
    lane = jnp.arange(LANES, dtype=jnp.int32)
    freqs = jnp.exp(
        -jnp.log(jnp.float32(ROPE_BASE)) * (lane % half).astype(jnp.float32) / half
    )
    angles = position.astype(jnp.float32)[:, None] * freqs[None, :]
    signs = jnp.where(lane % size < half, -1.0, 1.0)
    return (jnp.cos(angles), jnp.sin(angles) * signs[None, :])


def front_kernel(
    size, ffn_steps, pieces, row_ref, x_ref, gain_ref, win_ref, wout_ref,
    wq_ref, wk_ref, wv_ref, cos_ref, sin_ref, *refs,
):
    refs = refs[-(6 + pieces) :]
    out_ref, slope_ref, hid_ref, entered_ref, next_ref = refs[:5]
    outs, total = refs[5:-1], refs[-1]
    step = pl.program_id(0)

    @pl.when(step == 0)
    def _():
        gain = gain_ref[0:1, :]
        entered_ref[...] = layer_norm(x_ref[0].astype(F32), gain)[0].astype(BF16)
        total[...] = jnp.zeros_like(total)

    @pl.when(step < ffn_steps)
    def _():
        hidden, slope = hidden_units(dot(entered_ref[...], win_ref[...]))
        slope_ref[...] = slope
        hid_ref[...] = hidden
        total[...] += dot(hidden, wout_ref[...])

    @pl.when(step == ffn_steps)
    def _():
        out = x_ref[0].astype(F32) + 0.5 * total[...]
        out_ref[...] = out
        next_ref[...] = layer_norm(out, gain_ref[1:2, :])[0].astype(BF16)

    each = (pl.num_programs(0) - ffn_steps) // pieces
    for piece, out in enumerate(outs):

        @pl.when((step >= ffn_steps) & ((step - ffn_steps) // each == piece))
        def _():
            for place, weight in enumerate((wq_ref, wk_ref, wv_ref)):
                made = dot(next_ref[...], weight[...])
                if place < 2:
                    made = turn(made, cos_ref[...], sin_ref[...], size)
                made = made.astype(BF16)
                for target in range(out.shape[0]):
                    out[target, place, 0] = made[:, target * LANES : (target + 1) * LANES]


def front(
    frames, row, gains, weight_in, weight_out, weight, cosines, sines,
    places, chunks, size, before=(),
):
    given, rows, model = frames.shape
    units = weight_in.shape[1]
    wide = min(units, 1024)
    ffn_steps = units // wide
    turned_wide = TURNED
    turns = model // turned_wide
    pieces = model // (places * LANES)
    each = turns // pieces
    piece = jax.ShapeDtypeStruct((places, 3, chunks, rows, LANES), BF16)

    def ffn_at(s, row):
        return jnp.minimum(s, ffn_steps - 1)

    def turn_at(s):
        return jnp.maximum(s - ffn_steps, 0)

    def piece_at(number):
        return lambda s, row: (
            jnp.clip(s - ffn_steps - number * each, 0, each - 1), 0, row[0], 0, 0
        )

    row_block = pl.BlockSpec((rows, model), lambda s, row: (row[0], 0))
    unit_block = pl.BlockSpec((rows, wide), lambda s, row: (row[0], ffn_at(s, row)))
    angle_block = pl.BlockSpec((rows, LANES), lambda s, row: (row[0], 0))
    out_shape = [
        jax.ShapeDtypeStruct((chunks * rows, model), F32),
        jax.ShapeDtypeStruct((chunks * rows, units), BF16),
        jax.ShapeDtypeStruct((chunks * rows, units), BF16),
        jax.ShapeDtypeStruct((chunks * rows, model), BF16),
        jax.ShapeDtypeStruct((chunks * rows, model), BF16),
    ] + [piece] * pieces
    in_specs = [
        pl.BlockSpec((1, rows, model), lambda s, row: (row[0] if given > 1 else 0, 0, 0)),
        whole(gains.shape),
        pl.BlockSpec((model, wide), lambda s, row: (0, ffn_at(s, row))),
        pl.BlockSpec((wide, model), lambda s, row: (ffn_at(s, row), 0)),
        pl.BlockSpec((model, turned_wide), lambda s, row: (0, turn_at(s))),
        pl.BlockSpec((model, turned_wide), lambda s, row: (0, turns + turn_at(s))),
        pl.BlockSpec((model, turned_wide), lambda s, row: (0, 2 * turns + turn_at(s))),
        angle_block,
        angle_block,
    ]
    grid_spec = pltpu.PrefetchScalarGridSpec(
        num_scalar_prefetch=1,
        grid=(ffn_steps + turns,),
        in_specs=in_specs + [pl.BlockSpec(memory_space=pl.ANY)] * len(before),
        out_specs=[row_block, unit_block, unit_block, row_block, row_block]
        + [
            pl.BlockSpec((turned_wide // LANES, 3, 1, rows, LANES), piece_at(number))
            for number in range(pieces)
        ],
        scratch_shapes=[pltpu.VMEM((rows, model), F32)],
    )
    return pl.pallas_call(
        functools.partial(front_kernel, size, ffn_steps, pieces),
        grid_spec=grid_spec,
        out_shape=out_shape,
        input_output_aliases={1 + len(in_specs) + i: i for i in range(len(before))},
        compiler_params=compiler_params(),
        cost_estimate=cost(
            4 * rows * model * units + 6 * rows * model * model,
            4 * model * units + 6 * model * model + 4 * rows * units + 16 * rows * model,
        ),
        name="front",
    )(
        row, frames, gains, weight_in, weight_out, weight, weight, weight,
        cosines, sines, *before,
    )


def projection_kernel(
    size, pieces, cos_ref, sin_ref, x_ref, gain_ref, up_ref, weight_ref, *refs
):
    backs, refs = refs[:pieces], refs[pieces:]
    grad_ref, down_ref, half_ref, gain_grad_ref, total = refs
    step = pl.program_id(0)

    @pl.when(step == 0)
    def _():
        total[...] = jnp.zeros_like(total)

    rotated = step < 2
    cosines = jnp.where(rotated, cos_ref[...], 1.0)
    sines = jnp.where(rotated, -sin_ref[...], 0.0)
    places, _, chunks, frames, _ = backs[0].shape
    per = TURNED // LANES
    for piece, back in enumerate(backs):
        for first in range(0, places, per):
            for chunk in range(chunks):
                rows = slice(chunk * frames, (chunk + 1) * frames)
                field = jnp.concatenate([back[first + i, 0, chunk] for i in range(per)], 1)
                made = turn(field.astype(F32), cosines[rows], sines[rows], size).astype(BF16)
                start = (piece * places + first) * LANES
                grad_ref[rows, start : start + TURNED] = made
    total[...] += dot(grad_ref[...], weight_ref[...], NT)

    @pl.when(step == pl.num_programs(0) - 1)
    def _():
        gain = gain_ref[...]
        normed, inverse = layer_norm(x_ref[...], gain)[1:]
        through, grad_gain = norm_back(total[...], normed, inverse, gain)
        down = up_ref[...] + through
        down_ref[...] = down
        half_ref[...] = (0.5 * down).astype(BF16)
        gain_grad_ref[...] = grad_gain


def projection_backward(backs, cosines, sines, size, upstream, stream, gain_row, weight):
    places, kinds, chunks, frames, _ = backs[0].shape
    pieces = len(backs)
    rows, model = stream.shape
    block = pl.BlockSpec((places, 1, chunks, frames, LANES), lambda s: (0, s, 0, 0, 0))
    return pl.pallas_call(
        functools.partial(projection_kernel, size, pieces),
        grid=(kinds,),
        in_specs=[
            whole(cosines.shape),
            whole(sines.shape),
            whole((rows, model)),
            whole((1, model)),
            whole((rows, model)),
            pl.BlockSpec((model, model), lambda s: (0, s)),
        ]
        + [block] * pieces,
        out_specs=[
            pl.BlockSpec((rows, model), lambda s: (0, s)),
            whole((rows, model)),
            whole((rows, model)),
            whole((1, model)),
        ],
        out_shape=[
            jax.ShapeDtypeStruct((rows, kinds * model), BF16),
            jax.ShapeDtypeStruct((rows, model), F32),
            jax.ShapeDtypeStruct((rows, model), BF16),
            jax.ShapeDtypeStruct((1, model), F32),
        ],
        scratch_shapes=[pltpu.VMEM((rows, model), F32)],
        compiler_params=compiler_params(),
        cost_estimate=cost(6 * rows * model * model, 6 * model * model + 22 * rows * model),
        name="projection_backward",
    )(cosines, sines, stream, gain_row, upstream, weight, *backs)


def flipped(axis_bit, count):
    axis, bit = axis_bit
    items, heads = count
    if axis == "items":
        return [(i * heads + h, (i ^ bit) * heads + h) for i in range(items) for h in range(heads)]
    return [(i * heads + h, i * heads + (h ^ bit)) for i in range(items) for h in range(heads)]


def swap(value, axis_bit):
    count = (lax.axis_size("items"), lax.axis_size("heads"))
    return lax.ppermute(value, EVERY, flipped(axis_bit, count))


def branched(always, work):
    def empty():
        return jax.tree.map(lambda leaf: jnp.zeros(leaf.shape, leaf.dtype), jax.eval_shape(work))

    return lax.optimization_barrier(lax.cond(always, work, empty))


def fenced(always, scatters, work):
    def run():
        moves = [scatter.move() for scatter in scatters]
        return (branched(always, work) if any(moves) else work(), moves)

    result, moves = branched(always, run)
    for scatter, parts in zip(scatters, moves):
        scatter.take(parts)
    return result


def moved(scatter):
    scatter.take(scatter.move())


def other_core(value):
    return swap(value, ("heads", 1))


def exchange(value):
    half = lax.axis_size("heads") // 2
    groups = [[side * half + i for i in range(half)] for side in range(2)]
    return lax.all_to_all(
        value, "heads", split_axis=0, concat_axis=0, tiled=True, axis_index_groups=groups
    )


def across(value):
    return swap(value, ("heads", lax.axis_size("heads") // 2))


def gathered(own, other, side):
    return jnp.concatenate([jnp.where(side == 0, own, other), jnp.where(side == 0, other, own)], 0)


def parted(value, side):
    low, high = jnp.split(value, 2, 0)
    return (jnp.where(side == 0, low, high), jnp.where(side == 0, high, low))


def own_rows(left_ref, heads, core, target, first):
    rows, model = left_ref.shape
    each = model // heads
    for place in range(heads // 2):
        if each % LANES == 0:
            start = pl.multiple_of((2 * place + core) * each, each)
            mine = jnp.transpose(left_ref[:, pl.ds(start, each)].astype(F32)).astype(BF16)
        else:
            pair = left_ref[:, 2 * place * each : 2 * (place + 1) * each]
            pair = jnp.transpose(pair.astype(F32))
            mine = jnp.where(core == 0, pair[:each], pair[each:]).astype(BF16)
        for half in range(2):
            start = (half * (heads // 2) + place) * (each // 2)
            target[start : start + each // 2, first : first + rows] = mine[
                half * (each // 2) : (half + 1) * (each // 2)
            ]


def turned_items(left, items, own, target, first):
    rows, model = left.shape
    each = model // items
    for item in range(items):
        part = jnp.transpose(left[:, item * each : (item + 1) * each].astype(F32)).astype(BF16)
        place = pl.multiple_of((own ^ item) * each, each)
        target[pl.ds(place, each), first : first + rows] = part


def share_shapes(items, heads, model, columns):
    lead = 2 if items > 1 else 1
    shape = (lead, heads // 2, model // heads // 2, columns // items)
    return [jax.ShapeDtypeStruct(shape, BF16)] * (4 if items > 1 else 2)


def out_grad_kernel(place_ref, up_own, up_other, hid_own, hid_other, *refs):
    targets, turned = refs[:-1], refs[-1]
    rows, model = up_own.shape
    items = 4 if len(targets) == 4 else 1

    @pl.when(pl.program_id(0) == 0)
    def _():
        turned_items(up_own[...], items, place_ref[1], turned, 0)
        turned_items(up_other[...], items, place_ref[1], turned, rows)

    hidden = jnp.concatenate([hid_own[...], hid_other[...]], 0)
    grad = dot(turned[...], hidden).astype(BF16)
    wide = grad.shape[1]
    each = targets[0].shape[2]
    parts = model // items // (2 * each)
    for r in range(items):
        for part in range(parts):
            for half in range(2):
                first = ((r * parts + part) * 2 + half) * each
                piece = grad[first : first + each]
                if half == 0:
                    target, at = targets[2 * (r % 2)], r // 2
                else:
                    target, at = targets[1 + 2 * (r // 2)], r % 2
                target[at, 0, :, part * wide : (part + 1) * wide] = piece


def out_grad(upstream, hidden, heads, place, items):
    rows, model = upstream[0].shape
    units = hidden[0].shape[1]
    wide = units // heads
    shapes = share_shapes(items, heads, model, units)
    block = (shapes[0].shape[0], 1) + shapes[0].shape[2:]
    hid_block = pl.BlockSpec((rows, wide), lambda s, place: (0, 2 * s + place[0]))
    grid_spec = pltpu.PrefetchScalarGridSpec(
        num_scalar_prefetch=1,
        grid=(heads // 2,),
        in_specs=[whole((rows, model))] * 2 + [hid_block] * 2,
        out_specs=[pl.BlockSpec(block, lambda s, place: (0, s, 0, 0))] * len(shapes),
        scratch_shapes=[pltpu.VMEM((model, 2 * rows), BF16)],
    )
    return pl.pallas_call(
        out_grad_kernel,
        grid_spec=grid_spec,
        out_shape=shapes,
        compiler_params=compiler_params(),
        cost_estimate=cost(2 * rows * model * units, 2 * model * units + 4 * rows * units),
        name="out_grad",
    )(place, *upstream, *hidden)


def column_grad_kernel(heads, items, split, place_ref, *refs):
    count = len(split)
    lefts, refs = refs[: 2 * count], refs[2 * count :]
    rights, refs = refs[: 2 * (count + sum(split))], refs[2 * (count + sum(split)) :]
    targets, turned = refs[:-count], refs[-count:]
    r = pl.program_id(0)
    rows = lefts[0].shape[0]

    @pl.when(r == 0)
    def _():
        for number in range(count):
            for other in range(2):
                own_rows(
                    lefts[2 * number + other], heads, place_ref[0], turned[number], other * rows
                )

    made = []
    at = 0
    for number in range(count):
        right = jnp.concatenate([rights[at][...], rights[at + 1][...]], 0)
        at += 2
        if split[number]:
            second = jnp.concatenate([rights[at][...], rights[at + 1][...]], 0)
            at += 2
            right = jnp.where((r ^ place_ref[1]) < items // 2, right, second)
        made.append(dot(turned[number][...], right).astype(BF16))
    made = made[0] if count == 1 else jnp.concatenate(made, 1)
    half = made.shape[0] // 2
    top, low = made[:half].reshape(targets[0].shape), made[half:].reshape(targets[0].shape)
    if len(targets) == 2:
        targets[0][...] = top
        targets[1][...] = low
        return

    @pl.when(r % 2 == 0)
    def _():
        targets[0][...] = top

    @pl.when(r % 2 == 1)
    def _():
        targets[2][...] = top

    @pl.when(r < 2)
    def _():
        targets[1][...] = low

    @pl.when(r >= 2)
    def _():
        targets[3][...] = low


def column_grads(lefts, rights, heads, place, items):
    if items == 1:
        flat = [
            (left, part)
            for left, right in zip(lefts, rights)
            for part in (right if isinstance(right[0], tuple) else (right,))
        ]
        lefts, rights = [left for left, _ in flat], [right for _, right in flat]
    split = [isinstance(right[0], tuple) for right in rights]
    rows, model = lefts[0][0].shape
    parts = []
    for right, two in zip(rights, split):
        parts += [part for pair in right for part in pair] if two else list(right)
    columns = sum(part.shape[1] for part in parts) // 2
    shapes = share_shapes(items, heads, model, columns)
    block = (1,) + shapes[0].shape[1:]
    right_specs = []
    for right, two in zip(rights, split):
        if two:
            share = pl.BlockSpec(
                (rows, right[0][0].shape[1] * 2 // items),
                lambda r, place: (0, (r ^ place[1]) % (items // 2)),
            )
            right_specs += [share] * 4
        else:
            share = pl.BlockSpec(
                (rows, right[0].shape[1] // items), lambda r, place: (0, r ^ place[1])
            )
            right_specs += [share] * 2
    maps = [
        lambda r, place: (r // 2, 0, 0, 0),
        lambda r, place: (jnp.minimum(r, 1), 0, 0, 0),
        lambda r, place: (r // 3, 0, 0, 0),
        lambda r, place: (r // 3, 0, 0, 0),
    ]
    grid_spec = pltpu.PrefetchScalarGridSpec(
        num_scalar_prefetch=1,
        grid=(items,),
        in_specs=[whole((rows, model))] * (2 * len(lefts)) + right_specs,
        out_specs=[pl.BlockSpec(block, index) for index in maps[: len(shapes)]],
        scratch_shapes=[pltpu.VMEM((model // 2, 2 * rows), BF16)] * len(lefts),
    )
    return pl.pallas_call(
        functools.partial(column_grad_kernel, heads, items, split),
        grid_spec=grid_spec,
        out_shape=shapes,
        compiler_params=compiler_params(),
        cost_estimate=cost(2 * rows * model * columns, 4 * model * columns),
        name="column_grads",
    )(place, *[part for left in lefts for part in left], *parts)


class Scatter:
    def __init__(self, keep_top, keep_low, *sends):
        self.keep = [keep_top, keep_low]
        self.got, self.early = [], []
        self.route(list(sends), FIRST[: len(sends)])

    def route(self, sends, routes):
        self.sends, self.routes = sends, routes

    def move(self):
        return [swap(send, route) for send, route in zip(self.sends, self.routes)]

    def take(self, moved):
        self.early, self.got = self.got, moved
        self.route([], [])

    def second(self, sends):
        self.route(sends, FIRST[::-1][: len(sends)])


def second_kernel(*refs):
    count = len(refs) // 3
    for number in range(count):
        keep, got, out = refs[2 * number], refs[2 * number + 1], refs[2 * count + number]
        out[...] = (keep[0].astype(F32) + got[0].astype(F32)).astype(BF16)


def second_sums(*scatters):
    terms = [
        part
        for scatter in scatters
        if scatter.got
        for keep, got in zip(scatter.keep, scatter.got)
        for part in (keep, got)
    ]
    if not terms:
        return [[] for _ in scatters]
    shape = terms[0].shape
    outs = []
    in_specs, out_specs = [], []
    for term in terms:
        in_specs.append(
            pl.BlockSpec((1, 2) + term.shape[2:], lambda g: (1, g, 0, 0))
        )
    for term in terms[::2]:
        out_specs.append(pl.BlockSpec((2,) + term.shape[2:], lambda g: (g, 0, 0)))
        outs.append(jax.ShapeDtypeStruct(term.shape[1:], BF16))
    made = pl.pallas_call(
        second_kernel,
        grid=(shape[1] // 2,),
        in_specs=in_specs,
        out_specs=out_specs,
        out_shape=outs,
        compiler_params=compiler_params(),
        cost_estimate=cost(0, 6 * sum(out.size for out in outs)),
        name="second_sums",
    )(*terms)
    return [list(made[2 * i : 2 * i + 2]) for i in range(len(scatters))]


def last_kernel(*refs):
    out = refs[-1]
    for number in range(out.shape[1]):
        for half in range(2):
            terms = refs[6 * number + 3 * half : 6 * number + 3 * half + 3]
            out[:, number, half] = (
                terms[0][0].astype(F32) + terms[1][0].astype(F32) + terms[2][...].astype(F32)
            ).astype(BF16)


def last_sum(*scatters, columns=None):
    if not scatters[0].got:
        items = lax.axis_size("items")
        values = []
        for scatter in scatters:
            value = jnp.stack([keep[0] for keep in scatter.keep], 1)
            if columns is not None:
                starts = [sum(columns[:i]) for i in range(len(columns))]
                parts = [
                    value[..., start : start + size].reshape(value.shape[:3] + (items, -1))
                    for start, size in zip(starts, columns)
                ]
                value = jnp.concatenate(parts, 4).reshape(value.shape)
            values.append(lax.psum_scatter(value, "items", scatter_dimension=3, tiled=True))
        return jnp.stack(values, 1)
    terms = [
        part
        for scatter in scatters
        for parts in zip(scatter.keep, scatter.early, scatter.got)
        for part in parts
    ]
    _, places, rows, wide = terms[0].shape
    held = pl.BlockSpec((1, 2, rows, wide), lambda g: (0, g, 0, 0))
    late = pl.BlockSpec((2, rows, wide), lambda g: (g, 0, 0))
    shape = (places, len(scatters), 2, rows, wide)
    return pl.pallas_call(
        last_kernel,
        grid=(places // 2,),
        in_specs=[held, held, late] * (2 * len(scatters)),
        out_specs=pl.BlockSpec((2,) + shape[1:], lambda g: (g, 0, 0, 0, 0)),
        out_shape=jax.ShapeDtypeStruct(shape, BF16),
        compiler_params=compiler_params(),
        cost_estimate=cost(0, 8 * places * len(scatters) * 2 * rows * wide),
        name="last_sum",
    )(*terms)


def along_z(value):
    heads = lax.axis_size("heads")
    groups = [[core + 2 * z for z in range(heads // 2)] for core in range(2)]
    made = lax.psum_scatter(
        value, "heads", scatter_dimension=0, tiled=False, axis_index_groups=groups
    )
    return [made[i].reshape(-1, made.shape[-1]) for i in range(made.shape[0])]


def unfold_kernel(share_ref, out_ref):
    each = share_ref.shape[0]
    span = out_ref.shape[0]
    for part in range(share_ref.shape[1] // span):
        turned = jnp.transpose(share_ref[:, part * span : (part + 1) * span].astype(F32))
        out_ref[:, part * each : (part + 1) * each] = turned


def unfolded(share, span):
    each, wide = share.shape
    shape = (span, each * wide // span)
    return pl.pallas_call(
        unfold_kernel,
        out_shape=jax.ShapeDtypeStruct(shape, F32),
        cost_estimate=cost(0, 6 * each * wide),
        name="unfolded",
    )(share)


def heads_kernel(grad_ref, weight_ref, *outs):
    step = pl.program_id(0)
    made = dot(grad_ref[...], weight_ref[...], NT).astype(BF16)
    for piece, out in enumerate(outs):

        @pl.when(step == piece)
        def _():
            places, chunks, frames, _ = out.shape
            for place in range(places):
                for chunk in range(chunks):
                    out[place, chunk] = made[
                        chunk * frames : (chunk + 1) * frames, place * LANES : (place + 1) * LANES
                    ]


def heads_gradient(grad, weight, places, chunks):
    rows, model = grad.shape
    wide = places * LANES
    pieces = model // wide
    shape = (places, chunks, rows // chunks, LANES)
    return pl.pallas_call(
        heads_kernel,
        grid=(pieces,),
        in_specs=[whole((rows, model)), pl.BlockSpec((wide, model), lambda s: (s, 0))],
        out_specs=[whole(shape)] * pieces,
        out_shape=[jax.ShapeDtypeStruct(shape, BF16)] * pieces,
        compiler_params=compiler_params(),
        cost_estimate=cost(2 * rows * model * model, 2 * model * model + 4 * rows * model),
        name="heads_gradient",
    )(grad, weight)


def sum_everywhere(value):
    for axis in EVERY:
        bit = 1
        while bit < lax.axis_size(axis):
            value = value + swap(value, (axis, bit))
            bit *= 2
    return value


def edges(block, width):
    ways = lax.axis_size("heads")
    half = ways // 2
    place = lax.axis_index("heads") % half
    ring = [(side * half + i, side * half + (i + 1) % half) for side in range(2) for i in range(half)]
    low = lax.ppermute(block[:, block.shape[1] - width :], "heads", ring)
    high = lax.ppermute(block[:, :width], "heads", [(to, at) for at, to in ring])
    low = jnp.where(place == 0, jnp.roll(low, 1, 0), low)
    high = jnp.where(place == half - 1, jnp.roll(high, -1, 0), high)
    return jnp.concatenate([low, block, high], axis=1)


def body(
    frames, cotangent, bucket_counts, gains, w_ffn1_in, w_ffn1_out, w_qkv, w_out,
    w_point_in, w_depth, w_point_out, w_ffn2_in, w_ffn2_out,
):
    chunks, here, model = frames.shape
    ways = lax.axis_size("heads")
    half = ways // 2
    items = 4 if lax.axis_size("items") == 4 else 1
    span = here * half
    group_len = here * ways
    size = model // HEADS
    reach = (KERNEL - 1) // 2
    rows = chunks * here
    pieces = model // (half * LANES)
    place = lax.axis_index("heads")
    side = place // half
    where = jnp.stack(
        [place % 2, lax.axis_index("items") if items > 1 else 0 * place]
    ).astype(jnp.int32)
    always = place >= 0
    first = jnp.arange(chunks, dtype=jnp.int32)[:, None] * span + place % half * here
    position = first + jnp.arange(here, dtype=jnp.int32)[None]
    cosines, sines = rope_tables(position.reshape(-1), size)
    depth_rows = w_depth.astype(F32)
    gain = [gains[i : i + 1] for i in range(6)]
    counts = lax.dynamic_index_in_dim(bucket_counts[:, 0], side, 0, keepdims=False)
    wide_position = first - reach + jnp.arange(here + 2 * reach, dtype=jnp.int32)[None]
    seg_wide = segment_ids(wide_position, counts[0], counts[1], group_len)
    seg_own = seg_wide[:, reach : reach + here]

    def mine(value):
        return lax.dynamic_index_in_dim(value, side, 0, keepdims=False)

    def theirs(value):
        return lax.dynamic_index_in_dim(value, 1 - side, 0, keepdims=False)

    def begin(chunk, row, before=()):
        return front(
            chunk, row.reshape(1).astype(jnp.int32), gains, w_ffn1_in, w_ffn1_out, w_qkv,
            cosines, sines, half, chunks, size, before,
        )

    before, other_frames = fenced(
        always, (), lambda: (begin(frames, side), across(theirs(frames)))
    )
    stream_one, slope_one, hid_one, ent_one, ent_att, *sent = begin(
        other_frames[None], 1 - side, before
    )
    stream = gathered(mine(frames), other_frames, side)
    qkv = [exchange(sent[0])]
    kept, contexts = [], []
    for number in range(pieces):

        def attend_now():
            return attend_forward(qkv[number], counts, size)

        def beside():
            extra = []
            if number + 1 < pieces:
                extra.append(exchange(sent[number + 1]))
            if number > 0:
                extra.append(exchange(kept[number - 1][0]))
            return extra

        def early():
            if number == 0:
                return [other_core(part) for part in (hid_one, ent_one, ent_att)]
            return [across(theirs(cotangent))] if number == 1 else []

        made, extra, others = fenced(always, (), lambda: (attend_now(), beside(), early()))
        kept.append(made)
        if number == 0:
            hid_one, ent_one, ent_att = zip((hid_one, ent_one, ent_att), others)
        elif number == 1:
            cot_other = others[0]
        if number + 1 < pieces:
            qkv.append(extra.pop(0))
        if number > 0:
            contexts.append(extra.pop(0))
    contexts.append(exchange(kept[-1][0]))
    if pieces == 1:
        cot_other = across(theirs(cotangent))
    fulls = [made[1] for made in kept]
    lses = [made[2] for made in kept]
    contexts = [part.transpose(1, 2, 0, 3).reshape(rows, -1) for part in contexts]
    context = jnp.concatenate(contexts, 1)
    stream_two = stream_one
    for number, part in enumerate(contexts):
        wide = part.shape[1]
        stream_two = stream_two + dot(part, w_out[number * wide : (number + 1) * wide])
    shaped, conv_normed, conv_inverse = layer_norm(stream_two, gain[2])
    conv_entered = shaped.astype(BF16)
    pointwise = dot(conv_entered, w_point_in)
    linear = pointwise[:, :model]
    sigmoid_gate = jax.nn.sigmoid(pointwise[:, model:])
    gated_low = (linear * sigmoid_gate).astype(BF16).reshape(chunks, here, model)
    widened = edges(gated_low, reach)
    depth_out = jnp.zeros((chunks, here, model), F32)
    for offset in range(KERNEL):
        same = (seg_wide[:, offset : offset + here] == seg_own)[:, :, None]
        depth_out = depth_out + depth_rows[offset] * jnp.where(
            same, widened[:, offset : offset + here], 0.0
        )
    depth_out = depth_out.reshape(rows, model)
    depth_shaped, depth_normed, depth_inverse = layer_norm(depth_out, gain[3])
    mixed_low = (depth_shaped * jax.nn.sigmoid(depth_shaped)).astype(BF16)
    stream_three = stream_two + dot(mixed_low, w_point_out)
    layer_out, grad_four, gain_five, slope_two, hid_two, ent_two = ffn_forward(
        stream_three, gain[4], w_ffn2_in, w_ffn2_out, gain[5],
        gathered(mine(cotangent), cot_other, side),
    )
    (grad_three, gain_four, half_two, grad_pre_two), hid_other, ent_other = fenced(
        always,
        (),
        lambda: (
            ffn_backward(grad_four, stream_three, slope_two, gain[4], w_ffn2_in, w_ffn2_out),
            other_core(hid_two),
            other_core(ent_two),
        ),
    )
    half_other, grad_pre_other = other_core(half_two), other_core(grad_pre_two)
    grad_mix = grad_three.astype(BF16)
    grad_norm_in = dot(grad_mix, w_point_out, NT) * silu_slope(depth_shaped)
    grad_depth, gain_three = norm_back(grad_norm_in, depth_normed, depth_inverse, gain[3])
    grad_depth_low = grad_depth.astype(BF16).reshape(chunks, here, model)
    grad_widened = edges(grad_depth_low, reach)
    grad_gated = jnp.zeros((chunks, here, model), F32)
    for offset in range(KERNEL):
        mirror = 2 * reach - offset
        same_back = (seg_wide[:, mirror : mirror + here] == seg_own)[:, :, None]
        grad_gated = grad_gated + depth_rows[offset] * jnp.where(
            same_back, grad_widened[:, mirror : mirror + here], 0.0
        )
    grad_gated = grad_gated.reshape(rows, model)
    grad_a = (grad_gated * sigmoid_gate).astype(BF16)
    grad_b = (grad_gated * linear * sigmoid_gate * (1.0 - sigmoid_gate)).astype(BF16)
    through, gain_two = norm_back(
        dot(grad_a, w_point_in[:, :model], NT) + dot(grad_b, w_point_in[:, model:], NT),
        conv_normed, conv_inverse, gain[2],
    )
    grad_two = grad_three + through
    grad_attn_out = grad_two.astype(BF16)
    grad_heads = list(heads_gradient(grad_attn_out, w_out, half, chunks))
    lefts = (mixed_low, conv_entered, context)

    def ffn_grads():
        return (
            [other_core(part) for part in lefts + (grad_a, grad_b)],
            exchange(grad_heads[0]),
            out_grad((half_two, half_other), (hid_two, hid_other), ways, where, items),
            column_grads(
                [(ent_two, ent_other)], [(grad_pre_two, grad_pre_other)], ways, where, items
            ),
        )

    others, grad_heads[0], shares_out, shares_in = fenced(always, (), ffn_grads)
    two_out, two_in = Scatter(*shares_out), Scatter(*shares_in)
    out_own, out_theirs = parted(layer_out, side)
    grads, backs = [], []
    for number in range(pieces):
        last = number == pieces - 1

        def beside():
            extra = []
            if not last:
                extra.append(exchange(grad_heads[number + 1]))
            if number > 0:
                extra.append(exchange(grads[number - 1]))
            if number == 0:
                extra.append(across(out_theirs))
                extra += [other_core(grad_mix), other_core(grad_attn_out)]
            return extra

        def attend_now():
            return attend_backward(
                qkv[number], counts, size, fulls[number], lses[number], grad_heads[number]
            )

        moving = (two_out,) if number == 0 else (two_out, two_in) if number == 1 else ()
        made, extra = fenced(always, moving, lambda: (attend_now(), beside()))
        grads.append(made)
        if not last:
            grad_heads[number + 1] = extra.pop(0)
        if number > 0:
            backs.append(extra.pop(0))
        if number == 0:
            out_other, *late = extra
            two_out.second(second_sums(two_out)[0])
    two_in.second(second_sums(two_in)[0])

    def middle_part():
        back = exchange(grads[-1])
        scatter = copy.copy(two_in)
        moved(scatter)
        shares = column_grads(
            list(zip(lefts, others[:3])),
            [
                (grad_mix, late[0]),
                ((grad_a, others[3]), (grad_b, others[4])),
                (grad_attn_out, late[1]),
            ],
            ways, where, items,
        )
        return (back, shares, last_sum(two_out, scatter))

    back, shares, two_sum = fenced(always, (), middle_part)
    backs.append(back)
    middle = Scatter(*shares)

    def attention_part():
        two_grads = along_z(two_sum)
        scatter = copy.copy(middle)

        def projection_part():
            grad_proj, *down = projection_backward(
                backs, cosines, sines, size, grad_two, stream_one, gain[1], w_qkv
            )
            return ((grad_proj, other_core(grad_proj)), down)

        grad_proj, (grad_one, half_one, gain_one) = fenced(always, (scatter,), projection_part)
        first = scatter.got
        scatter.second(second_sums(scatter)[0])

        def qkv_part():
            half_other = other_core(half_one)
            return (half_other, column_grads([ent_att], [grad_proj], ways, where, items))

        half_other, shares = fenced(always, (scatter,), qkv_part)
        attn = Scatter(*shares)

        def hidden_part():
            half_own, grad_pre = hidden_gradient(grad_one, slope_one, w_ffn1_out)
            shares = out_grad((half_own, half_other), hid_one, ways, where, items)
            return (grad_pre, shares)

        grad_pre, shares_out = fenced(always, (attn,), hidden_part)
        return (
            two_grads, first, scatter.got, (grad_one, gain_one), shares[:2], attn.got,
            grad_pre, shares_out,
        )

    two_grads, first, got, (grad_one, gain_one), shares, attn_got, grad_pre, shares_out = fenced(
        always, (), attention_part
    )
    middle.take(first)
    middle.take(got)
    attn = Scatter(*shares)
    attn.take(attn_got)
    attn.second(second_sums(attn)[0])
    one_out = Scatter(*shares_out)
    middle_columns = [w.shape[1] for w in (w_point_out, w_point_in, w_out)]
    def input_part():
        middle_grad = along_z(last_sum(middle, columns=middle_columns))
        grad_zero, _, gain_zero = stream_gradient(
            grad_one, stream, grad_pre, gain[0], w_ffn1_in, BF16
        )
        shares = column_grads([ent_one], [(grad_pre, other_core(grad_pre))], ways, where, items)
        return (middle_grad, shares, parted(grad_zero, side), gain_zero)

    middle_grad, shares, (grad_own, grad_theirs), gain_zero = fenced(
        always, (one_out, attn), input_part
    )
    one_in = Scatter(*shares)
    one_out.second(second_sums(one_out)[0])
    hidden = w_ffn1_in.shape[1]

    def tap_sums_here():
        rows_of = []
        for offset in range(KERNEL):
            same = (seg_wide[:, offset : offset + here] == seg_own)[:, :, None]
            product = grad_depth_low.astype(F32) * widened[:, offset : offset + here]
            rows_of.append(jnp.sum(jnp.where(same, product, 0.0), (0, 1))[None])
        return rows_of

    def last_part():
        grad_other = across(grad_theirs)
        attn_grad = along_z(last_sum(attn))
        out, scatter = copy.copy(one_out), copy.copy(one_in)
        fenced(always, (out,), lambda: ())
        out_grads = along_z(last_sum(out))
        fenced(always, (scatter,), lambda: ())
        scatter.second(second_sums(scatter)[0])
        fenced(always, (scatter,), lambda: ())
        last, grad_other = branched(
            always,
            lambda: (last_sum(scatter), grad_other),
        )
        small = sum_everywhere(
            jnp.concatenate(
                [gain_zero, gain_one, gain_two, gain_three, gain_four, gain_five]
                + tap_sums_here(),
                0,
            )
        )
        middle_parts = []
        start = 0
        for columns in middle_columns:
            each = columns // lax.axis_size("items")
            middle_parts.append(middle_grad[0][:, start : start + each].astype(F32))
            start += each
        ready = (
            gathered(out_own[None], out_other[None], side),
            gathered(grad_own[None], grad_other[None], side),
            attn_grad[0].astype(F32),
            middle_parts,
            two_grads[1].astype(F32),
            unfolded(two_grads[0], hidden // ways),
            unfolded(out_grads[0], hidden // ways),
        )
        return (along_z(last), small[:6], small[6:], ready)

    one_in_grad, gain_sums, tap_sums, ready = fenced(always, (), last_part)
    out, grad_in, attn_full, middle_parts, two_in_full, two_out_full, one_out_full = ready
    return (
        out,
        grad_in,
        gain_sums,
        one_in_grad[0].astype(F32),
        one_out_full,
        attn_full,
        middle_parts[2],
        middle_parts[1],
        tap_sums,
        middle_parts[0],
        two_in_full,
        two_out_full,
    )


def solution(mesh):
    split = P(None, EVERY, None)
    shares = P("heads", "items")
    in_specs = (split, split, P(None, "items", None)) + (P(),) * 10
    out_specs = (split, split, P(), shares, shares, shares, shares, shares, P()) + (shares,) * 3
    return jax.shard_map(body, mesh=mesh, in_specs=in_specs, out_specs=out_specs, check_vma=False)
```
